32 devices in a mesh: rows: 16 (over z, y, x), heads: 2 (over core).
Axes of the slice: x: 2, y: 2, z: 4, core: 2. Of those that a mesh axis runs over, the one named last changes fastest.
Arguments:
- dec_input: bfloat16 [24576, 512], P('rows'), may hold values from -6 to 6
- enc_output: bfloat16 [24576, 512], P('rows'), may hold values from -6 to 6
- dec_lengths: int32 [16, 16], P('rows'), may hold values from 1 to 768, 1536 in all within a row
- enc_lengths: int32 [16, 16], P('rows'), may hold values from 1 to 768, 1536 in all within a row
- w_self_qkv: bfloat16 [3, 512, 512], P(None, None, 'heads'), may hold values from -0.25 to 0.25
- w_self_out: bfloat16 [512, 512], P('heads'), may hold values from -1 to 1
- w_cross_q: bfloat16 [512, 512], P(None, 'heads'), may hold values from -0.25 to 0.25
- w_cross_kv: bfloat16 [2, 512, 512], P(None, None, 'heads'), may hold values from -0.25 to 0.25
- w_cross_out: bfloat16 [512, 512], P('heads'), may hold values from -1 to 1
- w_ffn_in: bfloat16 [512, 2048], P(None, 'heads'), may hold values from -0.25 to 0.25
- w_ffn_out: bfloat16 [2048, 512], P('heads'), may hold values from -0.125 to 0.125
- norm_gain: float32 [3, 512], replicated, may hold values from 0.25 to 1.75
- norm_bias: float32 [3, 512], replicated, may hold values from -1.75 to 1.75
- out_grad: bfloat16 [24576, 512], P('rows'), may hold values from -6 to 6
Outputs:
- layer_out: float32 [24576, 512], P(('rows', 'heads'))
- input_grad: float32 [24576, 512], P(('rows', 'heads'))
- enc_grad: float32 [24576, 512], P(('rows', 'heads'))
- grad_self_qkv: float32 [3, 512, 512], P(None, None, 'heads')
- grad_self_out: float32 [512, 512], P('heads')
- grad_cross_q: float32 [512, 512], P(None, 'heads')
- grad_cross_kv: float32 [2, 512, 512], P(None, None, 'heads')
- grad_cross_out: float32 [512, 512], P('heads')
- grad_ffn_in: float32 [512, 2048], P(None, 'heads')
- grad_ffn_out: float32 [2048, 512], P('heads')
- grad_norm_gain: float32 [3, 512], replicated
- grad_norm_bias: float32 [3, 512], replicated
The draws below stay inside these ranges and needn't reach their ends.
Inputs may be any that keep to these rules, and one draw needn't show every extreme that they name: `dec_lengths`: in every row the 16 lengths sum to 1536 and the largest is exactly 768. `enc_lengths`: in every row the 16 lengths sum to 1536 and the largest is exactly 768.
All inputs are finite; a program needn't handle non-finite values.
Results may differ from the reference program's by a relative error of at most 0.025.
The reference program's roundings to bfloat16 on the way count: a program that leaves them out, or rounds other values in their place, can miss the bound.
Values may be sent and summed in bfloat16 or wider, within the bound.
A program may use at most 256 MiB of HBM per device.

```python
import math
import jax
import jax.numpy as jnp
import numpy as np
from jax import lax

D = 512
HEADS = 8
FF = 2048
HEAD_DIM = 64
ROW_LEN = 1536
SEGS = 16
MOST = 768
ROWS = 16
TOKENS = 24576


def shard_levels(rng, dims, shards, low, top_value):
    factor_of, own = 1.0, jax.random.fold_in(rng, 6)
    for position, shards_of in shards:
        steps = jnp.exp(jax.random.uniform(jax.random.fold_in(own, position), (shards_of,), jnp.float32, low / len(shards), top_value / len(shards)))
        factor_of = factor_of * jnp.repeat(steps, dims[position] // shards_of).reshape([-1 if axis == position else 1 for axis in range(len(dims))])
    return factor_of


def length_profile(number_of, total, reach, skew):
    portions = [(1 << 20) // math.isqrt(standing ** skew) + 1 for standing in range(2, number_of + 1)]
    rest, holding = total - reach - (number_of - 1), [1] * (number_of - 1)
    while rest > 0:
        movable = [i for i in range(number_of - 1) if holding[i] < reach]
        whole, remaining = sum([portions[i] for i in movable]), rest
        for i in movable:
            more = min(reach - holding[i], max(1, remaining * portions[i] // whole), rest)
            holding[i] = holding[i] + more
            rest = rest - more
    return np.array([reach] + holding)


def ragged_sizes(rng, count, total, bound, lean):
    if count == 2:
        one = jax.random.randint(rng, (), max(1, total - bound), min(bound, total - 1) + 1)
        return jnp.stack([one, total - one])
    tallies = jnp.asarray(length_profile(count, total, bound, lean), jnp.int32)
    twos = (count - 1) // 2
    source_of, receiver = tallies[1:1 + 2 * twos:2], tallies[2:2 + 2 * twos:2]
    room = jnp.minimum(source_of - 1, bound - receiver)
    shifted = jax.random.randint(jax.random.fold_in(rng, 1), (twos,), 0, 1 << 20) % (room + 1)
    tallies = tallies.at[1:1 + 2 * twos:2].set(source_of - shifted).at[2:2 + 2 * twos:2].set(receiver + shifted)
    return tallies[jax.random.permutation(jax.random.fold_in(rng, 2), count)]


def scatter_about(stream_key, shape, width, limit, shards=(), kind=jnp.bfloat16):
    entries = width * jax.random.normal(stream_key, shape, jnp.float32)
    if shards:
        entries = entries * shard_levels(stream_key, shape, shards, -0.22, 0.18)
    return jnp.clip(entries, -limit, limit).astype(kind)


def setup_inputs(seed: int = 0) -> dict:
    arg_keys = jax.random.split(jax.random.key(seed), 15)
    dec_input = scatter_about(arg_keys[0], (TOKENS, D), 1.0, 6.0, ((0, 16),))
    enc_output = scatter_about(arg_keys[1], (TOKENS, D), 1.0, 6.0, ((0, 16),))
    dec_lengths = jax.vmap(lambda own: ragged_sizes(own, SEGS, ROW_LEN, MOST, 2))(jax.random.split(arg_keys[2], ROWS)).reshape((ROWS, SEGS)).astype(jnp.int32)
    enc_lengths = jax.vmap(lambda own: ragged_sizes(own, SEGS, ROW_LEN, MOST, 2))(jax.random.split(arg_keys[3], ROWS)).reshape((ROWS, SEGS)).astype(jnp.int32)
    w_self_qkv = scatter_about(arg_keys[4], (3, D, D), D ** -0.5, 0.25, ((2, 2),))
    w_self_out = scatter_about(arg_keys[5], (D, D), (D // 16) ** -0.5, 1.0, ((0, 2),))
    w_cross_q = scatter_about(arg_keys[6], (D, D), D ** -0.5, 0.25, ((1, 2),))
    w_cross_kv = scatter_about(arg_keys[7], (2, D, D), D ** -0.5, 0.25, ((2, 2),))
    w_cross_out = scatter_about(arg_keys[8], (D, D), (D // 16) ** -0.5, 1.0, ((0, 2),))
    w_ffn_in = scatter_about(arg_keys[9], (D, FF), D ** -0.5, 0.25, ((1, 2),))
    w_ffn_out = scatter_about(arg_keys[10], (FF, D), FF ** -0.5, 0.125, ((0, 2),))
    norm_gain = jnp.clip(1.0 + 0.15 * jax.random.normal(arg_keys[11], (3, D), jnp.float32), 0.25, 1.75)
    norm_bias = scatter_about(arg_keys[12], (3, D), 0.3, 1.75, (), jnp.float32)
    out_grad = scatter_about(arg_keys[13], (TOKENS, D), 1.0, 6.0, ((0, 16),))
    return {"dec_input": dec_input, "enc_output": enc_output, "dec_lengths": dec_lengths, "enc_lengths": enc_lengths, "w_self_qkv": w_self_qkv, "w_self_out": w_self_out, "w_cross_q": w_cross_q, "w_cross_kv": w_cross_kv, "w_cross_out": w_cross_out, "w_ffn_in": w_ffn_in, "w_ffn_out": w_ffn_out, "norm_gain": norm_gain, "norm_bias": norm_bias, "out_grad": out_grad}


NORM_EPS = 1e-05
MASKED_SCORE = -1e+30

@jax.custom_vjp
def low(v):
    return lax.optimization_barrier(v.astype(jnp.bfloat16)).astype(jnp.float32)

@jax.custom_vjp
def low_back(v):
    return v

def low_keep(v):
    return (low(v), None)

def low_pass(kept, grad):
    return (grad,)

def back_keep(v):
    return (v, None)

def back_low(kept, grad):
    return (low(grad),)
low.defvjp(low_keep, low_pass)
low_back.defvjp(back_keep, back_low)

def gelu_tanh(value):
    inner_arg = 0.7978845608028654 * (value + 0.044715 * value * value * value)
    return 0.5 * value * (1.0 + jnp.tanh(inner_arg))

def segment_ids(lengths, length):
    segment_ends = jnp.cumsum(lengths, axis=1)
    places = jnp.arange(length, dtype=jnp.int32)
    return lax.optimization_barrier(jnp.sum((places[None, :, None] >= segment_ends[:, None, :]).astype(jnp.int32), axis=2))

def exact_dot(left, right):
    return jnp.dot(left, right, precision=lax.Precision.HIGHEST)

def round_both(value):
    return low_back(low(value))

def layer_norm(summed, gain_row, bias_row):
    center = summed - lax.optimization_barrier(jnp.mean(summed, axis=1, keepdims=True))
    return center * lax.rsqrt(lax.optimization_barrier(jnp.mean(center * center, axis=1, keepdims=True)) + NORM_EPS) * gain_row + bias_row

def attend_row(row_inputs):
    query_row, key_row, value_row, query_ids, key_ids = row_inputs
    raw_scores = jnp.einsum('qhe,khe->hqk', query_row, key_row, precision=lax.Precision.HIGHEST) * HEAD_DIM ** (-0.5)
    scores = jnp.where((query_ids[:, None] == key_ids[None, :])[None], low_back(raw_scores), MASKED_SCORE)
    row_peak = lax.optimization_barrier(jnp.max(scores, axis=2, keepdims=True))
    raised = jnp.exp(scores - row_peak)
    weights = low(raised / lax.optimization_barrier(jnp.sum(raised, axis=2, keepdims=True)))
    return jnp.einsum('hqk,khe->qhe', weights, value_row, precision=lax.Precision.HIGHEST)

def attention(queries, keys, values, query_ids, key_ids):
    blocked = (ROWS, ROW_LEN, HEADS, HEAD_DIM)
    result = lax.map(jax.checkpoint(attend_row), (queries.reshape(blocked), keys.reshape(blocked), values.reshape(blocked), query_ids, key_ids))
    return result.reshape(TOKENS, D)

def reference(dec_input, enc_output, dec_lengths, enc_lengths, w_self_qkv, w_self_out, w_cross_q, w_cross_kv, w_cross_out, w_ffn_in, w_ffn_out, norm_gain, norm_bias, out_grad):
    dec_ids = segment_ids(dec_lengths, ROW_LEN)
    enc_ids = segment_ids(enc_lengths, ROW_LEN)

    def decoder_layer(inputs, encoded, self_qkv, self_out, cross_q, cross_kv, cross_out, ffn_in, ffn_out, gain_rows, biases):
        projected = round_both(jnp.einsum('td,cde->cte', inputs, self_qkv, precision=lax.Precision.HIGHEST))
        context = round_both(attention(projected[0], projected[1], projected[2], dec_ids, dec_ids))
        first_out = layer_norm(inputs + low_back(exact_dot(context, self_out)), gain_rows[0], biases[0])
        first_low = low(first_out)
        cross_query = round_both(exact_dot(first_low, cross_q))
        keys_values = round_both(jnp.einsum('td,cde->cte', encoded, cross_kv, precision=lax.Precision.HIGHEST))
        cross_context = round_both(attention(cross_query, keys_values[0], keys_values[1], dec_ids, enc_ids))
        second_out = layer_norm(first_out + low_back(exact_dot(cross_context, cross_out)), gain_rows[1], biases[1])
        second_low = low(second_out)
        hidden = low(gelu_tanh(low_back(exact_dot(second_low, ffn_in))))
        return layer_norm(second_out + low_back(exact_dot(hidden, ffn_out)), gain_rows[2], biases[2])
    layer_out, pullback = jax.vjp(decoder_layer, dec_input.astype(jnp.float32), enc_output.astype(jnp.float32), w_self_qkv.astype(jnp.float32), w_self_out.astype(jnp.float32), w_cross_q.astype(jnp.float32), w_cross_kv.astype(jnp.float32), w_cross_out.astype(jnp.float32), w_ffn_in.astype(jnp.float32), w_ffn_out.astype(jnp.float32), norm_gain, norm_bias)
    gradients = pullback(out_grad.astype(jnp.float32))
    return (layer_out, gradients[0], gradients[1], gradients[2], gradients[3], gradients[4], gradients[5], gradients[6], gradients[7], gradients[8], gradients[9], gradients[10])
```

```python
import functools

import jax
import jax.numpy as jnp
from jax import lax
from jax.experimental import pallas as pl
from jax.experimental.pallas import tpu as pltpu
from jax.sharding import PartitionSpec as P

HEAD_DIM = 64
LANES = 128
SPAN = 256
NORM_EPS = 1e-05
MASKED_SCORE = -1e30
LOG2_E = 1.4426950408889634
GELU_RATE = 0.7978845608028654
GELU_CUBE = 0.044715
F32 = jnp.float32
BF16 = jnp.bfloat16
NT = (((1,), (1,)), ((), ()))
TN = (((0,), (0,)), ((), ()))
VMEM = pl.BlockSpec(memory_space=pltpu.VMEM)
SMEM = pl.BlockSpec(memory_space=pltpu.SMEM)


def dot(left, right):
    return jnp.dot(left, right, preferred_element_type=F32)


def dot_nt(left, right):
    return lax.dot_general(left, right, NT, preferred_element_type=F32)


def dot_tn(left, right):
    return lax.dot_general(left, right, TN, preferred_element_type=F32)


def shape_of(dims, kind):
    return jax.ShapeDtypeStruct(dims, kind)


def call(kernel, outs, scratch, mib, *args, smem=0):
    return pl.pallas_call(
        kernel,
        out_shape=outs,
        in_specs=[SMEM] * smem + [VMEM] * (len(args) - smem),
        out_specs=jax.tree.map(lambda _: VMEM, outs),
        scratch_shapes=scratch,
        compiler_params=pltpu.CompilerParams(vmem_limit_bytes=mib * 2**20),
    )(*args)


def segment_bounds(len_ref):
    starts, ends, total = [], [], jnp.int32(0)
    for k in range(len_ref.shape[1]):
        starts.append(total)
        total = total + len_ref[0, k]
        ends.append(total)
    return starts, ends


def bound_lanes(starts, ends):
    lane = lax.broadcasted_iota(jnp.int32, (1, LANES), 1)
    first = jnp.full((1, LANES), 1 << 30, jnp.int32)
    last = jnp.zeros((1, LANES), jnp.int32)
    for k, (start, end) in enumerate(zip(starts, ends)):
        first = jnp.where(lane == HEAD_DIM + k, start, first)
        last = jnp.where(lane == HEAD_DIM + k, end, last)
    return first, last


def lanes_of(rows):
    return lax.broadcasted_iota(jnp.int32, (rows, LANES), 1)


def membership(first_row, rows, bounds):
    place = lax.broadcasted_iota(jnp.int32, (rows, LANES), 0) + first_row
    return (place >= bounds[0]) & (place < bounds[1])


def query_extra(first_row, rows, bounds):
    return jnp.where(membership(first_row, rows, bounds), F32(MASKED_SCORE), F32(0.0))


def key_extra(first_row, rows, bounds, segs):
    lane = lanes_of(rows)
    used = (lane >= HEAD_DIM) & (lane < HEAD_DIM + segs + 3)
    return jnp.where(used & ~membership(first_row, rows, bounds), F32(1.0), F32(0.0))


def value_extra(rows):
    lane = lanes_of(rows)
    return jnp.where((lane >= HEAD_DIM) & (lane < HEAD_DIM + 2), F32(1.0), F32(0.0))


def head_slab(wide, head):
    if wide.shape[1] < LANES:
        return jnp.concatenate([wide, jnp.zeros_like(wide)], axis=1)
    first = head // 2 * LANES
    slab = wide[:, first : first + LANES]
    if head % 2:
        slab = pltpu.roll(slab, HEAD_DIM, 1)
    return slab


def put_heads(dest, where, wide, extra):
    low_lanes = lanes_of(wide.shape[0]) < HEAD_DIM
    for head in range(dest.shape[0]):
        dest[head, where, :] = jnp.where(low_lanes, head_slab(wide, head), extra).astype(dest.dtype)


def join_heads(dest, where, slabs):
    if len(slabs) == 1:
        dest[where, :] = slabs[0][:, :HEAD_DIM].astype(dest.dtype)
        return
    low_lanes = lanes_of(slabs[0].shape[0]) < HEAD_DIM
    for pair in range(len(slabs) // 2):
        both = jnp.where(low_lanes, slabs[2 * pair], pltpu.roll(slabs[2 * pair + 1], HEAD_DIM, 1))
        dest[where, pair * LANES : (pair + 1) * LANES] = both.astype(dest.dtype)


def span_for(block, length, from_starts, to_starts, to_ends):
    first_row = block * SPAN
    last_row = first_row + SPAN - 1
    low, high = jnp.int32(0), jnp.int32(0)
    for start, to_start, to_end in zip(from_starts, to_starts, to_ends):
        low = jnp.where(start <= first_row, to_start, low)
        high = jnp.where(start <= last_row, to_end, high)
    low = (low >> 7) << 7
    pieces = (high - low + SPAN - 1) >> 8
    return jnp.minimum(low, length - pieces * SPAN), pieces


def each_span(length, starts_from, starts_to, ends_to, body):
    def step(block, carry):
        start, pieces = span_for(block, length, starts_from, starts_to, ends_to)
        start = pl.multiple_of(start, LANES)
        rows = pl.ds(pl.multiple_of(block * SPAN, SPAN), SPAN)
        for count in range(1, length // SPAN + 1):

            @pl.when(pieces == count)
            def _():
                body(rows, pl.ds(start, count * SPAN))

        return carry

    lax.fori_loop(0, length // SPAN, step, 0)


def attend_body(qx, kx, vx, ctx, segs, rows, keys):
    scale = LOG2_E * HEAD_DIM**-0.5
    lane = lanes_of(SPAN)
    slabs = []
    for head in range(qx.shape[0]):
        query = qx[head, rows, :]
        scores = dot_nt(query, kx[head, keys, :])
        peak = jnp.max(scores, axis=1, keepdims=True)
        raised = jnp.exp2((scores - peak) * scale).astype(BF16)
        mixed = dot(raised, vx[head, keys, :])
        total = mixed[:, HEAD_DIM : HEAD_DIM + 1]
        slabs.append(mixed / total)
        level = -(peak + jnp.log(total) * (HEAD_DIM**0.5))
        high = level.astype(BF16).astype(F32)
        middle = (level - high).astype(BF16).astype(F32)
        low = level - high - middle
        base = HEAD_DIM + segs
        wide = query.astype(F32)
        wide = jnp.where(lane == base, high, wide)
        wide = jnp.where(lane == base + 1, middle, wide)
        wide = jnp.where(lane == base + 2, low, wide)
        qx[head, rows, :] = wide.astype(BF16)
    join_heads(ctx, rows, slabs)


def split_out(source, keep, send, share):
    me = lax.axis_index("heads")
    parts = send.shape[0] + 1
    for k in range(parts):
        owner = lax.rem(me + k, parts)
        rows = pl.ds(pl.multiple_of(owner * share, share), share)
        if k == 0:
            keep[...] = source[rows, :].astype(keep.dtype)
        else:
            send[k - 1] = source[rows, :].astype(send.dtype)


def self_forward_kernel(len_ref, x_ref, w_ref, keep, send, ctx, qx, kx, vx):
    length = x_ref.shape[0]
    segs = len_ref.shape[1]
    starts, ends = segment_bounds(len_ref)
    bounds = bound_lanes(starts, ends)

    def project(block, carry):
        first = pl.multiple_of(block * SPAN, SPAN)
        rows = pl.ds(first, SPAN)
        tokens = x_ref[rows, :]
        put_heads(qx, rows, dot(tokens, w_ref[0]), query_extra(first, SPAN, bounds))
        put_heads(kx, rows, dot(tokens, w_ref[1]), key_extra(first, SPAN, bounds, segs))
        put_heads(vx, rows, dot(tokens, w_ref[2]), value_extra(SPAN))
        return carry

    lax.fori_loop(0, length // SPAN, project, 0)
    each_span(
        length, starts, starts, ends, functools.partial(attend_body, qx, kx, vx, ctx, segs)
    )
    split_out(ctx, keep, send, keep.shape[0])


def cross_keys_kernel(len_ref, x_ref, w_ref, kx, vx):
    length = x_ref.shape[0]
    bounds = bound_lanes(*segment_bounds(len_ref))
    segs = len_ref.shape[1]

    def project(block, carry):
        first = pl.multiple_of(block * SPAN, SPAN)
        rows = pl.ds(first, SPAN)
        tokens = x_ref[rows, :]
        put_heads(kx, rows, dot(tokens, w_ref[0]), key_extra(first, SPAN, bounds, segs))
        put_heads(vx, rows, dot(tokens, w_ref[1]), value_extra(SPAN))
        return carry

    lax.fori_loop(0, length // SPAN, project, 0)


def gather_rows(dest, own, others):
    me = lax.axis_index("heads")
    parts = len(others) + 1
    share = own.shape[0]
    for k, source in enumerate([own, *others]):
        owner = lax.rem(me + k, parts)
        dest[pl.ds(pl.multiple_of(owner * share, share), share), :] = source[...]


def cross_forward_kernel(parts, dec_ref, enc_ref, kx, vx, *refs):
    pieces, (keep, send, ctx, qx, flat) = refs[:parts], refs[parts:]
    length = ctx.shape[0]
    segs = dec_ref.shape[1]
    dec_starts, dec_ends = segment_bounds(dec_ref)
    enc_starts, enc_ends = segment_bounds(enc_ref)
    bounds = bound_lanes(dec_starts, dec_ends)
    gather_rows(flat, pieces[0], pieces[1:])

    def widen(block, carry):
        first = pl.multiple_of(block * SPAN, SPAN)
        rows = pl.ds(first, SPAN)
        put_heads(qx, rows, flat[rows, :].astype(F32), query_extra(first, SPAN, bounds))
        return carry

    lax.fori_loop(0, length // SPAN, widen, 0)
    each_span(
        length, dec_starts, enc_starts, enc_ends,
        functools.partial(attend_body, qx, kx, vx, ctx, segs),
    )
    split_out(ctx, keep, send, keep.shape[0])


def attend_back_body(qx, kx, vx, gx, dq, dk, dv, rows, queries):
    scale = LOG2_E * HEAD_DIM**-0.5
    key_slabs, value_slabs = [], []
    for head in range(qx.shape[0]):
        keys = kx[head, rows, :]
        query = qx[head, queries, :]
        grads = gx[head, queries, :]
        weights = jnp.exp2(dot_nt(keys, query) * scale)
        raised = dot_nt(vx[head, rows, :], grads)
        value_slabs.append(dot(weights.astype(BF16), grads))
        inner = (weights * raised).astype(BF16)
        key_slabs.append(dot(inner, query) * (HEAD_DIM**-0.5))
        dq[head, queries, :] += dot_tn(inner, keys)
    join_heads(dk, rows, key_slabs)
    join_heads(dv, rows, value_slabs)


def attend_back(key_starts, key_ends, query_starts, query_ends, qx, kx, vx, ctx, grad, gx, dq, sq, sk, sv):
    length = ctx.shape[0]
    heads = qx.shape[0]
    lane = lanes_of(SPAN)

    def widen(block, carry):
        rows = pl.ds(pl.multiple_of(block * SPAN, SPAN), SPAN)
        wide = grad[rows, :].astype(F32)
        product = wide * ctx[rows, :].astype(F32)
        for head in range(heads):
            slab = head_slab(product, head)
            level = -jnp.sum(jnp.where(lane < HEAD_DIM, slab, 0.0), axis=1, keepdims=True)
            high = level.astype(BF16).astype(F32)
            extra = jnp.where(lane == HEAD_DIM, high, 0.0)
            extra = jnp.where(lane == HEAD_DIM + 1, level - high, extra)
            full = jnp.where(lane < HEAD_DIM, head_slab(wide, head), extra)
            gx[head, rows, :] = full.astype(BF16)
            dq[head, rows, :] = jnp.zeros((SPAN, LANES), F32)
        return carry

    lax.fori_loop(0, length // SPAN, widen, 0)
    each_span(
        length, key_starts, query_starts, query_ends,
        functools.partial(attend_back_body, qx, kx, vx, gx, dq, sk, sv),
    )

    def finish(block, carry):
        rows = pl.ds(pl.multiple_of(block * SPAN, SPAN), SPAN)
        join_heads(sq, rows, [dq[head, rows, :] * (HEAD_DIM**-0.5) for head in range(heads)])
        return carry

    lax.fori_loop(0, length // SPAN, finish, 0)


def norm_forward(summed, gain, bias):
    center = summed - jnp.mean(summed, axis=1, keepdims=True)
    inverse_dev = lax.rsqrt(jnp.mean(center * center, axis=1, keepdims=True) + NORM_EPS)
    normed = center * inverse_dev
    return normed * gain + bias, normed, inverse_dev


def norm_back(grad, normed, inverse_dev, gain):
    scaled = grad * gain
    back = inverse_dev * (
        scaled
        - jnp.mean(scaled, axis=1, keepdims=True)
        - normed * jnp.mean(scaled * normed, axis=1, keepdims=True)
    )
    gain_grad = jnp.sum(grad * normed, axis=0, keepdims=True)
    return back, gain_grad, jnp.sum(grad, axis=0, keepdims=True)


def share_block(share):
    return 256 if share % 256 == 0 else share


def own_rows(share, first, rows):
    start = lax.axis_index("heads") * share + first
    return pl.ds(pl.multiple_of(start, 64), rows)


def first_norm_kernel(parts, x_ref, gain, bias, *refs):
    ctx, w_out, w_query = refs[:parts], refs[parts : 2 * parts], refs[2 * parts : 3 * parts]
    first_out, first_low, normed_out, dev_out, keep, send = refs[3 * parts :]
    share = first_out.shape[0]
    block = share_block(share)

    def step(index, carry):
        first = pl.multiple_of(index * block, block)
        rows = pl.ds(first, block)
        total = x_ref[own_rows(share, first, block), :].astype(F32)
        for k in range(parts):
            total = total + dot(ctx[k][rows, :], w_out[k][...])
        result, normed, inverse_dev = norm_forward(total, gain[0:1, :], bias[0:1, :])
        low = result.astype(BF16)
        first_out[rows, :] = result
        first_low[rows, :] = low
        normed_out[rows, :] = normed
        dev_out[rows, :] = inverse_dev
        for k in range(parts):
            value = dot(low, w_query[k][...]).astype(BF16)
            if k == 0:
                keep[rows, :] = value
            else:
                send[k - 1, rows, :] = value
        return carry

    lax.fori_loop(0, share // block, step, 0)


def middle_kernel(parts, gain, bias, first_out, out_grad, *refs):
    groups = [refs[g * parts : (g + 1) * parts] for g in range(4)]
    ctx, w_cross, w_in, w_out = groups
    (layer_out, grad_mid, gains, biases, g_out_keep, g_out_send, g_in_keep, g_in_send,
     g_cross_keep, g_cross_send, back_keep, back_send,
     second, second_low, normed2, dev2, total, hidden, slope, top_low, back_sum) = refs[4 * parts :]
    share = first_out.shape[0]
    block = share_block(share)
    units = w_in[0].shape[1]
    chunk = min(256, units)

    def enter(index, carry):
        rows = pl.ds(pl.multiple_of(index * block, block), block)
        summed = first_out[rows, :]
        for k in range(parts):
            summed = summed + dot(ctx[k][rows, :], w_cross[k][...])
        result, normed, inverse_dev = norm_forward(summed, gain[1:2, :], bias[1:2, :])
        second[rows, :] = result
        second_low[rows, :] = result.astype(BF16)
        normed2[rows, :] = normed
        dev2[rows, :] = inverse_dev
        return carry

    lax.fori_loop(0, share // block, enter, 0)
    total[...] = second[...]
    for k in range(parts):

        def expand(index, carry):
            cols = pl.ds(pl.multiple_of(index * chunk, chunk), chunk)
            spot = k * (units // chunk) + index
            pre = dot(second_low[...], w_in[k][:, cols])
            square = pre * pre
            bent = jnp.tanh(pre * (GELU_RATE + (GELU_RATE * GELU_CUBE) * square))
            half = 0.5 + 0.5 * bent
            act = (pre * half).astype(BF16)
            hidden[spot] = act
            bend = (0.5 - 0.5 * bent * bent) * (
                GELU_RATE + (3.0 * GELU_RATE * GELU_CUBE) * square
            )
            slope[spot] = half + pre * bend
            total[...] += dot(act, w_out[k][cols, :])
            return carry

        lax.fori_loop(0, units // chunk, expand, 0)

    gains[...] = jnp.zeros_like(gains)
    biases[...] = jnp.zeros_like(biases)

    def turn(index, carry):
        first = pl.multiple_of(index * block, block)
        rows = pl.ds(first, block)
        result, normed, inverse_dev = norm_forward(total[rows, :], gain[2:3, :], bias[2:3, :])
        layer_out[rows, :] = result
        grad = out_grad[own_rows(share, first, block), :].astype(F32)
        back, gain_grad, bias_grad = norm_back(grad, normed, inverse_dev, gain[2:3, :])
        gains[1:2, :] += gain_grad
        biases[1:2, :] += bias_grad
        back_sum[rows, :] = back
        top_low[rows, :] = back.astype(BF16)
        return carry

    lax.fori_loop(0, share // block, turn, 0)
    for k in range(parts):

        def contract(index, carry):
            cols = pl.ds(pl.multiple_of(index * chunk, chunk), chunk)
            spot = k * (units // chunk) + index
            weight_out = dot_tn(hidden[spot], top_low[...]).astype(BF16)
            pre = (dot_nt(top_low[...], w_out[k][cols, :]) * slope[spot]).astype(BF16)
            weight_in = dot_tn(second_low[...], pre).astype(BF16)
            if k == 0:
                g_out_keep[cols, :] = weight_out
                g_in_keep[:, cols] = weight_in
            else:
                g_out_send[k - 1, cols, :] = weight_out
                g_in_send[k - 1, :, cols] = weight_in
            back_sum[...] += dot_nt(pre, w_in[k][:, cols])
            return carry

        lax.fori_loop(0, units // chunk, contract, 0)

    def leave(index, carry):
        rows = pl.ds(pl.multiple_of(index * block, block), block)
        back, gain_grad, bias_grad = norm_back(
            back_sum[rows, :], normed2[rows, :], dev2[rows, :], gain[1:2, :]
        )
        gains[0:1, :] += gain_grad
        biases[0:1, :] += bias_grad
        grad_mid[rows, :] = back
        low = back.astype(BF16)
        top_low[rows, :] = low
        for k in range(parts):
            value = dot_nt(low, w_cross[k][...]).astype(BF16)
            if k == 0:
                back_keep[rows, :] = value
            else:
                back_send[k - 1, rows, :] = value
        return carry

    lax.fori_loop(0, share // block, leave, 0)
    for k in range(parts):
        value = dot_tn(ctx[k][...], top_low[...]).astype(BF16)
        if k == 0:
            g_cross_keep[...] = value
        else:
            g_cross_send[k - 1] = value


def cross_back_kernel(parts, dec_ref, enc_ref, qx, kx, vx, ctx, enc, w_kv, *refs):
    pieces = refs[:parts]
    (gq_keep, gq_send, g_kv, enc_keep, enc_send, grad, gx, dq, sq, sk, sv, wide) = refs[parts:]
    length = ctx.shape[0]
    dec_starts, dec_ends = segment_bounds(dec_ref)
    enc_starts, enc_ends = segment_bounds(enc_ref)
    gather_rows(grad, pieces[0], pieces[1:])
    attend_back(
        enc_starts, enc_ends, dec_starts, dec_ends, qx, kx, vx, ctx, grad, gx, dq, sq, sk, sv
    )
    split_out(sq, gq_keep, gq_send, gq_keep.shape[0])
    g_kv[0] = dot_tn(enc[...], sk[...]).astype(BF16)
    g_kv[1] = dot_tn(enc[...], sv[...]).astype(BF16)

    def step(block, carry):
        rows = pl.ds(pl.multiple_of(block * SPAN, SPAN), SPAN)
        wide[rows, :] = dot_nt(sk[rows, :], w_kv[0]) + dot_nt(sv[rows, :], w_kv[1])
        return carry

    lax.fori_loop(0, length // SPAN, step, 0)
    split_out(wide, enc_keep, enc_send, enc_keep.shape[0])


def first_back_kernel(parts, gain, grad_mid, first_low, normed, dev, *refs):
    groups = [refs[g * parts : (g + 1) * parts] for g in range(4)]
    gq, w_query, ctx, w_out = groups
    (grad_base, gains, biases, g_query_keep, g_query_send, g_out_keep, g_out_send,
     back_keep, back_send, low_ref) = refs[4 * parts :]
    share = grad_mid.shape[0]
    block = share_block(share)
    gains[...] = jnp.zeros_like(gains)
    biases[...] = jnp.zeros_like(biases)

    def step(index, carry):
        rows = pl.ds(pl.multiple_of(index * block, block), block)
        grad = grad_mid[rows, :]
        for k in range(parts):
            grad = grad + dot_nt(gq[k][rows, :], w_query[k][...])
        back, gain_grad, bias_grad = norm_back(grad, normed[rows, :], dev[rows, :], gain[0:1, :])
        gains[...] += gain_grad
        biases[...] += bias_grad
        grad_base[rows, :] = back
        low = back.astype(BF16)
        low_ref[rows, :] = low
        for k in range(parts):
            value = dot_nt(low, w_out[k][...]).astype(BF16)
            if k == 0:
                back_keep[rows, :] = value
            else:
                back_send[k - 1, rows, :] = value
        return carry

    lax.fori_loop(0, share // block, step, 0)
    for k in range(parts):
        query_grad = dot_tn(first_low[...], gq[k][...]).astype(BF16)
        out_grad = dot_tn(ctx[k][...], low_ref[...]).astype(BF16)
        if k == 0:
            g_query_keep[...] = query_grad
            g_out_keep[...] = out_grad
        else:
            g_query_send[k - 1] = query_grad
            g_out_send[k - 1] = out_grad


def self_back_kernel(parts, dec_ref, qx, kx, vx, ctx, x_ref, w_qkv, *refs):
    pieces = refs[:parts]
    g_qkv, in_keep, in_send, grad, gx, dq, sq, sk, sv, wide = refs[parts:]
    length = ctx.shape[0]
    starts, ends = segment_bounds(dec_ref)
    gather_rows(grad, pieces[0], pieces[1:])
    attend_back(starts, ends, starts, ends, qx, kx, vx, ctx, grad, gx, dq, sq, sk, sv)
    for c, source in enumerate((sq, sk, sv)):
        g_qkv[c] = dot_tn(x_ref[...], source[...]).astype(BF16)

    def step(block, carry):
        rows = pl.ds(pl.multiple_of(block * SPAN, SPAN), SPAN)
        wide[rows, :] = (
            dot_nt(sq[rows, :], w_qkv[0])
            + dot_nt(sk[rows, :], w_qkv[1])
            + dot_nt(sv[rows, :], w_qkv[2])
        )
        return carry

    lax.fori_loop(0, length // SPAN, step, 0)
    split_out(wide, in_keep, in_send, in_keep.shape[0])


def body(
    dec_input,
    enc_output,
    dec_lengths,
    enc_lengths,
    w_self_qkv,
    w_self_out,
    w_cross_q,
    w_cross_kv,
    w_cross_out,
    w_ffn_in,
    w_ffn_out,
    norm_gain,
    norm_bias,
    out_grad,
):
    parts = lax.axis_size("heads")
    length, width = dec_input.shape
    local = w_self_out.shape[0]
    heads = local // HEAD_DIM
    share = length // parts
    units = w_ffn_in.shape[1]
    chunk = min(256, units)
    chunks = parts * units // chunk

    def shift(value, k):
        return lax.ppermute(value, "heads", [(d, (d + k) % parts) for d in range(parts)])

    def slots(shard):
        return [shard] + [shift(shard, parts - k) for k in range(1, parts)]

    def swap(keep, send):
        return [keep] + [shift(send[parts - k - 1], parts - k) for k in range(1, parts)]

    def collect(keep, send):
        total = keep.astype(F32)
        for k in range(1, parts):
            total = total + shift(send[k - 1], k).astype(F32)
        return total

    self_out, cross_q, cross_out = slots(w_self_out), slots(w_cross_q), slots(w_cross_out)
    ffn_in, ffn_out = slots(w_ffn_in), slots(w_ffn_out)

    def sent(*dims, kind=BF16):
        return shape_of((parts - 1, *dims), kind)

    def own(*dims, kind=BF16):
        return shape_of(dims, kind)

    wide_heads = own(heads, length, LANES)
    self_keep, self_send, self_ctx, self_qx, self_kx, self_vx = call(
        self_forward_kernel,
        [own(share, local), sent(share, local), own(length, local), wide_heads, wide_heads, wide_heads],
        [], 40, dec_lengths, dec_input, w_self_qkv, smem=1,
    )
    self_slots = swap(self_keep, self_send)
    cross_kx, cross_vx = call(
        cross_keys_kernel, [wide_heads, wide_heads], [], 32,
        enc_lengths, enc_output, w_cross_kv, smem=1,
    )
    first_out, first_low, first_normed, first_dev, query_keep, query_send = call(
        functools.partial(first_norm_kernel, parts),
        [own(share, width, kind=F32), own(share, width), own(share, width, kind=F32),
         own(share, 1, kind=F32), own(share, local), sent(share, local)],
        [], 32, dec_input, norm_gain, norm_bias, *self_slots, *self_out, *cross_q,
    )
    cross_keep, cross_send, cross_ctx, cross_qx = call(
        functools.partial(cross_forward_kernel, parts),
        [own(share, local), sent(share, local), own(length, local), wide_heads],
        [pltpu.VMEM((length, local), BF16)], 40,
        dec_lengths, enc_lengths, cross_kx, cross_vx, *swap(query_keep, query_send), smem=2,
    )
    cross_slots = swap(cross_keep, cross_send)
    (layer_out, grad_mid, gains_high, biases_high, g_ffn_out, g_ffn_out_send, g_ffn_in,
     g_ffn_in_send, g_cross_out, g_cross_out_send, back_keep, back_send) = call(
        functools.partial(middle_kernel, parts),
        [own(share, width, kind=F32), own(share, width, kind=F32),
         own(2, width, kind=F32), own(2, width, kind=F32),
         own(units, width), sent(units, width), own(width, units), sent(width, units),
         own(local, width), sent(local, width), own(share, local), sent(share, local)],
        [pltpu.VMEM((share, width), F32), pltpu.VMEM((share, width), BF16),
         pltpu.VMEM((share, width), F32), pltpu.VMEM((share, 1), F32),
         pltpu.VMEM((share, width), F32), pltpu.VMEM((chunks, share, chunk), BF16),
         pltpu.VMEM((chunks, share, chunk), F32), pltpu.VMEM((share, width), BF16),
         pltpu.VMEM((share, width), F32)],
        56, norm_gain, norm_bias, first_out, out_grad,
        *cross_slots, *cross_out, *ffn_in, *ffn_out,
    )
    back_scratch = [
        pltpu.VMEM((length, local), BF16),
        pltpu.VMEM((heads, length, LANES), BF16),
        pltpu.VMEM((heads, length, LANES), F32),
        pltpu.VMEM((length, local), BF16),
        pltpu.VMEM((length, local), BF16),
        pltpu.VMEM((length, local), BF16),
        pltpu.VMEM((length, width), F32),
    ]
    gq_keep, gq_send, g_cross_kv, enc_keep, enc_send = call(
        functools.partial(cross_back_kernel, parts),
        [own(share, local), sent(share, local), own(2, width, local),
         own(share, width, kind=F32), sent(share, width)],
        back_scratch, 56, dec_lengths, enc_lengths, cross_qx, cross_kx, cross_vx, cross_ctx,
        enc_output, w_cross_kv, *swap(back_keep, back_send), smem=2,
    )
    enc_grad = collect(enc_keep, enc_send)
    (grad_base, gains_low, biases_low, g_cross_q, g_cross_q_send, g_self_out, g_self_out_send,
     self_back_keep, self_back_send) = call(
        functools.partial(first_back_kernel, parts),
        [own(share, width, kind=F32), own(1, width, kind=F32), own(1, width, kind=F32),
         own(width, local), sent(width, local), own(local, width), sent(local, width),
         own(share, local), sent(share, local)],
        [pltpu.VMEM((share, width), BF16)], 40,
        norm_gain, grad_mid, first_low, first_normed, first_dev,
        *swap(gq_keep, gq_send), *cross_q, *self_slots, *self_out,
    )
    g_self_qkv, in_keep, in_send = call(
        functools.partial(self_back_kernel, parts),
        [own(3, width, local), own(share, width, kind=F32), sent(share, width)],
        back_scratch, 56, dec_lengths, self_qx, self_kx, self_vx, self_ctx, dec_input,
        w_self_qkv, *swap(self_back_keep, self_back_send), smem=1,
    )
    input_grad = grad_base + collect(in_keep, in_send)

    def over_rows(value):
        return lax.psum(value.astype(BF16), "rows").astype(F32)

    return (
        layer_out,
        input_grad,
        enc_grad,
        over_rows(g_self_qkv),
        over_rows(collect(g_self_out, g_self_out_send)),
        over_rows(collect(g_cross_q, g_cross_q_send)),
        over_rows(g_cross_kv),
        over_rows(collect(g_cross_out, g_cross_out_send)),
        over_rows(collect(g_ffn_in, g_ffn_in_send)),
        over_rows(collect(g_ffn_out, g_ffn_out_send)),
        lax.psum(jnp.concatenate([gains_low, gains_high]), ("rows", "heads")),
        lax.psum(jnp.concatenate([biases_low, biases_high]), ("rows", "heads")),
    )


def solution(mesh):
    in_specs = (
        P("rows", None),
        P("rows", None),
        P("rows", None),
        P("rows", None),
        P(None, None, "heads"),
        P("heads", None),
        P(None, "heads"),
        P(None, None, "heads"),
        P("heads", None),
        P(None, "heads"),
        P("heads", None),
        P(),
        P(),
        P("rows", None),
    )
    out_specs = (
        P(("rows", "heads"), None),
        P(("rows", "heads"), None),
        P(("rows", "heads"), None),
        P(None, None, "heads"),
        P("heads", None),
        P(None, "heads"),
        P(None, None, "heads"),
        P("heads", None),
        P(None, "heads"),
        P("heads", None),
        P(),
        P(),
    )
    return jax.shard_map(body, mesh=mesh, in_specs=in_specs, out_specs=out_specs, check_vma=False)
```

```python
import functools

import jax
import jax.numpy as jnp
from jax import lax
from jax.experimental import pallas as pl
from jax.experimental.pallas import tpu as pltpu
from jax.sharding import PartitionSpec as P

HEAD_DIM = 64
LANES = 128
SPAN = 256
NORM_EPS = 1e-05
MASKED_SCORE = -1e30
LOG2_E = 1.4426950408889634
GELU_RATE = 0.7978845608028654
GELU_CUBE = 0.044715
F32 = jnp.float32
BF16 = jnp.bfloat16
NT = (((1,), (1,)), ((), ()))
TN = (((0,), (0,)), ((), ()))
VMEM = pl.BlockSpec(memory_space=pltpu.VMEM)
SMEM = pl.BlockSpec(memory_space=pltpu.SMEM)


def dot(left, right):
    return jnp.dot(left, right, preferred_element_type=F32)


def dot_nt(left, right):
    return lax.dot_general(left, right, NT, preferred_element_type=F32)


def dot_tn(left, right):
    return lax.dot_general(left, right, TN, preferred_element_type=F32)


def shape_of(dims, kind):
    return jax.ShapeDtypeStruct(dims, kind)


def call(kernel, outs, scratch, mib, *args, smem=0):
    return pl.pallas_call(
        kernel,
        out_shape=outs,
        in_specs=[SMEM] * smem + [VMEM] * (len(args) - smem),
        out_specs=jax.tree.map(lambda _: VMEM, outs),
        scratch_shapes=scratch,
        compiler_params=pltpu.CompilerParams(vmem_limit_bytes=mib * 2**20),
    )(*args)


def segment_bounds(len_ref):
    starts, ends, total = [], [], jnp.int32(0)
    for k in range(len_ref.shape[1]):
        starts.append(total)
        total = total + len_ref[0, k]
        ends.append(total)
    return starts, ends


def bound_lanes(starts, ends):
    lane = lax.broadcasted_iota(jnp.int32, (1, LANES), 1)
    first = jnp.full((1, LANES), 1 << 30, jnp.int32)
    last = jnp.zeros((1, LANES), jnp.int32)
    for k, (start, end) in enumerate(zip(starts, ends)):
        first = jnp.where(lane == HEAD_DIM + k, start, first)
        last = jnp.where(lane == HEAD_DIM + k, end, last)
    return first, last


def lanes_of(rows):
    return lax.broadcasted_iota(jnp.int32, (rows, LANES), 1)


def membership(first_row, rows, bounds):
    place = lax.broadcasted_iota(jnp.int32, (rows, LANES), 0) + first_row
    return (place >= bounds[0]) & (place < bounds[1])


def query_extra(first_row, rows, bounds):
    return jnp.where(membership(first_row, rows, bounds), F32(MASKED_SCORE), F32(0.0))


def key_extra(first_row, rows, bounds, segs):
    lane = lanes_of(rows)
    used = (lane >= HEAD_DIM) & (lane < HEAD_DIM + segs + 3)
    return jnp.where(used & ~membership(first_row, rows, bounds), F32(1.0), F32(0.0))


def value_extra(rows):
    lane = lanes_of(rows)
    return jnp.where((lane >= HEAD_DIM) & (lane < HEAD_DIM + 2), F32(1.0), F32(0.0))


def head_slab(wide, head):
    if wide.shape[1] < LANES:
        return jnp.concatenate([wide, jnp.zeros_like(wide)], axis=1)
    first = head // 2 * LANES
    slab = wide[:, first : first + LANES]
    if head % 2:
        slab = pltpu.roll(slab, HEAD_DIM, 1)
    return slab


def put_heads(dest, where, wide, extra):
    low_lanes = lanes_of(wide.shape[0]) < HEAD_DIM
    for head in range(dest.shape[0]):
        dest[head, where, :] = jnp.where(low_lanes, head_slab(wide, head), extra).astype(dest.dtype)


def join_heads(dest, where, slabs):
    if len(slabs) == 1:
        dest[where, :] = slabs[0][:, :HEAD_DIM].astype(dest.dtype)
        return
    low_lanes = lanes_of(slabs[0].shape[0]) < HEAD_DIM
    for pair in range(len(slabs) // 2):
        both = jnp.where(low_lanes, slabs[2 * pair], pltpu.roll(slabs[2 * pair + 1], HEAD_DIM, 1))
        dest[where, pair * LANES : (pair + 1) * LANES] = both.astype(dest.dtype)


def span_for(block, length, from_starts, to_starts, to_ends):
    first_row = block * SPAN
    last_row = first_row + SPAN - 1
    low, high = jnp.int32(0), jnp.int32(0)
    for start, to_start, to_end in zip(from_starts, to_starts, to_ends):
        low = jnp.where(start <= first_row, to_start, low)
        high = jnp.where(start <= last_row, to_end, high)
    low = (low >> 7) << 7
    pieces = (high - low + SPAN - 1) >> 8
    return jnp.minimum(low, length - pieces * SPAN), pieces


def each_span(length, starts_from, starts_to, ends_to, body):
    def step(block, carry):
        start, pieces = span_for(block, length, starts_from, starts_to, ends_to)
        start = pl.multiple_of(start, LANES)
        rows = pl.ds(pl.multiple_of(block * SPAN, SPAN), SPAN)
        for count in range(1, length // SPAN + 1):

            @pl.when(pieces == count)
            def _():
                body(rows, pl.ds(start, count * SPAN))

        return carry

    lax.fori_loop(0, length // SPAN, step, 0)


def attend_body(qx, kx, vx, ctx, segs, rows, keys):
    scale = LOG2_E * HEAD_DIM**-0.5
    lane = lanes_of(SPAN)
    slabs = []
    for head in range(qx.shape[0]):
        query = qx[head, rows, :]
        scores = dot_nt(query, kx[head, keys, :])
        peak = jnp.max(scores, axis=1, keepdims=True)
        raised = jnp.exp2((scores - peak) * scale).astype(BF16)
        mixed = dot(raised, vx[head, keys, :])
        total = mixed[:, HEAD_DIM : HEAD_DIM + 1]
        slabs.append(mixed / total)
        level = -(peak + jnp.log(total) * (HEAD_DIM**0.5))
        high = level.astype(BF16).astype(F32)
        middle = (level - high).astype(BF16).astype(F32)
        low = level - high - middle
        base = HEAD_DIM + segs
        wide = query.astype(F32)
        wide = jnp.where(lane == base, high, wide)
        wide = jnp.where(lane == base + 1, middle, wide)
        wide = jnp.where(lane == base + 2, low, wide)
        qx[head, rows, :] = wide.astype(BF16)
    join_heads(ctx, rows, slabs)


def split_out(source, keep, send, share):
    me = lax.axis_index("heads")
    parts = send.shape[0] + 1
    for k in range(parts):
        owner = lax.rem(me + k, parts)
        rows = pl.ds(pl.multiple_of(owner * share, share), share)
        if k == 0:
            keep[...] = source[rows, :].astype(keep.dtype)
        else:
            send[k - 1] = source[rows, :].astype(send.dtype)


def self_forward_kernel(len_ref, x_ref, w_ref, keep, send, ctx, qx, kx, vx):
    length = x_ref.shape[0]
    segs = len_ref.shape[1]
    starts, ends = segment_bounds(len_ref)
    bounds = bound_lanes(starts, ends)

    def project(block, carry):
        first = pl.multiple_of(block * SPAN, SPAN)
        rows = pl.ds(first, SPAN)
        tokens = x_ref[rows, :]
        put_heads(qx, rows, dot(tokens, w_ref[0]), query_extra(first, SPAN, bounds))
        put_heads(kx, rows, dot(tokens, w_ref[1]), key_extra(first, SPAN, bounds, segs))
        put_heads(vx, rows, dot(tokens, w_ref[2]), value_extra(SPAN))
        return carry

    lax.fori_loop(0, length // SPAN, project, 0)
    each_span(
        length, starts, starts, ends, functools.partial(attend_body, qx, kx, vx, ctx, segs)
    )
    split_out(ctx, keep, send, keep.shape[0])


def cross_keys_kernel(len_ref, x_ref, w_ref, kx, vx):
    length = x_ref.shape[0]
    bounds = bound_lanes(*segment_bounds(len_ref))
    segs = len_ref.shape[1]

    def project(block, carry):
        first = pl.multiple_of(block * SPAN, SPAN)
        rows = pl.ds(first, SPAN)
        tokens = x_ref[rows, :]
        put_heads(kx, rows, dot(tokens, w_ref[0]), key_extra(first, SPAN, bounds, segs))
        put_heads(vx, rows, dot(tokens, w_ref[1]), value_extra(SPAN))
        return carry

    lax.fori_loop(0, length // SPAN, project, 0)


def gather_rows(dest, own, others):
    me = lax.axis_index("heads")
    parts = len(others) + 1
    share = own.shape[0]
    for k, source in enumerate([own, *others]):
        owner = lax.rem(me + k, parts)
        dest[pl.ds(pl.multiple_of(owner * share, share), share), :] = source[...]


def cross_forward_kernel(parts, dec_ref, enc_ref, kx, vx, *refs):
    pieces, (keep, send, ctx, qx, flat) = refs[:parts], refs[parts:]
    length = ctx.shape[0]
    segs = dec_ref.shape[1]
    dec_starts, dec_ends = segment_bounds(dec_ref)
    enc_starts, enc_ends = segment_bounds(enc_ref)
    bounds = bound_lanes(dec_starts, dec_ends)
    gather_rows(flat, pieces[0], pieces[1:])

    def widen(block, carry):
        first = pl.multiple_of(block * SPAN, SPAN)
        rows = pl.ds(first, SPAN)
        put_heads(qx, rows, flat[rows, :].astype(F32), query_extra(first, SPAN, bounds))
        return carry

    lax.fori_loop(0, length // SPAN, widen, 0)
    each_span(
        length, dec_starts, enc_starts, enc_ends,
        functools.partial(attend_body, qx, kx, vx, ctx, segs),
    )
    split_out(ctx, keep, send, keep.shape[0])


def attend_back_body(qx, kx, vx, gx, dq, dk, dv, rows, queries):
    scale = LOG2_E * HEAD_DIM**-0.5
    key_slabs, value_slabs = [], []
    for head in range(qx.shape[0]):
        keys = kx[head, rows, :]
        query = qx[head, queries, :]
        grads = gx[head, queries, :]
        weights = jnp.exp2(dot_nt(keys, query) * scale)
        raised = dot_nt(vx[head, rows, :], grads)
        value_slabs.append(dot(weights.astype(BF16), grads))
        inner = (weights * raised).astype(BF16)
        key_slabs.append(dot(inner, query) * (HEAD_DIM**-0.5))
        dq[head, queries, :] += dot_tn(inner, keys)
    join_heads(dk, rows, key_slabs)
    join_heads(dv, rows, value_slabs)


def attend_back(key_starts, key_ends, query_starts, query_ends, qx, kx, vx, ctx, grad, gx, dq, sq, sk, sv):
    length = ctx.shape[0]
    heads = qx.shape[0]
    lane = lanes_of(SPAN)

    def widen(block, carry):
        rows = pl.ds(pl.multiple_of(block * SPAN, SPAN), SPAN)
        wide = grad[rows, :].astype(F32)
        product = wide * ctx[rows, :].astype(F32)
        for head in range(heads):
            slab = head_slab(product, head)
            level = -jnp.sum(jnp.where(lane < HEAD_DIM, slab, 0.0), axis=1, keepdims=True)
            high = level.astype(BF16).astype(F32)
            extra = jnp.where(lane == HEAD_DIM, high, 0.0)
            extra = jnp.where(lane == HEAD_DIM + 1, level - high, extra)
            full = jnp.where(lane < HEAD_DIM, head_slab(wide, head), extra)
            gx[head, rows, :] = full.astype(BF16)
            dq[head, rows, :] = jnp.zeros((SPAN, LANES), F32)
        return carry

    lax.fori_loop(0, length // SPAN, widen, 0)
    each_span(
        length, key_starts, query_starts, query_ends,
        functools.partial(attend_back_body, qx, kx, vx, gx, dq, sk, sv),
    )

    def finish(block, carry):
        rows = pl.ds(pl.multiple_of(block * SPAN, SPAN), SPAN)
        join_heads(sq, rows, [dq[head, rows, :] * (HEAD_DIM**-0.5) for head in range(heads)])
        return carry

    lax.fori_loop(0, length // SPAN, finish, 0)


def norm_forward(summed, gain, bias):
    center = summed - jnp.mean(summed, axis=1, keepdims=True)
    inverse_dev = lax.rsqrt(jnp.mean(center * center, axis=1, keepdims=True) + NORM_EPS)
    normed = center * inverse_dev
    return normed * gain + bias, normed, inverse_dev


def norm_back(grad, normed, inverse_dev, gain):
    scaled = grad * gain
    back = inverse_dev * (
        scaled
        - jnp.mean(scaled, axis=1, keepdims=True)
        - normed * jnp.mean(scaled * normed, axis=1, keepdims=True)
    )
    gain_grad = jnp.sum(grad * normed, axis=0, keepdims=True)
    return back, gain_grad, jnp.sum(grad, axis=0, keepdims=True)


def share_block(share):
    return 256 if share % 256 == 0 else share


def own_rows(share, first, rows):
    start = lax.axis_index("heads") * share + first
    return pl.ds(pl.multiple_of(start, 64), rows)


def first_norm_kernel(parts, x_ref, gain, bias, *refs):
    ctx, w_out, w_query = refs[:parts], refs[parts : 2 * parts], refs[2 * parts : 3 * parts]
    first_out, first_low, normed_out, dev_out, keep, send = refs[3 * parts :]
    share = first_out.shape[0]
    block = share_block(share)

    def step(index, carry):
        first = pl.multiple_of(index * block, block)
        rows = pl.ds(first, block)
        total = x_ref[own_rows(share, first, block), :].astype(F32)
        for k in range(parts):
            total = total + dot(ctx[k][rows, :], w_out[k][...])
        result, normed, inverse_dev = norm_forward(total, gain[0:1, :], bias[0:1, :])
        low = result.astype(BF16)
        first_out[rows, :] = result
        first_low[rows, :] = low
        normed_out[rows, :] = normed
        dev_out[rows, :] = inverse_dev
        for k in range(parts):
            value = dot(low, w_query[k][...]).astype(BF16)
            if k == 0:
                keep[rows, :] = value
            else:
                send[k - 1, rows, :] = value
        return carry

    lax.fori_loop(0, share // block, step, 0)


def middle_kernel(parts, gain, bias, first_out, out_grad, *refs):
    groups = [refs[g * parts : (g + 1) * parts] for g in range(4)]
    ctx, w_cross, w_in, w_out = groups
    (layer_out, grad_mid, gains, biases, g_out_keep, g_out_send, g_in_keep, g_in_send,
     g_cross_keep, g_cross_send, back_keep, back_send,
     second, second_low, normed2, dev2, total, hidden, slope, top_low, back_sum) = refs[4 * parts :]
    share = first_out.shape[0]
    block = share_block(share)
    units = w_in[0].shape[1]
    chunk = min(256, units)

    def enter(index, carry):
        rows = pl.ds(pl.multiple_of(index * block, block), block)
        summed = first_out[rows, :]
        for k in range(parts):
            summed = summed + dot(ctx[k][rows, :], w_cross[k][...])
        result, normed, inverse_dev = norm_forward(summed, gain[1:2, :], bias[1:2, :])
        second[rows, :] = result
        second_low[rows, :] = result.astype(BF16)
        normed2[rows, :] = normed
        dev2[rows, :] = inverse_dev
        return carry

    lax.fori_loop(0, share // block, enter, 0)
    total[...] = second[...]
    for k in range(parts):

        def expand(index, carry):
            cols = pl.ds(pl.multiple_of(index * chunk, chunk), chunk)
            spot = k * (units // chunk) + index
            pre = dot(second_low[...], w_in[k][:, cols])
            square = pre * pre
            bent = jnp.tanh(pre * (GELU_RATE + (GELU_RATE * GELU_CUBE) * square))
            half = 0.5 + 0.5 * bent
            act = (pre * half).astype(BF16)
            hidden[spot] = act
            bend = (0.5 - 0.5 * bent * bent) * (
                GELU_RATE + (3.0 * GELU_RATE * GELU_CUBE) * square
            )
            slope[spot] = half + pre * bend
            total[...] += dot(act, w_out[k][cols, :])
            return carry

        lax.fori_loop(0, units // chunk, expand, 0)

    gains[...] = jnp.zeros_like(gains)
    biases[...] = jnp.zeros_like(biases)

    def turn(index, carry):
        first = pl.multiple_of(index * block, block)
        rows = pl.ds(first, block)
        result, normed, inverse_dev = norm_forward(total[rows, :], gain[2:3, :], bias[2:3, :])
        layer_out[rows, :] = result
        grad = out_grad[own_rows(share, first, block), :].astype(F32)
        back, gain_grad, bias_grad = norm_back(grad, normed, inverse_dev, gain[2:3, :])
        gains[1:2, :] += gain_grad
        biases[1:2, :] += bias_grad
        back_sum[rows, :] = back
        top_low[rows, :] = back.astype(BF16)
        return carry

    lax.fori_loop(0, share // block, turn, 0)
    for k in range(parts):

        def contract(index, carry):
            cols = pl.ds(pl.multiple_of(index * chunk, chunk), chunk)
            spot = k * (units // chunk) + index
            weight_out = dot_tn(hidden[spot], top_low[...]).astype(BF16)
            pre = (dot_nt(top_low[...], w_out[k][cols, :]) * slope[spot]).astype(BF16)
            weight_in = dot_tn(second_low[...], pre).astype(BF16)
            if k == 0:
                g_out_keep[cols, :] = weight_out
                g_in_keep[:, cols] = weight_in
            else:
                g_out_send[k - 1, cols, :] = weight_out
                g_in_send[k - 1, :, cols] = weight_in
            back_sum[...] += dot_nt(pre, w_in[k][:, cols])
            return carry

        lax.fori_loop(0, units // chunk, contract, 0)

    def leave(index, carry):
        rows = pl.ds(pl.multiple_of(index * block, block), block)
        back, gain_grad, bias_grad = norm_back(
            back_sum[rows, :], normed2[rows, :], dev2[rows, :], gain[1:2, :]
        )
        gains[0:1, :] += gain_grad
        biases[0:1, :] += bias_grad
        grad_mid[rows, :] = back
        low = back.astype(BF16)
        top_low[rows, :] = low
        for k in range(parts):
            value = dot_nt(low, w_cross[k][...]).astype(BF16)
            if k == 0:
                back_keep[rows, :] = value
            else:
                back_send[k - 1, rows, :] = value
        return carry

    lax.fori_loop(0, share // block, leave, 0)
    for k in range(parts):
        value = dot_tn(ctx[k][...], top_low[...]).astype(BF16)
        if k == 0:
            g_cross_keep[...] = value
        else:
            g_cross_send[k - 1] = value


def cross_back_kernel(parts, dec_ref, enc_ref, qx, kx, vx, ctx, enc, w_kv, *refs):
    pieces = refs[:parts]
    (gq_keep, gq_send, g_kv, enc_keep, enc_send, grad, gx, dq, sq, sk, sv, wide) = refs[parts:]
    length = ctx.shape[0]
    dec_starts, dec_ends = segment_bounds(dec_ref)
    enc_starts, enc_ends = segment_bounds(enc_ref)
    gather_rows(grad, pieces[0], pieces[1:])
    attend_back(
        enc_starts, enc_ends, dec_starts, dec_ends, qx, kx, vx, ctx, grad, gx, dq, sq, sk, sv
    )
    split_out(sq, gq_keep, gq_send, gq_keep.shape[0])
    g_kv[0] = dot_tn(enc[...], sk[...]).astype(BF16)
    g_kv[1] = dot_tn(enc[...], sv[...]).astype(BF16)

    def step(block, carry):
        rows = pl.ds(pl.multiple_of(block * SPAN, SPAN), SPAN)
        wide[rows, :] = dot_nt(sk[rows, :], w_kv[0]) + dot_nt(sv[rows, :], w_kv[1])
        return carry

    lax.fori_loop(0, length // SPAN, step, 0)
    split_out(wide, enc_keep, enc_send, enc_keep.shape[0])


def first_back_kernel(parts, gain, grad_mid, first_low, normed, dev, *refs):
    groups = [refs[g * parts : (g + 1) * parts] for g in range(4)]
    gq, w_query, ctx, w_out = groups
    (grad_base, gains, biases, g_query_keep, g_query_send, g_out_keep, g_out_send,
     back_keep, back_send, low_ref) = refs[4 * parts :]
    share = grad_mid.shape[0]
    block = share_block(share)
    gains[...] = jnp.zeros_like(gains)
    biases[...] = jnp.zeros_like(biases)

    def step(index, carry):
        rows = pl.ds(pl.multiple_of(index * block, block), block)
        grad = grad_mid[rows, :]
        for k in range(parts):
            grad = grad + dot_nt(gq[k][rows, :], w_query[k][...])
        back, gain_grad, bias_grad = norm_back(grad, normed[rows, :], dev[rows, :], gain[0:1, :])
        gains[...] += gain_grad
        biases[...] += bias_grad
        grad_base[rows, :] = back
        low = back.astype(BF16)
        low_ref[rows, :] = low
        for k in range(parts):
            value = dot_nt(low, w_out[k][...]).astype(BF16)
            if k == 0:
                back_keep[rows, :] = value
            else:
                back_send[k - 1, rows, :] = value
        return carry

    lax.fori_loop(0, share // block, step, 0)
    for k in range(parts):
        query_grad = dot_tn(first_low[...], gq[k][...]).astype(BF16)
        out_grad = dot_tn(ctx[k][...], low_ref[...]).astype(BF16)
        if k == 0:
            g_query_keep[...] = query_grad
            g_out_keep[...] = out_grad
        else:
            g_query_send[k - 1] = query_grad
            g_out_send[k - 1] = out_grad


def self_back_kernel(parts, dec_ref, qx, kx, vx, ctx, x_ref, w_qkv, *refs):
    pieces = refs[:parts]
    g_qkv, in_keep, in_send, grad, gx, dq, sq, sk, sv, wide = refs[parts:]
    length = ctx.shape[0]
    starts, ends = segment_bounds(dec_ref)
    gather_rows(grad, pieces[0], pieces[1:])
    attend_back(starts, ends, starts, ends, qx, kx, vx, ctx, grad, gx, dq, sq, sk, sv)
    for c, source in enumerate((sq, sk, sv)):
        g_qkv[c] = dot_tn(x_ref[...], source[...]).astype(BF16)

    def step(block, carry):
        rows = pl.ds(pl.multiple_of(block * SPAN, SPAN), SPAN)
        wide[rows, :] = (
            dot_nt(sq[rows, :], w_qkv[0])
            + dot_nt(sk[rows, :], w_qkv[1])
            + dot_nt(sv[rows, :], w_qkv[2])
        )
        return carry

    lax.fori_loop(0, length // SPAN, step, 0)
    split_out(wide, in_keep, in_send, in_keep.shape[0])


LINK_RATE = 0.088
HOP_TIME = 2.0


def transfer_plan(orders, ready, sizes, bits):
    steps = 2 * bits
    busy = {}
    left = {p: 0 for p in range(len(orders))}
    at = {p: ready[p] for p in range(len(orders))}
    plan, flying, clock = [], [], 0.0

    def bit_of(p, step):
        return orders[p][step] if step < bits else orders[p][steps - 1 - step]

    def cost(p, step):
        depth = step if step < bits else steps - 1 - step
        amount = sizes[p] / 2 ** (depth + 1) * 2 / LINK_RATE
        bit = bit_of(p, step)
        if bit == bits - 1 and bits == 4:
            return {3: 2 * amount, 2: amount}
        return {bit: amount}

    def rest(p):
        return sum(max(cost(p, s).values()) + HOP_TIME for s in range(left[p], steps))

    waiting = set(range(len(orders)))
    while waiting or flying:
        chosen = None
        for p in sorted(waiting, key=lambda p: (-rest(p), p)):
            need = cost(p, left[p])
            if at[p] <= clock and all(busy.get(b, 0.0) <= clock + 1.0 for b in need):
                chosen = p
                break
        if chosen is not None:
            need = cost(chosen, left[chosen])
            done = clock
            for b, amount in need.items():
                busy[b] = max(busy.get(b, 0.0), clock) + amount
                done = max(done, busy[b])
            plan.append(("send", chosen, left[chosen]))
            flying.append((done + HOP_TIME, chosen))
            waiting.discard(chosen)
            continue
        times = [t for t, _ in flying]
        times += [at[p] for p in waiting if at[p] > clock]
        times += [t - 1.0 for t in busy.values() if t - 1.0 > clock and waiting]
        clock = max(clock, min(times))
        for t, p in sorted(flying):
            if t <= clock:
                flying.remove((t, p))
                plan.append(("take", p, left[p]))
                left[p] += 1
                at[p] = clock
                if left[p] < steps:
                    waiting.add(p)
    return plan


def rows_sum_kernel(table, bits, *refs):
    count = len(table)
    sources = max(max(e[0], -1 if e[1] is None else e[1]) for e in table) + 1
    arrays, small, outs = refs[:sources], refs[sources], refs[sources + 1 : sources + 1 + table[-1][7] + 1]
    small_out = refs[sources + 1 + len(outs)]
    rest = list(refs[sources + 2 + len(outs) :])
    take = lambda number: [rest.pop(0) for _ in range(number)]
    held, mate, landing, final = take(count), take(count), take(count), take(count)
    small_land, load_sem, mate_sem, send_sem, land_sem, store_sem, small_send, small_sem = rest
    steps = 2 * bits
    me = lax.axis_index("rows")
    core = lax.axis_index("heads")

    def partner(bit):
        return {"rows": me + (1 << bit) - 2 * (me & (1 << bit)), "heads": core}

    peers = [partner(bit) for bit in range(bits)] + [{"rows": me, "heads": 1 - core}]
    barrier = pltpu.get_barrier_semaphore()
    loads = []
    for p, (source, pair, row, col, rows, cols, _, _) in enumerate(table):
        window = (pl.ds(row, rows), pl.ds(col, cols))
        pieces = [pltpu.make_async_copy(arrays[source].at[window], held[p], load_sem.at[p])]
        if pair is not None:
            pieces.append(pltpu.make_async_copy(arrays[pair].at[window], mate[p], mate_sem.at[p]))
        for piece in pieces:
            piece.start()
        loads.append(pieces)
    for peer in peers:
        pl.semaphore_signal(barrier, inc=1, device_id=peer, device_id_type=pl.DeviceIdType.MESH)
    pl.semaphore_wait(barrier, len(peers))

    def remote(source, dest, send, land, peer):
        copy = pltpu.make_async_remote_copy(
            src_ref=source, dst_ref=dest, send_sem=send, recv_sem=land,
            device_id=peer, device_id_type=pl.DeviceIdType.MESH,
        )
        copy.start()
        return copy

    def add(dest, rows, left, right, left_rows, right_rows):
        total = left[left_rows, :].astype(F32) + right[right_rows, :].astype(F32)
        dest[rows, :] = total.astype(BF16)

    small_out[...] = small[...]
    offset = [jnp.int32(0)] * count
    copies = {}
    stores = []
    small_step = 0
    small_copy = None
    plan = transfer_plan(
        [e[6] for e in table], [0.0] * count, [e[4] * e[5] * 2e-6 for e in table], bits
    )
    for number, (kind, p, step) in enumerate(plan):
        _, _, row, col, rows, cols, order, out = table[p]
        depth = step if step < bits else steps - 1 - step
        bit = order[depth]
        size = rows >> (depth + 1)
        side = lax.shift_right_logical(me, bit) & 1
        if kind == "send" and step < bits:
            if step == 0:
                for piece in loads[p]:
                    piece.wait()
                if len(loads[p]) == 2:
                    add(held[p], slice(None), held[p], mate[p], slice(None), slice(None))
            away = pl.ds(pl.multiple_of(offset[p] + (1 - side) * size, 16), size)
            spot = pl.ds(rows - 2 * size, size)
            copies[p] = remote(
                held[p].at[away, :], landing[p].at[spot, :],
                send_sem.at[p, step], land_sem.at[p, step], peers[bit],
            )
        elif kind == "send":
            mine = pl.ds(pl.multiple_of(offset[p], 16), size)
            copies[p] = remote(
                final[p].at[mine, :], final[p].at[mine, :],
                send_sem.at[p, step], land_sem.at[p, step], peers[bit],
            )
        elif step < bits:
            copies[p].wait()
            offset[p] = offset[p] + side * size
            mine = pl.ds(pl.multiple_of(offset[p], 16), size)
            spot = pl.ds(rows - 2 * size, size)
            add(final[p] if step == bits - 1 else held[p], mine, held[p], landing[p], mine, spot)
        else:
            copies[p].wait()
            offset[p] = offset[p] - side * size
            if step == steps - 1:
                window = (pl.ds(row, rows), pl.ds(col, cols))
                store = pltpu.make_async_copy(final[p], outs[out].at[window], store_sem.at[p])
                store.start()
                stores.append(store)
        if number % 4 == 0 and small_step <= len(peers):
            if small_copy is not None:
                small_copy.wait()
                small_out[...] += small_land[small_step - 1]
            if small_step < len(peers):
                small_copy = remote(
                    small_out, small_land.at[small_step], small_send.at[small_step],
                    small_sem.at[small_step], peers[small_step],
                )
            small_step += 1
    for store in stores:
        store.wait()


def widen_kernel(table, *refs):
    outs = table[-1][7] + 1
    arrays, dests = refs[:outs], refs[outs : 2 * outs]
    rest = list(refs[2 * outs :])
    low = [rest.pop(0) for _ in table]
    wide = [rest.pop(0) for _ in table]
    load_sem, store_sem = rest
    loads, stores = [], []
    for p, (_, _, row, col, rows, cols, _, out) in enumerate(table):
        window = (pl.ds(row, rows), pl.ds(col, cols))
        loads.append(pltpu.make_async_copy(arrays[out].at[window], low[p], load_sem.at[p]))
        stores.append(pltpu.make_async_copy(wide[p], dests[out].at[window], store_sem.at[p]))
        loads[p].start()
    for p in range(len(table)):
        loads[p].wait()
        wide[p][...] = low[p][...].astype(F32)
        stores[p].start()
    for store in stores:
        store.wait()


def sum_over_rows(pairs, small):
    size = lax.axis_size("rows")
    bits = size.bit_length() - 1
    arrays, table = [], []
    for out, (own, other) in enumerate(pairs):
        source = len(arrays)
        arrays.append(own)
        pair = None
        if other is not None:
            pair = source + 1
            arrays.append(other)
        rows, cols = own.shape
        high, broad = (256, 512) if cols == 512 else (512, 256)
        for row in range(0, rows, high):
            for col in range(0, cols, broad):
                table.append([source, pair, row, col, high, broad, None, out])
    x_first, y_first = (0, 1, 2, 3), (1, 0, 2, 3)
    z_first, z_other = (2, 0, 1, 3), (2, 1, 0, 3)
    cycle = [x_first, y_first, z_first, x_first, y_first, z_other]
    for p, entry in enumerate(table):
        entry[6] = cycle[p % len(cycle)]
    count = len(table)
    buffers = [pltpu.VMEM((e[4], e[5]), BF16) for e in table]
    small_shape = small.shape
    sums = pl.pallas_call(
        functools.partial(rows_sum_kernel, table, bits),
        out_shape=[shape_of(own.shape, BF16) for own, _ in pairs] + [shape_of(small_shape, F32)],
        in_specs=[pl.BlockSpec(memory_space=pl.ANY)] * len(arrays) + [VMEM],
        out_specs=[pl.BlockSpec(memory_space=pl.ANY)] * len(pairs) + [VMEM],
        scratch_shapes=buffers * 4
        + [pltpu.VMEM((bits + 1, *small_shape), F32)]
        + [pltpu.SemaphoreType.DMA((count,))] * 2
        + [pltpu.SemaphoreType.DMA((count, 2 * bits))] * 2
        + [pltpu.SemaphoreType.DMA((count,))]
        + [pltpu.SemaphoreType.DMA((bits + 1,))] * 2,
        compiler_params=pltpu.CompilerParams(
            vmem_limit_bytes=40 * 2**20, collective_id=0, has_side_effects=True
        ),
    )(*arrays, small)
    wide = pl.pallas_call(
        functools.partial(widen_kernel, table),
        out_shape=[shape_of(own.shape, F32) for own, _ in pairs],
        in_specs=[pl.BlockSpec(memory_space=pl.ANY)] * len(pairs),
        out_specs=[pl.BlockSpec(memory_space=pl.ANY)] * len(pairs),
        scratch_shapes=buffers
        + [pltpu.VMEM((e[4], e[5]), F32) for e in table]
        + [pltpu.SemaphoreType.DMA((count,))] * 2,
        compiler_params=pltpu.CompilerParams(vmem_limit_bytes=40 * 2**20),
    )(*sums[:-1])
    return [*wide, sums[-1]]


def fits_kernel(pairs):
    fits = all(
        own.shape[1] == 512 and own.shape[0] % 256 == 0
        or own.shape[1] % 256 == 0 and own.shape[0] % 512 == 0
        for own, _ in pairs
    )
    return fits and lax.axis_size("rows") == 16 and lax.axis_size("heads") == 2


def body(
    dec_input,
    enc_output,
    dec_lengths,
    enc_lengths,
    w_self_qkv,
    w_self_out,
    w_cross_q,
    w_cross_kv,
    w_cross_out,
    w_ffn_in,
    w_ffn_out,
    norm_gain,
    norm_bias,
    out_grad,
):
    parts = lax.axis_size("heads")
    length, width = dec_input.shape
    local = w_self_out.shape[0]
    heads = local // HEAD_DIM
    share = length // parts
    units = w_ffn_in.shape[1]
    chunk = min(256, units)
    chunks = parts * units // chunk

    def shift(value, k):
        return lax.ppermute(value, "heads", [(d, (d + k) % parts) for d in range(parts)])

    def slots(shard):
        return [shard] + [shift(shard, parts - k) for k in range(1, parts)]

    def swap(keep, send):
        return [keep] + [shift(send[parts - k - 1], parts - k) for k in range(1, parts)]

    def collect(keep, send):
        total = keep.astype(F32)
        for k in range(1, parts):
            total = total + shift(send[k - 1], k).astype(F32)
        return total

    self_out, cross_q, cross_out = slots(w_self_out), slots(w_cross_q), slots(w_cross_out)
    ffn_in, ffn_out = slots(w_ffn_in), slots(w_ffn_out)

    def sent(*dims, kind=BF16):
        return shape_of((parts - 1, *dims), kind)

    def own(*dims, kind=BF16):
        return shape_of(dims, kind)

    wide_heads = own(heads, length, LANES)
    self_keep, self_send, self_ctx, self_qx, self_kx, self_vx = call(
        self_forward_kernel,
        [own(share, local), sent(share, local), own(length, local), wide_heads, wide_heads, wide_heads],
        [], 40, dec_lengths, dec_input, w_self_qkv, smem=1,
    )
    self_slots = swap(self_keep, self_send)
    cross_kx, cross_vx = call(
        cross_keys_kernel, [wide_heads, wide_heads], [], 32,
        enc_lengths, enc_output, w_cross_kv, smem=1,
    )
    first_out, first_low, first_normed, first_dev, query_keep, query_send = call(
        functools.partial(first_norm_kernel, parts),
        [own(share, width, kind=F32), own(share, width), own(share, width, kind=F32),
         own(share, 1, kind=F32), own(share, local), sent(share, local)],
        [], 32, dec_input, norm_gain, norm_bias, *self_slots, *self_out, *cross_q,
    )
    cross_keep, cross_send, cross_ctx, cross_qx = call(
        functools.partial(cross_forward_kernel, parts),
        [own(share, local), sent(share, local), own(length, local), wide_heads],
        [pltpu.VMEM((length, local), BF16)], 40,
        dec_lengths, enc_lengths, cross_kx, cross_vx, *swap(query_keep, query_send), smem=2,
    )
    cross_slots = swap(cross_keep, cross_send)
    (layer_out, grad_mid, gains_high, biases_high, g_ffn_out, g_ffn_out_send, g_ffn_in,
     g_ffn_in_send, g_cross_out, g_cross_out_send, back_keep, back_send) = call(
        functools.partial(middle_kernel, parts),
        [own(share, width, kind=F32), own(share, width, kind=F32),
         own(2, width, kind=F32), own(2, width, kind=F32),
         own(units, width), sent(units, width), own(width, units), sent(width, units),
         own(local, width), sent(local, width), own(share, local), sent(share, local)],
        [pltpu.VMEM((share, width), F32), pltpu.VMEM((share, width), BF16),
         pltpu.VMEM((share, width), F32), pltpu.VMEM((share, 1), F32),
         pltpu.VMEM((share, width), F32), pltpu.VMEM((chunks, share, chunk), BF16),
         pltpu.VMEM((chunks, share, chunk), F32), pltpu.VMEM((share, width), BF16),
         pltpu.VMEM((share, width), F32)],
        56, norm_gain, norm_bias, first_out, out_grad,
        *cross_slots, *cross_out, *ffn_in, *ffn_out,
    )
    back_scratch = [
        pltpu.VMEM((length, local), BF16),
        pltpu.VMEM((heads, length, LANES), BF16),
        pltpu.VMEM((heads, length, LANES), F32),
        pltpu.VMEM((length, local), BF16),
        pltpu.VMEM((length, local), BF16),
        pltpu.VMEM((length, local), BF16),
        pltpu.VMEM((length, width), F32),
    ]
    gq_keep, gq_send, g_cross_kv, enc_keep, enc_send = call(
        functools.partial(cross_back_kernel, parts),
        [own(share, local), sent(share, local), own(2, width, local),
         own(share, width, kind=F32), sent(share, width)],
        back_scratch, 56, dec_lengths, enc_lengths, cross_qx, cross_kx, cross_vx, cross_ctx,
        enc_output, w_cross_kv, *swap(back_keep, back_send), smem=2,
    )
    enc_grad = collect(enc_keep, enc_send)
    (grad_base, gains_low, biases_low, g_cross_q, g_cross_q_send, g_self_out, g_self_out_send,
     self_back_keep, self_back_send) = call(
        functools.partial(first_back_kernel, parts),
        [own(share, width, kind=F32), own(1, width, kind=F32), own(1, width, kind=F32),
         own(width, local), sent(width, local), own(local, width), sent(local, width),
         own(share, local), sent(share, local)],
        [pltpu.VMEM((share, width), BF16)], 40,
        norm_gain, grad_mid, first_low, first_normed, first_dev,
        *swap(gq_keep, gq_send), *cross_q, *self_slots, *self_out,
    )
    g_self_qkv, in_keep, in_send = call(
        functools.partial(self_back_kernel, parts),
        [own(3, width, local), own(share, width, kind=F32), sent(share, width)],
        back_scratch, 56, dec_lengths, self_qx, self_kx, self_vx, self_ctx, dec_input,
        w_self_qkv, *swap(self_back_keep, self_back_send), smem=1,
    )
    input_grad = grad_base + collect(in_keep, in_send)

    small = jnp.concatenate(
        [gains_low, gains_high, biases_low, biases_high, jnp.zeros((2, width), F32)]
    )
    halves = [
        (g_ffn_out, g_ffn_out_send),
        (g_ffn_in, g_ffn_in_send),
        (g_cross_out, g_cross_out_send),
        (g_cross_q, g_cross_q_send),
        (g_cross_kv.reshape(2 * width, local), None),
        (g_self_out, g_self_out_send),
        (g_self_qkv.reshape(3 * width, local), None),
    ]
    if fits_kernel(halves):
        pairs = [(own, None if away is None else shift(away[0], 1)) for own, away in halves]
        sums = sum_over_rows(pairs, small)
    else:
        totals = [own if away is None else collect(own, away) for own, away in halves]
        sums = [lax.psum(total.astype(BF16), "rows").astype(F32) for total in totals]
        sums.append(lax.psum(small, ("rows", "heads")))
    s_ffn_out, s_ffn_in, s_cross_out, s_cross_q, s_cross_kv, s_self_out, s_self_qkv, sums_small = sums
    return (
        layer_out,
        input_grad,
        enc_grad,
        s_self_qkv.reshape(3, width, local),
        s_self_out,
        s_cross_q,
        s_cross_kv.reshape(2, width, local),
        s_cross_out,
        s_ffn_in,
        s_ffn_out,
        sums_small[:3],
        sums_small[3:6],
    )


def solution(mesh):
    in_specs = (
        P("rows", None),
        P("rows", None),
        P("rows", None),
        P("rows", None),
        P(None, None, "heads"),
        P("heads", None),
        P(None, "heads"),
        P(None, None, "heads"),
        P("heads", None),
        P(None, "heads"),
        P("heads", None),
        P(),
        P(),
        P("rows", None),
    )
    out_specs = (
        P(("rows", "heads"), None),
        P(("rows", "heads"), None),
        P(("rows", "heads"), None),
        P(None, None, "heads"),
        P("heads", None),
        P(None, "heads"),
        P(None, None, "heads"),
        P("heads", None),
        P(None, "heads"),
        P("heads", None),
        P(),
        P(),
    )
    return jax.shard_map(body, mesh=mesh, in_specs=in_specs, out_specs=out_specs, check_vma=False)
```

```python
import functools

import jax
import jax.numpy as jnp
from jax import lax
from jax.experimental import pallas as pl
from jax.experimental.pallas import tpu as pltpu
from jax.sharding import PartitionSpec as P

HEAD_DIM = 64
LANES = 128
SPAN = 256
NORM_EPS = 1e-05
MASKED_SCORE = -1e30
LOG2_E = 1.4426950408889634
GELU_RATE = 0.7978845608028654
GELU_CUBE = 0.044715
F32 = jnp.float32
BF16 = jnp.bfloat16
NT = (((1,), (1,)), ((), ()))
TN = (((0,), (0,)), ((), ()))
VMEM = pl.BlockSpec(memory_space=pltpu.VMEM)
SMEM = pl.BlockSpec(memory_space=pltpu.SMEM)


def dot(left, right):
    return jnp.dot(left, right, preferred_element_type=F32)


def dot_nt(left, right):
    return lax.dot_general(left, right, NT, preferred_element_type=F32)


def dot_tn(left, right):
    return lax.dot_general(left, right, TN, preferred_element_type=F32)


def shape_of(dims, kind):
    return jax.ShapeDtypeStruct(dims, kind)


def call(kernel, outs, scratch, mib, *args, smem=0):
    return pl.pallas_call(
        kernel,
        out_shape=outs,
        in_specs=[SMEM] * smem + [VMEM] * (len(args) - smem),
        out_specs=jax.tree.map(lambda _: VMEM, outs),
        scratch_shapes=scratch,
        compiler_params=pltpu.CompilerParams(vmem_limit_bytes=60 * 2**20),
    )(*args)


def segment_bounds(len_ref):
    starts, ends, total = [], [], jnp.int32(0)
    for k in range(len_ref.shape[1]):
        starts.append(total)
        total = total + len_ref[0, k]
        ends.append(total)
    return starts, ends


def bound_lanes(starts, ends):
    lane = lax.broadcasted_iota(jnp.int32, (1, LANES), 1)
    first = jnp.full((1, LANES), 1 << 30, jnp.int32)
    last = jnp.zeros((1, LANES), jnp.int32)
    for k, (start, end) in enumerate(zip(starts, ends)):
        first = jnp.where(lane == HEAD_DIM + k, start, first)
        last = jnp.where(lane == HEAD_DIM + k, end, last)
    return first, last


def lanes_of(rows):
    return lax.broadcasted_iota(jnp.int32, (rows, LANES), 1)


def membership(first_row, rows, bounds):
    place = lax.broadcasted_iota(jnp.int32, (rows, LANES), 0) + first_row
    return (place >= bounds[0]) & (place < bounds[1])


def query_extra(first_row, rows, bounds):
    return jnp.where(membership(first_row, rows, bounds), F32(MASKED_SCORE), F32(0.0))


def key_extra(first_row, rows, bounds, segs):
    lane = lanes_of(rows)
    used = (lane >= HEAD_DIM) & (lane < HEAD_DIM + segs + 3)
    return jnp.where(used & ~membership(first_row, rows, bounds), F32(1.0), F32(0.0))


def value_extra(rows):
    lane = lanes_of(rows)
    return jnp.where((lane >= HEAD_DIM) & (lane < HEAD_DIM + 2), F32(1.0), F32(0.0))


def head_slab(wide, head):
    if wide.shape[1] < LANES:
        return jnp.concatenate([wide, jnp.zeros_like(wide)], axis=1)
    first = head // 2 * LANES
    slab = wide[:, first : first + LANES]
    if head % 2:
        slab = pltpu.roll(slab, HEAD_DIM, 1)
    return slab


def put_heads(dest, where, wide, extra):
    low_lanes = lanes_of(wide.shape[0]) < HEAD_DIM
    for head in range(dest.shape[0]):
        dest[head, where, :] = jnp.where(low_lanes, head_slab(wide, head), extra).astype(dest.dtype)


def join_heads(dest, where, slabs):
    if len(slabs) == 1:
        dest[where, :] = slabs[0][:, :HEAD_DIM].astype(dest.dtype)
        return
    low_lanes = lanes_of(slabs[0].shape[0]) < HEAD_DIM
    for pair in range(len(slabs) // 2):
        both = jnp.where(low_lanes, slabs[2 * pair], pltpu.roll(slabs[2 * pair + 1], HEAD_DIM, 1))
        dest[where, pair * LANES : (pair + 1) * LANES] = both.astype(dest.dtype)


def span_for(block, length, from_starts, to_starts, to_ends):
    first_row = block * SPAN
    last_row = first_row + SPAN - 1
    low, high = jnp.int32(0), jnp.int32(0)
    for start, to_start, to_end in zip(from_starts, to_starts, to_ends):
        low = jnp.where(start <= first_row, to_start, low)
        high = jnp.where(start <= last_row, to_end, high)
    low = (low >> 7) << 7
    pieces = (high - low + SPAN - 1) >> 8
    return jnp.minimum(low, length - pieces * SPAN), pieces


def each_span(length, starts_from, starts_to, ends_to, body):
    def step(block, carry):
        start, pieces = span_for(block, length, starts_from, starts_to, ends_to)
        start = pl.multiple_of(start, LANES)
        rows = pl.ds(pl.multiple_of(block * SPAN, SPAN), SPAN)
        for count in range(1, length // SPAN + 1):

            @pl.when(pieces == count)
            def _():
                body(rows, pl.ds(start, count * SPAN))

        return carry

    lax.fori_loop(0, length // SPAN, step, 0)


def attend_body(qx, kx, vx, ctx, segs, rows, keys):
    scale = LOG2_E * HEAD_DIM**-0.5
    lane = lanes_of(SPAN)
    slabs = []
    for head in range(qx.shape[0]):
        query = qx[head, rows, :]
        scores = dot_nt(query, kx[head, keys, :])
        peak = jnp.max(scores, axis=1, keepdims=True)
        raised = jnp.exp2((scores - peak) * scale).astype(BF16)
        mixed = dot(raised, vx[head, keys, :])
        total = mixed[:, HEAD_DIM : HEAD_DIM + 1]
        slabs.append(mixed / total)
        level = -(peak + jnp.log(total) * (HEAD_DIM**0.5))
        high = level.astype(BF16).astype(F32)
        middle = (level - high).astype(BF16).astype(F32)
        low = level - high - middle
        base = HEAD_DIM + segs
        wide = query.astype(F32)
        wide = jnp.where(lane == base, high, wide)
        wide = jnp.where(lane == base + 1, middle, wide)
        wide = jnp.where(lane == base + 2, low, wide)
        qx[head, rows, :] = wide.astype(BF16)
    join_heads(ctx, rows, slabs)


def split_out(source, keep, send, share):
    me = lax.axis_index("heads")
    parts = send.shape[0] + 1
    for k in range(parts):
        owner = lax.rem(me + k, parts)
        rows = pl.ds(pl.multiple_of(owner * share, share), share)
        if k == 0:
            keep[...] = source[rows, :].astype(keep.dtype)
        else:
            send[k - 1] = source[rows, :].astype(send.dtype)


def self_forward_kernel(len_ref, x_ref, w_ref, keep, send, ctx, qx, kx, vx):
    length = x_ref.shape[0]
    segs = len_ref.shape[1]
    starts, ends = segment_bounds(len_ref)
    bounds = bound_lanes(starts, ends)

    def project(block, carry):
        first = pl.multiple_of(block * SPAN, SPAN)
        rows = pl.ds(first, SPAN)
        tokens = x_ref[rows, :]
        put_heads(qx, rows, dot(tokens, w_ref[0]), query_extra(first, SPAN, bounds))
        put_heads(kx, rows, dot(tokens, w_ref[1]), key_extra(first, SPAN, bounds, segs))
        put_heads(vx, rows, dot(tokens, w_ref[2]), value_extra(SPAN))
        return carry

    lax.fori_loop(0, length // SPAN, project, 0)
    each_span(
        length, starts, starts, ends, functools.partial(attend_body, qx, kx, vx, ctx, segs)
    )
    split_out(ctx, keep, send, keep.shape[0])


def cross_keys_kernel(len_ref, x_ref, w_ref, kx, vx):
    length = x_ref.shape[0]
    bounds = bound_lanes(*segment_bounds(len_ref))
    segs = len_ref.shape[1]

    def project(block, carry):
        first = pl.multiple_of(block * SPAN, SPAN)
        rows = pl.ds(first, SPAN)
        tokens = x_ref[rows, :]
        put_heads(kx, rows, dot(tokens, w_ref[0]), key_extra(first, SPAN, bounds, segs))
        put_heads(vx, rows, dot(tokens, w_ref[1]), value_extra(SPAN))
        return carry

    lax.fori_loop(0, length // SPAN, project, 0)


def gather_rows(dest, own, others):
    me = lax.axis_index("heads")
    parts = len(others) + 1
    share = own.shape[0]
    for k, source in enumerate([own, *others]):
        owner = lax.rem(me + k, parts)
        dest[pl.ds(pl.multiple_of(owner * share, share), share), :] = source[...]


def cross_forward_kernel(parts, dec_ref, enc_ref, kx, vx, *refs):
    pieces, (keep, send, ctx, qx, flat) = refs[:parts], refs[parts:]
    length = ctx.shape[0]
    segs = dec_ref.shape[1]
    dec_starts, dec_ends = segment_bounds(dec_ref)
    enc_starts, enc_ends = segment_bounds(enc_ref)
    bounds = bound_lanes(dec_starts, dec_ends)
    gather_rows(flat, pieces[0], pieces[1:])

    def widen(block, carry):
        first = pl.multiple_of(block * SPAN, SPAN)
        rows = pl.ds(first, SPAN)
        put_heads(qx, rows, flat[rows, :].astype(F32), query_extra(first, SPAN, bounds))
        return carry

    lax.fori_loop(0, length // SPAN, widen, 0)
    each_span(
        length, dec_starts, enc_starts, enc_ends,
        functools.partial(attend_body, qx, kx, vx, ctx, segs),
    )
    split_out(ctx, keep, send, keep.shape[0])


def attend_back_body(qx, kx, vx, gx, dq, dk, dv, rows, queries):
    scale = LOG2_E * HEAD_DIM**-0.5
    key_slabs, value_slabs = [], []
    for head in range(qx.shape[0]):
        keys = kx[head, rows, :]
        query = qx[head, queries, :]
        grads = gx[head, queries, :]
        weights = jnp.exp2(dot_nt(keys, query) * scale)
        raised = dot_nt(vx[head, rows, :], grads)
        value_slabs.append(dot(weights.astype(BF16), grads))
        inner = (weights * raised).astype(BF16)
        key_slabs.append(dot(inner, query) * (HEAD_DIM**-0.5))
        dq[head, queries, :] += dot_tn(inner, keys)
    join_heads(dk, rows, key_slabs)
    join_heads(dv, rows, value_slabs)


def attend_back(key_starts, key_ends, query_starts, query_ends, qx, kx, vx, ctx, grad, gx, dq, sq, sk, sv):
    length = ctx.shape[0]
    heads = qx.shape[0]
    lane = lanes_of(SPAN)

    def widen(block, carry):
        rows = pl.ds(pl.multiple_of(block * SPAN, SPAN), SPAN)
        wide = grad[rows, :].astype(F32)
        product = wide * ctx[rows, :].astype(F32)
        for head in range(heads):
            slab = head_slab(product, head)
            level = -jnp.sum(jnp.where(lane < HEAD_DIM, slab, 0.0), axis=1, keepdims=True)
            high = level.astype(BF16).astype(F32)
            extra = jnp.where(lane == HEAD_DIM, high, 0.0)
            extra = jnp.where(lane == HEAD_DIM + 1, level - high, extra)
            full = jnp.where(lane < HEAD_DIM, head_slab(wide, head), extra)
            gx[head, rows, :] = full.astype(BF16)
            dq[head, rows, :] = jnp.zeros((SPAN, LANES), F32)
        return carry

    lax.fori_loop(0, length // SPAN, widen, 0)
    each_span(
        length, key_starts, query_starts, query_ends,
        functools.partial(attend_back_body, qx, kx, vx, gx, dq, sk, sv),
    )

    def finish(block, carry):
        rows = pl.ds(pl.multiple_of(block * SPAN, SPAN), SPAN)
        join_heads(sq, rows, [dq[head, rows, :] * (HEAD_DIM**-0.5) for head in range(heads)])
        return carry

    lax.fori_loop(0, length // SPAN, finish, 0)


def norm_forward(summed, gain, bias):
    center = summed - jnp.mean(summed, axis=1, keepdims=True)
    inverse_dev = lax.rsqrt(jnp.mean(center * center, axis=1, keepdims=True) + NORM_EPS)
    normed = center * inverse_dev
    return normed * gain + bias, normed, inverse_dev


def norm_back(grad, normed, inverse_dev, gain):
    scaled = grad * gain
    back = inverse_dev * (
        scaled
        - jnp.mean(scaled, axis=1, keepdims=True)
        - normed * jnp.mean(scaled * normed, axis=1, keepdims=True)
    )
    gain_grad = jnp.sum(grad * normed, axis=0, keepdims=True)
    return back, gain_grad, jnp.sum(grad, axis=0, keepdims=True)


def share_block(share):
    return 256 if share % 256 == 0 else share


def own_rows(share, first, rows):
    start = lax.axis_index("heads") * share + first
    return pl.ds(pl.multiple_of(start, 64), rows)


def first_norm_kernel(parts, x_ref, gain, bias, *refs):
    ctx, w_out, w_query = refs[:parts], refs[parts : 2 * parts], refs[2 * parts : 3 * parts]
    first_out, first_low, normed_out, dev_out, keep, send = refs[3 * parts :]
    share = first_out.shape[0]
    block = share_block(share)

    def step(index, carry):
        first = pl.multiple_of(index * block, block)
        rows = pl.ds(first, block)
        total = x_ref[own_rows(share, first, block), :].astype(F32)
        for k in range(parts):
            total = total + dot(ctx[k][rows, :], w_out[k][...])
        result, normed, inverse_dev = norm_forward(total, gain[0:1, :], bias[0:1, :])
        low = result.astype(BF16)
        first_out[rows, :] = result
        first_low[rows, :] = low
        normed_out[rows, :] = normed
        dev_out[rows, :] = inverse_dev
        for k in range(parts):
            value = dot(low, w_query[k][...]).astype(BF16)
            if k == 0:
                keep[rows, :] = value
            else:
                send[k - 1, rows, :] = value
        return carry

    lax.fori_loop(0, share // block, step, 0)


def middle_kernel(parts, gain, bias, first_out, out_grad, *refs):
    groups = [refs[g * parts : (g + 1) * parts] for g in range(4)]
    ctx, w_cross, w_in, w_out = groups
    (layer_out, grad_mid, gains, biases, g_out_keep, g_out_send, g_in_keep, g_in_send,
     g_cross_keep, g_cross_send, back_keep, back_send,
     second, second_low, normed2, dev2, total, hidden, slope, top_low, back_sum) = refs[4 * parts :]
    share = first_out.shape[0]
    block = share_block(share)
    units = w_in[0].shape[1]
    chunk = min(256, units)

    def enter(index, carry):
        rows = pl.ds(pl.multiple_of(index * block, block), block)
        summed = first_out[rows, :]
        for k in range(parts):
            summed = summed + dot(ctx[k][rows, :], w_cross[k][...])
        result, normed, inverse_dev = norm_forward(summed, gain[1:2, :], bias[1:2, :])
        second[rows, :] = result
        second_low[rows, :] = result.astype(BF16)
        normed2[rows, :] = normed
        dev2[rows, :] = inverse_dev
        return carry

    lax.fori_loop(0, share // block, enter, 0)
    total[...] = second[...]
    for k in range(parts):

        def expand(index, carry):
            cols = pl.ds(pl.multiple_of(index * chunk, chunk), chunk)
            spot = k * (units // chunk) + index
            pre = dot(second_low[...], w_in[k][:, cols])
            square = pre * pre
            bent = jnp.tanh(pre * (GELU_RATE + (GELU_RATE * GELU_CUBE) * square))
            half = 0.5 + 0.5 * bent
            act = (pre * half).astype(BF16)
            hidden[spot] = act
            bend = (0.5 - 0.5 * bent * bent) * (
                GELU_RATE + (3.0 * GELU_RATE * GELU_CUBE) * square
            )
            slope[spot] = half + pre * bend
            total[...] += dot(act, w_out[k][cols, :])
            return carry

        lax.fori_loop(0, units // chunk, expand, 0)

    gains[...] = jnp.zeros_like(gains)
    biases[...] = jnp.zeros_like(biases)

    def turn(index, carry):
        first = pl.multiple_of(index * block, block)
        rows = pl.ds(first, block)
        result, normed, inverse_dev = norm_forward(total[rows, :], gain[2:3, :], bias[2:3, :])
        layer_out[rows, :] = result
        grad = out_grad[own_rows(share, first, block), :].astype(F32)
        back, gain_grad, bias_grad = norm_back(grad, normed, inverse_dev, gain[2:3, :])
        gains[1:2, :] += gain_grad
        biases[1:2, :] += bias_grad
        back_sum[rows, :] = back
        top_low[rows, :] = back.astype(BF16)
        return carry

    lax.fori_loop(0, share // block, turn, 0)
    for k in range(parts):

        def contract(index, carry):
            cols = pl.ds(pl.multiple_of(index * chunk, chunk), chunk)
            spot = k * (units // chunk) + index
            weight_out = dot_tn(hidden[spot], top_low[...]).astype(BF16)
            pre = (dot_nt(top_low[...], w_out[k][cols, :]) * slope[spot]).astype(BF16)
            weight_in = dot_tn(second_low[...], pre).astype(BF16)
            if k == 0:
                g_out_keep[cols, :] = weight_out
                g_in_keep[:, cols] = weight_in
            else:
                g_out_send[k - 1, cols, :] = weight_out
                g_in_send[k - 1, :, cols] = weight_in
            back_sum[...] += dot_nt(pre, w_in[k][:, cols])
            return carry

        lax.fori_loop(0, units // chunk, contract, 0)

    def leave(index, carry):
        rows = pl.ds(pl.multiple_of(index * block, block), block)
        back, gain_grad, bias_grad = norm_back(
            back_sum[rows, :], normed2[rows, :], dev2[rows, :], gain[1:2, :]
        )
        gains[0:1, :] += gain_grad
        biases[0:1, :] += bias_grad
        grad_mid[rows, :] = back
        low = back.astype(BF16)
        top_low[rows, :] = low
        for k in range(parts):
            value = dot_nt(low, w_cross[k][...]).astype(BF16)
            if k == 0:
                back_keep[rows, :] = value
            else:
                back_send[k - 1, rows, :] = value
        return carry

    lax.fori_loop(0, share // block, leave, 0)
    for k in range(parts):
        value = dot_tn(ctx[k][...], top_low[...]).astype(BF16)
        if k == 0:
            g_cross_keep[...] = value
        else:
            g_cross_send[k - 1] = value


def cross_back_kernel(parts, dec_ref, enc_ref, qx, kx, vx, ctx, enc, w_kv, *refs):
    pieces = refs[:parts]
    (gq_keep, gq_send, g_kv, enc_keep, enc_send, grad, gx, dq, sq, sk, sv, wide) = refs[parts:]
    length = ctx.shape[0]
    dec_starts, dec_ends = segment_bounds(dec_ref)
    enc_starts, enc_ends = segment_bounds(enc_ref)
    gather_rows(grad, pieces[0], pieces[1:])
    attend_back(
        enc_starts, enc_ends, dec_starts, dec_ends, qx, kx, vx, ctx, grad, gx, dq, sq, sk, sv
    )
    split_out(sq, gq_keep, gq_send, gq_keep.shape[0])
    g_kv[0] = dot_tn(enc[...], sk[...]).astype(BF16)
    g_kv[1] = dot_tn(enc[...], sv[...]).astype(BF16)

    def step(block, carry):
        rows = pl.ds(pl.multiple_of(block * SPAN, SPAN), SPAN)
        wide[rows, :] = dot_nt(sk[rows, :], w_kv[0]) + dot_nt(sv[rows, :], w_kv[1])
        return carry

    lax.fori_loop(0, length // SPAN, step, 0)
    split_out(wide, enc_keep, enc_send, enc_keep.shape[0])


def first_back_kernel(parts, gain, grad_mid, first_low, normed, dev, *refs):
    groups = [refs[g * parts : (g + 1) * parts] for g in range(4)]
    gq, w_query, ctx, w_out = groups
    (grad_base, gains, biases, g_query_keep, g_query_send, g_out_keep, g_out_send,
     back_keep, back_send, low_ref) = refs[4 * parts :]
    share = grad_mid.shape[0]
    block = share_block(share)
    gains[...] = jnp.zeros_like(gains)
    biases[...] = jnp.zeros_like(biases)

    def step(index, carry):
        rows = pl.ds(pl.multiple_of(index * block, block), block)
        grad = grad_mid[rows, :]
        for k in range(parts):
            grad = grad + dot_nt(gq[k][rows, :], w_query[k][...])
        back, gain_grad, bias_grad = norm_back(grad, normed[rows, :], dev[rows, :], gain[0:1, :])
        gains[...] += gain_grad
        biases[...] += bias_grad
        grad_base[rows, :] = back
        low = back.astype(BF16)
        low_ref[rows, :] = low
        for k in range(parts):
            value = dot_nt(low, w_out[k][...]).astype(BF16)
            if k == 0:
                back_keep[rows, :] = value
            else:
                back_send[k - 1, rows, :] = value
        return carry

    lax.fori_loop(0, share // block, step, 0)
    for k in range(parts):
        query_grad = dot_tn(first_low[...], gq[k][...]).astype(BF16)
        out_grad = dot_tn(ctx[k][...], low_ref[...]).astype(BF16)
        if k == 0:
            g_query_keep[...] = query_grad
            g_out_keep[...] = out_grad
        else:
            g_query_send[k - 1] = query_grad
            g_out_send[k - 1] = out_grad


def self_back_kernel(parts, dec_ref, qx, kx, vx, ctx, x_ref, w_qkv, *refs):
    pieces = refs[:parts]
    g_qkv, in_keep, in_send, grad, gx, dq, sq, sk, sv, wide = refs[parts:]
    length = ctx.shape[0]
    starts, ends = segment_bounds(dec_ref)
    gather_rows(grad, pieces[0], pieces[1:])
    attend_back(starts, ends, starts, ends, qx, kx, vx, ctx, grad, gx, dq, sq, sk, sv)
    for c, source in enumerate((sq, sk, sv)):
        g_qkv[c] = dot_tn(x_ref[...], source[...]).astype(BF16)

    def step(block, carry):
        rows = pl.ds(pl.multiple_of(block * SPAN, SPAN), SPAN)
        wide[rows, :] = (
            dot_nt(sq[rows, :], w_qkv[0])
            + dot_nt(sk[rows, :], w_qkv[1])
            + dot_nt(sv[rows, :], w_qkv[2])
        )
        return carry

    lax.fori_loop(0, length // SPAN, step, 0)
    split_out(wide, in_keep, in_send, in_keep.shape[0])


LINK_RATE = 0.088
HOP_TIME = 2.0
TAKE_TIME = 0.15
SLACK = 1.0


class Part:
    def __init__(self, out, row, col, rows, cols, ready):
        self.out, self.row, self.col, self.rows, self.cols = out, row, col, rows, cols
        self.ready = ready
        self.order = None

    def window(self):
        return (pl.ds(self.row, self.rows), pl.ds(self.col, self.cols))


def link_cost(part, step, bits):
    depth = step if step < bits else 2 * bits - 1 - step
    amount = part.rows * part.cols * 2e-6 / 2 ** (depth + 1) * 2 / LINK_RATE
    bit = part.order[depth]
    return {bit: 2 * amount, bit - 1: amount} if bit == bits - 1 else {bit: amount}


def choose_orders(parts, bits):
    last = bits - 1
    options = [(0, 1, 2, last), (1, 0, 2, last), (2, 0, 1, last), (2, 1, 0, last)]
    load = dict.fromkeys(range(bits), 0.0)
    for part in parts:
        best = None
        for order in options:
            part.order = order
            trial = dict(load)
            for step in range(2 * bits):
                for bit, amount in link_cost(part, step, bits).items():
                    trial[bit] += amount
            score = sum(value * value for value in trial.values())
            if best is None or score < best[0]:
                best = (score, order, trial)
        _, part.order, load = best


def plan_transfers(parts, bits, spans):
    steps = 2 * bits
    busy = dict.fromkeys(range(bits), 0.0)
    left = [0] * len(parts)
    since = [None] * len(parts)
    flying = []

    def rest(p):
        return sum(max(link_cost(parts[p], s, bits).values()) + HOP_TIME for s in range(left[p], steps))

    def serve(clock, ahead, slack, found):
        for entry in sorted(flying):
            if entry[0] + slack <= clock:
                flying.remove(entry)
                found.append(("take", entry[1], left[entry[1]]))
                left[entry[1]] += 1
                since[entry[1]] = clock if left[entry[1]] < steps else None
                clock += TAKE_TIME
        for p in sorted((p for p in range(len(parts)) if since[p] is not None), key=lambda p: (-rest(p), p)):
            cost = link_cost(parts[p], left[p], bits)
            if since[p] <= clock and all(busy[b] <= clock + ahead for b in cost):
                done = clock
                for b, amount in cost.items():
                    busy[b] = max(busy[b], clock) + amount
                    done = max(done, busy[b])
                found.append(("send", p, left[p]))
                flying.append((done + HOP_TIME, p))
                since[p] = None
        return clock

    slots, clock = [], 0.0
    for unit, span in enumerate(spans):
        for p, part in enumerate(parts):
            if part.ready[0] == unit:
                since[p] = clock + part.ready[1]
        found = []
        clock = serve(clock, span + 0.5, SLACK, found)
        slots.append(found)
        clock += span
    for p, part in enumerate(parts):
        if part.ready[0] >= len(spans):
            since[p] = clock + part.ready[1]
    found = []
    while flying or any(value is not None for value in since):
        before = len(found)
        clock = serve(clock, 1.0, 0.0, found)
        if len(found) == before:
            clock += 0.05
    slots.append(found)
    return slots


class RowsSum:
    def __init__(self, parts, bits, held, landing, final, outs, send_sem, land_sem, store_sem):
        self.parts, self.bits = parts, bits
        self.held, self.landing, self.final, self.outs = held, landing, final, outs
        self.send_sem, self.land_sem, self.store_sem = send_sem, land_sem, store_sem
        self.begin = [lambda: None] * len(parts)

    def side(self, bit):
        return lax.shift_right_logical(lax.axis_index("rows"), bit) & 1

    def peer(self, bit):
        me = lax.axis_index("rows")
        return {"rows": me + (1 << bit) - 2 * (me & (1 << bit)), "heads": lax.axis_index("heads")}

    def offset(self, p, depth):
        part, total = self.parts[p], jnp.int32(0)
        for d in range(depth):
            total = total + self.side(part.order[d]) * (part.rows >> (d + 1))
        return total

    def copy(self, p, step):
        part = self.parts[p]
        depth = step if step < self.bits else 2 * self.bits - 1 - step
        bit = part.order[depth]
        size = part.rows >> (depth + 1)
        if step < self.bits:
            first = self.offset(p, depth) + (1 - self.side(bit)) * size
            source = self.held[p].at[pl.ds(pl.multiple_of(first, 16), size), :]
            dest = self.landing[p].at[pl.ds(part.rows - 2 * size, size), :]
        else:
            first = self.offset(p, depth + 1)
            source = self.final[p].at[pl.ds(pl.multiple_of(first, 16), size), :]
            dest = source
        return pltpu.make_async_remote_copy(
            src_ref=source, dst_ref=dest, send_sem=self.send_sem.at[p, step],
            recv_sem=self.land_sem.at[p, step], device_id=self.peer(bit),
            device_id_type=pl.DeviceIdType.MESH,
        )

    def store(self, p):
        part = self.parts[p]
        return pltpu.make_async_copy(
            self.final[p], self.outs[part.out].at[part.window()], self.store_sem.at[p]
        )

    def run(self, ops):
        for kind, p, step in ops:
            if kind == "send":
                if step == 0:
                    self.begin[p]()
                self.copy(p, step).start()
                continue
            self.copy(p, step).wait()
            if step < self.bits:
                part = self.parts[p]
                size = part.rows >> (step + 1)
                mine = pl.ds(pl.multiple_of(self.offset(p, step + 1), 16), size)
                spot = pl.ds(part.rows - 2 * size, size)
                total = self.held[p][mine, :].astype(F32) + self.landing[p][spot, :].astype(F32)
                dest = self.final[p] if step == self.bits - 1 else self.held[p]
                dest[mine, :] = total.astype(BF16)
            elif step == 2 * self.bits - 1:
                self.store(p).start()


def add_into(dest, other):
    dest[...] = (dest[...].astype(F32) + other[...].astype(F32)).astype(dest.dtype)


def back_unit(qx, kx, vx, gx, dq, sk, sv, head, block):
    scale = LOG2_E * HEAD_DIM**-0.5
    rows = pl.ds(pl.multiple_of(block * SPAN, SPAN), SPAN)
    keys = kx[head, rows, :]
    query = qx[head]
    grads = gx[head]
    weights = jnp.exp2(dot_nt(keys, query) * scale)
    raised = dot_nt(vx[head, rows, :], grads)
    value_slab = dot(weights.astype(BF16), grads)
    inner = (weights * raised).astype(BF16)
    key_slab = dot(inner, query) * (HEAD_DIM**-0.5)
    dq[head] += dot_tn(inner, keys)
    odd = (head & 1) == 1
    low_lanes = lanes_of(SPAN) < HEAD_DIM
    cols = pl.ds(pl.multiple_of((head >> 1) * LANES, LANES), LANES)
    for dest, slab in ((sk, key_slab), (sv, value_slab)):
        old = dest[rows, cols].astype(F32)
        turned = pltpu.roll(slab, HEAD_DIM, 1)
        first = jnp.where(odd, old, slab)
        second = jnp.where(odd, turned, slab)
        dest[rows, cols] = jnp.where(low_lanes, first, second).astype(BF16)


def tail_kernel(parts, bits, plan, gain, gains_high, biases_high, *refs):
    rest = list(refs)
    take = lambda number: [rest.pop(0) for _ in range(number)]
    (gq_keep_in, gq_send_in, grad_mid_in, first_low_in, normed_in, dev_in, wq0_in, wq1_in, ctx0_in, ctx1_in,
     wo0_in, wo1_in, qx_in, kx_in, vx_in, ctx_in, x_in, w_in) = take(18)
    ffn_out_own, ffn_out_away, ffn_in_own, ffn_in_away, cross_own, cross_away, kv_own = take(7)
    outs = take(7)
    small_out, in_keep, in_land_out = take(3)
    count = len(parts)
    held, landing, final = take(count), take(count), take(count)
    mates = dict(zip([p for p in range(count) if parts[p].out in (0, 1, 2, 3, 5)], rest))
    take(len(mates))
    (gq, gq_land, grad_mid, first_low, normed, dev, wq0, wq1, ctx0, ctx1, wo0, wo1, qx, kx, vx, ctx, x_ref, w_ref,
     grad, gx, dq, sq, sk, sv, wide, low, back_out, query_out, self_out, in_out, in_land, small_land) = take(32)
    (send_sem, land_sem, store_sem, load_sem, part_sem, mate_send, mate_land, core_send, core_land,
     small_send, small_sem, out_sem) = rest
    share, width = grad_mid.shape
    length = x_ref.shape[0]
    heads = qx.shape[0]
    block = 256
    me, core = lax.axis_index("rows"), lax.axis_index("heads")
    other_core = {"rows": me, "heads": 1 - core}
    summing = RowsSum(parts, bits, held, landing, final, outs, send_sem, land_sem, store_sem)

    def across(source, dest, send, land, peer=other_core):
        return pltpu.make_async_remote_copy(
            src_ref=source, dst_ref=dest, send_sem=send, recv_sem=land,
            device_id=peer, device_id_type=pl.DeviceIdType.MESH,
        )

    pairs = [
        (gq_keep_in, gq), (grad_mid_in, grad_mid), (wq0_in, wq0), (wq1_in, wq1), (normed_in, normed), (dev_in, dev),
        (wo0_in, wo0), (wo1_in, wo1), (first_low_in, first_low), (ctx0_in, ctx0), (ctx1_in, ctx1), (ctx_in, ctx),
        (qx_in, qx), (kx_in, kx), (vx_in, vx), (x_in, x_ref), (w_in, w_ref),
    ]
    loads = [pltpu.make_async_copy(a, b, load_sem.at[k]) for k, (a, b) in enumerate(pairs)]
    own_arrays = {0: ffn_out_own, 1: ffn_in_own, 2: cross_own, 4: kv_own}
    away_arrays = {0: ffn_out_away, 1: ffn_in_away, 2: cross_away}
    for load in loads[:6]:
        load.start()
    peers = [summing.peer(bit) for bit in range(bits)] + [other_core]
    barrier = pltpu.get_barrier_semaphore()
    for peer in peers:
        pl.semaphore_signal(barrier, inc=1, device_id=peer, device_id_type=pl.DeviceIdType.MESH)
    pl.semaphore_wait(barrier, len(peers))
    gq_copy = across(gq_send_in.at[0], gq_land, core_send.at[0], core_land.at[0])
    gq_copy.start()
    part_loads, mate_copies = {}, {}
    for p, part in enumerate(parts):
        if part.out in own_arrays:
            part_loads[p] = pltpu.make_async_copy(
                own_arrays[part.out].at[part.window()], held[p], part_sem.at[p]
            )
            part_loads[p].start()
        if part.out in away_arrays:
            mate_copies[p] = across(
                away_arrays[part.out].at[(0, *part.window())], mates[p], mate_send.at[p], mate_land.at[p]
            )
            mate_copies[p].start()
    for load in loads[6:]:
        load.start()
    for p, part in enumerate(parts):
        if part.out == 3:
            mate_copies[p] = across(query_out, mates[p], mate_send.at[p], mate_land.at[p])
        if part.out == 5:
            mate_copies[p] = across(self_out, mates[p], mate_send.at[p], mate_land.at[p])

        def begin(p=p):
            if p in part_loads:
                part_loads[p].wait()
            if p in mate_copies:
                mate_copies[p].wait()
                add_into(held[p], mates[p])

        summing.begin[p] = begin

    slots = list(plan)
    for load in loads[:6]:
        load.wait()
    gq_copy.wait()
    for load in loads[6:8]:
        load.wait()
    small_out[...] = jnp.zeros_like(small_out)
    small_out[1:3, :] = gains_high[...]
    small_out[4:6, :] = biases_high[...]
    back_copies = []
    for index in range(share // block):
        summing.run(slots.pop(0))
        rows = pl.ds(index * block, block)
        mine = own_rows(share, index * block, block)
        value = grad_mid[rows, :] + dot_nt(gq[rows, :], wq0[...]) + dot_nt(gq_land[rows, :], wq1[...])
        back, gain_grad, bias_grad = norm_back(value, normed[rows, :], dev[rows, :], gain[0:1, :])
        small_out[0:1, :] += gain_grad
        small_out[3:4, :] += bias_grad
        in_keep[rows, :] = back
        low_part = back.astype(BF16)
        low[rows, :] = low_part
        grad[mine, :] = dot_nt(low_part, wo0[...]).astype(BF16)
        back_out[rows, :] = dot_nt(low_part, wo1[...]).astype(BF16)
        copy = across(back_out.at[rows, :], grad.at[mine, :], core_send.at[1 + index], core_land.at[1 + index])
        copy.start()
        back_copies.append(copy)
    summing.run(slots.pop(0))
    for load in loads[8:12]:
        load.wait()
    query_out[...] = dot_tn(first_low[...], gq_land[...]).astype(BF16)
    self_out[...] = dot_tn(ctx1[...], low[...]).astype(BF16)
    for p, part in enumerate(parts):
        if part.out in (3, 5):
            mate_copies[p].start()
        if part.out == 3:
            held[p][...] = dot_tn(first_low[...], gq[...]).astype(BF16)
        if part.out == 5:
            held[p][...] = dot_tn(ctx0[...], low[...]).astype(BF16)
    summing.run(slots.pop(0))
    for copy in back_copies:
        copy.wait()
    for load in loads[12:]:
        load.wait()
    lane = lanes_of(SPAN)

    def widen(index, carry):
        rows = pl.ds(pl.multiple_of(index * SPAN, SPAN), SPAN)
        broad = grad[rows, :].astype(F32)
        product = broad * ctx[rows, :].astype(F32)
        for head in range(heads):
            slab = head_slab(product, head)
            level = -jnp.sum(jnp.where(lane < HEAD_DIM, slab, 0.0), axis=1, keepdims=True)
            high = level.astype(BF16).astype(F32)
            extra = jnp.where(lane == HEAD_DIM, high, 0.0)
            extra = jnp.where(lane == HEAD_DIM + 1, level - high, extra)
            full = jnp.where(lane < HEAD_DIM, head_slab(broad, head), extra)
            gx[head, rows, :] = full.astype(BF16)
            dq[head, rows, :] = jnp.zeros((SPAN, LANES), F32)
        return carry

    lax.fori_loop(0, length // SPAN, widen, 0)
    blocks = length // SPAN
    in_copy = across(in_out, in_land, core_send.at[1 + share // block], core_land.at[1 + share // block])
    for pair in range(heads // 2):
        mine = [slots.pop(0) for _ in range(2 * blocks)]

        def unit(index, carry):
            lax.switch(index, [functools.partial(summing.run, ops) for ops in mine])
            back_unit(
                qx, kx, vx, gx, dq, sk, sv, 2 * pair + lax.div(index, blocks), lax.rem(index, blocks)
            )
            return carry

        lax.fori_loop(0, 2 * blocks, unit, 0)
        cols = pl.ds(pair * LANES, LANES)
        summing.run(slots.pop(0))

        def finish(index, carry):
            rows = pl.ds(pl.multiple_of(index * SPAN, SPAN), SPAN)
            join_heads(
                sq.at[:, cols], rows,
                [dq[head, rows, :] * (HEAD_DIM**-0.5) for head in (2 * pair, 2 * pair + 1)],
            )
            return carry

        lax.fori_loop(0, blocks, finish, 0)
        for p, part in enumerate(parts):
            if part.out == 6 and part.col == pair * LANES:
                source = (sq, sk, sv)[part.row // width]
                held[p][...] = dot_tn(x_ref[...], source[:, cols]).astype(BF16)
        summing.run(slots.pop(0))

        def spread(index, carry):
            rows = pl.ds(pl.multiple_of(index * SPAN, SPAN), SPAN)
            value = dot_nt(sq[rows, cols], w_ref[0, :, cols])
            value = value + dot_nt(sk[rows, cols], w_ref[1, :, cols])
            value = value + dot_nt(sv[rows, cols], w_ref[2, :, cols])
            if pair == 0:
                wide[rows, :] = value
            else:
                wide[rows, :] += value
            return carry

        lax.fori_loop(0, blocks, spread, 0)
    away = pl.ds(pl.multiple_of((1 - core) * share, share), share)
    in_out[...] = wide[away, :].astype(BF16)
    in_copy.start()
    here = pl.ds(pl.multiple_of(core * share, share), share)
    in_keep[...] += wide[here, :]
    last = slots.pop(0)
    small_copy = None
    for k in range(len(peers) + 1):
        cut = len(last) * k // (len(peers) + 1), len(last) * (k + 1) // (len(peers) + 1)
        if small_copy is not None:
            small_copy.wait()
            small_out[...] += small_land[k - 1]
        if k < len(peers):
            small_copy = across(
                small_out, small_land.at[k], small_send.at[k], small_sem.at[k], peers[k]
            )
            small_copy.start()
        if k == len(peers):
            in_copy.wait()
            in_store = pltpu.make_async_copy(in_land, in_land_out, out_sem)
            in_store.start()
        summing.run(last[cut[0] : cut[1]])
    in_store.wait()
    for p in range(count):
        summing.store(p).wait()


def widen_kernel(table, *refs):
    sources = 1 + max(max(e[0], -1 if e[1] is None else e[1]) for e in table)
    outs = 1 + max(e[2] for e in table)
    arrays, dests = refs[:sources], refs[sources : sources + outs]
    rest = list(refs[sources + outs :])
    low = [rest.pop(0) for _ in table]
    more = {k: rest.pop(0) for k, e in enumerate(table) if e[1] is not None}
    wide = [rest.pop(0) for _ in table]
    load_sem, more_sem, store_sem = rest
    loads, stores = [], []
    for k, (source, second, out, window) in enumerate(table):
        window = tuple(pl.ds(*w) for w in window)
        loads.append([pltpu.make_async_copy(arrays[source].at[window], low[k], load_sem.at[k])])
        if second is not None:
            loads[k].append(pltpu.make_async_copy(arrays[second].at[window], more[k], more_sem.at[k]))
        stores.append(pltpu.make_async_copy(wide[k], dests[out].at[window], store_sem.at[k]))
        for load in loads[k]:
            load.start()
    for k in range(len(table)):
        for load in loads[k]:
            load.wait()
        value = low[k][...].astype(F32)
        if k in more:
            value = value + more[k][...].astype(F32)
        wide[k][...] = value
        stores[k].start()
    for store in stores:
        store.wait()


def widen_all(entries):
    arrays, table, shapes = [], [], []
    for out, (first, second) in enumerate(entries):
        source = len(arrays)
        arrays.append(first)
        if second is not None:
            arrays.append(second)
        rows, cols = first.shape
        shapes.append(shape_of((rows, cols), F32))
        high = 256 if cols >= 512 else 512
        for row in range(0, rows, high):
            table.append((source, None if second is None else source + 1, out, ((row, high), (0, cols))))
    spaces = [pl.BlockSpec(memory_space=pl.ANY)]
    sized = lambda e: (e[3][0][1], e[3][1][1])
    return pl.pallas_call(
        functools.partial(widen_kernel, table),
        out_shape=shapes,
        in_specs=spaces * len(arrays),
        out_specs=spaces * len(shapes),
        scratch_shapes=[pltpu.VMEM(sized(e), arrays[e[0]].dtype) for e in table]
        + [pltpu.VMEM(sized(e), arrays[e[1]].dtype) for e in table if e[1] is not None]
        + [pltpu.VMEM(sized(e), F32) for e in table]
        + [pltpu.SemaphoreType.DMA((len(table),))] * 3,
        compiler_params=pltpu.CompilerParams(vmem_limit_bytes=60 * 2**20),
    )(*arrays)


def run_tail(gain, gains_high, biases_high, first_args, halves, shapes):
    bits = lax.axis_size("rows").bit_length() - 1
    share, local = first_args[0].shape
    width = first_args[2].shape[1]
    length = 2 * share
    heads = local // HEAD_DIM
    blocks = length // SPAN
    norm_units, pairs = share // 256, heads // 2
    spans = [1.3] * norm_units + [1.8, 1.5]
    pair_end = []
    for _ in range(pairs):
        spans += [1.15] * (2 * blocks) + [2.0, 2.5]
        pair_end.append(len(spans) - 1)
    parts = []
    began = 0.0
    for out, (rows, cols) in enumerate(shapes):
        high, broad = (256, 512) if cols == 512 else (512, 256)
        if out == 6:
            broad = LANES
        for col in range(0, cols, broad):
            for row in range(0, rows, high):
                if out in (0, 1, 2):
                    began += 0.6
                ready = (0, began)
                if out in (3, 5):
                    ready = (norm_units + 1, 1.0)
                if out == 6:
                    ready = (pair_end[col // LANES], 0.0)
                parts.append(Part(out, row, col, high, broad, ready))
    choose_orders(parts, bits)
    plan = plan_transfers(parts, bits, spans)
    count = len(parts)
    buffers = [pltpu.VMEM((p.rows, p.cols), BF16) for p in parts]
    mated = [b for b, p in zip(buffers, parts) if p.out in (0, 1, 2, 3, 5)]
    vm = lambda kind, *dims: pltpu.VMEM(dims, kind)
    wide_heads = vm(BF16, heads, length, LANES)
    own = [
        vm(BF16, share, local), vm(BF16, share, local), vm(F32, share, width), vm(BF16, share, width),
        vm(F32, share, width), vm(F32, share, 1), vm(BF16, width, local), vm(BF16, width, local),
        vm(BF16, share, local), vm(BF16, share, local), vm(BF16, local, width), vm(BF16, local, width),
        wide_heads, wide_heads, wide_heads, vm(BF16, length, local), vm(BF16, length, width),
        vm(BF16, 3, width, local),
        vm(BF16, length, local), wide_heads, vm(F32, heads, length, LANES),
        vm(BF16, length, local), vm(BF16, length, local), vm(BF16, length, local), vm(F32, length, width),
        vm(BF16, share, width), vm(BF16, share, local), vm(BF16, width, local), vm(BF16, local, width),
        vm(BF16, share, width), vm(BF16, share, width), vm(F32, bits + 1, 8, width),
    ]
    sems = [
        (count, 2 * bits), (count, 2 * bits), (count,), (17,), (count,), (count,), (count,),
        (2 + norm_units,), (2 + norm_units,), (bits + 1,), (bits + 1,),
    ]
    anyspace = pl.BlockSpec(memory_space=pl.ANY)
    return pl.pallas_call(
        functools.partial(tail_kernel, parts, bits, plan),
        out_shape=[shape_of(dims, BF16) for dims in shapes]
        + [shape_of((8, width), F32), shape_of((share, width), F32), shape_of((share, width), BF16)],
        in_specs=[VMEM] * 3 + [anyspace] * (len(first_args) + len(halves)),
        out_specs=[anyspace] * len(shapes) + [VMEM, VMEM, anyspace],
        scratch_shapes=buffers * 3 + mated + own
        + [pltpu.SemaphoreType.DMA(dims) for dims in sems] + [pltpu.SemaphoreType.DMA],
        compiler_params=pltpu.CompilerParams(
            vmem_limit_bytes=62 * 2**20, collective_id=0, has_side_effects=True
        ),
    )(gain, gains_high, biases_high, *first_args, *halves)


def fits_tail(length, width, local, units):
    return (
        lax.axis_size("rows") == 16
        and lax.axis_size("heads") == 2
        and (width, local) == (512, 256)
        and length % 512 == 0
        and units % 512 == 0
    )


def body(
    dec_input,
    enc_output,
    dec_lengths,
    enc_lengths,
    w_self_qkv,
    w_self_out,
    w_cross_q,
    w_cross_kv,
    w_cross_out,
    w_ffn_in,
    w_ffn_out,
    norm_gain,
    norm_bias,
    out_grad,
):
    parts = lax.axis_size("heads")
    length, width = dec_input.shape
    local = w_self_out.shape[0]
    heads = local // HEAD_DIM
    share = length // parts
    units = w_ffn_in.shape[1]
    chunk = min(256, units)
    chunks = parts * units // chunk

    def shift(value, k):
        return lax.ppermute(value, "heads", [(d, (d + k) % parts) for d in range(parts)])

    def slots(shard):
        return [shard] + [shift(shard, parts - k) for k in range(1, parts)]

    def swap(keep, send):
        return [keep] + [shift(send[parts - k - 1], parts - k) for k in range(1, parts)]

    def collect(keep, send):
        total = keep.astype(F32)
        for k in range(1, parts):
            total = total + shift(send[k - 1], k).astype(F32)
        return total

    self_out, cross_q, cross_out = slots(w_self_out), slots(w_cross_q), slots(w_cross_out)
    ffn_in, ffn_out = slots(w_ffn_in), slots(w_ffn_out)

    def sent(*dims, kind=BF16):
        return shape_of((parts - 1, *dims), kind)

    def own(*dims, kind=BF16):
        return shape_of(dims, kind)

    wide_heads = own(heads, length, LANES)
    self_keep, self_send, self_ctx, self_qx, self_kx, self_vx = call(
        self_forward_kernel,
        [own(share, local), sent(share, local), own(length, local), wide_heads, wide_heads, wide_heads],
        [], 40, dec_lengths, dec_input, w_self_qkv, smem=1,
    )
    self_slots = swap(self_keep, self_send)
    cross_kx, cross_vx = call(
        cross_keys_kernel, [wide_heads, wide_heads], [], 32,
        enc_lengths, enc_output, w_cross_kv, smem=1,
    )
    first_out, first_low, first_normed, first_dev, query_keep, query_send = call(
        functools.partial(first_norm_kernel, parts),
        [own(share, width, kind=F32), own(share, width), own(share, width, kind=F32),
         own(share, 1, kind=F32), own(share, local), sent(share, local)],
        [], 32, dec_input, norm_gain, norm_bias, *self_slots, *self_out, *cross_q,
    )
    cross_keep, cross_send, cross_ctx, cross_qx = call(
        functools.partial(cross_forward_kernel, parts),
        [own(share, local), sent(share, local), own(length, local), wide_heads],
        [pltpu.VMEM((length, local), BF16)], 40,
        dec_lengths, enc_lengths, cross_kx, cross_vx, *swap(query_keep, query_send), smem=2,
    )
    cross_slots = swap(cross_keep, cross_send)
    (layer_out, grad_mid, gains_high, biases_high, g_ffn_out, g_ffn_out_send, g_ffn_in,
     g_ffn_in_send, g_cross_out, g_cross_out_send, back_keep, back_send) = call(
        functools.partial(middle_kernel, parts),
        [own(share, width, kind=F32), own(share, width, kind=F32),
         own(2, width, kind=F32), own(2, width, kind=F32),
         own(units, width), sent(units, width), own(width, units), sent(width, units),
         own(local, width), sent(local, width), own(share, local), sent(share, local)],
        [pltpu.VMEM((share, width), F32), pltpu.VMEM((share, width), BF16),
         pltpu.VMEM((share, width), F32), pltpu.VMEM((share, 1), F32),
         pltpu.VMEM((share, width), F32), pltpu.VMEM((chunks, share, chunk), BF16),
         pltpu.VMEM((chunks, share, chunk), F32), pltpu.VMEM((share, width), BF16),
         pltpu.VMEM((share, width), F32)],
        56, norm_gain, norm_bias, first_out, out_grad,
        *cross_slots, *cross_out, *ffn_in, *ffn_out,
    )
    back_scratch = [
        pltpu.VMEM((length, local), BF16),
        pltpu.VMEM((heads, length, LANES), BF16),
        pltpu.VMEM((heads, length, LANES), F32),
        pltpu.VMEM((length, local), BF16),
        pltpu.VMEM((length, local), BF16),
        pltpu.VMEM((length, local), BF16),
        pltpu.VMEM((length, width), F32),
    ]
    gq_keep, gq_send, g_cross_kv, enc_keep, enc_send = call(
        functools.partial(cross_back_kernel, parts),
        [own(share, local), sent(share, local), own(2, width, local),
         own(share, width, kind=F32), sent(share, width)],
        back_scratch, 56, dec_lengths, enc_lengths, cross_qx, cross_kx, cross_vx, cross_ctx,
        enc_output, w_cross_kv, *swap(back_keep, back_send), smem=2,
    )
    if fits_tail(length, width, local, units):
        shapes = [
            (units, width), (width, units), (local, width), (width, local),
            (2 * width, local), (local, width), (3 * width, local),
        ]
        *sums, small, in_keep, in_land = run_tail(
            norm_gain, gains_high, biases_high,
            [gq_keep, gq_send, grad_mid, first_low, first_normed, first_dev, *cross_q,
             *self_slots, *self_out, self_qx, self_kx, self_vx, self_ctx, dec_input, w_self_qkv],
            [g_ffn_out, g_ffn_out_send, g_ffn_in, g_ffn_in_send, g_cross_out, g_cross_out_send,
             g_cross_kv.reshape(2 * width, local)],
            shapes,
        )
        (s_ffn_out, s_ffn_in, s_cross_out, s_cross_q, s_cross_kv, s_self_out, s_self_qkv,
         input_grad, enc_grad) = widen_all(
            [(value, None) for value in sums]
            + [(in_keep, in_land), (enc_keep, shift(enc_send[0], 1))]
        )
        return (
            layer_out, input_grad, enc_grad, s_self_qkv.reshape(3, width, local), s_self_out, s_cross_q,
            s_cross_kv.reshape(2, width, local), s_cross_out, s_ffn_in, s_ffn_out, small[:3], small[3:6],
        )
    enc_grad = collect(enc_keep, enc_send)
    (grad_base, gains_low, biases_low, g_cross_q, g_cross_q_send, g_self_out, g_self_out_send,
     self_back_keep, self_back_send) = call(
        functools.partial(first_back_kernel, parts),
        [own(share, width, kind=F32), own(1, width, kind=F32), own(1, width, kind=F32),
         own(width, local), sent(width, local), own(local, width), sent(local, width),
         own(share, local), sent(share, local)],
        [pltpu.VMEM((share, width), BF16)], 40,
        norm_gain, grad_mid, first_low, first_normed, first_dev,
        *swap(gq_keep, gq_send), *cross_q, *self_slots, *self_out,
    )
    g_self_qkv, in_keep, in_send = call(
        functools.partial(self_back_kernel, parts),
        [own(3, width, local), own(share, width, kind=F32), sent(share, width)],
        back_scratch, 56, dec_lengths, self_qx, self_kx, self_vx, self_ctx, dec_input,
        w_self_qkv, *swap(self_back_keep, self_back_send), smem=1,
    )
    input_grad = grad_base + collect(in_keep, in_send)

    def over_rows(value):
        return lax.psum(value.astype(BF16), "rows").astype(F32)

    return (
        layer_out,
        input_grad,
        enc_grad,
        over_rows(g_self_qkv),
        over_rows(collect(g_self_out, g_self_out_send)),
        over_rows(collect(g_cross_q, g_cross_q_send)),
        over_rows(g_cross_kv),
        over_rows(collect(g_cross_out, g_cross_out_send)),
        over_rows(collect(g_ffn_in, g_ffn_in_send)),
        over_rows(collect(g_ffn_out, g_ffn_out_send)),
        lax.psum(jnp.concatenate([gains_low, gains_high]), ("rows", "heads")),
        lax.psum(jnp.concatenate([biases_low, biases_high]), ("rows", "heads")),
    )


def solution(mesh):
    in_specs = (
        P("rows", None),
        P("rows", None),
        P("rows", None),
        P("rows", None),
        P(None, None, "heads"),
        P("heads", None),
        P(None, "heads"),
        P(None, None, "heads"),
        P("heads", None),
        P(None, "heads"),
        P("heads", None),
        P(),
        P(),
        P("rows", None),
    )
    out_specs = (
        P(("rows", "heads"), None),
        P(("rows", "heads"), None),
        P(("rows", "heads"), None),
        P(None, None, "heads"),
        P("heads", None),
        P(None, "heads"),
        P(None, None, "heads"),
        P("heads", None),
        P(None, "heads"),
        P("heads", None),
        P(),
        P(),
    )
    return jax.shard_map(body, mesh=mesh, in_specs=in_specs, out_specs=out_specs, check_vma=False)
```

```python
import functools

import jax
import jax.numpy as jnp
from jax import lax
from jax.experimental import pallas as pl
from jax.experimental.pallas import tpu as pltpu
from jax.sharding import PartitionSpec as P

HEAD_DIM = 64
LANES = 128
SPAN = 256
KEY_SPAN = 512
VMEM_BYTES = 2**26 - 2**17
NORM_EPS = 1e-05
MASKED_SCORE = -1e30
LOG2_E = 1.4426950408889634
GELU_RATE = 0.7978845608028654
GELU_CUBE = 0.044715
F32 = jnp.float32
BF16 = jnp.bfloat16
NT = (((1,), (1,)), ((), ()))
TN = (((0,), (0,)), ((), ()))
VMEM = pl.BlockSpec(memory_space=pltpu.VMEM)
SMEM = pl.BlockSpec(memory_space=pltpu.SMEM)


def dot(left, right):
    return jnp.dot(left, right, preferred_element_type=F32)


def dot_nt(left, right):
    return lax.dot_general(left, right, NT, preferred_element_type=F32)


def dot_tn(left, right):
    return lax.dot_general(left, right, TN, preferred_element_type=F32)


def shape_of(dims, kind):
    return jax.ShapeDtypeStruct(dims, kind)


def call(kernel, outs, scratch, mib, *args, smem=0, far=0):
    anyspace = pl.BlockSpec(memory_space=pl.ANY)
    return pl.pallas_call(
        kernel,
        out_shape=outs,
        in_specs=[SMEM] * smem + [VMEM] * (len(args) - smem - far) + [anyspace] * far,
        out_specs=[VMEM] * (len(outs) - far) + [anyspace] * far,
        scratch_shapes=scratch,
        compiler_params=pltpu.CompilerParams(vmem_limit_bytes=VMEM_BYTES),
        cost_estimate=pl.CostEstimate(flops=2 * 10**10, bytes_accessed=2 * 10**7, transcendentals=0),
    )(*args)


def segment_bounds(len_ref):
    starts, ends, total = [], [], jnp.int32(0)
    for k in range(len_ref.shape[1]):
        starts.append(total)
        total = total + len_ref[0, k]
        ends.append(total)
    return starts, ends


def bound_lanes(starts, ends):
    lane = lax.broadcasted_iota(jnp.int32, (1, LANES), 1)
    first = jnp.full((1, LANES), 1 << 30, jnp.int32)
    last = jnp.zeros((1, LANES), jnp.int32)
    for k, (start, end) in enumerate(zip(starts, ends)):
        first = jnp.where(lane == HEAD_DIM + k, start, first)
        last = jnp.where(lane == HEAD_DIM + k, end, last)
    return first, last


def lanes_of(rows):
    return lax.broadcasted_iota(jnp.int32, (rows, LANES), 1)


def membership(first_row, rows, bounds):
    place = lax.broadcasted_iota(jnp.int32, (rows, LANES), 0) + first_row
    return (place >= bounds[0]) & (place < bounds[1])


def query_extra(first_row, rows, bounds):
    return jnp.where(membership(first_row, rows, bounds), F32(MASKED_SCORE), F32(0.0))


def key_extra(first_row, rows, bounds, segs):
    lane = lanes_of(rows)
    used = (lane >= HEAD_DIM) & (lane < HEAD_DIM + segs + 3)
    return jnp.where(used & ~membership(first_row, rows, bounds), F32(1.0), F32(0.0))


def value_extra(rows):
    lane = lanes_of(rows)
    return jnp.where((lane >= HEAD_DIM) & (lane < HEAD_DIM + 2), F32(1.0), F32(0.0))


def head_slab(wide, head):
    if wide.shape[1] < LANES:
        return jnp.concatenate([wide, jnp.zeros_like(wide)], axis=1)
    first = head // 2 * LANES
    slab = wide[:, first : first + LANES]
    if head % 2:
        slab = pltpu.roll(slab, HEAD_DIM, 1)
    return slab


def put_heads(dest, where, wide, extra):
    low_lanes = lanes_of(wide.shape[0]) < HEAD_DIM
    for head in range(dest.shape[0]):
        dest[head, where, :] = jnp.where(low_lanes, head_slab(wide, head), extra).astype(dest.dtype)


def join_heads(dest, where, slabs):
    if len(slabs) == 1:
        dest[where, :] = slabs[0][:, :HEAD_DIM].astype(dest.dtype)
        return
    low_lanes = lanes_of(slabs[0].shape[0]) < HEAD_DIM
    for pair in range(len(slabs) // 2):
        both = jnp.where(low_lanes, slabs[2 * pair], pltpu.roll(slabs[2 * pair + 1], HEAD_DIM, 1))
        dest[where, pair * LANES : (pair + 1) * LANES] = both.astype(dest.dtype)


def span_for(block, length, from_starts, to_starts, to_ends):
    first_row = block * SPAN
    last_row = first_row + SPAN - 1
    low, high = jnp.int32(0), jnp.int32(0)
    for start, to_start, to_end in zip(from_starts, to_starts, to_ends):
        low = jnp.where(start <= first_row, to_start, low)
        high = jnp.where(start <= last_row, to_end, high)
    low = (low >> 7) << 7
    pieces = (high - low + SPAN - 1) >> 8
    return jnp.minimum(low, length - pieces * SPAN), pieces


def each_span(length, starts_from, starts_to, ends_to, body):
    def step(block, carry):
        start, pieces = span_for(block, length, starts_from, starts_to, ends_to)
        start = pl.multiple_of(start, LANES)
        rows = pl.ds(pl.multiple_of(block * SPAN, SPAN), SPAN)
        for count in range(1, length // SPAN + 1):

            @pl.when(pieces == count)
            def _():
                body(rows, pl.ds(start, count * SPAN))

        return carry

    lax.fori_loop(0, length // SPAN, step, 0)


def merge_head(dest, rows, head, slab):
    if dest.shape[1] < LANES:
        dest[rows, :] = slab[:, :HEAD_DIM].astype(dest.dtype)
        return
    odd = (head & 1) == 1
    low_lanes = lanes_of(slab.shape[0]) < HEAD_DIM
    cols = pl.ds(pl.multiple_of((head >> 1) * LANES, LANES), LANES)
    old = dest[rows, cols].astype(F32)
    first = jnp.where(odd, old, slab)
    second = jnp.where(odd, pltpu.roll(slab, HEAD_DIM, 1), slab)
    dest[rows, cols] = jnp.where(low_lanes, first, second).astype(dest.dtype)


def attend_body(qx, kx, vx, ctx, segs, rows, keys):
    scale = LOG2_E * HEAD_DIM**-0.5
    base = HEAD_DIM + segs
    lane = lanes_of(SPAN)
    slabs = []
    for head in range(qx.shape[0]):
        query = qx[head, rows, :]
        scores = dot_nt(query, kx[head, keys, :])
        peak = jnp.max(scores, axis=1, keepdims=True)
        raised = jnp.exp2((scores - peak) * scale).astype(BF16)
        mixed = dot(raised, vx[head, keys, :])
        total = mixed[:, HEAD_DIM : HEAD_DIM + 1]
        slabs.append(mixed / total)
        level = -(peak + jnp.log(total) * (HEAD_DIM**0.5))
        high = level.astype(BF16).astype(F32)
        middle = (level - high).astype(BF16).astype(F32)
        low = level - high - middle
        wide = query.astype(F32)
        wide = jnp.where(lane == base, high, wide)
        wide = jnp.where(lane == base + 1, middle, wide)
        wide = jnp.where(lane == base + 2, low, wide)
        qx[head, rows, :] = wide.astype(BF16)
    join_heads(ctx, rows, slabs)


def split_out(source, keep, send, share):
    me = lax.axis_index("heads")
    parts = send.shape[0] + 1
    for k in range(parts):
        owner = lax.rem(me + k, parts)
        rows = pl.ds(pl.multiple_of(owner * share, share), share)
        if k == 0:
            keep[...] = source[rows, :].astype(keep.dtype)
        else:
            send[k - 1] = source[rows, :].astype(send.dtype)


def self_forward_kernel(len_ref, x_ref, w_ref, keep, send, ctx, qx, kx, vx):
    length = x_ref.shape[0]
    segs = len_ref.shape[1]
    starts, ends = segment_bounds(len_ref)
    bounds = bound_lanes(starts, ends)

    def project(block, carry):
        first = pl.multiple_of(block * SPAN, SPAN)
        rows = pl.ds(first, SPAN)
        tokens = x_ref[rows, :]
        put_heads(qx, rows, dot(tokens, w_ref[0]), query_extra(first, SPAN, bounds))
        put_heads(kx, rows, dot(tokens, w_ref[1]), key_extra(first, SPAN, bounds, segs))
        put_heads(vx, rows, dot(tokens, w_ref[2]), value_extra(SPAN))
        return carry

    lax.fori_loop(0, length // SPAN, project, 0)
    each_span(
        length, starts, starts, ends, functools.partial(attend_body, qx, kx, vx, ctx, segs)
    )
    split_out(ctx, keep, send, keep.shape[0])


def cross_keys_kernel(len_ref, x_ref, w_ref, kx, vx):
    length = x_ref.shape[0]
    bounds = bound_lanes(*segment_bounds(len_ref))
    segs = len_ref.shape[1]

    def project(block, carry):
        first = pl.multiple_of(block * SPAN, SPAN)
        rows = pl.ds(first, SPAN)
        tokens = x_ref[rows, :]
        put_heads(kx, rows, dot(tokens, w_ref[0]), key_extra(first, SPAN, bounds, segs))
        put_heads(vx, rows, dot(tokens, w_ref[1]), value_extra(SPAN))
        return carry

    lax.fori_loop(0, length // SPAN, project, 0)


def gather_rows(dest, own, others):
    me = lax.axis_index("heads")
    parts = len(others) + 1
    share = own.shape[0]
    for k, source in enumerate([own, *others]):
        owner = lax.rem(me + k, parts)
        dest[pl.ds(pl.multiple_of(owner * share, share), share), :] = source[...]


def cross_forward_kernel(parts, dec_ref, enc_ref, kx, vx, *refs):
    pieces, (keep, send, ctx, qx, flat) = refs[:parts], refs[parts:]
    length = ctx.shape[0]
    segs = dec_ref.shape[1]
    dec_starts, dec_ends = segment_bounds(dec_ref)
    enc_starts, enc_ends = segment_bounds(enc_ref)
    bounds = bound_lanes(dec_starts, dec_ends)
    gather_rows(flat, pieces[0], pieces[1:])

    def widen(block, carry):
        first = pl.multiple_of(block * SPAN, SPAN)
        rows = pl.ds(first, SPAN)
        put_heads(qx, rows, flat[rows, :].astype(F32), query_extra(first, SPAN, bounds))
        return carry

    lax.fori_loop(0, length // SPAN, widen, 0)
    each_span(
        length, dec_starts, enc_starts, enc_ends,
        functools.partial(attend_body, qx, kx, vx, ctx, segs),
    )
    split_out(ctx, keep, send, keep.shape[0])


def attend_back_body(qx, kx, vx, gx, dq, kt, dk, dv, rows, queries):
    heads = qx.shape[0]
    group = 2 if heads % 2 == 0 else 1

    def unit(index, carry):
        for k in range(group):
            back_unit(qx, kx, vx, gx, dq, kt, dk, dv, group * index + k, rows, queries)
        return carry

    lax.fori_loop(0, heads // group, unit, 0)


def head_sums(width, heads):
    row = lax.broadcasted_iota(jnp.int32, (width, heads * LANES), 0)
    col = lax.broadcasted_iota(jnp.int32, (width, heads * LANES), 1)
    lane = col & (LANES - 1)
    hit = ((row >> 6) == (col >> 7)) & (lane >= HEAD_DIM) & (lane < HEAD_DIM + 2)
    return jnp.where(hit, F32(1.0), F32(0.0)).astype(BF16)


def prepare_back(grad, ctx, kx, gx, dq, kt, sums):
    heads = gx.shape[0]
    lane = lanes_of(SPAN)

    def widen(block, carry):
        rows = pl.ds(pl.multiple_of(block * SPAN, SPAN), SPAN)
        wide = grad[rows, :].astype(F32)
        product = wide * ctx[rows, :].astype(F32)
        high = product.astype(BF16)
        low = (product - high.astype(F32)).astype(BF16)
        totals = dot(high, sums[...]) + dot(low, sums[...])
        for head in range(heads):
            level = -totals[:, head * LANES : (head + 1) * LANES]
            rounded = level.astype(BF16).astype(F32)
            extra = jnp.where(lane == HEAD_DIM + 1, level - rounded, rounded)
            full = jnp.where(lane < HEAD_DIM, head_slab(wide, head), extra)
            gx[head, rows, :] = full.astype(BF16)
            dq[head, :, rows] = jnp.zeros((HEAD_DIM, SPAN), F32)
            kt[head, :, rows] = kx[head, rows, :].astype(F32).T[:HEAD_DIM].astype(BF16)
        return carry

    lax.fori_loop(0, grad.shape[0] // SPAN, widen, 0)


def turn_queries(dq, sq, pairs):
    length = sq.shape[0]

    def finish(block, carry):
        rows = pl.ds(pl.multiple_of(block * SPAN, SPAN), SPAN)
        for pair in pairs:
            if dq.shape[0] == 1:
                sq[rows, :] = (dq[0, :, rows].T * (HEAD_DIM**-0.5)).astype(BF16)
            else:
                both = jnp.concatenate([dq[2 * pair, :, rows], dq[2 * pair + 1, :, rows]], axis=0)
                sq[rows, pair * LANES : (pair + 1) * LANES] = (both.T * (HEAD_DIM**-0.5)).astype(BF16)
        return carry

    lax.fori_loop(0, length // SPAN, finish, 0)


def attend_back(key_starts, key_ends, query_starts, query_ends, qx, kx, vx, ctx, grad, gx, dq, kt, sums, sq, sk, sv):
    length = ctx.shape[0]
    heads = qx.shape[0]
    sums[...] = head_sums(ctx.shape[1], heads)
    prepare_back(grad, ctx, kx, gx, dq, kt, sums)
    each_span(
        length, key_starts, query_starts, query_ends,
        functools.partial(attend_back_body, qx, kx, vx, gx, dq, kt, sk, sv),
    )
    turn_queries(dq, sq, range(max(1, heads // 2)))


def norm_forward(summed, gain, bias):
    center = summed - jnp.mean(summed, axis=1, keepdims=True)
    inverse_dev = lax.rsqrt(jnp.mean(center * center, axis=1, keepdims=True) + NORM_EPS)
    normed = center * inverse_dev
    return normed * gain + bias, normed, inverse_dev


def norm_back(grad, normed, inverse_dev, gain):
    scaled = grad * gain
    back = inverse_dev * (
        scaled
        - jnp.mean(scaled, axis=1, keepdims=True)
        - normed * jnp.mean(scaled * normed, axis=1, keepdims=True)
    )
    gain_grad = jnp.sum(grad * normed, axis=0, keepdims=True)
    return back, gain_grad, jnp.sum(grad, axis=0, keepdims=True)


def share_block(share):
    return 256 if share % 256 == 0 else share


def own_rows(share, first, rows):
    start = lax.axis_index("heads") * share + first
    return pl.ds(pl.multiple_of(start, 64), rows)


def first_norm_kernel(parts, x_ref, gain, bias, *refs):
    ctx, w_out, w_query = refs[:parts], refs[parts : 2 * parts], refs[2 * parts : 3 * parts]
    first_out, first_low, normed_out, dev_out, keep, send = refs[3 * parts :]
    share = first_out.shape[0]
    block = share_block(share)

    def step(index, carry):
        first = pl.multiple_of(index * block, block)
        rows = pl.ds(first, block)
        total = x_ref[own_rows(share, first, block), :].astype(F32)
        for k in range(parts):
            total = total + dot(ctx[k][rows, :], w_out[k][...])
        result, normed, inverse_dev = norm_forward(total, gain[0:1, :], bias[0:1, :])
        low = result.astype(BF16)
        first_out[rows, :] = result
        first_low[rows, :] = low
        normed_out[rows, :] = normed
        dev_out[rows, :] = inverse_dev
        for k in range(parts):
            value = dot(low, w_query[k][...]).astype(BF16)
            if k == 0:
                keep[rows, :] = value
            else:
                send[k - 1, rows, :] = value
        return carry

    lax.fori_loop(0, share // block, step, 0)


def middle_kernel(parts, gain, bias, first_out, out_grad, *refs):
    groups = [refs[g * parts : (g + 1) * parts] for g in range(4)]
    ctx, w_cross, w_in, w_out = groups
    (layer_out, grad_mid, gains, biases, g_out_keep, g_out_send, g_in_keep, g_in_send,
     g_cross_keep, g_cross_send, back_keep, back_send,
     second, second_low, normed2, dev2, total, hidden, slope, top_low, back_sum) = refs[4 * parts :]
    share = first_out.shape[0]
    block = share_block(share)
    units = w_in[0].shape[1]
    chunk = min(256, units)

    def enter(index, carry):
        rows = pl.ds(pl.multiple_of(index * block, block), block)
        summed = first_out[rows, :]
        for k in range(parts):
            summed = summed + dot(ctx[k][rows, :], w_cross[k][...])
        result, normed, inverse_dev = norm_forward(summed, gain[1:2, :], bias[1:2, :])
        second[rows, :] = result
        second_low[rows, :] = result.astype(BF16)
        normed2[rows, :] = normed
        dev2[rows, :] = inverse_dev
        return carry

    lax.fori_loop(0, share // block, enter, 0)
    total[...] = second[...]
    for k in range(parts):

        def expand(index, carry):
            cols = pl.ds(pl.multiple_of(index * chunk, chunk), chunk)
            spot = k * (units // chunk) + index
            pre = dot(second_low[...], w_in[k][:, cols])
            square = pre * pre
            bent = jnp.tanh(pre * (GELU_RATE + (GELU_RATE * GELU_CUBE) * square))
            half = 0.5 + 0.5 * bent
            act = (pre * half).astype(BF16)
            hidden[spot] = act
            bend = (0.5 - 0.5 * bent * bent) * (
                GELU_RATE + (3.0 * GELU_RATE * GELU_CUBE) * square
            )
            slope[spot] = half + pre * bend
            total[...] += dot(act, w_out[k][cols, :])
            return carry

        lax.fori_loop(0, units // chunk, expand, 0)

    gains[...] = jnp.zeros_like(gains)
    biases[...] = jnp.zeros_like(biases)

    def turn(index, carry):
        first = pl.multiple_of(index * block, block)
        rows = pl.ds(first, block)
        result, normed, inverse_dev = norm_forward(total[rows, :], gain[2:3, :], bias[2:3, :])
        layer_out[rows, :] = result
        grad = out_grad[own_rows(share, first, block), :].astype(F32)
        back, gain_grad, bias_grad = norm_back(grad, normed, inverse_dev, gain[2:3, :])
        gains[1:2, :] += gain_grad
        biases[1:2, :] += bias_grad
        back_sum[rows, :] = back
        top_low[rows, :] = back.astype(BF16)
        return carry

    lax.fori_loop(0, share // block, turn, 0)
    for k in range(parts):

        def contract(index, carry):
            cols = pl.ds(pl.multiple_of(index * chunk, chunk), chunk)
            spot = k * (units // chunk) + index
            weight_out = dot_tn(hidden[spot], top_low[...]).astype(BF16)
            pre = (dot_nt(top_low[...], w_out[k][cols, :]) * slope[spot]).astype(BF16)
            weight_in = dot_tn(second_low[...], pre).astype(BF16)
            if k == 0:
                g_out_keep[cols, :] = weight_out
                g_in_keep[:, cols] = weight_in
            else:
                g_out_send[k - 1, cols, :] = weight_out
                g_in_send[k - 1, :, cols] = weight_in
            back_sum[...] += dot_nt(pre, w_in[k][:, cols])
            return carry

        lax.fori_loop(0, units // chunk, contract, 0)

    def leave(index, carry):
        rows = pl.ds(pl.multiple_of(index * block, block), block)
        back, gain_grad, bias_grad = norm_back(
            back_sum[rows, :], normed2[rows, :], dev2[rows, :], gain[1:2, :]
        )
        gains[0:1, :] += gain_grad
        biases[0:1, :] += bias_grad
        grad_mid[rows, :] = back
        low = back.astype(BF16)
        top_low[rows, :] = low
        for k in range(parts):
            value = dot_nt(low, w_cross[k][...]).astype(BF16)
            if k == 0:
                back_keep[rows, :] = value
            else:
                back_send[k - 1, rows, :] = value
        return carry

    lax.fori_loop(0, share // block, leave, 0)
    for k in range(parts):
        value = dot_tn(ctx[k][...], top_low[...]).astype(BF16)
        if k == 0:
            g_cross_keep[...] = value
        else:
            g_cross_send[k - 1] = value


def middle_remote_kernel(parts, gain, bias, *refs):
    rest = list(refs)
    take = lambda number: [rest.pop(0) for _ in range(number)]
    first_in, top_in, ctx_in, send_in, wc0_in, wc1_in, wi0_in, wi1_in, wo0_in, wo1_in = take(10)
    layer_out, mid_out, small_out, sum_out, sum_in, sum_cross, cgrad_out = take(7)
    away_out = take(3)
    (first, top, ctx0, ctx1, wc0, wc1, wi0, wi1, wo0, wo1) = loaded = take(10)
    (second, second_low, normed2, dev2, total, hidden, slope, top_low, back_sum, layer, mid,
     own_out, land_out, gone_out, own_in, land_in, gone_in, own_cross, land_cross, gone_cross, own_back, gone_back) = take(22)
    load_sem, store_sem, part_sem, core_send, core_land = rest
    share, width = first.shape
    units = wi0.shape[1]
    block = 256
    chunk = hidden.shape[2]
    chunks = units // chunk
    core = lax.axis_index("heads")
    other = {"rows": lax.axis_index("rows"), "heads": 1 - core}
    mine = pl.ds(pl.multiple_of(core * share, share), share)
    w_in, w_out, w_cross, ctx = (wi0, wi1), (wo0, wo1), (wc0, wc1), (ctx0, ctx1)
    own_sends = {}

    def across(number, source, dest):
        copy = pltpu.make_async_remote_copy(
            src_ref=source, dst_ref=dest, send_sem=core_send.at[number], recv_sem=core_land.at[number],
            device_id=other, device_id_type=pl.DeviceIdType.MESH,
        )
        own_sends[number] = copy
        return copy

    sources = [first_in, top_in.at[mine, :], ctx_in, None, wc0_in, wc1_in, wi0_in, wi1_in, wo0_in, wo1_in]
    loads = [
        None if source is None else pltpu.make_async_copy(source, dest, load_sem.at[k])
        for k, (source, dest) in enumerate(zip(sources, loaded))
    ]
    for k in (0, 2, 4, 5, 6, 7, 8, 9, 1):
        loads[k].start()
    barrier = pltpu.get_barrier_semaphore()
    pl.semaphore_signal(barrier, inc=1, device_id=other, device_id_type=pl.DeviceIdType.MESH)
    pl.semaphore_wait(barrier, 1)
    across(0, send_in.at[0], ctx1).start()
    for k in (0, 2, 4, 5):
        loads[k].wait()
    own_sends[0].wait()

    def enter(index, carry):
        rows = pl.ds(pl.multiple_of(index * block, block), block)
        summed = first[rows, :] + dot(ctx0[rows, :], wc0[...]) + dot(ctx1[rows, :], wc1[...])
        result, normed, inverse_dev = norm_forward(summed, gain[1:2, :], bias[1:2, :])
        second[rows, :] = result
        second_low[rows, :] = result.astype(BF16)
        normed2[rows, :] = normed
        dev2[rows, :] = inverse_dev
        return carry

    lax.fori_loop(0, share // block, enter, 0)
    total[...] = second[...]
    for k in range(2):
        loads[6 + k].wait()
        loads[8 + k].wait()

        def expand(index, carry):
            cols = pl.ds(pl.multiple_of(index * chunk, chunk), chunk)
            spot = k * chunks + index
            pre = dot(second_low[...], w_in[k][:, cols])
            square = pre * pre
            bent = jnp.tanh(pre * (GELU_RATE + (GELU_RATE * GELU_CUBE) * square))
            half = 0.5 + 0.5 * bent
            act = (pre * half).astype(BF16)
            hidden[spot] = act
            bend = (0.5 - 0.5 * bent * bent) * (
                GELU_RATE + (3.0 * GELU_RATE * GELU_CUBE) * square
            )
            slope[spot] = half + pre * bend
            total[...] += dot(act, w_out[k][cols, :])
            return carry

        lax.fori_loop(0, chunks, expand, 0)
    loads[1].wait()
    small_out[...] = jnp.zeros_like(small_out)

    def turn(index, carry):
        rows = pl.ds(pl.multiple_of(index * block, block), block)
        result, normed, inverse_dev = norm_forward(total[rows, :], gain[2:3, :], bias[2:3, :])
        layer[rows, :] = result
        grad = top[rows, :].astype(F32)
        back, gain_grad, bias_grad = norm_back(grad, normed, inverse_dev, gain[2:3, :])
        small_out[2:3, :] += gain_grad
        small_out[5:6, :] += bias_grad
        back_sum[rows, :] = back
        top_low[rows, :] = back.astype(BF16)
        return carry

    lax.fori_loop(0, share // block, turn, 0)
    stores = [pltpu.make_async_copy(layer, layer_out, store_sem.at[0])]
    stores[0].start()
    for k in (1, 0):
        weight_out, weight_in = (own_out, own_in) if k == 0 else (gone_out, gone_in)

        def contract(index, carry):
            cols = pl.ds(pl.multiple_of(index * chunk, chunk), chunk)
            spot = k * chunks + index
            weight_out[cols, :] = dot_tn(hidden[spot], top_low[...]).astype(BF16)
            pre = (dot_nt(top_low[...], w_out[k][cols, :]) * slope[spot]).astype(BF16)
            weight_in[:, cols] = dot_tn(second_low[...], pre).astype(BF16)
            back_sum[...] += dot_nt(pre, w_in[k][:, cols])
            return carry

        lax.fori_loop(0, chunks, contract, 0)
        if k == 1:
            across(1, gone_out, land_out).start()
            across(2, gone_in, land_in).start()
    count = share // block
    for index in range(count):
        rows = pl.ds(index * block, block)
        back, gain_grad, bias_grad = norm_back(
            back_sum[rows, :], normed2[rows, :], dev2[rows, :], gain[1:2, :]
        )
        small_out[1:2, :] += gain_grad
        small_out[4:5, :] += bias_grad
        mid[rows, :] = back
        low = back.astype(BF16)
        top_low[rows, :] = low
        gone_back[rows, :] = dot_nt(low, wc1[...]).astype(BF16)
        across(
            4 + index, gone_back.at[rows, :], cgrad_out.at[own_rows(share, index * block, block), :]
        ).start()
        own_back[rows, :] = dot_nt(low, wc0[...]).astype(BF16)
    stores.append(pltpu.make_async_copy(mid, mid_out, store_sem.at[1]))
    stores.append(pltpu.make_async_copy(own_back, cgrad_out.at[mine, :], store_sem.at[2]))
    for store in stores[1:]:
        store.start()
    gone_cross[...] = dot_tn(ctx1[...], top_low[...]).astype(BF16)
    across(3, gone_cross, land_cross).start()
    own_sends[1].wait()
    add_into(own_out, land_out)
    stores.append(pltpu.make_async_copy(own_out, sum_out, store_sem.at[3]))
    stores[-1].start()
    own_sends[2].wait()
    add_into(own_in, land_in)
    stores.append(pltpu.make_async_copy(own_in, sum_in, store_sem.at[4]))
    stores[-1].start()
    for number, (part, bit, spot) in enumerate(parts):
        for source, dest in away_windows(part, bit, spot, (own_out, own_in)[part.out], away_out[bit]):
            stores.append(pltpu.make_async_copy(source, dest, part_sem.at[len(stores) - 5]))
            stores[-1].start()
    own_cross[...] = dot_tn(ctx0[...], top_low[...]).astype(BF16)
    own_sends[3].wait()
    add_into(own_cross, land_cross)
    stores.append(pltpu.make_async_copy(own_cross, sum_cross, store_sem.at[5]))
    stores[-1].start()
    for index in range(count):
        own_sends[4 + index].wait()
    for store in stores:
        store.wait()


def away_windows(part, bit, spot, source, dest):
    half = part.rows // 2
    side = lax.shift_right_logical(lax.axis_index("rows"), bit) & 1
    first = part.row + (1 - side) * half
    pairs = []
    for piece in range(half // 128):
        rows = pl.ds(pl.multiple_of(first + piece * 128, 128), 128)
        place = pl.ds(spot * 128, 128)
        cols = pl.ds(piece * part.cols, part.cols)
        pairs.append((source.at[rows, pl.ds(part.col, part.cols)], dest.at[place, cols]))
    return pairs


def first_steps(parts):
    filled = [0, 0, 0]
    found = []
    for part in parts:
        if part.out < 2:
            bit = part.order[0]
            found.append((part, bit, filled[bit]))
            filled[bit] += 1
    return found, [128 * max(1, n) for n in filled]


def run_middle(parts, gain, bias, args, units):
    share, width = args[0].shape
    local = args[2].shape[1]
    found, heights = first_steps(parts)
    chunk = 512
    vm = lambda kind, *dims: pltpu.VMEM(dims, kind)
    token, token_low = vm(F32, share, width), vm(BF16, share, width)
    scratch = [
        token, token_low, vm(BF16, share, local), vm(BF16, share, local),
        vm(BF16, local, width), vm(BF16, local, width), vm(BF16, width, units), vm(BF16, width, units),
        vm(BF16, units, width), vm(BF16, units, width),
        token, token_low, token, vm(F32, share, 1), token,
        vm(BF16, 2 * units // chunk, share, chunk), vm(F32, 2 * units // chunk, share, chunk),
        token_low, token, token, token,
        *[vm(BF16, units, width)] * 3, *[vm(BF16, width, units)] * 3, *[vm(BF16, local, width)] * 3,
        vm(BF16, share, local), vm(BF16, share, local),
    ]
    sems = [10, 6, 2 * len(found), 4 + share // 256, 4 + share // 256]
    anyspace = pl.BlockSpec(memory_space=pl.ANY)
    return pl.pallas_call(
        functools.partial(middle_remote_kernel, found),
        out_shape=[
            shape_of((share, width), F32), shape_of((share, width), F32), shape_of((8, width), F32),
            shape_of((units, width), BF16), shape_of((width, units), BF16), shape_of((local, width), BF16),
            shape_of((2 * share, local), BF16), *[shape_of((h, width), BF16) for h in heights],
        ],
        in_specs=[VMEM] * 2 + [anyspace] * len(args),
        out_specs=[anyspace] * 2 + [VMEM] + [anyspace] * 7,
        scratch_shapes=scratch + [pltpu.SemaphoreType.DMA((n,)) for n in sems],
        compiler_params=pltpu.CompilerParams(
            vmem_limit_bytes=VMEM_BYTES, collective_id=1, has_side_effects=True
        ),
    )(gain, bias, *args)


def cross_back_kernel(parts, dec_ref, enc_ref, qx, kx, vx, ctx, enc, w_kv, *refs):
    pieces = refs[:parts]
    layer, refs = refs[parts], refs[parts + 1 :]
    (gq_keep, gq_send, g_kv, enc_keep, enc_send, layer_out, grad, gx, dq, kt, sums, sq, sk, sv, wide, held, sems) = refs
    layer_load = pltpu.make_async_copy(layer, held, sems.at[0])
    layer_store = pltpu.make_async_copy(held, layer_out, sems.at[1])
    layer_load.start()
    length = ctx.shape[0]
    dec_starts, dec_ends = segment_bounds(dec_ref)
    enc_starts, enc_ends = segment_bounds(enc_ref)
    gather_rows(grad, pieces[0], pieces[1:])
    attend_back(
        enc_starts, enc_ends, dec_starts, dec_ends, qx, kx, vx, ctx, grad, gx, dq, kt, sums, sq, sk, sv
    )
    layer_load.wait()
    layer_store.start()
    split_out(sq, gq_keep, gq_send, gq_keep.shape[0])
    g_kv[0] = dot_tn(enc[...], sk[...]).astype(BF16)
    g_kv[1] = dot_tn(enc[...], sv[...]).astype(BF16)

    def step(block, carry):
        rows = pl.ds(pl.multiple_of(block * SPAN, SPAN), SPAN)
        wide[rows, :] = dot_nt(sk[rows, :], w_kv[0]) + dot_nt(sv[rows, :], w_kv[1])
        return carry

    lax.fori_loop(0, length // SPAN, step, 0)
    split_out(wide, enc_keep, enc_send, enc_keep.shape[0])
    layer_store.wait()


def first_back_kernel(parts, gain, grad_mid, first_low, normed, dev, *refs):
    groups = [refs[g * parts : (g + 1) * parts] for g in range(4)]
    gq, w_query, ctx, w_out = groups
    (grad_base, gains, biases, g_query_keep, g_query_send, g_out_keep, g_out_send,
     back_keep, back_send, low_ref) = refs[4 * parts :]
    share = grad_mid.shape[0]
    block = share_block(share)
    gains[...] = jnp.zeros_like(gains)
    biases[...] = jnp.zeros_like(biases)

    def step(index, carry):
        rows = pl.ds(pl.multiple_of(index * block, block), block)
        grad = grad_mid[rows, :]
        for k in range(parts):
            grad = grad + dot_nt(gq[k][rows, :], w_query[k][...])
        back, gain_grad, bias_grad = norm_back(grad, normed[rows, :], dev[rows, :], gain[0:1, :])
        gains[...] += gain_grad
        biases[...] += bias_grad
        grad_base[rows, :] = back
        low = back.astype(BF16)
        low_ref[rows, :] = low
        for k in range(parts):
            value = dot_nt(low, w_out[k][...]).astype(BF16)
            if k == 0:
                back_keep[rows, :] = value
            else:
                back_send[k - 1, rows, :] = value
        return carry

    lax.fori_loop(0, share // block, step, 0)
    for k in range(parts):
        query_grad = dot_tn(first_low[...], gq[k][...]).astype(BF16)
        out_grad = dot_tn(ctx[k][...], low_ref[...]).astype(BF16)
        if k == 0:
            g_query_keep[...] = query_grad
            g_out_keep[...] = out_grad
        else:
            g_query_send[k - 1] = query_grad
            g_out_send[k - 1] = out_grad


def self_back_kernel(parts, dec_ref, qx, kx, vx, ctx, x_ref, w_qkv, *refs):
    pieces = refs[:parts]
    g_qkv, in_keep, in_send, grad, gx, dq, kt, sums, sq, sk, sv, wide = refs[parts:]
    length = ctx.shape[0]
    starts, ends = segment_bounds(dec_ref)
    gather_rows(grad, pieces[0], pieces[1:])
    attend_back(starts, ends, starts, ends, qx, kx, vx, ctx, grad, gx, dq, kt, sums, sq, sk, sv)
    for c, source in enumerate((sq, sk, sv)):
        g_qkv[c] = dot_tn(x_ref[...], source[...]).astype(BF16)

    def step(block, carry):
        rows = pl.ds(pl.multiple_of(block * SPAN, SPAN), SPAN)
        wide[rows, :] = (
            dot_nt(sq[rows, :], w_qkv[0])
            + dot_nt(sk[rows, :], w_qkv[1])
            + dot_nt(sv[rows, :], w_qkv[2])
        )
        return carry

    lax.fori_loop(0, length // SPAN, step, 0)
    split_out(wide, in_keep, in_send, in_keep.shape[0])


LINK_RATE = 0.088
HOP_TIME = 2.0
TAKE_TIME = 0.15
SLACK = 1.0
AHEAD = 0.5
LAST_AHEAD = 1.0


class Part:
    def __init__(self, out, row, col, rows, cols, ready):
        self.out, self.row, self.col, self.rows, self.cols = out, row, col, rows, cols
        self.ready = ready
        self.order = None
        self.first = 0

    def window(self):
        return (pl.ds(self.row, self.rows), pl.ds(self.col, self.cols))


def link_cost(part, step, bits):
    depth = step if step < bits else 2 * bits - 1 - step
    amount = part.rows * part.cols * 2e-6 / 2 ** (depth + 1) * 2 / LINK_RATE
    bit = part.order[depth]
    return {bit: 2 * amount, bit - 1: amount} if bit == bits - 1 else {bit: amount}


def choose_orders(parts, bits):
    last = bits - 1
    options = [(0, 1, 2, last), (1, 0, 2, last), (2, 0, 1, last), (2, 1, 0, last)]
    load = dict.fromkeys(range(bits), 0.0)
    for part in parts:
        best = None
        for order in options:
            part.order = order
            trial = dict(load)
            for step in range(2 * bits):
                for bit, amount in link_cost(part, step, bits).items():
                    trial[bit] += amount
            score = sum(value * value for value in trial.values())
            if best is None or score < best[0]:
                best = (score, order, trial)
        _, part.order, load = best


def plan_transfers(parts, bits, spans):
    steps = 2 * bits
    busy = dict.fromkeys(range(bits), 0.0)
    left = [part.first for part in parts]
    since = [None] * len(parts)
    flying = []

    def rest(p):
        return sum(max(link_cost(parts[p], s, bits).values()) + HOP_TIME for s in range(left[p], steps))

    def serve(clock, ahead, slack, found):
        for entry in sorted(flying):
            if entry[0] + slack <= clock:
                flying.remove(entry)
                found.append(("take", entry[1], left[entry[1]]))
                left[entry[1]] += 1
                since[entry[1]] = clock if left[entry[1]] < steps else None
                clock += TAKE_TIME
        for p in sorted((p for p in range(len(parts)) if since[p] is not None), key=lambda p: (-rest(p), p)):
            cost = link_cost(parts[p], left[p], bits)
            if since[p] <= clock and all(busy[b] <= clock + ahead for b in cost):
                done = clock
                for b, amount in cost.items():
                    busy[b] = max(busy[b], clock) + amount
                    done = max(done, busy[b])
                found.append(("send", p, left[p]))
                flying.append((done + HOP_TIME, p))
                since[p] = None
        return clock

    slots, clock = [], 0.0
    for unit, span in enumerate(spans):
        for p, part in enumerate(parts):
            if part.ready[0] == unit:
                since[p] = clock + part.ready[1]
        found = []
        clock = serve(clock, span + AHEAD, SLACK, found)
        slots.append(found)
        clock += span
    for p, part in enumerate(parts):
        if part.ready[0] >= len(spans):
            since[p] = clock + part.ready[1]
    found = []
    while flying or any(value is not None for value in since):
        before = len(found)
        clock = serve(clock, LAST_AHEAD, 0.0, found)
        if len(found) == before:
            clock += 0.05
    slots.append(found)
    return slots


class RowsSum:
    def __init__(self, parts, bits, held, landing, final, outs, send_sem, land_sem, store_sem):
        self.parts, self.bits = parts, bits
        self.held, self.landing, self.final, self.outs = held, landing, final, outs
        self.send_sem, self.land_sem, self.store_sem = send_sem, land_sem, store_sem
        self.begin = [lambda: None] * len(parts)

    def side(self, bit):
        return lax.shift_right_logical(lax.axis_index("rows"), bit) & 1

    def peer(self, bit):
        me = lax.axis_index("rows")
        return {"rows": me + (1 << bit) - 2 * (me & (1 << bit)), "heads": lax.axis_index("heads")}

    def offset(self, p, depth):
        part, total = self.parts[p], jnp.int32(0)
        for d in range(depth):
            total = total + self.side(part.order[d]) * (part.rows >> (d + 1))
        return total

    def copy(self, p, step):
        part = self.parts[p]
        depth = step if step < self.bits else 2 * self.bits - 1 - step
        bit = part.order[depth]
        size = part.rows >> (depth + 1)
        if step < self.bits:
            first = self.offset(p, depth) + (1 - self.side(bit)) * size
            source = self.held[p].at[pl.ds(pl.multiple_of(first, 16), size), :]
            dest = self.landing[p].at[pl.ds(part.rows - 2 * size, size), :]
        else:
            first = self.offset(p, depth + 1)
            source = self.final[p].at[pl.ds(pl.multiple_of(first, 16), size), :]
            dest = source
        return pltpu.make_async_remote_copy(
            src_ref=source, dst_ref=dest, send_sem=self.send_sem.at[p, step],
            recv_sem=self.land_sem.at[p, step], device_id=self.peer(bit),
            device_id_type=pl.DeviceIdType.MESH,
        )

    def absorb(self, p, step):
        part = self.parts[p]
        size = part.rows >> (step + 1)
        mine = pl.ds(pl.multiple_of(self.offset(p, step + 1), 16), size)
        spot = pl.ds(part.rows - 2 * size, size)
        total = self.held[p][mine, :].astype(F32) + self.landing[p][spot, :].astype(F32)
        dest = self.final[p] if step == self.bits - 1 else self.held[p]
        dest[mine, :] = total.astype(BF16)

    def store(self, p):
        part = self.parts[p]
        return pltpu.make_async_copy(
            self.final[p], self.outs[part.out].at[part.window()], self.store_sem.at[p]
        )

    def run(self, ops):
        for kind, p, step in ops:
            if kind == "send":
                if step == self.parts[p].first:
                    self.begin[p]()
                self.copy(p, step).start()
                continue
            self.copy(p, step).wait()
            if step < self.bits:
                self.absorb(p, step)
            elif step == 2 * self.bits - 1:
                self.store(p).start()


def add_into(dest, other):
    dest[...] = (dest[...].astype(F32) + other[...].astype(F32)).astype(dest.dtype)


def back_unit(qx, kx, vx, gx, dq, kt, sk, sv, head, rows, queries):
    scale = LOG2_E * HEAD_DIM**-0.5
    keys = kx[head, rows, :]
    query = qx[head, queries, :]
    grads = gx[head, queries, :]
    weights = jnp.exp2(dot_nt(keys, query) * scale)
    raised = dot_nt(vx[head, rows, :], grads)
    value_slab = dot(weights.astype(BF16), grads)
    inner = (weights * raised).astype(BF16)
    key_slab = dot(inner, query) * (HEAD_DIM**-0.5)
    dq[head, :, queries] += dot(kt[head, :, rows], inner)
    merge_head(sk, rows, head, key_slab)
    merge_head(sv, rows, head, value_slab)


def tail_kernel(parts, bits, plan, gain, small_in, *refs):
    rest = list(refs)
    take = lambda number: [rest.pop(0) for _ in range(number)]
    (gq_keep_in, gq_send_in, grad_mid_in, first_low_in, normed_in, dev_in, wq0_in, wq1_in, ctx0_in, ctx1_in,
     wo0_in, wo1_in, qx_in, kx_in, vx_in, ctx_in, x_in, w_in, enc_in) = take(19)
    ffn_out_own, ffn_in_own, cross_own, kv_own, *arrived = take(7)
    outs = take(7)
    small_out, in_keep, in_land_out, enc_out = take(4)
    count = len(parts)
    held, landing, final = take(count), take(count), take(count)
    mates = dict(zip([p for p in range(count) if parts[p].out in (3, 5)], rest))
    take(len(mates))
    (gq, gq_land, grad_mid, first_low, normed, dev, wq0, wq1, ctx0, ctx1, wo0, wo1, qx, kx, vx, ctx, x_ref, w_ref,
     grad, gx, dq, kt, sums, sq, sk, sv, wide, low, back_out, query_out, self_out, in_out, in_land, small_land) = take(34)
    (send_sem, land_sem, store_sem, load_sem, part_sem, mate_send, mate_land, core_send, core_land,
     small_send, small_sem, out_sem) = rest
    share, width = grad_mid.shape
    length = x_ref.shape[0]
    heads = qx.shape[0]
    block = 256
    me, core = lax.axis_index("rows"), lax.axis_index("heads")
    other_core = {"rows": me, "heads": 1 - core}
    summing = RowsSum(parts, bits, held, landing, final, outs, send_sem, land_sem, store_sem)

    def across(source, dest, send, land, peer=other_core):
        return pltpu.make_async_remote_copy(
            src_ref=source, dst_ref=dest, send_sem=send, recv_sem=land,
            device_id=peer, device_id_type=pl.DeviceIdType.MESH,
        )

    pairs = [
        (gq_keep_in, gq), (grad_mid_in, grad_mid), (wq0_in, wq0), (wq1_in, wq1), (normed_in, normed), (dev_in, dev),
        (wo0_in, wo0), (wo1_in, wo1), (first_low_in, first_low), (ctx0_in, ctx0), (ctx1_in, ctx1), (ctx_in, ctx),
        (qx_in, qx), (kx_in, kx), (vx_in, vx), (x_in, x_ref), (w_in, w_ref),
    ]
    loads = [pltpu.make_async_copy(a, b, load_sem.at[k]) for k, (a, b) in enumerate(pairs)]
    own_arrays = {0: ffn_out_own, 1: ffn_in_own, 2: cross_own, 4: kv_own}
    early = {id(part): (bit, spot) for part, bit, spot in first_steps(parts)[0]}
    part_loads, mate_copies = {}, {}
    for p, part in enumerate(parts):
        part_loads[p] = []
        if part.first:
            half = part.rows // 2
            bit, spot = early[id(part)]
            keep = part.row + summing.side(bit) * half
            rows = pl.ds(pl.multiple_of(keep, 128), half)
            here = pl.ds(pl.multiple_of(keep - part.row, 128), half)
            moves = [(own_arrays[part.out].at[rows, pl.ds(part.col, part.cols)], held[p].at[here, :])]
            for piece in range(half // 128):
                window = (pl.ds(spot * 128, 128), pl.ds(piece * part.cols, part.cols))
                moves.append((arrived[bit].at[window], landing[p].at[pl.ds(piece * 128, 128), :]))
        elif part.out in own_arrays:
            moves = [(own_arrays[part.out].at[part.window()], held[p])]
        else:
            moves = []
        for k, (source, dest) in enumerate(moves):
            part_loads[p].append(pltpu.make_async_copy(source, dest, part_sem.at[p, k]))
            part_loads[p][-1].start()
    for load in loads[:6]:
        load.start()
    peers = [summing.peer(bit) for bit in range(bits)] + [other_core]
    barrier = pltpu.get_barrier_semaphore()
    for peer in peers:
        pl.semaphore_signal(barrier, inc=1, device_id=peer, device_id_type=pl.DeviceIdType.MESH)
    pl.semaphore_wait(barrier, len(peers))
    gq_copy = across(gq_send_in.at[0], gq_land, core_send.at[0], core_land.at[0])
    gq_copy.start()
    enc_copy = across(
        enc_in.at[0], enc_out, core_send.at[2 + share // block], core_land.at[2 + share // block]
    )
    for load in loads[6:]:
        load.start()
    for p, part in enumerate(parts):
        if part.out == 3:
            mate_copies[p] = across(query_out, mates[p], mate_send.at[p], mate_land.at[p])
        if part.out == 5:
            mate_copies[p] = across(self_out, mates[p], mate_send.at[p], mate_land.at[p])

        def begin(p=p):
            for load in part_loads[p]:
                load.wait()
            if parts[p].first:
                summing.absorb(p, 0)
            if p in mate_copies:
                mate_copies[p].wait()
                add_into(held[p], mates[p])

        summing.begin[p] = begin

    slots = list(plan)
    summing.run(slots.pop(0))
    for load in loads[:6]:
        load.wait()
    gq_copy.wait()
    for load in loads[6:8]:
        load.wait()
    small_out[...] = small_in[...]
    back_copies = []
    for index in range(share // block):
        summing.run(slots.pop(0))
        rows = pl.ds(index * block, block)
        mine = own_rows(share, index * block, block)
        value = grad_mid[rows, :] + dot_nt(gq[rows, :], wq0[...]) + dot_nt(gq_land[rows, :], wq1[...])
        back, gain_grad, bias_grad = norm_back(value, normed[rows, :], dev[rows, :], gain[0:1, :])
        small_out[0:1, :] += gain_grad
        small_out[3:4, :] += bias_grad
        in_keep[rows, :] = back
        low_part = back.astype(BF16)
        low[rows, :] = low_part
        grad[mine, :] = dot_nt(low_part, wo0[...]).astype(BF16)
        back_out[rows, :] = dot_nt(low_part, wo1[...]).astype(BF16)
        copy = across(back_out.at[rows, :], grad.at[mine, :], core_send.at[1 + index], core_land.at[1 + index])
        copy.start()
        back_copies.append(copy)
    summing.run(slots.pop(0))
    for load in loads[8:12]:
        load.wait()
    query_out[...] = dot_tn(first_low[...], gq_land[...]).astype(BF16)
    self_out[...] = dot_tn(ctx1[...], low[...]).astype(BF16)
    for p, part in enumerate(parts):
        if part.out in (3, 5):
            mate_copies[p].start()
        if part.out == 3:
            held[p][...] = dot_tn(first_low[...], gq[...]).astype(BF16)
        if part.out == 5:
            held[p][...] = dot_tn(ctx0[...], low[...]).astype(BF16)
    summing.run(slots.pop(0))
    enc_copy.start()
    for copy in back_copies:
        copy.wait()
    for load in loads[12:]:
        load.wait()
    sums[...] = head_sums(ctx.shape[1], heads)
    prepare_back(grad, ctx, kx, gx, dq, kt, sums)
    blocks = length // KEY_SPAN
    in_copy = across(in_out, in_land, core_send.at[1 + share // block], core_land.at[1 + share // block])
    for pair in range(heads // 2):
        mine = [slots.pop(0) for _ in range(2 * blocks)]

        def unit(index, carry):
            lax.switch(index, [functools.partial(summing.run, ops) for ops in mine])
            rows = pl.ds(pl.multiple_of(lax.rem(index, blocks) * KEY_SPAN, KEY_SPAN), KEY_SPAN)
            head = 2 * pair + lax.div(index, blocks)
            back_unit(qx, kx, vx, gx, dq, kt, sk, sv, head, rows, pl.ds(0, length))
            return carry

        lax.fori_loop(0, 2 * blocks, unit, 0)
        cols = pl.ds(pair * LANES, LANES)
        summing.run(slots.pop(0))
        turn_queries(dq, sq, [pair])
        for p, part in enumerate(parts):
            if part.out == 6 and part.col == pair * LANES:
                source = (sq, sk, sv)[part.row // width]
                held[p][...] = dot_tn(x_ref[...], source[:, cols]).astype(BF16)
    last = slots.pop(0)
    early_ops = 24
    summing.run(last[:early_ops])
    last = last[early_ops:]

    def spread(index, carry):
        rows = pl.ds(pl.multiple_of(index * SPAN, SPAN), SPAN)
        value = dot_nt(sq[rows, :], w_ref[0]) + dot_nt(sk[rows, :], w_ref[1])
        wide[rows, :] = value + dot_nt(sv[rows, :], w_ref[2])
        return carry

    lax.fori_loop(0, length // SPAN, spread, 0)
    away = pl.ds(pl.multiple_of((1 - core) * share, share), share)
    in_out[...] = wide[away, :].astype(BF16)
    in_copy.start()
    here = pl.ds(pl.multiple_of(core * share, share), share)
    in_keep[...] += wide[here, :]
    enc_copy.wait()
    small_copy = None
    for k in range(len(peers) + 1):
        cut = len(last) * k // (len(peers) + 1), len(last) * (k + 1) // (len(peers) + 1)
        if small_copy is not None:
            small_copy.wait()
            small_out[...] += small_land[k - 1]
        if k < len(peers):
            small_copy = across(
                small_out, small_land.at[k], small_send.at[k], small_sem.at[k], peers[k]
            )
            small_copy.start()
        if k == len(peers):
            in_copy.wait()
            in_store = pltpu.make_async_copy(in_land, in_land_out, out_sem)
            in_store.start()
        summing.run(last[cut[0] : cut[1]])
    in_store.wait()
    for p in range(count):
        summing.store(p).wait()


def widen_kernel(table, small, *refs):
    sources = 1 + max(max(e[0], -1 if e[1] is None else e[1]) for e in table)
    outs = 1 + max(e[2] for e in table)
    arrays, dests = refs[:sources], refs[sources : sources + outs]
    gain_out, bias_out = refs[sources + outs : sources + outs + 2]
    rest = list(refs[sources + outs + 2 :])
    low = [rest.pop(0) for _ in table]
    more = {k: rest.pop(0) for k, e in enumerate(table) if e[1] is not None}
    wide = [rest.pop(0) for _ in table]
    load_sem, more_sem, store_sem = rest
    loads, stores = [], []
    for k, (source, second, out, window) in enumerate(table):
        window = tuple(pl.ds(*w) for w in window)
        loads.append([pltpu.make_async_copy(arrays[source].at[window], low[k], load_sem.at[k])])
        if second is not None:
            loads[k].append(pltpu.make_async_copy(arrays[second].at[window], more[k], more_sem.at[k]))
        stores.append(pltpu.make_async_copy(wide[k], dests[out].at[window], store_sem.at[k]))
        for load in loads[k]:
            load.start()
    gain_out[...] = small[0:3, :]
    bias_out[...] = small[3:6, :]
    for k in range(len(table)):
        for load in loads[k]:
            load.wait()
        value = low[k][...].astype(F32)
        if k in more:
            value = value + more[k][...].astype(F32)
        wide[k][...] = value
        stores[k].start()
    for store in stores:
        store.wait()


def widen_all(small, entries):
    arrays, table, shapes = [], [], []
    for out, (first, second) in enumerate(entries):
        source = len(arrays)
        arrays.append(first)
        if second is not None:
            arrays.append(second)
        rows, cols = first.shape
        shapes.append(shape_of((rows, cols), F32))
        high = 256 if cols >= 512 else 512
        for row in range(0, rows, high):
            table.append((source, None if second is None else source + 1, out, ((row, high), (0, cols))))
    spaces = [pl.BlockSpec(memory_space=pl.ANY)]
    sized = lambda e: (e[3][0][1], e[3][1][1])
    return pl.pallas_call(
        functools.partial(widen_kernel, table),
        out_shape=shapes + [shape_of((3, small.shape[1]), F32)] * 2,
        in_specs=[VMEM] + spaces * len(arrays),
        out_specs=spaces * len(shapes) + [VMEM] * 2,
        scratch_shapes=[pltpu.VMEM(sized(e), arrays[e[0]].dtype) for e in table]
        + [pltpu.VMEM(sized(e), arrays[e[1]].dtype) for e in table if e[1] is not None]
        + [pltpu.VMEM(sized(e), F32) for e in table]
        + [pltpu.SemaphoreType.DMA((len(table),))] * 3,
        compiler_params=pltpu.CompilerParams(vmem_limit_bytes=VMEM_BYTES),
    )(small, *arrays)


def unit_spans(share, heads):
    spans = [3.0] + [1.3] * (share // 256) + [1.8, 2.0]
    made = len(spans) - 1
    pair_end = []
    for _ in range(heads // 2):
        spans += [2.2] * (4 * share // KEY_SPAN) + [1.8]
        pair_end.append(len(spans))
    return spans, made, pair_end


def gradient_parts(shapes, share, heads, bits):
    spans, made, pair_end = unit_spans(share, heads)
    parts = []
    for out, (rows, cols) in enumerate(shapes):
        high, broad = (256, 512) if cols == 512 else (512, 256)
        if out == 6:
            broad = LANES
        for col in range(0, cols, broad):
            for row in range(0, rows, high):
                ready = (0, 0.0)
                if out in (3, 5):
                    ready = (made, 1.0)
                if out == 6:
                    ready = (pair_end[col // LANES], 0.0)
                parts.append(Part(out, row, col, high, broad, ready))
                parts[-1].first = 1 if out < 2 else 0
    choose_orders(parts, bits)
    return parts


def run_tail(parts, gain, small, first_args, halves, shapes):
    bits = lax.axis_size("rows").bit_length() - 1
    share, local = first_args[0].shape
    width = first_args[2].shape[1]
    length = 2 * share
    heads = local // HEAD_DIM
    norm_units = share // 256
    plan = plan_transfers(parts, bits, unit_spans(share, heads)[0])
    count = len(parts)
    buffers = [pltpu.VMEM((p.rows, p.cols), BF16) for p in parts]
    mated = [b for b, p in zip(buffers, parts) if p.out in (3, 5)]
    vm = lambda kind, *dims: pltpu.VMEM(dims, kind)
    wide_heads = vm(BF16, heads, length, LANES)
    own = [
        vm(BF16, share, local), vm(BF16, share, local), vm(F32, share, width), vm(BF16, share, width),
        vm(F32, share, width), vm(F32, share, 1), vm(BF16, width, local), vm(BF16, width, local),
        vm(BF16, share, local), vm(BF16, share, local), vm(BF16, local, width), vm(BF16, local, width),
        wide_heads, wide_heads, wide_heads, vm(BF16, length, local), vm(BF16, length, width),
        vm(BF16, 3, width, local),
        vm(BF16, length, local), wide_heads, vm(F32, heads, HEAD_DIM, length),
        vm(BF16, heads, HEAD_DIM, length), vm(BF16, local, heads * LANES),
        vm(BF16, length, local), vm(BF16, length, local), vm(BF16, length, local), vm(F32, length, width),
        vm(BF16, share, width), vm(BF16, share, local), vm(BF16, width, local), vm(BF16, local, width),
        vm(BF16, share, width), vm(BF16, share, width), vm(F32, bits + 1, 8, width),
    ]
    sems = [
        (count, 2 * bits), (count, 2 * bits), (count,), (17,), (count, 3), (count,), (count,),
        (3 + norm_units,), (3 + norm_units,), (bits + 1,), (bits + 1,),
    ]
    anyspace = pl.BlockSpec(memory_space=pl.ANY)
    return pl.pallas_call(
        functools.partial(tail_kernel, parts, bits, plan),
        out_shape=[shape_of(dims, BF16) for dims in shapes]
        + [shape_of((8, width), F32), shape_of((share, width), F32)]
        + [shape_of((share, width), BF16)] * 2,
        in_specs=[VMEM] * 2 + [anyspace] * (len(first_args) + len(halves)),
        out_specs=[anyspace] * len(shapes) + [VMEM, VMEM, anyspace, anyspace],
        scratch_shapes=buffers * 3 + mated + own
        + [pltpu.SemaphoreType.DMA(dims) for dims in sems] + [pltpu.SemaphoreType.DMA],
        compiler_params=pltpu.CompilerParams(
            vmem_limit_bytes=VMEM_BYTES, collective_id=0, has_side_effects=True
        ),
    )(gain, small, *first_args, *halves)


def fits_tail(length, width, local, units):
    return (
        lax.axis_size("rows") == 16
        and lax.axis_size("heads") == 2
        and (width, local) == (512, 256)
        and length % 512 == 0
        and units % 512 == 0
    )


def body(
    dec_input,
    enc_output,
    dec_lengths,
    enc_lengths,
    w_self_qkv,
    w_self_out,
    w_cross_q,
    w_cross_kv,
    w_cross_out,
    w_ffn_in,
    w_ffn_out,
    norm_gain,
    norm_bias,
    out_grad,
):
    parts = lax.axis_size("heads")
    length, width = dec_input.shape
    local = w_self_out.shape[0]
    heads = local // HEAD_DIM
    share = length // parts
    units = w_ffn_in.shape[1]
    chunk = min(256, units)
    chunks = parts * units // chunk

    def shift(value, k):
        return lax.ppermute(value, "heads", [(d, (d + k) % parts) for d in range(parts)])

    def slots(shard):
        return [shard] + [shift(shard, parts - k) for k in range(1, parts)]

    def swap(keep, send):
        return [keep] + [shift(send[parts - k - 1], parts - k) for k in range(1, parts)]

    def collect(keep, send):
        total = keep.astype(F32)
        for k in range(1, parts):
            total = total + shift(send[k - 1], k).astype(F32)
        return total

    self_out, cross_q, cross_out = slots(w_self_out), slots(w_cross_q), slots(w_cross_out)
    ffn_in, ffn_out = slots(w_ffn_in), slots(w_ffn_out)

    def sent(*dims, kind=BF16):
        return shape_of((parts - 1, *dims), kind)

    def own(*dims, kind=BF16):
        return shape_of(dims, kind)

    wide_heads = own(heads, length, LANES)
    self_keep, self_send, self_ctx, self_qx, self_kx, self_vx = call(
        self_forward_kernel,
        [own(share, local), sent(share, local), own(length, local), wide_heads, wide_heads, wide_heads],
        [], 40, dec_lengths, dec_input, w_self_qkv, smem=1,
    )
    self_slots = swap(self_keep, self_send)
    cross_kx, cross_vx = call(
        cross_keys_kernel, [wide_heads, wide_heads], [], 32,
        enc_lengths, enc_output, w_cross_kv, smem=1,
    )
    first_out, first_low, first_normed, first_dev, query_keep, query_send = call(
        functools.partial(first_norm_kernel, parts),
        [own(share, width, kind=F32), own(share, width), own(share, width, kind=F32),
         own(share, 1, kind=F32), own(share, local), sent(share, local)],
        [], 32, dec_input, norm_gain, norm_bias, *self_slots, *self_out, *cross_q,
    )
    cross_keep, cross_send, cross_ctx, cross_qx = call(
        functools.partial(cross_forward_kernel, parts),
        [own(share, local), sent(share, local), own(length, local), wide_heads],
        [pltpu.VMEM((length, local), BF16)], 40,
        dec_lengths, enc_lengths, cross_kx, cross_vx, *swap(query_keep, query_send), smem=2,
    )
    fits = fits_tail(length, width, local, units)
    if fits:
        bits = lax.axis_size("rows").bit_length() - 1
        shapes = [
            (units, width), (width, units), (local, width), (width, local),
            (2 * width, local), (local, width), (3 * width, local),
        ]
        pieces = gradient_parts(shapes, share, heads, bits)
        (layer_out, grad_mid, small, g_ffn_out, g_ffn_in, g_cross_out, cross_grad, *away) = run_middle(
            pieces, norm_gain, norm_bias,
            [first_out, out_grad, cross_keep, cross_send, *cross_out,
             *ffn_in, *ffn_out], units,
        )
        size = lax.axis_size("rows")
        arrived = [
            lax.ppermute(value, "rows", [(r, r ^ (1 << bit)) for r in range(size)])
            for bit, value in enumerate(away)
        ]
        grad_slots = [cross_grad]
    else:
        cross_slots = swap(cross_keep, cross_send)
        (layer_out, grad_mid, gains_high, biases_high, g_ffn_out, g_ffn_out_send, g_ffn_in,
         g_ffn_in_send, g_cross_out, g_cross_out_send, back_keep, back_send) = call(
            functools.partial(middle_kernel, parts),
            [own(share, width, kind=F32), own(share, width, kind=F32),
             own(2, width, kind=F32), own(2, width, kind=F32),
             own(units, width), sent(units, width), own(width, units), sent(width, units),
             own(local, width), sent(local, width), own(share, local), sent(share, local)],
            [pltpu.VMEM((share, width), F32), pltpu.VMEM((share, width), BF16),
             pltpu.VMEM((share, width), F32), pltpu.VMEM((share, 1), F32),
             pltpu.VMEM((share, width), F32), pltpu.VMEM((chunks, share, chunk), BF16),
             pltpu.VMEM((chunks, share, chunk), F32), pltpu.VMEM((share, width), BF16),
             pltpu.VMEM((share, width), F32)],
            56, norm_gain, norm_bias, first_out, out_grad,
            *cross_slots, *cross_out, *ffn_in, *ffn_out,
        )
        grad_slots = swap(back_keep, back_send)
    back_scratch = [
        pltpu.VMEM((length, local), BF16),
        pltpu.VMEM((heads, length, LANES), BF16),
        pltpu.VMEM((heads, HEAD_DIM, length), F32),
        pltpu.VMEM((heads, HEAD_DIM, length), BF16),
        pltpu.VMEM((local, heads * LANES), BF16),
        pltpu.VMEM((length, local), BF16),
        pltpu.VMEM((length, local), BF16),
        pltpu.VMEM((length, local), BF16),
        pltpu.VMEM((length, width), F32),
    ]
    gq_keep, gq_send, g_cross_kv, enc_keep, enc_send, layer_out = call(
        functools.partial(cross_back_kernel, len(grad_slots)),
        [own(share, local), sent(share, local), own(2, width, local),
         own(share, width, kind=F32), sent(share, width), own(share, width, kind=F32)],
        back_scratch + [pltpu.VMEM((share, width), F32), pltpu.SemaphoreType.DMA((2,))], 56, dec_lengths, enc_lengths, cross_qx, cross_kx, cross_vx, cross_ctx,
        enc_output, w_cross_kv, *grad_slots, layer_out, smem=2, far=1,
    )
    if fits:
        *sums, small, in_keep, in_land, enc_land = run_tail(
            pieces, norm_gain, small,
            [gq_keep, gq_send, grad_mid, first_low, first_normed, first_dev, *cross_q,
             *self_slots, *self_out, self_qx, self_kx, self_vx, self_ctx, dec_input, w_self_qkv,
             enc_send],
            [g_ffn_out, g_ffn_in, g_cross_out, g_cross_kv.reshape(2 * width, local), *arrived],
            shapes,
        )
        (s_ffn_out, s_ffn_in, s_cross_out, s_cross_q, s_cross_kv, s_self_out, s_self_qkv,
         input_grad, enc_grad, gain_grad, bias_grad) = widen_all(
            small, [(value, None) for value in sums]
            + [(in_keep, in_land), (enc_keep, enc_land)]
        )
        return (
            layer_out, input_grad, enc_grad, s_self_qkv.reshape(3, width, local), s_self_out, s_cross_q,
            s_cross_kv.reshape(2, width, local), s_cross_out, s_ffn_in, s_ffn_out, gain_grad, bias_grad,
        )
    enc_grad = collect(enc_keep, enc_send)
    (grad_base, gains_low, biases_low, g_cross_q, g_cross_q_send, g_self_out, g_self_out_send,
     self_back_keep, self_back_send) = call(
        functools.partial(first_back_kernel, parts),
        [own(share, width, kind=F32), own(1, width, kind=F32), own(1, width, kind=F32),
         own(width, local), sent(width, local), own(local, width), sent(local, width),
         own(share, local), sent(share, local)],
        [pltpu.VMEM((share, width), BF16)], 40,
        norm_gain, grad_mid, first_low, first_normed, first_dev,
        *swap(gq_keep, gq_send), *cross_q, *self_slots, *self_out,
    )
    g_self_qkv, in_keep, in_send = call(
        functools.partial(self_back_kernel, parts),
        [own(3, width, local), own(share, width, kind=F32), sent(share, width)],
        back_scratch, 56, dec_lengths, self_qx, self_kx, self_vx, self_ctx, dec_input,
        w_self_qkv, *swap(self_back_keep, self_back_send), smem=1,
    )
    input_grad = grad_base + collect(in_keep, in_send)

    def over_rows(value):
        return lax.psum(value.astype(BF16), "rows").astype(F32)

    return (
        layer_out,
        input_grad,
        enc_grad,
        over_rows(g_self_qkv),
        over_rows(collect(g_self_out, g_self_out_send)),
        over_rows(collect(g_cross_q, g_cross_q_send)),
        over_rows(g_cross_kv),
        over_rows(collect(g_cross_out, g_cross_out_send)),
        over_rows(collect(g_ffn_in, g_ffn_in_send)),
        over_rows(collect(g_ffn_out, g_ffn_out_send)),
        lax.psum(jnp.concatenate([gains_low, gains_high]), ("rows", "heads")),
        lax.psum(jnp.concatenate([biases_low, biases_high]), ("rows", "heads")),
    )


def solution(mesh):
    in_specs = (
        P("rows", None),
        P("rows", None),
        P("rows", None),
        P("rows", None),
        P(None, None, "heads"),
        P("heads", None),
        P(None, "heads"),
        P(None, None, "heads"),
        P("heads", None),
        P(None, "heads"),
        P("heads", None),
        P(),
        P(),
        P("rows", None),
    )
    out_specs = (
        P(("rows", "heads"), None),
        P(("rows", "heads"), None),
        P(("rows", "heads"), None),
        P(None, None, "heads"),
        P("heads", None),
        P(None, "heads"),
        P(None, None, "heads"),
        P("heads", None),
        P(None, "heads"),
        P("heads", None),
        P(),
        P(),
    )
    return jax.shard_map(body, mesh=mesh, in_specs=in_specs, out_specs=out_specs, check_vma=False)
```

```python
import functools

import jax
import jax.numpy as jnp
from jax import lax
from jax.experimental import pallas as pl
from jax.experimental.pallas import tpu as pltpu
from jax.sharding import PartitionSpec as P

HEAD_DIM = 64
LANES = 128
SPAN = 256
KEY_SPAN = 512
VMEM_BYTES = 2**26 - 2**17
NORM_EPS = 1e-05
MASKED_SCORE = -1e30
LOG2_E = 1.4426950408889634
GELU_RATE = 0.7978845608028654
GELU_CUBE = 0.044715
F32 = jnp.float32
BF16 = jnp.bfloat16
NT = (((1,), (1,)), ((), ()))
TN = (((0,), (0,)), ((), ()))
VMEM = pl.BlockSpec(memory_space=pltpu.VMEM)
SMEM = pl.BlockSpec(memory_space=pltpu.SMEM)


def dot(left, right):
    return jnp.dot(left, right, preferred_element_type=F32)


def dot_nt(left, right):
    return lax.dot_general(left, right, NT, preferred_element_type=F32)


def dot_tn(left, right):
    return lax.dot_general(left, right, TN, preferred_element_type=F32)


def shape_of(dims, kind):
    return jax.ShapeDtypeStruct(dims, kind)


def call(kernel, outs, scratch, mib, *args, smem=0, far=0, out_far=0, out_places=()):
    anyspace = pl.BlockSpec(memory_space=pl.ANY)
    return pl.pallas_call(
        kernel,
        out_shape=outs,
        in_specs=[SMEM] * smem + [VMEM] * (len(args) - smem - far) + [anyspace] * far,
        out_specs=[
            anyspace if k in out_places or k >= len(outs) - out_far else VMEM for k in range(len(outs))
        ],
        scratch_shapes=scratch,
        compiler_params=pltpu.CompilerParams(vmem_limit_bytes=VMEM_BYTES),
        cost_estimate=pl.CostEstimate(flops=2 * 10**10, bytes_accessed=2 * 10**7, transcendentals=0),
    )(*args)


def segment_bounds(len_ref):
    starts, ends, total = [], [], jnp.int32(0)
    for k in range(len_ref.shape[1]):
        starts.append(total)
        total = total + len_ref[0, k]
        ends.append(total)
    return starts, ends


def bound_lanes(starts, ends):
    lane = lax.broadcasted_iota(jnp.int32, (1, LANES), 1)
    first = jnp.full((1, LANES), 1 << 30, jnp.int32)
    last = jnp.zeros((1, LANES), jnp.int32)
    for k, (start, end) in enumerate(zip(starts, ends)):
        first = jnp.where(lane == HEAD_DIM + k, start, first)
        last = jnp.where(lane == HEAD_DIM + k, end, last)
    return first, last


def lanes_of(rows):
    return lax.broadcasted_iota(jnp.int32, (rows, LANES), 1)


def membership(first_row, rows, bounds):
    place = lax.broadcasted_iota(jnp.int32, (rows, LANES), 0) + first_row
    return (place >= bounds[0]) & (place < bounds[1])


def query_extra(first_row, rows, bounds):
    return jnp.where(membership(first_row, rows, bounds), F32(MASKED_SCORE), F32(0.0))


def key_extra(first_row, rows, bounds, segs):
    lane = lanes_of(rows)
    used = (lane >= HEAD_DIM) & (lane < HEAD_DIM + segs + 3)
    return jnp.where(used & ~membership(first_row, rows, bounds), F32(1.0), F32(0.0))


def value_extra(rows):
    lane = lanes_of(rows)
    return jnp.where((lane >= HEAD_DIM) & (lane < HEAD_DIM + 2), F32(1.0), F32(0.0))


def head_slab(wide, head):
    if wide.shape[1] < LANES:
        return jnp.concatenate([wide, jnp.zeros_like(wide)], axis=1)
    first = head // 2 * LANES
    slab = wide[:, first : first + LANES]
    if head % 2:
        slab = pltpu.roll(slab, HEAD_DIM, 1)
    return slab


def put_heads(dest, where, wide, extra):
    low_lanes = lanes_of(wide.shape[0]) < HEAD_DIM
    for head in range(dest.shape[0]):
        dest[head, where, :] = jnp.where(low_lanes, head_slab(wide, head), extra).astype(dest.dtype)


def join_heads(dest, where, slabs):
    if len(slabs) == 1:
        dest[where, :] = slabs[0][:, :HEAD_DIM].astype(dest.dtype)
        return
    low_lanes = lanes_of(slabs[0].shape[0]) < HEAD_DIM
    for pair in range(len(slabs) // 2):
        both = jnp.where(low_lanes, slabs[2 * pair], pltpu.roll(slabs[2 * pair + 1], HEAD_DIM, 1))
        dest[where, pair * LANES : (pair + 1) * LANES] = both.astype(dest.dtype)


def span_for(block, length, from_starts, to_starts, to_ends):
    first_row = block * SPAN
    last_row = first_row + SPAN - 1
    low, high = jnp.int32(0), jnp.int32(0)
    for start, to_start, to_end in zip(from_starts, to_starts, to_ends):
        low = jnp.where(start <= first_row, to_start, low)
        high = jnp.where(start <= last_row, to_end, high)
    low = (low >> 7) << 7
    pieces = (high - low + SPAN - 1) >> 8
    return jnp.minimum(low, length - pieces * SPAN), pieces


def each_span(length, starts_from, starts_to, ends_to, body, after=None):
    def step(block, carry):
        start, pieces = span_for(block, length, starts_from, starts_to, ends_to)
        start = pl.multiple_of(start, LANES)
        rows = pl.ds(pl.multiple_of(block * SPAN, SPAN), SPAN)
        for count in range(1, length // SPAN + 1):

            @pl.when(pieces == count)
            def _():
                body(rows, pl.ds(start, count * SPAN))

        if after is not None:
            after(block, rows)
        return carry

    lax.fori_loop(0, length // SPAN, step, 0)


def merge_head(dest, rows, head, slab):
    if dest.shape[1] < LANES:
        dest[rows, :] = slab[:, :HEAD_DIM].astype(dest.dtype)
        return
    odd = (head & 1) == 1
    low_lanes = lanes_of(slab.shape[0]) < HEAD_DIM
    cols = pl.ds(pl.multiple_of((head >> 1) * LANES, LANES), LANES)
    old = dest[rows, cols].astype(F32)
    first = jnp.where(odd, old, slab)
    second = jnp.where(odd, pltpu.roll(slab, HEAD_DIM, 1), slab)
    dest[rows, cols] = jnp.where(low_lanes, first, second).astype(dest.dtype)


def attend_body(qx, kx, vx, ctx, segs, rows, keys):
    scale = LOG2_E * HEAD_DIM**-0.5
    base = HEAD_DIM + segs
    lane = lanes_of(SPAN)
    slabs = []
    for head in range(qx.shape[0]):
        query = qx[head, rows, :]
        scores = dot_nt(query, kx[head, keys, :])
        peak = jnp.max(scores, axis=1, keepdims=True)
        raised = jnp.exp2((scores - peak) * scale).astype(BF16)
        mixed = dot(raised, vx[head, keys, :])
        total = mixed[:, HEAD_DIM : HEAD_DIM + 1]
        slabs.append(mixed / total)
        level = -(peak + jnp.log(total) * (HEAD_DIM**0.5))
        high = level.astype(BF16).astype(F32)
        middle = (level - high).astype(BF16).astype(F32)
        low = level - high - middle
        wide = query.astype(F32)
        wide = jnp.where(lane == base, high, wide)
        wide = jnp.where(lane == base + 1, middle, wide)
        wide = jnp.where(lane == base + 2, low, wide)
        qx[head, rows, :] = wide.astype(BF16)
    join_heads(ctx, rows, slabs)


def split_out(source, keep, send, share):
    me = lax.axis_index("heads")
    parts = send.shape[0] + 1
    for k in range(parts):
        owner = lax.rem(me + k, parts)
        rows = pl.ds(pl.multiple_of(owner * share, share), share)
        if k == 0:
            keep[...] = source[rows, :].astype(keep.dtype)
        else:
            send[k - 1] = source[rows, :].astype(send.dtype)


def self_forward_kernel(len_ref, x_ref, w_ref, keep, send, ctx, qx, kx, vx):
    length = x_ref.shape[0]
    segs = len_ref.shape[1]
    starts, ends = segment_bounds(len_ref)
    bounds = bound_lanes(starts, ends)

    def project(block, carry):
        first = pl.multiple_of(block * SPAN, SPAN)
        rows = pl.ds(first, SPAN)
        tokens = x_ref[rows, :]
        put_heads(qx, rows, dot(tokens, w_ref[0]), query_extra(first, SPAN, bounds))
        put_heads(kx, rows, dot(tokens, w_ref[1]), key_extra(first, SPAN, bounds, segs))
        put_heads(vx, rows, dot(tokens, w_ref[2]), value_extra(SPAN))
        return carry

    lax.fori_loop(0, length // SPAN, project, 0)
    each_span(
        length, starts, starts, ends, functools.partial(attend_body, qx, kx, vx, ctx, segs)
    )
    split_out(ctx, keep, send, keep.shape[0])


def cross_keys_kernel(len_ref, x_ref, w_ref, kx, vx):
    length = x_ref.shape[0]
    bounds = bound_lanes(*segment_bounds(len_ref))
    segs = len_ref.shape[1]

    def project(block, carry):
        first = pl.multiple_of(block * SPAN, SPAN)
        rows = pl.ds(first, SPAN)
        tokens = x_ref[rows, :]
        put_heads(kx, rows, dot(tokens, w_ref[0]), key_extra(first, SPAN, bounds, segs))
        put_heads(vx, rows, dot(tokens, w_ref[1]), value_extra(SPAN))
        return carry

    lax.fori_loop(0, length // SPAN, project, 0)


def gather_rows(dest, own, others):
    me = lax.axis_index("heads")
    parts = len(others) + 1
    share = own.shape[0]
    for k, source in enumerate([own, *others]):
        owner = lax.rem(me + k, parts)
        dest[pl.ds(pl.multiple_of(owner * share, share), share), :] = source[...]


def cross_forward_kernel(parts, dec_ref, enc_ref, kx, vx, *refs):
    pieces, (keep, send, ctx, qx, flat) = refs[:parts], refs[parts:]
    length = ctx.shape[0]
    segs = dec_ref.shape[1]
    dec_starts, dec_ends = segment_bounds(dec_ref)
    enc_starts, enc_ends = segment_bounds(enc_ref)
    bounds = bound_lanes(dec_starts, dec_ends)
    gather_rows(flat, pieces[0], pieces[1:])

    def widen(block, carry):
        first = pl.multiple_of(block * SPAN, SPAN)
        rows = pl.ds(first, SPAN)
        put_heads(qx, rows, flat[rows, :].astype(F32), query_extra(first, SPAN, bounds))
        return carry

    lax.fori_loop(0, length // SPAN, widen, 0)
    each_span(
        length, dec_starts, enc_starts, enc_ends,
        functools.partial(attend_body, qx, kx, vx, ctx, segs),
    )
    split_out(ctx, keep, send, keep.shape[0])


def row_store(source, dest, rows, sem, block, heads):
    where = (slice(None), rows, slice(None)) if heads else (rows, slice(None))
    return pltpu.make_async_copy(source.at[where], dest.at[where], sem.at[block])


def self_forward_fast(len_ref, x_ref, w_ref, ctx_out, qx_out, kx_out, vx_out, ctx, qx, kx, vx, sems, far):
    length = x_ref.shape[0]
    segs = len_ref.shape[1]
    starts, ends = segment_bounds(len_ref)
    bounds = bound_lanes(starts, ends)

    def project(block, carry):
        first = pl.multiple_of(block * SPAN, SPAN)
        rows = pl.ds(first, SPAN)
        tokens = x_ref[rows, :]
        put_heads(qx, rows, dot(tokens, w_ref[0]), query_extra(first, SPAN, bounds))
        put_heads(kx, rows, dot(tokens, w_ref[1]), key_extra(first, SPAN, bounds, segs))
        put_heads(vx, rows, dot(tokens, w_ref[2]), value_extra(SPAN))
        return carry

    lax.fori_loop(0, length // SPAN, project, 0)
    whole = [pltpu.make_async_copy(kx, kx_out, far.at[0]), pltpu.make_async_copy(vx, vx_out, far.at[1])]
    for copy in whole:
        copy.start()

    def after(block, rows):
        row_store(ctx, ctx_out, rows, sems.at[0], block, False).start()
        row_store(qx, qx_out, rows, sems.at[1], block, True).start()

    each_span(
        length, starts, starts, ends, functools.partial(attend_body, qx, kx, vx, ctx, segs), after
    )
    for block in range(length // SPAN):
        rows = pl.ds(block * SPAN, SPAN)
        row_store(ctx, ctx_out, rows, sems.at[0], block, False).wait()
        row_store(qx, qx_out, rows, sems.at[1], block, True).wait()
    for copy in whole:
        copy.wait()


def cross_forward_fast(dec_ref, enc_ref, flat, kx_in, vx_in, ctx_out, qx_out, ctx, qx, kx, vx, sems, far):
    length = ctx.shape[0]
    segs = dec_ref.shape[1]
    loads = [pltpu.make_async_copy(kx_in, kx, far.at[0]), pltpu.make_async_copy(vx_in, vx, far.at[1])]
    for load in loads:
        load.start()
    dec_starts, dec_ends = segment_bounds(dec_ref)
    enc_starts, enc_ends = segment_bounds(enc_ref)
    bounds = bound_lanes(dec_starts, dec_ends)

    def widen(block, carry):
        first = pl.multiple_of(block * SPAN, SPAN)
        rows = pl.ds(first, SPAN)
        put_heads(qx, rows, flat[rows, :].astype(F32), query_extra(first, SPAN, bounds))
        return carry

    lax.fori_loop(0, length // SPAN, widen, 0)
    for load in loads:
        load.wait()

    def after(block, rows):
        row_store(ctx, ctx_out, rows, sems.at[0], block, False).start()
        row_store(qx, qx_out, rows, sems.at[1], block, True).start()

    each_span(
        length, dec_starts, enc_starts, enc_ends,
        functools.partial(attend_body, qx, kx, vx, ctx, segs), after,
    )
    for block in range(length // SPAN):
        rows = pl.ds(block * SPAN, SPAN)
        row_store(ctx, ctx_out, rows, sems.at[0], block, False).wait()
        row_store(qx, qx_out, rows, sems.at[1], block, True).wait()


def core_half(core, share):
    return pl.ds(pl.multiple_of(core * share, share), share)


def entry_remote_kernel(enc_ref, gain, bias, *refs):
    rest = list(refs)
    take = lambda number: [rest.pop(0) for _ in range(number)]
    x_in, enc_in, w_kv_in, ctx_in, wo_in, wq_in, far_cross, far_in, far_out = take(9)
    first_out, first_low, normed_out, dev_out, q_out, kx_out, vx_out, ctx_far, wo_far, wq_far = take(10)
    away_cross, away_in, away_out = take(3)
    x, enc, w_kv, ctx0, ctx1, wo0, wo1, wq0, wq1 = take(9)
    first, low, normed, q_own, q_gone, kx, vx = take(7)
    load_sem, store_sem, core_send, core_land = rest
    share, width = first.shape
    length = enc.shape[0]
    block = 256
    segs = enc_ref.shape[1]
    core = lax.axis_index("heads")
    other = {"rows": lax.axis_index("rows"), "heads": 1 - core}
    mine, theirs = core_half(core, share), core_half(1 - core, share)

    def across(number, source, dest):
        return pltpu.make_async_remote_copy(
            src_ref=source, dst_ref=dest, send_sem=core_send.at[number], recv_sem=core_land.at[number],
            device_id=other, device_id_type=pl.DeviceIdType.MESH,
        )

    moves = [(enc_in, enc), (w_kv_in, w_kv), (x_in.at[mine, :], x), (ctx_in.at[mine, :], ctx0), (wo_in, wo0), (wq_in, wq0)]
    loads = [pltpu.make_async_copy(a, b, load_sem.at[k]) for k, (a, b) in enumerate(moves)]
    for load in loads:
        load.start()
    barrier = pltpu.get_barrier_semaphore()
    pl.semaphore_signal(barrier, inc=1, device_id=other, device_id_type=pl.DeviceIdType.MESH)
    pl.semaphore_wait(barrier, 1)
    exchange = [
        across(0, ctx_in.at[theirs, :], ctx1), across(1, wo_in, wo1), across(2, wq_in, wq1),
        across(3, far_cross, away_cross), across(4, far_in, away_in), across(5, far_out, away_out),
    ]
    for copy in exchange:
        copy.start()
    bounds = bound_lanes(*segment_bounds(enc_ref))
    for load in loads[:2]:
        load.wait()

    def project(index, carry):
        top = pl.multiple_of(index * SPAN, SPAN)
        rows = pl.ds(top, SPAN)
        tokens = enc[rows, :]
        put_heads(kx, rows, dot(tokens, w_kv[0]), key_extra(top, SPAN, bounds, segs))
        put_heads(vx, rows, dot(tokens, w_kv[1]), value_extra(SPAN))
        return carry

    lax.fori_loop(0, length // SPAN, project, 0)
    stores = []

    def store(source, dest):
        stores.append(pltpu.make_async_copy(source, dest, store_sem.at[len(stores)]))
        stores[-1].start()

    store(kx, kx_out)
    store(vx, vx_out)
    for load in loads[2:]:
        load.wait()
    for copy in exchange[:3]:
        copy.wait()
    store(ctx1, ctx_far)
    store(wo1, wo_far)
    store(wq1, wq_far)
    copies = []
    for index in range(share // block):
        rows = pl.ds(index * block, block)
        total = x[rows, :].astype(F32) + dot(ctx0[rows, :], wo0[...]) + dot(ctx1[rows, :], wo1[...])
        result, spread, inverse_dev = norm_forward(total, gain[0:1, :], bias[0:1, :])
        low_part = result.astype(BF16)
        first[rows, :] = result
        low[rows, :] = low_part
        normed[rows, :] = spread
        dev_out[rows, :] = inverse_dev
        q_gone[rows, :] = dot(low_part, wq1[...]).astype(BF16)
        here = own_rows(share, index * block, block)
        copies.append(across(6 + index, q_gone.at[rows, :], q_out.at[here, :]))
        copies[-1].start()
        q_own[rows, :] = dot(low_part, wq0[...]).astype(BF16)
        store(q_own.at[rows, :], q_out.at[here, :])
        store(first.at[rows, :], first_out.at[rows, :])
        store(low.at[rows, :], first_low.at[rows, :])
        store(normed.at[rows, :], normed_out.at[rows, :])
    for copy in exchange[3:] + copies:
        copy.wait()
    for copy in stores:
        copy.wait()


def run_entry(enc_lengths, gain, bias, args):
    length, width = args[0].shape
    local = args[4].shape[0]
    share, heads, units = length // 2, local // HEAD_DIM, args[7].shape[1]
    vm = lambda kind, *dims: pltpu.VMEM(dims, kind)
    wide_heads = (heads, length, LANES)
    blocks = share // 256
    anyspace = pl.BlockSpec(memory_space=pl.ANY)
    return pl.pallas_call(
        entry_remote_kernel,
        out_shape=[
            shape_of((share, width), F32), shape_of((share, width), BF16), shape_of((share, width), F32),
            shape_of((share, 1), F32), shape_of((length, local), BF16),
            shape_of(wide_heads, BF16), shape_of(wide_heads, BF16),
            shape_of((share, local), BF16), shape_of((local, width), BF16), shape_of((width, local), BF16),
            shape_of((local, width), BF16), shape_of((width, units), BF16), shape_of((units, width), BF16),
        ],
        in_specs=[SMEM, VMEM, VMEM] + [anyspace] * len(args),
        out_specs=[anyspace] * 3 + [VMEM] + [anyspace] * 9,
        scratch_shapes=[
            vm(BF16, share, width), vm(BF16, length, width), vm(BF16, 2, width, local),
            vm(BF16, share, local), vm(BF16, share, local), vm(BF16, local, width), vm(BF16, local, width),
            vm(BF16, width, local), vm(BF16, width, local),
            vm(F32, share, width), vm(BF16, share, width), vm(F32, share, width),
            vm(BF16, share, local), vm(BF16, share, local), vm(BF16, *wide_heads), vm(BF16, *wide_heads),
        ] + [pltpu.SemaphoreType.DMA((n,)) for n in (6, 5 + 4 * blocks, 6 + blocks, 6 + blocks)],
        compiler_params=pltpu.CompilerParams(
            vmem_limit_bytes=VMEM_BYTES, collective_id=2, has_side_effects=True
        ),
    )(enc_lengths, gain, bias, *args)


def attend_back_body(qx, kx, vx, gx, dq, kt, dk, dv, rows, queries):
    heads = qx.shape[0]
    group = 2 if heads % 2 == 0 else 1

    def unit(index, carry):
        for k in range(group):
            back_unit(qx, kx, vx, gx, dq, kt, dk, dv, group * index + k, rows, queries)
        return carry

    lax.fori_loop(0, heads // group, unit, 0)


def head_sums(width, heads):
    row = lax.broadcasted_iota(jnp.int32, (width, heads * LANES), 0)
    col = lax.broadcasted_iota(jnp.int32, (width, heads * LANES), 1)
    lane = col & (LANES - 1)
    hit = ((row >> 6) == (col >> 7)) & (lane >= HEAD_DIM) & (lane < HEAD_DIM + 2)
    return jnp.where(hit, F32(1.0), F32(0.0)).astype(BF16)


def prepare_back(grad, ctx, kx, gx, dq, kt, sums):
    heads = gx.shape[0]
    lane = lanes_of(SPAN)

    def widen(block, carry):
        rows = pl.ds(pl.multiple_of(block * SPAN, SPAN), SPAN)
        wide = grad[rows, :].astype(F32)
        product = wide * ctx[rows, :].astype(F32)
        high = product.astype(BF16)
        low = (product - high.astype(F32)).astype(BF16)
        totals = dot(high, sums[...]) + dot(low, sums[...])
        for head in range(heads):
            level = -totals[:, head * LANES : (head + 1) * LANES]
            rounded = level.astype(BF16).astype(F32)
            extra = jnp.where(lane == HEAD_DIM + 1, level - rounded, rounded)
            full = jnp.where(lane < HEAD_DIM, head_slab(wide, head), extra)
            gx[head, rows, :] = full.astype(BF16)
            dq[head, :, rows] = jnp.zeros((HEAD_DIM, SPAN), F32)
            kt[head, :, rows] = kx[head, rows, :].astype(F32).T[:HEAD_DIM].astype(BF16)
        return carry

    lax.fori_loop(0, grad.shape[0] // SPAN, widen, 0)


def turn_queries(dq, sq, pairs):
    length = sq.shape[0]

    def finish(block, carry):
        rows = pl.ds(pl.multiple_of(block * SPAN, SPAN), SPAN)
        for pair in pairs:
            if dq.shape[0] == 1:
                sq[rows, :] = (dq[0, :, rows].T * (HEAD_DIM**-0.5)).astype(BF16)
            else:
                both = jnp.concatenate([dq[2 * pair, :, rows], dq[2 * pair + 1, :, rows]], axis=0)
                sq[rows, pair * LANES : (pair + 1) * LANES] = (both.T * (HEAD_DIM**-0.5)).astype(BF16)
        return carry

    lax.fori_loop(0, length // SPAN, finish, 0)


def attend_back(key_starts, key_ends, query_starts, query_ends, qx, kx, vx, ctx, grad, gx, dq, kt, sums, sq, sk, sv):
    length = ctx.shape[0]
    heads = qx.shape[0]
    sums[...] = head_sums(ctx.shape[1], heads)
    prepare_back(grad, ctx, kx, gx, dq, kt, sums)
    each_span(
        length, key_starts, query_starts, query_ends,
        functools.partial(attend_back_body, qx, kx, vx, gx, dq, kt, sk, sv),
    )
    turn_queries(dq, sq, range(max(1, heads // 2)))


def norm_forward(summed, gain, bias):
    center = summed - jnp.mean(summed, axis=1, keepdims=True)
    inverse_dev = lax.rsqrt(jnp.mean(center * center, axis=1, keepdims=True) + NORM_EPS)
    normed = center * inverse_dev
    return normed * gain + bias, normed, inverse_dev


def norm_back(grad, normed, inverse_dev, gain):
    scaled = grad * gain
    back = inverse_dev * (
        scaled
        - jnp.mean(scaled, axis=1, keepdims=True)
        - normed * jnp.mean(scaled * normed, axis=1, keepdims=True)
    )
    gain_grad = jnp.sum(grad * normed, axis=0, keepdims=True)
    return back, gain_grad, jnp.sum(grad, axis=0, keepdims=True)


def share_block(share):
    return 256 if share % 256 == 0 else share


def own_rows(share, first, rows):
    start = lax.axis_index("heads") * share + first
    return pl.ds(pl.multiple_of(start, 64), rows)


def first_norm_kernel(parts, x_ref, gain, bias, *refs):
    ctx, w_out, w_query = refs[:parts], refs[parts : 2 * parts], refs[2 * parts : 3 * parts]
    first_out, first_low, normed_out, dev_out, keep, send = refs[3 * parts :]
    share = first_out.shape[0]
    block = share_block(share)

    def step(index, carry):
        first = pl.multiple_of(index * block, block)
        rows = pl.ds(first, block)
        total = x_ref[own_rows(share, first, block), :].astype(F32)
        for k in range(parts):
            total = total + dot(ctx[k][rows, :], w_out[k][...])
        result, normed, inverse_dev = norm_forward(total, gain[0:1, :], bias[0:1, :])
        low = result.astype(BF16)
        first_out[rows, :] = result
        first_low[rows, :] = low
        normed_out[rows, :] = normed
        dev_out[rows, :] = inverse_dev
        for k in range(parts):
            value = dot(low, w_query[k][...]).astype(BF16)
            if k == 0:
                keep[rows, :] = value
            else:
                send[k - 1, rows, :] = value
        return carry

    lax.fori_loop(0, share // block, step, 0)


def middle_kernel(parts, gain, bias, first_out, out_grad, *refs):
    groups = [refs[g * parts : (g + 1) * parts] for g in range(4)]
    ctx, w_cross, w_in, w_out = groups
    (layer_out, grad_mid, gains, biases, g_out_keep, g_out_send, g_in_keep, g_in_send,
     g_cross_keep, g_cross_send, back_keep, back_send,
     second, second_low, normed2, dev2, total, hidden, slope, top_low, back_sum) = refs[4 * parts :]
    share = first_out.shape[0]
    block = share_block(share)
    units = w_in[0].shape[1]
    chunk = min(256, units)

    def enter(index, carry):
        rows = pl.ds(pl.multiple_of(index * block, block), block)
        summed = first_out[rows, :]
        for k in range(parts):
            summed = summed + dot(ctx[k][rows, :], w_cross[k][...])
        result, normed, inverse_dev = norm_forward(summed, gain[1:2, :], bias[1:2, :])
        second[rows, :] = result
        second_low[rows, :] = result.astype(BF16)
        normed2[rows, :] = normed
        dev2[rows, :] = inverse_dev
        return carry

    lax.fori_loop(0, share // block, enter, 0)
    total[...] = second[...]
    for k in range(parts):

        def expand(index, carry):
            cols = pl.ds(pl.multiple_of(index * chunk, chunk), chunk)
            spot = k * (units // chunk) + index
            pre = dot(second_low[...], w_in[k][:, cols])
            square = pre * pre
            bent = jnp.tanh(pre * (GELU_RATE + (GELU_RATE * GELU_CUBE) * square))
            half = 0.5 + 0.5 * bent
            act = (pre * half).astype(BF16)
            hidden[spot] = act
            bend = (0.5 - 0.5 * bent * bent) * (
                GELU_RATE + (3.0 * GELU_RATE * GELU_CUBE) * square
            )
            slope[spot] = half + pre * bend
            total[...] += dot(act, w_out[k][cols, :])
            return carry

        lax.fori_loop(0, units // chunk, expand, 0)

    gains[...] = jnp.zeros_like(gains)
    biases[...] = jnp.zeros_like(biases)

    def turn(index, carry):
        first = pl.multiple_of(index * block, block)
        rows = pl.ds(first, block)
        result, normed, inverse_dev = norm_forward(total[rows, :], gain[2:3, :], bias[2:3, :])
        layer_out[rows, :] = result
        grad = out_grad[own_rows(share, first, block), :].astype(F32)
        back, gain_grad, bias_grad = norm_back(grad, normed, inverse_dev, gain[2:3, :])
        gains[1:2, :] += gain_grad
        biases[1:2, :] += bias_grad
        back_sum[rows, :] = back
        top_low[rows, :] = back.astype(BF16)
        return carry

    lax.fori_loop(0, share // block, turn, 0)
    for k in range(parts):

        def contract(index, carry):
            cols = pl.ds(pl.multiple_of(index * chunk, chunk), chunk)
            spot = k * (units // chunk) + index
            weight_out = dot_tn(hidden[spot], top_low[...]).astype(BF16)
            pre = (dot_nt(top_low[...], w_out[k][cols, :]) * slope[spot]).astype(BF16)
            weight_in = dot_tn(second_low[...], pre).astype(BF16)
            if k == 0:
                g_out_keep[cols, :] = weight_out
                g_in_keep[:, cols] = weight_in
            else:
                g_out_send[k - 1, cols, :] = weight_out
                g_in_send[k - 1, :, cols] = weight_in
            back_sum[...] += dot_nt(pre, w_in[k][:, cols])
            return carry

        lax.fori_loop(0, units // chunk, contract, 0)

    def leave(index, carry):
        rows = pl.ds(pl.multiple_of(index * block, block), block)
        back, gain_grad, bias_grad = norm_back(
            back_sum[rows, :], normed2[rows, :], dev2[rows, :], gain[1:2, :]
        )
        gains[0:1, :] += gain_grad
        biases[0:1, :] += bias_grad
        grad_mid[rows, :] = back
        low = back.astype(BF16)
        top_low[rows, :] = low
        for k in range(parts):
            value = dot_nt(low, w_cross[k][...]).astype(BF16)
            if k == 0:
                back_keep[rows, :] = value
            else:
                back_send[k - 1, rows, :] = value
        return carry

    lax.fori_loop(0, share // block, leave, 0)
    for k in range(parts):
        value = dot_tn(ctx[k][...], top_low[...]).astype(BF16)
        if k == 0:
            g_cross_keep[...] = value
        else:
            g_cross_send[k - 1] = value


def middle_remote_kernel(parts, gain, bias, *refs):
    rest = list(refs)
    take = lambda number: [rest.pop(0) for _ in range(number)]
    first_in, top_in, ctx_in, wc0_in, wc1_in, wi0_in, wi1_in, wo0_in, wo1_in = take(9)
    layer_out, mid_out, small_out, sum_out, sum_in, sum_cross, cgrad_out = take(7)
    away_out = take(3)
    (first, top, ctx0, ctx1, wc0, wc1, wi0, wi1, wo0, wo1) = loaded = take(10)
    (second, second_low, normed2, dev2, total, hidden, slope, top_low, back_sum, layer, mid,
     own_out, land_out, gone_out, own_in, land_in, gone_in, own_cross, land_cross, gone_cross, own_back, gone_back) = take(22)
    load_sem, store_sem, part_sem, core_send, core_land = rest
    share, width = first.shape
    units = wi0.shape[1]
    block = 256
    chunk = hidden.shape[2]
    chunks = units // chunk
    core = lax.axis_index("heads")
    other = {"rows": lax.axis_index("rows"), "heads": 1 - core}
    mine = pl.ds(pl.multiple_of(core * share, share), share)
    w_in, w_out, w_cross, ctx = (wi0, wi1), (wo0, wo1), (wc0, wc1), (ctx0, ctx1)
    own_sends = {}

    def across(number, source, dest):
        copy = pltpu.make_async_remote_copy(
            src_ref=source, dst_ref=dest, send_sem=core_send.at[number], recv_sem=core_land.at[number],
            device_id=other, device_id_type=pl.DeviceIdType.MESH,
        )
        own_sends[number] = copy
        return copy

    sources = [first_in, top_in.at[mine, :], ctx_in.at[mine, :], None, wc0_in, wc1_in, wi0_in, wi1_in, wo0_in, wo1_in]
    loads = [
        None if source is None else pltpu.make_async_copy(source, dest, load_sem.at[k])
        for k, (source, dest) in enumerate(zip(sources, loaded))
    ]
    for k in (0, 2, 4, 5, 6, 7, 8, 9, 1):
        loads[k].start()
    barrier = pltpu.get_barrier_semaphore()
    pl.semaphore_signal(barrier, inc=1, device_id=other, device_id_type=pl.DeviceIdType.MESH)
    pl.semaphore_wait(barrier, 1)
    across(0, ctx_in.at[core_half(1 - core, share), :], ctx1).start()
    for k in (0, 2, 4, 5):
        loads[k].wait()
    own_sends[0].wait()

    def enter(index, carry):
        rows = pl.ds(pl.multiple_of(index * block, block), block)
        summed = first[rows, :] + dot(ctx0[rows, :], wc0[...]) + dot(ctx1[rows, :], wc1[...])
        result, normed, inverse_dev = norm_forward(summed, gain[1:2, :], bias[1:2, :])
        second[rows, :] = result
        second_low[rows, :] = result.astype(BF16)
        normed2[rows, :] = normed
        dev2[rows, :] = inverse_dev
        return carry

    lax.fori_loop(0, share // block, enter, 0)
    total[...] = second[...]
    for k in range(2):
        loads[6 + k].wait()
        loads[8 + k].wait()

        def expand(index, carry):
            cols = pl.ds(pl.multiple_of(index * chunk, chunk), chunk)
            spot = k * chunks + index
            pre = dot(second_low[...], w_in[k][:, cols])
            square = pre * pre
            bent = jnp.tanh(pre * (GELU_RATE + (GELU_RATE * GELU_CUBE) * square))
            half = 0.5 + 0.5 * bent
            act = (pre * half).astype(BF16)
            hidden[spot] = act
            bend = (0.5 - 0.5 * bent * bent) * (
                GELU_RATE + (3.0 * GELU_RATE * GELU_CUBE) * square
            )
            slope[spot] = half + pre * bend
            total[...] += dot(act, w_out[k][cols, :])
            return carry

        lax.fori_loop(0, chunks, expand, 0)
    loads[1].wait()
    small_out[...] = jnp.zeros_like(small_out)

    def turn(index, carry):
        rows = pl.ds(pl.multiple_of(index * block, block), block)
        result, normed, inverse_dev = norm_forward(total[rows, :], gain[2:3, :], bias[2:3, :])
        layer[rows, :] = result
        grad = top[rows, :].astype(F32)
        back, gain_grad, bias_grad = norm_back(grad, normed, inverse_dev, gain[2:3, :])
        small_out[2:3, :] += gain_grad
        small_out[5:6, :] += bias_grad
        back_sum[rows, :] = back
        top_low[rows, :] = back.astype(BF16)
        return carry

    lax.fori_loop(0, share // block, turn, 0)
    stores = [pltpu.make_async_copy(layer, layer_out, store_sem.at[0])]
    stores[0].start()
    for k in (1, 0):
        weight_out, weight_in = (own_out, own_in) if k == 0 else (gone_out, gone_in)

        def contract(index, carry):
            cols = pl.ds(pl.multiple_of(index * chunk, chunk), chunk)
            spot = k * chunks + index
            weight_out[cols, :] = dot_tn(hidden[spot], top_low[...]).astype(BF16)
            pre = (dot_nt(top_low[...], w_out[k][cols, :]) * slope[spot]).astype(BF16)
            weight_in[:, cols] = dot_tn(second_low[...], pre).astype(BF16)
            back_sum[...] += dot_nt(pre, w_in[k][:, cols])
            return carry

        lax.fori_loop(0, chunks, contract, 0)
        if k == 1:
            across(1, gone_out, land_out).start()
            across(2, gone_in, land_in).start()
    count = share // block
    for index in range(count):
        rows = pl.ds(index * block, block)
        back, gain_grad, bias_grad = norm_back(
            back_sum[rows, :], normed2[rows, :], dev2[rows, :], gain[1:2, :]
        )
        small_out[1:2, :] += gain_grad
        small_out[4:5, :] += bias_grad
        mid[rows, :] = back
        low = back.astype(BF16)
        top_low[rows, :] = low
        gone_back[rows, :] = dot_nt(low, wc1[...]).astype(BF16)
        across(
            4 + index, gone_back.at[rows, :], cgrad_out.at[own_rows(share, index * block, block), :]
        ).start()
        own_back[rows, :] = dot_nt(low, wc0[...]).astype(BF16)
    stores.append(pltpu.make_async_copy(mid, mid_out, store_sem.at[1]))
    stores.append(pltpu.make_async_copy(own_back, cgrad_out.at[mine, :], store_sem.at[2]))
    for store in stores[1:]:
        store.start()
    gone_cross[...] = dot_tn(ctx1[...], top_low[...]).astype(BF16)
    across(3, gone_cross, land_cross).start()
    own_sends[1].wait()
    add_into(own_out, land_out)
    stores.append(pltpu.make_async_copy(own_out, sum_out, store_sem.at[3]))
    stores[-1].start()
    own_sends[2].wait()
    add_into(own_in, land_in)
    stores.append(pltpu.make_async_copy(own_in, sum_in, store_sem.at[4]))
    stores[-1].start()
    for number, (part, bit, spot) in enumerate(parts):
        for source, dest in away_windows(part, bit, spot, (own_out, own_in)[part.out], away_out[bit]):
            stores.append(pltpu.make_async_copy(source, dest, part_sem.at[len(stores) - 5]))
            stores[-1].start()
    own_cross[...] = dot_tn(ctx0[...], top_low[...]).astype(BF16)
    own_sends[3].wait()
    add_into(own_cross, land_cross)
    stores.append(pltpu.make_async_copy(own_cross, sum_cross, store_sem.at[5]))
    stores[-1].start()
    for index in range(count):
        own_sends[4 + index].wait()
    for store in stores:
        store.wait()


def away_windows(part, bit, spot, source, dest):
    half = part.rows // 2
    side = lax.shift_right_logical(lax.axis_index("rows"), bit) & 1
    first = part.row + (1 - side) * half
    pairs = []
    for piece in range(half // 128):
        rows = pl.ds(pl.multiple_of(first + piece * 128, 128), 128)
        place = pl.ds(spot * 128, 128)
        cols = pl.ds(piece * part.cols, part.cols)
        pairs.append((source.at[rows, pl.ds(part.col, part.cols)], dest.at[place, cols]))
    return pairs


def first_steps(parts):
    filled = [0, 0, 0]
    found = []
    for part in parts:
        if part.out < 2:
            bit = part.order[0]
            found.append((part, bit, filled[bit]))
            filled[bit] += 1
    return found, [128 * max(1, n) for n in filled]


def run_middle(parts, gain, bias, args, units):
    share, width = args[0].shape
    local = args[2].shape[1]
    found, heights = first_steps(parts)
    chunk = 512
    vm = lambda kind, *dims: pltpu.VMEM(dims, kind)
    token, token_low = vm(F32, share, width), vm(BF16, share, width)
    scratch = [
        token, token_low, vm(BF16, share, local), vm(BF16, share, local),
        vm(BF16, local, width), vm(BF16, local, width), vm(BF16, width, units), vm(BF16, width, units),
        vm(BF16, units, width), vm(BF16, units, width),
        token, token_low, token, vm(F32, share, 1), token,
        vm(BF16, 2 * units // chunk, share, chunk), vm(F32, 2 * units // chunk, share, chunk),
        token_low, token, token, token,
        *[vm(BF16, units, width)] * 3, *[vm(BF16, width, units)] * 3, *[vm(BF16, local, width)] * 3,
        vm(BF16, share, local), vm(BF16, share, local),
    ]
    sems = [10, 6, 2 * len(found), 4 + share // 256, 4 + share // 256]
    anyspace = pl.BlockSpec(memory_space=pl.ANY)
    return pl.pallas_call(
        functools.partial(middle_remote_kernel, found),
        out_shape=[
            shape_of((share, width), F32), shape_of((share, width), F32), shape_of((8, width), F32),
            shape_of((units, width), BF16), shape_of((width, units), BF16), shape_of((local, width), BF16),
            shape_of((2 * share, local), BF16), *[shape_of((h, width), BF16) for h in heights],
        ],
        in_specs=[VMEM] * 2 + [anyspace] * len(args),
        out_specs=[anyspace] * 2 + [VMEM] + [anyspace] * 7,
        scratch_shapes=scratch + [pltpu.SemaphoreType.DMA((n,)) for n in sems],
        compiler_params=pltpu.CompilerParams(
            vmem_limit_bytes=VMEM_BYTES, collective_id=1, has_side_effects=True
        ),
    )(gain, bias, *args)


def cross_back_kernel(parts, dec_ref, enc_ref, qx, kx, vx, ctx, enc, w_kv, *refs):
    pieces = refs[:parts]
    (gq_keep, gq_send, g_kv, enc_keep, enc_send, grad, gx, dq, kt, sums, sq, sk, sv, wide) = refs[parts:]
    length = ctx.shape[0]
    dec_starts, dec_ends = segment_bounds(dec_ref)
    enc_starts, enc_ends = segment_bounds(enc_ref)
    gather_rows(grad, pieces[0], pieces[1:])
    attend_back(
        enc_starts, enc_ends, dec_starts, dec_ends, qx, kx, vx, ctx, grad, gx, dq, kt, sums, sq, sk, sv
    )
    split_out(sq, gq_keep, gq_send, gq_keep.shape[0])
    g_kv[0] = dot_tn(enc[...], sk[...]).astype(BF16)
    g_kv[1] = dot_tn(enc[...], sv[...]).astype(BF16)

    def step(block, carry):
        rows = pl.ds(pl.multiple_of(block * SPAN, SPAN), SPAN)
        wide[rows, :] = dot_nt(sk[rows, :], w_kv[0]) + dot_nt(sv[rows, :], w_kv[1])
        return carry

    lax.fori_loop(0, length // SPAN, step, 0)
    split_out(wide, enc_keep, enc_send, enc_keep.shape[0])


def cross_back_fast(dec_ref, enc_ref, *refs):
    rest = list(refs)
    take = lambda number: [rest.pop(0) for _ in range(number)]
    sources = take(8)
    gq_out, g_kv, enc_keep, enc_send, layer_out = take(5)
    loaded = take(8)
    grad, ctx, kx, vx, qx, enc, w_kv, layer = loaded
    gx, dq, kt, sums, sq, sk, sv, wide, load_sem, store_sem = rest
    length = ctx.shape[0]
    heads = qx.shape[0]
    loads = [pltpu.make_async_copy(a, b, load_sem.at[k]) for k, (a, b) in enumerate(zip(sources, loaded))]
    for load in loads:
        load.start()
    dec_starts, dec_ends = segment_bounds(dec_ref)
    enc_starts, enc_ends = segment_bounds(enc_ref)
    sums[...] = head_sums(ctx.shape[1], heads)
    for load in loads[:3]:
        load.wait()
    prepare_back(grad, ctx, kx, gx, dq, kt, sums)
    for load in loads[3:5]:
        load.wait()
    each_span(
        length, enc_starts, dec_starts, dec_ends,
        functools.partial(attend_back_body, qx, kx, vx, gx, dq, kt, sk, sv),
    )
    for load in loads[5:]:
        load.wait()
    turn_queries(dq, sq, range(max(1, heads // 2)))
    stores = [
        pltpu.make_async_copy(layer, layer_out, store_sem.at[0]),
        pltpu.make_async_copy(sq, gq_out, store_sem.at[1]),
    ]
    for store in stores:
        store.start()
    g_kv[0] = dot_tn(enc[...], sk[...]).astype(BF16)
    g_kv[1] = dot_tn(enc[...], sv[...]).astype(BF16)

    def step(block, carry):
        rows = pl.ds(pl.multiple_of(block * SPAN, SPAN), SPAN)
        wide[rows, :] = dot_nt(sk[rows, :], w_kv[0]) + dot_nt(sv[rows, :], w_kv[1])
        return carry

    lax.fori_loop(0, length // SPAN, step, 0)
    split_out(wide, enc_keep, enc_send, enc_keep.shape[0])
    for store in stores:
        store.wait()


def first_back_kernel(parts, gain, grad_mid, first_low, normed, dev, *refs):
    groups = [refs[g * parts : (g + 1) * parts] for g in range(4)]
    gq, w_query, ctx, w_out = groups
    (grad_base, gains, biases, g_query_keep, g_query_send, g_out_keep, g_out_send,
     back_keep, back_send, low_ref) = refs[4 * parts :]
    share = grad_mid.shape[0]
    block = share_block(share)
    gains[...] = jnp.zeros_like(gains)
    biases[...] = jnp.zeros_like(biases)

    def step(index, carry):
        rows = pl.ds(pl.multiple_of(index * block, block), block)
        grad = grad_mid[rows, :]
        for k in range(parts):
            grad = grad + dot_nt(gq[k][rows, :], w_query[k][...])
        back, gain_grad, bias_grad = norm_back(grad, normed[rows, :], dev[rows, :], gain[0:1, :])
        gains[...] += gain_grad
        biases[...] += bias_grad
        grad_base[rows, :] = back
        low = back.astype(BF16)
        low_ref[rows, :] = low
        for k in range(parts):
            value = dot_nt(low, w_out[k][...]).astype(BF16)
            if k == 0:
                back_keep[rows, :] = value
            else:
                back_send[k - 1, rows, :] = value
        return carry

    lax.fori_loop(0, share // block, step, 0)
    for k in range(parts):
        query_grad = dot_tn(first_low[...], gq[k][...]).astype(BF16)
        out_grad = dot_tn(ctx[k][...], low_ref[...]).astype(BF16)
        if k == 0:
            g_query_keep[...] = query_grad
            g_out_keep[...] = out_grad
        else:
            g_query_send[k - 1] = query_grad
            g_out_send[k - 1] = out_grad


def self_back_kernel(parts, dec_ref, qx, kx, vx, ctx, x_ref, w_qkv, *refs):
    pieces = refs[:parts]
    g_qkv, in_keep, in_send, grad, gx, dq, kt, sums, sq, sk, sv, wide = refs[parts:]
    length = ctx.shape[0]
    starts, ends = segment_bounds(dec_ref)
    gather_rows(grad, pieces[0], pieces[1:])
    attend_back(starts, ends, starts, ends, qx, kx, vx, ctx, grad, gx, dq, kt, sums, sq, sk, sv)
    for c, source in enumerate((sq, sk, sv)):
        g_qkv[c] = dot_tn(x_ref[...], source[...]).astype(BF16)

    def step(block, carry):
        rows = pl.ds(pl.multiple_of(block * SPAN, SPAN), SPAN)
        wide[rows, :] = (
            dot_nt(sq[rows, :], w_qkv[0])
            + dot_nt(sk[rows, :], w_qkv[1])
            + dot_nt(sv[rows, :], w_qkv[2])
        )
        return carry

    lax.fori_loop(0, length // SPAN, step, 0)
    split_out(wide, in_keep, in_send, in_keep.shape[0])


LINK_RATE = 0.088
HOP_TIME = 2.0
TAKE_TIME = 0.05
ADD_RATE = 1.3
SEND_TIME = 0.03
SLACK = 0.5
AHEAD = 0.5
LAST_AHEAD = 1.0


class Part:
    def __init__(self, out, row, col, rows, cols, ready):
        self.out, self.row, self.col, self.rows, self.cols = out, row, col, rows, cols
        self.ready = ready
        self.order = None
        self.first = 0

    def window(self):
        return (pl.ds(self.row, self.rows), pl.ds(self.col, self.cols))


def step_shape(part, step, bits):
    depth = step if step < bits else 2 * bits - 2 - step
    return part.order[depth], part.rows >> min(depth + 1, bits - 1)


def link_cost(part, step, bits):
    bit, rows = step_shape(part, step, bits)
    amount = rows * part.cols * 2e-6 * 2 / LINK_RATE
    return {bit: 2 * amount, bit - 1: amount} if bit == bits - 1 else {bit: amount}


def choose_orders(parts, bits):
    last = bits - 1
    options = [(0, 1, 2, last), (1, 0, 2, last), (2, 0, 1, last), (2, 1, 0, last)]
    load = dict.fromkeys(range(bits), 0.0)
    for part in parts:
        best = None
        for order in options:
            part.order = order
            trial = dict(load)
            for step in range(part.first, 2 * bits - 1):
                for bit, amount in link_cost(part, step, bits).items():
                    trial[bit] += amount
            score = sum(value * value for value in trial.values())
            if best is None or score < best[0]:
                best = (score, order, trial)
        _, part.order, load = best


def plan_transfers(parts, bits, spans):
    steps = 2 * bits - 1
    busy = dict.fromkeys(range(bits), 0.0)
    left = [part.first for part in parts]
    since = [None] * len(parts)
    flying = []

    def rest(p):
        return sum(max(link_cost(parts[p], s, bits).values()) + HOP_TIME for s in range(left[p], steps))

    def serve(clock, ahead, slack, found):
        for entry in sorted(flying):
            if entry[0] + slack <= clock:
                flying.remove(entry)
                p = entry[1]
                found.append(("take", p, left[p]))
                clock += TAKE_TIME
                if left[p] < bits:
                    clock += step_shape(parts[p], left[p], bits)[1] * parts[p].cols * 2e-6 / ADD_RATE
                left[p] += 1
                since[p] = clock if left[p] < steps else None
        waiting = [p for p in range(len(parts)) if since[p] is not None]
        for p in sorted(waiting, key=lambda p: (-parts[p].ready[0], -rest(p), p)):
            cost = link_cost(parts[p], left[p], bits)
            if since[p] <= clock and all(busy[b] <= clock + ahead for b in cost):
                done = clock
                for b, amount in cost.items():
                    busy[b] = max(busy[b], clock) + amount
                    done = max(done, busy[b])
                clock += SEND_TIME
                found.append(("send", p, left[p]))
                flying.append((done + HOP_TIME, p))
                since[p] = None
        return clock

    slots, clock = [], 0.0
    for unit, span in enumerate(spans):
        for p, part in enumerate(parts):
            if part.ready[0] == unit:
                since[p] = clock + part.ready[1]
        found = []
        clock = serve(clock, span + AHEAD, SLACK, found)
        slots.append(found)
        clock += span
    for p, part in enumerate(parts):
        if part.ready[0] >= len(spans):
            since[p] = clock + part.ready[1]
    found = []
    while flying or any(value is not None for value in since):
        before = len(found)
        clock = serve(clock, LAST_AHEAD, 0.0, found)
        if len(found) == before:
            clock += 0.05
    slots.append(found)
    return slots


class RowsSum:
    def __init__(self, parts, bits, held, landing, final, outs, send_sem, land_sem, store_sem):
        self.parts, self.bits = parts, bits
        self.held, self.landing, self.final, self.outs = held, landing, final, outs
        self.send_sem, self.land_sem, self.store_sem = send_sem, land_sem, store_sem
        self.begin = [lambda: None] * len(parts)

    def side(self, bit):
        return lax.shift_right_logical(lax.axis_index("rows"), bit) & 1

    def peer(self, bit):
        me = lax.axis_index("rows")
        return {"rows": me + (1 << bit) - 2 * (me & (1 << bit)), "heads": lax.axis_index("heads")}

    def offset(self, p, depth):
        part, total = self.parts[p], jnp.int32(0)
        for d in range(depth):
            total = total + self.side(part.order[d]) * (part.rows >> (d + 1))
        return total

    def copy(self, p, step):
        part = self.parts[p]
        bit, size = step_shape(part, step, self.bits)
        if step < self.bits - 1:
            first = self.offset(p, step) + (1 - self.side(bit)) * size
        else:
            first = self.offset(p, min(step, 2 * self.bits - 2 - step) + (step >= self.bits))
        rows = pl.ds(pl.multiple_of(first, 16), size)
        if step < self.bits:
            source = self.held[p].at[rows, :]
            dest = self.landing[p].at[pl.ds(self.spot(p, step), size), :]
        else:
            source = self.final[p].at[rows, :]
            dest = source
        return pltpu.make_async_remote_copy(
            src_ref=source, dst_ref=dest, send_sem=self.send_sem.at[p, step],
            recv_sem=self.land_sem.at[p, step], device_id=self.peer(bit),
            device_id_type=pl.DeviceIdType.MESH,
        )

    def spot(self, p, step):
        part = self.parts[p]
        return part.rows - (part.rows >> step)

    def absorb(self, p, step):
        part = self.parts[p]
        size = step_shape(part, step, self.bits)[1]
        depth = min(step + 1, self.bits - 1)
        mine = pl.ds(pl.multiple_of(self.offset(p, depth), 16), size)
        spot = pl.ds(self.spot(p, step), size)
        total = self.held[p][mine, :].astype(F32) + self.landing[p][spot, :].astype(F32)
        dest = self.final[p] if step == self.bits - 1 else self.held[p]
        dest[mine, :] = total.astype(BF16)

    def store(self, p):
        part = self.parts[p]
        return pltpu.make_async_copy(
            self.final[p], self.outs[part.out].at[part.window()], self.store_sem.at[p]
        )

    def run(self, ops):
        for kind, p, step in ops:
            if kind == "send":
                if step == self.parts[p].first:
                    self.begin[p]()
                self.copy(p, step).start()
                continue
            self.copy(p, step).wait()
            if step < self.bits:
                self.absorb(p, step)
            elif step == 2 * self.bits - 2:
                self.store(p).start()


def add_into(dest, other):
    dest[...] = (dest[...].astype(F32) + other[...].astype(F32)).astype(dest.dtype)


def back_unit(qx, kx, vx, gx, dq, kt, sk, sv, head, rows, queries):
    scale = LOG2_E * HEAD_DIM**-0.5
    keys = kx[head, rows, :]
    query = qx[head, queries, :]
    grads = gx[head, queries, :]
    weights = jnp.exp2(dot_nt(keys, query) * scale)
    raised = dot_nt(vx[head, rows, :], grads)
    value_slab = dot(weights.astype(BF16), grads)
    inner = (weights * raised).astype(BF16)
    key_slab = dot(inner, query) * (HEAD_DIM**-0.5)
    dq[head, :, queries] += dot(kt[head, :, rows], inner)
    merge_head(sk, rows, head, key_slab)
    merge_head(sv, rows, head, value_slab)


def tail_kernel(parts, bits, plan, gain, small_in, *refs):
    rest = list(refs)
    take = lambda number: [rest.pop(0) for _ in range(number)]
    (gq_in, grad_mid_in, first_low_in, normed_in, dev_in, wq0_in, wq1_in, ctx1_in,
     wo0_in, wo1_in, qx_in, kx_in, vx_in, ctx_in, x_in, w_in, enc_in) = take(17)
    ffn_out_own, ffn_in_own, cross_own, kv_own, *arrived = take(7)
    outs = take(7)
    small_out, in_keep, in_land_out, enc_out = take(4)
    count = len(parts)
    held, landing, final = take(count), take(count), take(count)
    mates = dict(zip([p for p in range(count) if parts[p].out in (3, 5)], rest))
    take(len(mates))
    (gq, gq_land, grad_mid, first_low, normed, dev, wq0, wq1, ctx0, ctx1, wo0, wo1, qx, kx, vx, ctx, x_ref, w_ref,
     grad, gx, dq, kt, sums, sq, sk, sv, wide, low, back_out, query_out, self_out, in_out, in_land, small_land) = take(34)
    (send_sem, land_sem, store_sem, load_sem, part_sem, mate_send, mate_land, core_send, core_land,
     small_send, small_sem, out_sem) = rest
    share, width = grad_mid.shape
    length = x_ref.shape[0]
    heads = qx.shape[0]
    block = 256
    me, core = lax.axis_index("rows"), lax.axis_index("heads")
    other_core = {"rows": me, "heads": 1 - core}
    mine_rows = core_half(core, share)
    summing = RowsSum(parts, bits, held, landing, final, outs, send_sem, land_sem, store_sem)

    def across(source, dest, send, land, peer=other_core):
        return pltpu.make_async_remote_copy(
            src_ref=source, dst_ref=dest, send_sem=send, recv_sem=land,
            device_id=peer, device_id_type=pl.DeviceIdType.MESH,
        )

    pairs = [
        (gq_in.at[mine_rows, :], gq), (grad_mid_in, grad_mid), (wq0_in, wq0), (wq1_in, wq1), (normed_in, normed), (dev_in, dev),
        (wo0_in, wo0), (wo1_in, wo1), (first_low_in, first_low), (ctx_in.at[mine_rows, :], ctx0), (ctx1_in, ctx1), (ctx_in, ctx),
        (qx_in, qx), (kx_in, kx), (vx_in, vx), (x_in, x_ref), (w_in, w_ref),
    ]
    loads = [pltpu.make_async_copy(a, b, load_sem.at[k]) for k, (a, b) in enumerate(pairs)]
    own_arrays = {0: ffn_out_own, 1: ffn_in_own, 2: cross_own, 4: kv_own}
    early = {id(part): (bit, spot) for part, bit, spot in first_steps(parts)[0]}
    part_loads, mate_copies = {}, {}
    for p, part in enumerate(parts):
        part_loads[p] = []
        if part.first:
            half = part.rows // 2
            bit, spot = early[id(part)]
            keep = part.row + summing.side(bit) * half
            rows = pl.ds(pl.multiple_of(keep, 128), half)
            here = pl.ds(pl.multiple_of(keep - part.row, 128), half)
            moves = [(own_arrays[part.out].at[rows, pl.ds(part.col, part.cols)], held[p].at[here, :])]
            for piece in range(half // 128):
                window = (pl.ds(spot * 128, 128), pl.ds(piece * part.cols, part.cols))
                moves.append((arrived[bit].at[window], landing[p].at[pl.ds(piece * 128, 128), :]))
        elif part.out in own_arrays:
            moves = [(own_arrays[part.out].at[part.window()], held[p])]
        else:
            moves = []
        for k, (source, dest) in enumerate(moves):
            part_loads[p].append(pltpu.make_async_copy(source, dest, part_sem.at[p, k]))
            part_loads[p][-1].start()
    for load in loads[:6]:
        load.start()
    peers = [summing.peer(bit) for bit in range(bits)] + [other_core]
    barrier = pltpu.get_barrier_semaphore()
    for peer in peers:
        pl.semaphore_signal(barrier, inc=1, device_id=peer, device_id_type=pl.DeviceIdType.MESH)
    pl.semaphore_wait(barrier, len(peers))
    gq_copy = across(gq_in.at[core_half(1 - core, share), :], gq_land, core_send.at[0], core_land.at[0])
    gq_copy.start()
    enc_copy = across(
        enc_in.at[0], enc_out, core_send.at[2 + share // block], core_land.at[2 + share // block]
    )
    for load in loads[6:]:
        load.start()
    for p, part in enumerate(parts):
        if part.out == 3:
            mate_copies[p] = across(query_out, mates[p], mate_send.at[p], mate_land.at[p])
        if part.out == 5:
            mate_copies[p] = across(self_out, mates[p], mate_send.at[p], mate_land.at[p])

        def begin(p=p):
            for load in part_loads[p]:
                load.wait()
            if parts[p].first:
                summing.absorb(p, 0)
            if p in mate_copies:
                mate_copies[p].wait()
                add_into(held[p], mates[p])

        summing.begin[p] = begin

    slots = list(plan)
    summing.run(slots.pop(0))
    for load in loads[:6]:
        load.wait()
    gq_copy.wait()
    for load in loads[6:8]:
        load.wait()
    small_out[...] = small_in[...]
    back_copies = []
    for index in range(share // block):
        summing.run(slots.pop(0))
        rows = pl.ds(index * block, block)
        mine = own_rows(share, index * block, block)
        value = grad_mid[rows, :] + dot_nt(gq[rows, :], wq0[...]) + dot_nt(gq_land[rows, :], wq1[...])
        back, gain_grad, bias_grad = norm_back(value, normed[rows, :], dev[rows, :], gain[0:1, :])
        small_out[0:1, :] += gain_grad
        small_out[3:4, :] += bias_grad
        in_keep[rows, :] = back
        low_part = back.astype(BF16)
        low[rows, :] = low_part
        grad[mine, :] = dot_nt(low_part, wo0[...]).astype(BF16)
        back_out[rows, :] = dot_nt(low_part, wo1[...]).astype(BF16)
        copy = across(back_out.at[rows, :], grad.at[mine, :], core_send.at[1 + index], core_land.at[1 + index])
        copy.start()
        back_copies.append(copy)
    summing.run(slots.pop(0))
    for load in loads[8:12]:
        load.wait()
    query_out[...] = dot_tn(first_low[...], gq_land[...]).astype(BF16)
    self_out[...] = dot_tn(ctx1[...], low[...]).astype(BF16)
    for p, part in enumerate(parts):
        if part.out in (3, 5):
            mate_copies[p].start()
        if part.out == 3:
            held[p][...] = dot_tn(first_low[...], gq[...]).astype(BF16)
        if part.out == 5:
            held[p][...] = dot_tn(ctx0[...], low[...]).astype(BF16)
    summing.run(slots.pop(0))
    enc_copy.start()
    for copy in back_copies:
        copy.wait()
    for load in loads[12:]:
        load.wait()
    sums[...] = head_sums(ctx.shape[1], heads)
    prepare_back(grad, ctx, kx, gx, dq, kt, sums)
    blocks = length // KEY_SPAN
    in_copy = across(in_out, in_land, core_send.at[1 + share // block], core_land.at[1 + share // block])
    for pair in range(heads // 2):
        mine = [slots.pop(0) for _ in range(2 * blocks)]

        def unit(index, carry):
            lax.switch(index, [functools.partial(summing.run, ops) for ops in mine])
            rows = pl.ds(pl.multiple_of(lax.rem(index, blocks) * KEY_SPAN, KEY_SPAN), KEY_SPAN)
            head = 2 * pair + lax.div(index, blocks)
            back_unit(qx, kx, vx, gx, dq, kt, sk, sv, head, rows, pl.ds(0, length))
            return carry

        lax.fori_loop(0, 2 * blocks, unit, 0)
        cols = pl.ds(pair * LANES, LANES)
        summing.run(slots.pop(0))
        turn_queries(dq, sq, [pair])
        for p, part in enumerate(parts):
            if part.out == 6 and part.col == pair * LANES:
                source = (sq, sk, sv)[part.row // width]
                held[p][...] = dot_tn(x_ref[...], source[:, cols]).astype(BF16)
    last = slots.pop(0)
    early_ops = 24
    summing.run(last[:early_ops])
    last = last[early_ops:]

    def spread(index, carry):
        rows = pl.ds(pl.multiple_of(index * SPAN, SPAN), SPAN)
        value = dot_nt(sq[rows, :], w_ref[0]) + dot_nt(sk[rows, :], w_ref[1])
        wide[rows, :] = value + dot_nt(sv[rows, :], w_ref[2])
        return carry

    lax.fori_loop(0, length // SPAN, spread, 0)
    away = pl.ds(pl.multiple_of((1 - core) * share, share), share)
    in_out[...] = wide[away, :].astype(BF16)
    in_copy.start()
    here = pl.ds(pl.multiple_of(core * share, share), share)
    in_keep[...] += wide[here, :]
    enc_copy.wait()
    small_copy = None
    for k in range(len(peers) + 1):
        cut = len(last) * k // (len(peers) + 1), len(last) * (k + 1) // (len(peers) + 1)
        if small_copy is not None:
            small_copy.wait()
            small_out[...] += small_land[k - 1]
        if k < len(peers):
            small_copy = across(
                small_out, small_land.at[k], small_send.at[k], small_sem.at[k], peers[k]
            )
            small_copy.start()
        if k == len(peers):
            in_copy.wait()
            in_store = pltpu.make_async_copy(in_land, in_land_out, out_sem)
            in_store.start()
        summing.run(last[cut[0] : cut[1]])
    in_store.wait()
    for p in range(count):
        summing.store(p).wait()


def widen_kernel(table, small, *refs):
    sources = 1 + max(max(e[0], -1 if e[1] is None else e[1]) for e in table)
    outs = 1 + max(e[2] for e in table)
    arrays, dests = refs[:sources], refs[sources : sources + outs]
    gain_out, bias_out = refs[sources + outs : sources + outs + 2]
    rest = list(refs[sources + outs + 2 :])
    low = [rest.pop(0) for _ in table]
    more = {k: rest.pop(0) for k, e in enumerate(table) if e[1] is not None}
    wide = [rest.pop(0) for _ in table]
    load_sem, more_sem, store_sem = rest
    loads, stores = [], []
    for k, (source, second, out, window) in enumerate(table):
        window = tuple(pl.ds(*w) for w in window)
        loads.append([pltpu.make_async_copy(arrays[source].at[window], low[k], load_sem.at[k])])
        if second is not None:
            loads[k].append(pltpu.make_async_copy(arrays[second].at[window], more[k], more_sem.at[k]))
        stores.append(pltpu.make_async_copy(wide[k], dests[out].at[window], store_sem.at[k]))
        for load in loads[k]:
            load.start()
    gain_out[...] = small[0:3, :]
    bias_out[...] = small[3:6, :]
    for k in range(len(table)):
        for load in loads[k]:
            load.wait()
        value = low[k][...].astype(F32)
        if k in more:
            value = value + more[k][...].astype(F32)
        wide[k][...] = value
        stores[k].start()
    for store in stores:
        store.wait()


def widen_all(small, entries):
    arrays, table, shapes = [], [], []
    for out, (first, second) in enumerate(entries):
        source = len(arrays)
        arrays.append(first)
        if second is not None:
            arrays.append(second)
        rows, cols = first.shape
        shapes.append(shape_of((rows, cols), F32))
        high = 256 if cols >= 512 else 512
        for row in range(0, rows, high):
            table.append((source, None if second is None else source + 1, out, ((row, high), (0, cols))))
    spaces = [pl.BlockSpec(memory_space=pl.ANY)]
    sized = lambda e: (e[3][0][1], e[3][1][1])
    return pl.pallas_call(
        functools.partial(widen_kernel, table),
        out_shape=shapes + [shape_of((3, small.shape[1]), F32)] * 2,
        in_specs=[VMEM] + spaces * len(arrays),
        out_specs=spaces * len(shapes) + [VMEM] * 2,
        scratch_shapes=[pltpu.VMEM(sized(e), arrays[e[0]].dtype) for e in table]
        + [pltpu.VMEM(sized(e), arrays[e[1]].dtype) for e in table if e[1] is not None]
        + [pltpu.VMEM(sized(e), F32) for e in table]
        + [pltpu.SemaphoreType.DMA((len(table),))] * 3,
        compiler_params=pltpu.CompilerParams(vmem_limit_bytes=VMEM_BYTES),
    )(small, *arrays)


def unit_spans(share, heads):
    spans = [3.0] + [1.3] * (share // 256) + [1.8, 2.0]
    made = len(spans) - 1
    pair_end = []
    for _ in range(heads // 2):
        spans += [2.2] * (4 * share // KEY_SPAN) + [1.8]
        pair_end.append(len(spans))
    return spans, made, pair_end


def gradient_parts(shapes, share, heads, bits):
    spans, made, pair_end = unit_spans(share, heads)
    parts = []
    for out, (rows, cols) in enumerate(shapes):
        high, broad = (256, 512) if cols == 512 else (512, 256)
        if out == 6:
            broad = LANES
        for col in range(0, cols, broad):
            for row in range(0, rows, high):
                ready = (0, 0.0)
                if out in (3, 5):
                    ready = (made, 1.0)
                if out == 6:
                    ready = (pair_end[col // LANES], 0.0)
                parts.append(Part(out, row, col, high, broad, ready))
                parts[-1].first = 1 if out < 2 else 0
    choose_orders(parts, bits)
    return parts


def run_tail(parts, gain, small, first_args, halves, shapes):
    bits = lax.axis_size("rows").bit_length() - 1
    length, local = first_args[0].shape
    width = first_args[1].shape[1]
    share = length // 2
    heads = local // HEAD_DIM
    norm_units = share // 256
    plan = plan_transfers(parts, bits, unit_spans(share, heads)[0])
    count = len(parts)
    buffers = [pltpu.VMEM((p.rows, p.cols), BF16) for p in parts]
    mated = [b for b, p in zip(buffers, parts) if p.out in (3, 5)]
    vm = lambda kind, *dims: pltpu.VMEM(dims, kind)
    wide_heads = vm(BF16, heads, length, LANES)
    own = [
        vm(BF16, share, local), vm(BF16, share, local), vm(F32, share, width), vm(BF16, share, width),
        vm(F32, share, width), vm(F32, share, 1), vm(BF16, width, local), vm(BF16, width, local),
        vm(BF16, share, local), vm(BF16, share, local), vm(BF16, local, width), vm(BF16, local, width),
        wide_heads, wide_heads, wide_heads, vm(BF16, length, local), vm(BF16, length, width),
        vm(BF16, 3, width, local),
        vm(BF16, length, local), wide_heads, vm(F32, heads, HEAD_DIM, length),
        vm(BF16, heads, HEAD_DIM, length), vm(BF16, local, heads * LANES),
        vm(BF16, length, local), vm(BF16, length, local), vm(BF16, length, local), vm(F32, length, width),
        vm(BF16, share, width), vm(BF16, share, local), vm(BF16, width, local), vm(BF16, local, width),
        vm(BF16, share, width), vm(BF16, share, width), vm(F32, bits + 1, 8, width),
    ]
    sems = [
        (count, 2 * bits - 1), (count, 2 * bits - 1), (count,), (17,), (count, 3), (count,), (count,),
        (3 + norm_units,), (3 + norm_units,), (bits + 1,), (bits + 1,),
    ]
    anyspace = pl.BlockSpec(memory_space=pl.ANY)
    return pl.pallas_call(
        functools.partial(tail_kernel, parts, bits, plan),
        out_shape=[shape_of(dims, BF16) for dims in shapes]
        + [shape_of((8, width), F32), shape_of((share, width), F32)]
        + [shape_of((share, width), BF16)] * 2,
        in_specs=[VMEM] * 2 + [anyspace] * (len(first_args) + len(halves)),
        out_specs=[anyspace] * len(shapes) + [VMEM, VMEM, anyspace, anyspace],
        scratch_shapes=buffers * 3 + mated + own
        + [pltpu.SemaphoreType.DMA(dims) for dims in sems] + [pltpu.SemaphoreType.DMA],
        compiler_params=pltpu.CompilerParams(
            vmem_limit_bytes=VMEM_BYTES, collective_id=0, has_side_effects=True
        ),
    )(gain, small, *first_args, *halves)


def fits_tail(length, width, local, units):
    return (
        lax.axis_size("rows") == 16
        and lax.axis_size("heads") == 2
        and (width, local) == (512, 256)
        and length % 512 == 0
        and units % 512 == 0
    )


def fast_body(
    dec_input, enc_output, dec_lengths, enc_lengths, w_self_qkv, w_self_out, w_cross_q, w_cross_kv,
    w_cross_out, w_ffn_in, w_ffn_out, norm_gain, norm_bias, out_grad,
):
    length, width = dec_input.shape
    local = w_self_out.shape[0]
    heads = local // HEAD_DIM
    share = length // 2
    units = w_ffn_in.shape[1]
    size = lax.axis_size("rows")
    bits = size.bit_length() - 1
    blocks = length // SPAN
    vm = lambda kind, *dims: pltpu.VMEM(dims, kind)
    low, full = (lambda *dims: shape_of(dims, BF16)), (lambda *dims: shape_of(dims, F32))
    wide_heads, wide_scratch = low(heads, length, LANES), vm(BF16, heads, length, LANES)
    sems = [pltpu.SemaphoreType.DMA((2, blocks)), pltpu.SemaphoreType.DMA((2,))]
    self_ctx, self_qx, self_kx, self_vx = call(
        self_forward_fast, [low(length, local), wide_heads, wide_heads, wide_heads],
        [vm(BF16, length, local), wide_scratch, wide_scratch, wide_scratch] + sems, 0,
        dec_lengths, dec_input, w_self_qkv, smem=1, out_far=4,
    )
    (first_out, first_low, first_normed, first_dev, query, cross_kx, cross_vx, far_ctx, far_self_out,
     far_cross_q, far_cross_out, far_ffn_in, far_ffn_out) = run_entry(
        enc_lengths, norm_gain, norm_bias,
        [dec_input, enc_output, w_cross_kv, self_ctx, w_self_out, w_cross_q, w_cross_out, w_ffn_in, w_ffn_out],
    )
    cross_ctx, cross_qx = call(
        cross_forward_fast, [low(length, local), wide_heads],
        [vm(BF16, length, local), wide_scratch, wide_scratch, wide_scratch] + sems, 0,
        dec_lengths, enc_lengths, query, cross_kx, cross_vx, smem=2, far=2, out_far=2,
    )
    shapes = [
        (units, width), (width, units), (local, width), (width, local),
        (2 * width, local), (local, width), (3 * width, local),
    ]
    pieces = gradient_parts(shapes, share, heads, bits)
    (layer_out, grad_mid, small, g_ffn_out, g_ffn_in, g_cross_out, cross_grad, *away) = run_middle(
        pieces, norm_gain, norm_bias,
        [first_out, out_grad, cross_ctx, w_cross_out, far_cross_out, w_ffn_in, far_ffn_in,
         w_ffn_out, far_ffn_out], units,
    )
    arrived = [
        lax.ppermute(value, "rows", [(r, r ^ (1 << bit)) for r in range(size)])
        for bit, value in enumerate(away)
    ]
    flat = vm(BF16, length, local)
    gq, g_cross_kv, enc_keep, enc_send, layer_out = call(
        cross_back_fast,
        [low(length, local), low(2, width, local), full(share, width), low(1, share, width), full(share, width)],
        [flat, flat, wide_scratch, wide_scratch, wide_scratch, vm(BF16, length, width),
         vm(BF16, 2, width, local), vm(F32, share, width), wide_scratch, vm(F32, heads, HEAD_DIM, length),
         vm(BF16, heads, HEAD_DIM, length), vm(BF16, local, heads * LANES), flat, flat, flat,
         vm(F32, length, width), pltpu.SemaphoreType.DMA((8,)), pltpu.SemaphoreType.DMA((2,))],
        0, dec_lengths, enc_lengths, cross_grad, cross_ctx, cross_kx, cross_vx, cross_qx, enc_output,
        w_cross_kv, layer_out, smem=2, far=8, out_places=(0, 4),
    )
    *sums, small, in_keep, in_land, enc_land = run_tail(
        pieces, norm_gain, small,
        [gq, grad_mid, first_low, first_normed, first_dev, w_cross_q, far_cross_q, far_ctx,
         w_self_out, far_self_out, self_qx, self_kx, self_vx, self_ctx, dec_input, w_self_qkv, enc_send],
        [g_ffn_out, g_ffn_in, g_cross_out, g_cross_kv.reshape(2 * width, local), *arrived],
        shapes,
    )
    (s_ffn_out, s_ffn_in, s_cross_out, s_cross_q, s_cross_kv, s_self_out, s_self_qkv,
     input_grad, enc_grad, gain_grad, bias_grad) = widen_all(
        small, [(value, None) for value in sums] + [(in_keep, in_land), (enc_keep, enc_land)]
    )
    return (
        layer_out, input_grad, enc_grad, s_self_qkv.reshape(3, width, local), s_self_out, s_cross_q,
        s_cross_kv.reshape(2, width, local), s_cross_out, s_ffn_in, s_ffn_out, gain_grad, bias_grad,
    )


def body(*args):
    dec_input, w_self_out, w_ffn_in = args[0], args[5], args[9]
    if fits_tail(*dec_input.shape, w_self_out.shape[0], w_ffn_in.shape[1]):
        return fast_body(*args)
    return plain_body(*args)


def plain_body(
    dec_input,
    enc_output,
    dec_lengths,
    enc_lengths,
    w_self_qkv,
    w_self_out,
    w_cross_q,
    w_cross_kv,
    w_cross_out,
    w_ffn_in,
    w_ffn_out,
    norm_gain,
    norm_bias,
    out_grad,
):
    parts = lax.axis_size("heads")
    length, width = dec_input.shape
    local = w_self_out.shape[0]
    heads = local // HEAD_DIM
    share = length // parts
    units = w_ffn_in.shape[1]
    chunk = min(256, units)
    chunks = parts * units // chunk

    def shift(value, k):
        return lax.ppermute(value, "heads", [(d, (d + k) % parts) for d in range(parts)])

    def slots(shard):
        return [shard] + [shift(shard, parts - k) for k in range(1, parts)]

    def swap(keep, send):
        return [keep] + [shift(send[parts - k - 1], parts - k) for k in range(1, parts)]

    def collect(keep, send):
        total = keep.astype(F32)
        for k in range(1, parts):
            total = total + shift(send[k - 1], k).astype(F32)
        return total

    self_out, cross_q, cross_out = slots(w_self_out), slots(w_cross_q), slots(w_cross_out)
    ffn_in, ffn_out = slots(w_ffn_in), slots(w_ffn_out)

    def sent(*dims, kind=BF16):
        return shape_of((parts - 1, *dims), kind)

    def own(*dims, kind=BF16):
        return shape_of(dims, kind)

    wide_heads = own(heads, length, LANES)
    self_keep, self_send, self_ctx, self_qx, self_kx, self_vx = call(
        self_forward_kernel,
        [own(share, local), sent(share, local), own(length, local), wide_heads, wide_heads, wide_heads],
        [], 40, dec_lengths, dec_input, w_self_qkv, smem=1,
    )
    self_slots = swap(self_keep, self_send)
    cross_kx, cross_vx = call(
        cross_keys_kernel, [wide_heads, wide_heads], [], 32,
        enc_lengths, enc_output, w_cross_kv, smem=1,
    )
    first_out, first_low, first_normed, first_dev, query_keep, query_send = call(
        functools.partial(first_norm_kernel, parts),
        [own(share, width, kind=F32), own(share, width), own(share, width, kind=F32),
         own(share, 1, kind=F32), own(share, local), sent(share, local)],
        [], 32, dec_input, norm_gain, norm_bias, *self_slots, *self_out, *cross_q,
    )
    cross_keep, cross_send, cross_ctx, cross_qx = call(
        functools.partial(cross_forward_kernel, parts),
        [own(share, local), sent(share, local), own(length, local), wide_heads],
        [pltpu.VMEM((length, local), BF16)], 40,
        dec_lengths, enc_lengths, cross_kx, cross_vx, *swap(query_keep, query_send), smem=2,
    )
    cross_slots = swap(cross_keep, cross_send)
    (layer_out, grad_mid, gains_high, biases_high, g_ffn_out, g_ffn_out_send, g_ffn_in,
     g_ffn_in_send, g_cross_out, g_cross_out_send, back_keep, back_send) = call(
        functools.partial(middle_kernel, parts),
        [own(share, width, kind=F32), own(share, width, kind=F32),
         own(2, width, kind=F32), own(2, width, kind=F32),
         own(units, width), sent(units, width), own(width, units), sent(width, units),
         own(local, width), sent(local, width), own(share, local), sent(share, local)],
        [pltpu.VMEM((share, width), F32), pltpu.VMEM((share, width), BF16),
         pltpu.VMEM((share, width), F32), pltpu.VMEM((share, 1), F32),
         pltpu.VMEM((share, width), F32), pltpu.VMEM((chunks, share, chunk), BF16),
         pltpu.VMEM((chunks, share, chunk), F32), pltpu.VMEM((share, width), BF16),
         pltpu.VMEM((share, width), F32)],
        56, norm_gain, norm_bias, first_out, out_grad,
        *cross_slots, *cross_out, *ffn_in, *ffn_out,
    )
    grad_slots = swap(back_keep, back_send)
    back_scratch = [
        pltpu.VMEM((length, local), BF16),
        pltpu.VMEM((heads, length, LANES), BF16),
        pltpu.VMEM((heads, HEAD_DIM, length), F32),
        pltpu.VMEM((heads, HEAD_DIM, length), BF16),
        pltpu.VMEM((local, heads * LANES), BF16),
        pltpu.VMEM((length, local), BF16),
        pltpu.VMEM((length, local), BF16),
        pltpu.VMEM((length, local), BF16),
        pltpu.VMEM((length, width), F32),
    ]
    gq_keep, gq_send, g_cross_kv, enc_keep, enc_send = call(
        functools.partial(cross_back_kernel, len(grad_slots)),
        [own(share, local), sent(share, local), own(2, width, local),
         own(share, width, kind=F32), sent(share, width)],
        back_scratch, 56, dec_lengths, enc_lengths, cross_qx, cross_kx, cross_vx, cross_ctx,
        enc_output, w_cross_kv, *grad_slots, smem=2,
    )
    enc_grad = collect(enc_keep, enc_send)
    (grad_base, gains_low, biases_low, g_cross_q, g_cross_q_send, g_self_out, g_self_out_send,
     self_back_keep, self_back_send) = call(
        functools.partial(first_back_kernel, parts),
        [own(share, width, kind=F32), own(1, width, kind=F32), own(1, width, kind=F32),
         own(width, local), sent(width, local), own(local, width), sent(local, width),
         own(share, local), sent(share, local)],
        [pltpu.VMEM((share, width), BF16)], 40,
        norm_gain, grad_mid, first_low, first_normed, first_dev,
        *swap(gq_keep, gq_send), *cross_q, *self_slots, *self_out,
    )
    g_self_qkv, in_keep, in_send = call(
        functools.partial(self_back_kernel, parts),
        [own(3, width, local), own(share, width, kind=F32), sent(share, width)],
        back_scratch, 56, dec_lengths, self_qx, self_kx, self_vx, self_ctx, dec_input,
        w_self_qkv, *swap(self_back_keep, self_back_send), smem=1,
    )
    input_grad = grad_base + collect(in_keep, in_send)

    def over_rows(value):
        return lax.psum(value.astype(BF16), "rows").astype(F32)

    return (
        layer_out,
        input_grad,
        enc_grad,
        over_rows(g_self_qkv),
        over_rows(collect(g_self_out, g_self_out_send)),
        over_rows(collect(g_cross_q, g_cross_q_send)),
        over_rows(g_cross_kv),
        over_rows(collect(g_cross_out, g_cross_out_send)),
        over_rows(collect(g_ffn_in, g_ffn_in_send)),
        over_rows(collect(g_ffn_out, g_ffn_out_send)),
        lax.psum(jnp.concatenate([gains_low, gains_high]), ("rows", "heads")),
        lax.psum(jnp.concatenate([biases_low, biases_high]), ("rows", "heads")),
    )


def solution(mesh):
    in_specs = (
        P("rows", None),
        P("rows", None),
        P("rows", None),
        P("rows", None),
        P(None, None, "heads"),
        P("heads", None),
        P(None, "heads"),
        P(None, None, "heads"),
        P("heads", None),
        P(None, "heads"),
        P("heads", None),
        P(),
        P(),
        P("rows", None),
    )
    out_specs = (
        P(("rows", "heads"), None),
        P(("rows", "heads"), None),
        P(("rows", "heads"), None),
        P(None, None, "heads"),
        P("heads", None),
        P(None, "heads"),
        P(None, None, "heads"),
        P("heads", None),
        P(None, "heads"),
        P("heads", None),
        P(),
        P(),
    )
    return jax.shard_map(body, mesh=mesh, in_specs=in_specs, out_specs=out_specs, check_vma=False)
```

```python
import functools

import jax
import jax.numpy as jnp
from jax import lax
from jax.experimental import pallas as pl
from jax.experimental.pallas import tpu as pltpu
from jax.sharding import PartitionSpec as P

HEAD_DIM = 64
LANES = 128
SPAN = 256
KEY_SPAN = 512
VMEM_BYTES = 2**26 - 2**17
NORM_EPS = 1e-05
MASKED_SCORE = -1e30
LOG2_E = 1.4426950408889634
GELU_RATE = 0.7978845608028654
GELU_CUBE = 0.044715
F32 = jnp.float32
BF16 = jnp.bfloat16
NT = (((1,), (1,)), ((), ()))
TN = (((0,), (0,)), ((), ()))
VMEM = pl.BlockSpec(memory_space=pltpu.VMEM)
SMEM = pl.BlockSpec(memory_space=pltpu.SMEM)


def dot(left, right):
    return jnp.dot(left, right, preferred_element_type=F32)


def dot_nt(left, right):
    return lax.dot_general(left, right, NT, preferred_element_type=F32)


def dot_tn(left, right):
    return lax.dot_general(left, right, TN, preferred_element_type=F32)


def shape_of(dims, kind):
    return jax.ShapeDtypeStruct(dims, kind)


def call(kernel, outs, scratch, mib, *args, smem=0, far=0, out_far=0, out_places=()):
    anyspace = pl.BlockSpec(memory_space=pl.ANY)
    return pl.pallas_call(
        kernel,
        out_shape=outs,
        in_specs=[SMEM] * smem + [VMEM] * (len(args) - smem - far) + [anyspace] * far,
        out_specs=[
            anyspace if k in out_places or k >= len(outs) - out_far else VMEM for k in range(len(outs))
        ],
        scratch_shapes=scratch,
        compiler_params=pltpu.CompilerParams(vmem_limit_bytes=VMEM_BYTES),
        cost_estimate=pl.CostEstimate(flops=2 * 10**10, bytes_accessed=2 * 10**7, transcendentals=0),
    )(*args)


def unrolled(count, body):
    for index in range(count):
        body(index, 0)


def segment_bounds(len_ref):
    starts, ends, total = [], [], jnp.int32(0)
    for k in range(len_ref.shape[1]):
        starts.append(total)
        total = total + len_ref[0, k]
        ends.append(total)
    return starts, ends


def bound_lanes(starts, ends):
    lane = lax.broadcasted_iota(jnp.int32, (1, LANES), 1)
    first = jnp.full((1, LANES), 1 << 30, jnp.int32)
    last = jnp.zeros((1, LANES), jnp.int32)
    for k, (start, end) in enumerate(zip(starts, ends)):
        first = jnp.where(lane == HEAD_DIM + k, start, first)
        last = jnp.where(lane == HEAD_DIM + k, end, last)
    return first, last


def lanes_of(rows):
    return lax.broadcasted_iota(jnp.int32, (rows, LANES), 1)


def membership(first_row, rows, bounds):
    place = lax.broadcasted_iota(jnp.int32, (rows, LANES), 0) + first_row
    return (place >= bounds[0]) & (place < bounds[1])


def query_extra(first_row, rows, bounds):
    return jnp.where(membership(first_row, rows, bounds), F32(MASKED_SCORE), F32(0.0))


def key_extra(first_row, rows, bounds, segs):
    lane = lanes_of(rows)
    used = (lane >= HEAD_DIM) & (lane < HEAD_DIM + segs + 3)
    return jnp.where(used & ~membership(first_row, rows, bounds), F32(1.0), F32(0.0))


def value_extra(rows):
    return jnp.full((rows, LANES), 1.0, F32)


def head_slab(wide, head):
    if wide.shape[1] < LANES:
        return jnp.concatenate([wide, jnp.zeros_like(wide)], axis=1)
    first = head // 2 * LANES
    slab = wide[:, first : first + LANES]
    if head % 2:
        slab = pltpu.roll(slab, HEAD_DIM, 1)
    return slab


def put_heads(dest, where, wide, extra):
    low_lanes = lanes_of(wide.shape[0]) < HEAD_DIM
    for head in range(dest.shape[0]):
        dest[head, where, :] = jnp.where(low_lanes, head_slab(wide, head), extra).astype(dest.dtype)


def join_heads(dest, where, slabs):
    if len(slabs) == 1:
        dest[where, :] = slabs[0][:, :HEAD_DIM].astype(dest.dtype)
        return
    low_lanes = lanes_of(slabs[0].shape[0]) < HEAD_DIM
    for pair in range(len(slabs) // 2):
        both = jnp.where(low_lanes, slabs[2 * pair], pltpu.roll(slabs[2 * pair + 1], HEAD_DIM, 1))
        dest[where, pair * LANES : (pair + 1) * LANES] = both.astype(dest.dtype)


def span_for(block, length, from_starts, to_starts, to_ends):
    first_row = block * SPAN
    last_row = first_row + SPAN - 1
    low, high = jnp.int32(0), jnp.int32(0)
    for start, to_start, to_end in zip(from_starts, to_starts, to_ends):
        low = jnp.where(start <= first_row, to_start, low)
        high = jnp.where(start <= last_row, to_end, high)
    low = (low >> 7) << 7
    pieces = (high - low + SPAN - 1) >> 8
    return jnp.minimum(low, length - pieces * SPAN), pieces


def each_span(length, starts_from, starts_to, ends_to, body, after=None):
    def step(block, carry):
        start, pieces = span_for(block, length, starts_from, starts_to, ends_to)
        start = pl.multiple_of(start, LANES)
        rows = pl.ds(pl.multiple_of(block * SPAN, SPAN), SPAN)
        for count in range(1, length // SPAN + 1):

            @pl.when(pieces == count)
            def _():
                body(rows, pl.ds(start, count * SPAN))

        if after is not None:
            after(block, rows)
        return carry

    lax.fori_loop(0, length // SPAN, step, 0)


def merge_head(dest, rows, head, slab):
    if dest.shape[1] < LANES:
        dest[rows, :] = slab[:, :HEAD_DIM].astype(dest.dtype)
        return
    odd = (head & 1) == 1
    low_lanes = lanes_of(slab.shape[0]) < HEAD_DIM
    cols = pl.ds(pl.multiple_of((head >> 1) * LANES, LANES), LANES)
    old = dest[rows, cols].astype(F32)
    first = jnp.where(odd, old, slab)
    second = jnp.where(odd, pltpu.roll(slab, HEAD_DIM, 1), slab)
    dest[rows, cols] = jnp.where(low_lanes, first, second).astype(dest.dtype)


def attend_body(qx, kx, vx, ctx, segs, rows, keys):
    scale = LOG2_E * HEAD_DIM**-0.5
    base = HEAD_DIM + segs
    lane = lanes_of(SPAN)
    slabs = []
    for head in range(qx.shape[0]):
        query = qx[head, rows, :]
        scores = dot_nt(query, kx[head, keys, :])
        peak = jnp.max(scores, axis=1, keepdims=True)
        raised = jnp.exp2((scores - peak) * scale).astype(BF16)
        mixed = dot(raised, vx[head, keys, :])
        total = jnp.where(lane < HEAD_DIM, 1.0, mixed)
        slabs.append(mixed * pltpu.roll(1.0 / total, HEAD_DIM, 1))
        level = -(peak + jnp.log(total) * (HEAD_DIM**0.5))
        high = level.astype(BF16).astype(F32)
        middle = (level - high).astype(BF16).astype(F32)
        low = level - high - middle
        wide = query.astype(F32)
        wide = jnp.where(lane == base, high, wide)
        wide = jnp.where(lane == base + 1, middle, wide)
        wide = jnp.where(lane == base + 2, low, wide)
        qx[head, rows, :] = wide.astype(BF16)
    join_heads(ctx, rows, slabs)


def split_out(source, keep, send, share):
    me = lax.axis_index("heads")
    parts = send.shape[0] + 1
    for k in range(parts):
        owner = lax.rem(me + k, parts)
        rows = pl.ds(pl.multiple_of(owner * share, share), share)
        if k == 0:
            keep[...] = source[rows, :].astype(keep.dtype)
        else:
            send[k - 1] = source[rows, :].astype(send.dtype)


def self_forward_kernel(len_ref, x_ref, w_ref, keep, send, ctx, qx, kx, vx):
    length = x_ref.shape[0]
    segs = len_ref.shape[1]
    starts, ends = segment_bounds(len_ref)
    bounds = bound_lanes(starts, ends)

    def project(block, carry):
        first = pl.multiple_of(block * SPAN, SPAN)
        rows = pl.ds(first, SPAN)
        tokens = x_ref[rows, :]
        put_heads(qx, rows, dot(tokens, w_ref[0]), query_extra(first, SPAN, bounds))
        put_heads(kx, rows, dot(tokens, w_ref[1]), key_extra(first, SPAN, bounds, segs))
        put_heads(vx, rows, dot(tokens, w_ref[2]), value_extra(SPAN))
        return carry

    lax.fori_loop(0, length // SPAN, project, 0)
    each_span(
        length, starts, starts, ends, functools.partial(attend_body, qx, kx, vx, ctx, segs)
    )
    split_out(ctx, keep, send, keep.shape[0])


def cross_keys_kernel(len_ref, x_ref, w_ref, kx, vx):
    length = x_ref.shape[0]
    bounds = bound_lanes(*segment_bounds(len_ref))
    segs = len_ref.shape[1]

    def project(block, carry):
        first = pl.multiple_of(block * SPAN, SPAN)
        rows = pl.ds(first, SPAN)
        tokens = x_ref[rows, :]
        put_heads(kx, rows, dot(tokens, w_ref[0]), key_extra(first, SPAN, bounds, segs))
        put_heads(vx, rows, dot(tokens, w_ref[1]), value_extra(SPAN))
        return carry

    lax.fori_loop(0, length // SPAN, project, 0)


def gather_rows(dest, own, others):
    me = lax.axis_index("heads")
    parts = len(others) + 1
    share = own.shape[0]
    for k, source in enumerate([own, *others]):
        owner = lax.rem(me + k, parts)
        dest[pl.ds(pl.multiple_of(owner * share, share), share), :] = source[...]


def cross_forward_kernel(parts, dec_ref, enc_ref, kx, vx, *refs):
    pieces, (keep, send, ctx, qx, flat) = refs[:parts], refs[parts:]
    length = ctx.shape[0]
    segs = dec_ref.shape[1]
    dec_starts, dec_ends = segment_bounds(dec_ref)
    enc_starts, enc_ends = segment_bounds(enc_ref)
    bounds = bound_lanes(dec_starts, dec_ends)
    gather_rows(flat, pieces[0], pieces[1:])

    def widen(block, carry):
        first = pl.multiple_of(block * SPAN, SPAN)
        rows = pl.ds(first, SPAN)
        put_heads(qx, rows, flat[rows, :].astype(F32), query_extra(first, SPAN, bounds))
        return carry

    lax.fori_loop(0, length // SPAN, widen, 0)
    each_span(
        length, dec_starts, enc_starts, enc_ends,
        functools.partial(attend_body, qx, kx, vx, ctx, segs),
    )
    split_out(ctx, keep, send, keep.shape[0])


def row_store(source, dest, rows, sem, block, heads):
    where = (slice(None), rows, slice(None)) if heads else (rows, slice(None))
    return pltpu.make_async_copy(source.at[where], dest.at[where], sem.at[block])


def self_forward_fast(len_ref, x_ref, w_ref, ctx_out, qx_out, kx_out, vx_out, ctx, qx, kx, vx, sems, far):
    length = x_ref.shape[0]
    segs = len_ref.shape[1]
    starts, ends = segment_bounds(len_ref)
    bounds = bound_lanes(starts, ends)

    def project(block, carry):
        first = pl.multiple_of(block * SPAN, SPAN)
        rows = pl.ds(first, SPAN)
        tokens = x_ref[rows, :]
        put_heads(qx, rows, dot(tokens, w_ref[0]), query_extra(first, SPAN, bounds))
        put_heads(kx, rows, dot(tokens, w_ref[1]), key_extra(first, SPAN, bounds, segs))
        put_heads(vx, rows, dot(tokens, w_ref[2]), value_extra(SPAN))
        return carry

    unrolled(length // SPAN, project)
    whole = [pltpu.make_async_copy(kx, kx_out, far.at[0]), pltpu.make_async_copy(vx, vx_out, far.at[1])]
    for copy in whole:
        copy.start()

    def after(block, rows):
        row_store(ctx, ctx_out, rows, sems.at[0], block, False).start()
        row_store(qx, qx_out, rows, sems.at[1], block, True).start()

    each_span(
        length, starts, starts, ends, functools.partial(attend_body, qx, kx, vx, ctx, segs), after
    )
    for block in range(length // SPAN):
        rows = pl.ds(block * SPAN, SPAN)
        row_store(ctx, ctx_out, rows, sems.at[0], block, False).wait()
        row_store(qx, qx_out, rows, sems.at[1], block, True).wait()
    for copy in whole:
        copy.wait()


def cross_forward_fast(dec_ref, enc_ref, flat, kx_in, vx_in, ctx_out, qx_out, ctx, qx, kx, vx, sems, far):
    length = ctx.shape[0]
    segs = dec_ref.shape[1]
    loads = [pltpu.make_async_copy(kx_in, kx, far.at[0]), pltpu.make_async_copy(vx_in, vx, far.at[1])]
    for load in loads:
        load.start()
    dec_starts, dec_ends = segment_bounds(dec_ref)
    enc_starts, enc_ends = segment_bounds(enc_ref)
    bounds = bound_lanes(dec_starts, dec_ends)

    def widen(block, carry):
        first = pl.multiple_of(block * SPAN, SPAN)
        rows = pl.ds(first, SPAN)
        put_heads(qx, rows, flat[rows, :].astype(F32), query_extra(first, SPAN, bounds))
        return carry

    unrolled(length // SPAN, widen)
    for load in loads:
        load.wait()

    def after(block, rows):
        row_store(ctx, ctx_out, rows, sems.at[0], block, False).start()
        row_store(qx, qx_out, rows, sems.at[1], block, True).start()

    each_span(
        length, dec_starts, enc_starts, enc_ends,
        functools.partial(attend_body, qx, kx, vx, ctx, segs), after,
    )
    for block in range(length // SPAN):
        rows = pl.ds(block * SPAN, SPAN)
        row_store(ctx, ctx_out, rows, sems.at[0], block, False).wait()
        row_store(qx, qx_out, rows, sems.at[1], block, True).wait()


def core_half(core, share):
    return pl.ds(pl.multiple_of(core * share, share), share)


def entry_remote_kernel(enc_ref, gain, bias, *refs):
    rest = list(refs)
    take = lambda number: [rest.pop(0) for _ in range(number)]
    x_in, enc_in, w_kv_in, ctx_in, wo_in, wq_in, far_cross, far_in, far_out = take(9)
    first_out, first_low, normed_out, dev_out, q_out, kx_out, vx_out, ctx_far, wo_far, wq_far = take(10)
    away_cross, away_in, away_out = take(3)
    x, enc, w_kv, ctx0, ctx1, wo0, wo1, wq0, wq1 = take(9)
    first, low, normed, q_own, q_gone, kx, vx = take(7)
    load_sem, store_sem, core_send, core_land = rest
    share, width = first.shape
    length = enc.shape[0]
    block = 256
    segs = enc_ref.shape[1]
    core = lax.axis_index("heads")
    other = {"rows": lax.axis_index("rows"), "heads": 1 - core}
    mine, theirs = core_half(core, share), core_half(1 - core, share)

    def across(number, source, dest):
        return pltpu.make_async_remote_copy(
            src_ref=source, dst_ref=dest, send_sem=core_send.at[number], recv_sem=core_land.at[number],
            device_id=other, device_id_type=pl.DeviceIdType.MESH,
        )

    moves = [(enc_in, enc), (w_kv_in, w_kv), (x_in.at[mine, :], x), (ctx_in.at[mine, :], ctx0), (wo_in, wo0), (wq_in, wq0)]
    loads = [pltpu.make_async_copy(a, b, load_sem.at[k]) for k, (a, b) in enumerate(moves)]
    for load in loads:
        load.start()
    barrier = pltpu.get_barrier_semaphore()
    pl.semaphore_signal(barrier, inc=1, device_id=other, device_id_type=pl.DeviceIdType.MESH)
    pl.semaphore_wait(barrier, 1)
    exchange = [
        across(0, ctx_in.at[theirs, :], ctx1), across(1, wo_in, wo1), across(2, wq_in, wq1),
        across(3, far_cross, away_cross), across(4, far_in, away_in), across(5, far_out, away_out),
    ]
    for copy in exchange:
        copy.start()
    bounds = bound_lanes(*segment_bounds(enc_ref))
    for load in loads[:2]:
        load.wait()

    def project(index, carry):
        top = pl.multiple_of(index * SPAN, SPAN)
        rows = pl.ds(top, SPAN)
        tokens = enc[rows, :]
        put_heads(kx, rows, dot(tokens, w_kv[0]), key_extra(top, SPAN, bounds, segs))
        put_heads(vx, rows, dot(tokens, w_kv[1]), value_extra(SPAN))
        return carry

    unrolled(length // SPAN, project)
    stores = []

    def store(source, dest):
        stores.append(pltpu.make_async_copy(source, dest, store_sem.at[len(stores)]))
        stores[-1].start()

    store(kx, kx_out)
    store(vx, vx_out)
    for load in loads[2:]:
        load.wait()
    for copy in exchange[:3]:
        copy.wait()
    store(ctx1, ctx_far)
    store(wo1, wo_far)
    store(wq1, wq_far)
    copies = []
    for index in range(share // block):
        rows = pl.ds(index * block, block)
        total = x[rows, :].astype(F32) + dot(ctx0[rows, :], wo0[...]) + dot(ctx1[rows, :], wo1[...])
        result, spread, inverse_dev = norm_forward(total, gain[0:1, :], bias[0:1, :])
        low_part = result.astype(BF16)
        first[rows, :] = result
        low[rows, :] = low_part
        normed[rows, :] = spread
        dev_out[rows, :] = inverse_dev
        q_gone[rows, :] = dot(low_part, wq1[...]).astype(BF16)
        here = own_rows(share, index * block, block)
        copies.append(across(6 + index, q_gone.at[rows, :], q_out.at[here, :]))
        copies[-1].start()
        q_own[rows, :] = dot(low_part, wq0[...]).astype(BF16)
        store(q_own.at[rows, :], q_out.at[here, :])
        store(first.at[rows, :], first_out.at[rows, :])
        store(low.at[rows, :], first_low.at[rows, :])
        store(normed.at[rows, :], normed_out.at[rows, :])
    for copy in exchange[3:] + copies:
        copy.wait()
    for copy in stores:
        copy.wait()


def run_entry(enc_lengths, gain, bias, args):
    length, width = args[0].shape
    local = args[4].shape[0]
    share, heads, units = length // 2, local // HEAD_DIM, args[7].shape[1]
    vm = lambda kind, *dims: pltpu.VMEM(dims, kind)
    wide_heads = (heads, length, LANES)
    blocks = share // 256
    anyspace = pl.BlockSpec(memory_space=pl.ANY)
    return pl.pallas_call(
        entry_remote_kernel,
        out_shape=[
            shape_of((share, width), F32), shape_of((share, width), BF16), shape_of((share, width), F32),
            shape_of((share, 1), F32), shape_of((length, local), BF16),
            shape_of(wide_heads, BF16), shape_of(wide_heads, BF16),
            shape_of((share, local), BF16), shape_of((local, width), BF16), shape_of((width, local), BF16),
            shape_of((local, width), BF16), shape_of((width, units), BF16), shape_of((units, width), BF16),
        ],
        in_specs=[SMEM, VMEM, VMEM] + [anyspace] * len(args),
        out_specs=[anyspace] * 3 + [VMEM] + [anyspace] * 9,
        scratch_shapes=[
            vm(BF16, share, width), vm(BF16, length, width), vm(BF16, 2, width, local),
            vm(BF16, share, local), vm(BF16, share, local), vm(BF16, local, width), vm(BF16, local, width),
            vm(BF16, width, local), vm(BF16, width, local),
            vm(F32, share, width), vm(BF16, share, width), vm(F32, share, width),
            vm(BF16, share, local), vm(BF16, share, local), vm(BF16, *wide_heads), vm(BF16, *wide_heads),
        ] + [pltpu.SemaphoreType.DMA((n,)) for n in (6, 5 + 4 * blocks, 6 + blocks, 6 + blocks)],
        compiler_params=pltpu.CompilerParams(
            vmem_limit_bytes=VMEM_BYTES, collective_id=2, has_side_effects=True
        ),
    )(enc_lengths, gain, bias, *args)


def attend_back_body(qx, kx, vx, gx, dq, kt, dk, dv, rows, queries):
    heads = qx.shape[0]
    group = 2 if heads % 2 == 0 else 1

    def unit(index, carry):
        for k in range(group):
            back_unit(qx, kx, vx, gx, dq, kt, dk, dv, group * index + k, rows, queries)
        return carry

    lax.fori_loop(0, heads // group, unit, 0)


def head_sums(width, heads):
    row = lax.broadcasted_iota(jnp.int32, (width, heads * LANES), 0)
    col = lax.broadcasted_iota(jnp.int32, (width, heads * LANES), 1)
    lane = col & (LANES - 1)
    hit = ((row >> 6) == (col >> 7)) & (lane >= HEAD_DIM) & (lane < HEAD_DIM + 2)
    return jnp.where(hit, F32(1.0), F32(0.0)).astype(BF16)


def prepare_back(grad, ctx, kx, gx, dq, kt, sums):
    heads = gx.shape[0]
    lane = lanes_of(SPAN)

    def widen(block, carry):
        rows = pl.ds(pl.multiple_of(block * SPAN, SPAN), SPAN)
        wide = grad[rows, :].astype(F32)
        product = wide * ctx[rows, :].astype(F32)
        high = product.astype(BF16)
        low = (product - high.astype(F32)).astype(BF16)
        totals = dot(high, sums[...]) + dot(low, sums[...])
        for head in range(heads):
            level = -totals[:, head * LANES : (head + 1) * LANES]
            rounded = level.astype(BF16).astype(F32)
            extra = jnp.where(lane == HEAD_DIM + 1, level - rounded, rounded)
            full = jnp.where(lane < HEAD_DIM, head_slab(wide, head), extra)
            gx[head, rows, :] = full.astype(BF16)
            dq[head, :, rows] = jnp.zeros((HEAD_DIM, SPAN), F32)
            kt[head, :, rows] = kx[head, rows, :].astype(F32).T[:HEAD_DIM].astype(BF16)
        return carry

    unrolled(grad.shape[0] // SPAN, widen)


def turn_queries(dq, sq, pairs):
    length = sq.shape[0]

    def finish(block, carry):
        rows = pl.ds(pl.multiple_of(block * SPAN, SPAN), SPAN)
        for pair in pairs:
            if dq.shape[0] == 1:
                sq[rows, :] = (dq[0, :, rows].T * (HEAD_DIM**-0.5)).astype(BF16)
            else:
                both = jnp.concatenate([dq[2 * pair, :, rows], dq[2 * pair + 1, :, rows]], axis=0)
                sq[rows, pair * LANES : (pair + 1) * LANES] = (both.T * (HEAD_DIM**-0.5)).astype(BF16)
        return carry

    unrolled(length // SPAN, finish)


def attend_back(key_starts, key_ends, query_starts, query_ends, qx, kx, vx, ctx, grad, gx, dq, kt, sums, sq, sk, sv):
    length = ctx.shape[0]
    heads = qx.shape[0]
    sums[...] = head_sums(ctx.shape[1], heads)
    prepare_back(grad, ctx, kx, gx, dq, kt, sums)
    each_span(
        length, key_starts, query_starts, query_ends,
        functools.partial(attend_back_body, qx, kx, vx, gx, dq, kt, sk, sv),
    )
    turn_queries(dq, sq, range(max(1, heads // 2)))


def norm_forward(summed, gain, bias):
    center = summed - jnp.mean(summed, axis=1, keepdims=True)
    inverse_dev = lax.rsqrt(jnp.mean(center * center, axis=1, keepdims=True) + NORM_EPS)
    normed = center * inverse_dev
    return normed * gain + bias, normed, inverse_dev


def norm_back(grad, normed, inverse_dev, gain):
    scaled = grad * gain
    back = inverse_dev * (
        scaled
        - jnp.mean(scaled, axis=1, keepdims=True)
        - normed * jnp.mean(scaled * normed, axis=1, keepdims=True)
    )
    gain_grad = jnp.sum(grad * normed, axis=0, keepdims=True)
    return back, gain_grad, jnp.sum(grad, axis=0, keepdims=True)


def share_block(share):
    return 256 if share % 256 == 0 else share


def own_rows(share, first, rows):
    start = lax.axis_index("heads") * share + first
    return pl.ds(pl.multiple_of(start, 64), rows)


def first_norm_kernel(parts, x_ref, gain, bias, *refs):
    ctx, w_out, w_query = refs[:parts], refs[parts : 2 * parts], refs[2 * parts : 3 * parts]
    first_out, first_low, normed_out, dev_out, keep, send = refs[3 * parts :]
    share = first_out.shape[0]
    block = share_block(share)

    def step(index, carry):
        first = pl.multiple_of(index * block, block)
        rows = pl.ds(first, block)
        total = x_ref[own_rows(share, first, block), :].astype(F32)
        for k in range(parts):
            total = total + dot(ctx[k][rows, :], w_out[k][...])
        result, normed, inverse_dev = norm_forward(total, gain[0:1, :], bias[0:1, :])
        low = result.astype(BF16)
        first_out[rows, :] = result
        first_low[rows, :] = low
        normed_out[rows, :] = normed
        dev_out[rows, :] = inverse_dev
        for k in range(parts):
            value = dot(low, w_query[k][...]).astype(BF16)
            if k == 0:
                keep[rows, :] = value
            else:
                send[k - 1, rows, :] = value
        return carry

    lax.fori_loop(0, share // block, step, 0)


def middle_kernel(parts, gain, bias, first_out, out_grad, *refs):
    groups = [refs[g * parts : (g + 1) * parts] for g in range(4)]
    ctx, w_cross, w_in, w_out = groups
    (layer_out, grad_mid, gains, biases, g_out_keep, g_out_send, g_in_keep, g_in_send,
     g_cross_keep, g_cross_send, back_keep, back_send,
     second, second_low, normed2, dev2, total, hidden, slope, top_low, back_sum) = refs[4 * parts :]
    share = first_out.shape[0]
    block = share_block(share)
    units = w_in[0].shape[1]
    chunk = min(256, units)

    def enter(index, carry):
        rows = pl.ds(pl.multiple_of(index * block, block), block)
        summed = first_out[rows, :]
        for k in range(parts):
            summed = summed + dot(ctx[k][rows, :], w_cross[k][...])
        result, normed, inverse_dev = norm_forward(summed, gain[1:2, :], bias[1:2, :])
        second[rows, :] = result
        second_low[rows, :] = result.astype(BF16)
        normed2[rows, :] = normed
        dev2[rows, :] = inverse_dev
        return carry

    lax.fori_loop(0, share // block, enter, 0)
    total[...] = second[...]
    for k in range(parts):

        def expand(index, carry):
            cols = pl.ds(pl.multiple_of(index * chunk, chunk), chunk)
            spot = k * (units // chunk) + index
            pre = dot(second_low[...], w_in[k][:, cols])
            square = pre * pre
            bent = jnp.tanh(pre * (GELU_RATE + (GELU_RATE * GELU_CUBE) * square))
            half = 0.5 + 0.5 * bent
            act = (pre * half).astype(BF16)
            hidden[spot] = act
            bend = (0.5 - 0.5 * bent * bent) * (
                GELU_RATE + (3.0 * GELU_RATE * GELU_CUBE) * square
            )
            slope[spot] = half + pre * bend
            total[...] += dot(act, w_out[k][cols, :])
            return carry

        lax.fori_loop(0, units // chunk, expand, 0)

    gains[...] = jnp.zeros_like(gains)
    biases[...] = jnp.zeros_like(biases)

    def turn(index, carry):
        first = pl.multiple_of(index * block, block)
        rows = pl.ds(first, block)
        result, normed, inverse_dev = norm_forward(total[rows, :], gain[2:3, :], bias[2:3, :])
        layer_out[rows, :] = result
        grad = out_grad[own_rows(share, first, block), :].astype(F32)
        back, gain_grad, bias_grad = norm_back(grad, normed, inverse_dev, gain[2:3, :])
        gains[1:2, :] += gain_grad
        biases[1:2, :] += bias_grad
        back_sum[rows, :] = back
        top_low[rows, :] = back.astype(BF16)
        return carry

    lax.fori_loop(0, share // block, turn, 0)
    for k in range(parts):

        def contract(index, carry):
            cols = pl.ds(pl.multiple_of(index * chunk, chunk), chunk)
            spot = k * (units // chunk) + index
            weight_out = dot_tn(hidden[spot], top_low[...]).astype(BF16)
            pre = (dot_nt(top_low[...], w_out[k][cols, :]) * slope[spot]).astype(BF16)
            weight_in = dot_tn(second_low[...], pre).astype(BF16)
            if k == 0:
                g_out_keep[cols, :] = weight_out
                g_in_keep[:, cols] = weight_in
            else:
                g_out_send[k - 1, cols, :] = weight_out
                g_in_send[k - 1, :, cols] = weight_in
            back_sum[...] += dot_nt(pre, w_in[k][:, cols])
            return carry

        lax.fori_loop(0, units // chunk, contract, 0)

    def leave(index, carry):
        rows = pl.ds(pl.multiple_of(index * block, block), block)
        back, gain_grad, bias_grad = norm_back(
            back_sum[rows, :], normed2[rows, :], dev2[rows, :], gain[1:2, :]
        )
        gains[0:1, :] += gain_grad
        biases[0:1, :] += bias_grad
        grad_mid[rows, :] = back
        low = back.astype(BF16)
        top_low[rows, :] = low
        for k in range(parts):
            value = dot_nt(low, w_cross[k][...]).astype(BF16)
            if k == 0:
                back_keep[rows, :] = value
            else:
                back_send[k - 1, rows, :] = value
        return carry

    lax.fori_loop(0, share // block, leave, 0)
    for k in range(parts):
        value = dot_tn(ctx[k][...], top_low[...]).astype(BF16)
        if k == 0:
            g_cross_keep[...] = value
        else:
            g_cross_send[k - 1] = value


def middle_remote_kernel(parts, gain, bias, *refs):
    rest = list(refs)
    take = lambda number: [rest.pop(0) for _ in range(number)]
    first_in, top_in, ctx_in, wc0_in, wc1_in, wi0_in, wi1_in, wo0_in, wo1_in = take(9)
    layer_out, mid_out, small_out, sum_out, sum_in, sum_cross, cgrad_out = take(7)
    away_out = take(3)
    (first, top, ctx0, ctx1, wc0, wc1, wi0, wi1, wo0, wo1) = loaded = take(10)
    (second, second_low, normed2, dev2, total, hidden, slope, top_low, back_sum, layer, mid,
     own_out, land_out, gone_out, own_in, land_in, gone_in, own_cross, land_cross, gone_cross, own_back, gone_back) = take(22)
    load_sem, store_sem, part_sem, core_send, core_land = rest
    share, width = first.shape
    units = wi0.shape[1]
    block = 256
    chunk = hidden.shape[2]
    chunks = units // chunk
    core = lax.axis_index("heads")
    other = {"rows": lax.axis_index("rows"), "heads": 1 - core}
    mine = pl.ds(pl.multiple_of(core * share, share), share)
    w_in, w_out, w_cross, ctx = (wi0, wi1), (wo0, wo1), (wc0, wc1), (ctx0, ctx1)
    own_sends = {}

    def across(number, source, dest):
        copy = pltpu.make_async_remote_copy(
            src_ref=source, dst_ref=dest, send_sem=core_send.at[number], recv_sem=core_land.at[number],
            device_id=other, device_id_type=pl.DeviceIdType.MESH,
        )
        own_sends[number] = copy
        return copy

    sources = [first_in, top_in.at[mine, :], ctx_in.at[mine, :], None, wc0_in, wc1_in, wi0_in, wi1_in, wo0_in, wo1_in]
    loads = [
        None if source is None else pltpu.make_async_copy(source, dest, load_sem.at[k])
        for k, (source, dest) in enumerate(zip(sources, loaded))
    ]
    for k in (0, 2, 4, 5, 6, 7, 8, 9, 1):
        loads[k].start()
    barrier = pltpu.get_barrier_semaphore()
    pl.semaphore_signal(barrier, inc=1, device_id=other, device_id_type=pl.DeviceIdType.MESH)
    pl.semaphore_wait(barrier, 1)
    across(0, ctx_in.at[core_half(1 - core, share), :], ctx1).start()
    for k in (0, 2, 4, 5):
        loads[k].wait()
    own_sends[0].wait()

    def enter(index, carry):
        rows = pl.ds(pl.multiple_of(index * block, block), block)
        summed = first[rows, :] + dot(ctx0[rows, :], wc0[...]) + dot(ctx1[rows, :], wc1[...])
        result, normed, inverse_dev = norm_forward(summed, gain[1:2, :], bias[1:2, :])
        second[rows, :] = result
        second_low[rows, :] = result.astype(BF16)
        normed2[rows, :] = normed
        dev2[rows, :] = inverse_dev
        return carry

    unrolled(share // block, enter)
    total[...] = second[...]
    for k in range(2):
        loads[6 + k].wait()
        loads[8 + k].wait()

        def expand(index, carry):
            cols = pl.ds(pl.multiple_of(index * chunk, chunk), chunk)
            spot = k * chunks + index
            pre = dot(second_low[...], w_in[k][:, cols])
            square = pre * pre
            bent = jnp.tanh(pre * (GELU_RATE + (GELU_RATE * GELU_CUBE) * square))
            half = 0.5 + 0.5 * bent
            act = (pre * half).astype(BF16)
            hidden[spot] = act
            bend = (0.5 - 0.5 * bent * bent) * (
                GELU_RATE + (3.0 * GELU_RATE * GELU_CUBE) * square
            )
            slope[spot] = half + pre * bend
            total[...] += dot(act, w_out[k][cols, :])
            return carry

        unrolled(chunks, expand)
    loads[1].wait()
    small_out[...] = jnp.zeros_like(small_out)

    def turn(index, carry):
        rows = pl.ds(pl.multiple_of(index * block, block), block)
        result, normed, inverse_dev = norm_forward(total[rows, :], gain[2:3, :], bias[2:3, :])
        layer[rows, :] = result
        grad = top[rows, :].astype(F32)
        back, gain_grad, bias_grad = norm_back(grad, normed, inverse_dev, gain[2:3, :])
        small_out[2:3, :] += gain_grad
        small_out[5:6, :] += bias_grad
        back_sum[rows, :] = back
        top_low[rows, :] = back.astype(BF16)
        return carry

    unrolled(share // block, turn)
    stores = [pltpu.make_async_copy(layer, layer_out, store_sem.at[0])]
    stores[0].start()
    for k in (1, 0):
        weight_out, weight_in = (own_out, own_in) if k == 0 else (gone_out, gone_in)

        def contract(index, carry):
            cols = pl.ds(pl.multiple_of(index * chunk, chunk), chunk)
            spot = k * chunks + index
            weight_out[cols, :] = dot_tn(hidden[spot], top_low[...]).astype(BF16)
            pre = (dot_nt(top_low[...], w_out[k][cols, :]) * slope[spot]).astype(BF16)
            weight_in[:, cols] = dot_tn(second_low[...], pre).astype(BF16)
            back_sum[...] += dot_nt(pre, w_in[k][:, cols])
            return carry

        unrolled(chunks, contract)
        if k == 1:
            across(1, gone_out, land_out).start()
            across(2, gone_in, land_in).start()
    count = share // block
    for index in range(count):
        rows = pl.ds(index * block, block)
        back, gain_grad, bias_grad = norm_back(
            back_sum[rows, :], normed2[rows, :], dev2[rows, :], gain[1:2, :]
        )
        small_out[1:2, :] += gain_grad
        small_out[4:5, :] += bias_grad
        mid[rows, :] = back
        low = back.astype(BF16)
        top_low[rows, :] = low
        gone_back[rows, :] = dot_nt(low, wc1[...]).astype(BF16)
        across(
            4 + index, gone_back.at[rows, :], cgrad_out.at[own_rows(share, index * block, block), :]
        ).start()
        own_back[rows, :] = dot_nt(low, wc0[...]).astype(BF16)
    stores.append(pltpu.make_async_copy(mid, mid_out, store_sem.at[1]))
    stores.append(pltpu.make_async_copy(own_back, cgrad_out.at[mine, :], store_sem.at[2]))
    for store in stores[1:]:
        store.start()
    gone_cross[...] = dot_tn(ctx1[...], top_low[...]).astype(BF16)
    across(3, gone_cross, land_cross).start()
    own_sends[1].wait()
    add_into(own_out, land_out)
    stores.append(pltpu.make_async_copy(own_out, sum_out, store_sem.at[3]))
    stores[-1].start()
    own_sends[2].wait()
    add_into(own_in, land_in)
    stores.append(pltpu.make_async_copy(own_in, sum_in, store_sem.at[4]))
    stores[-1].start()
    for number, (part, bit, spot) in enumerate(parts):
        for source, dest in away_windows(part, bit, spot, (own_out, own_in)[part.out], away_out[bit]):
            stores.append(pltpu.make_async_copy(source, dest, part_sem.at[len(stores) - 5]))
            stores[-1].start()
    own_cross[...] = dot_tn(ctx0[...], top_low[...]).astype(BF16)
    own_sends[3].wait()
    add_into(own_cross, land_cross)
    stores.append(pltpu.make_async_copy(own_cross, sum_cross, store_sem.at[5]))
    stores[-1].start()
    for index in range(count):
        own_sends[4 + index].wait()
    for store in stores:
        store.wait()


def away_windows(part, bit, spot, source, dest):
    half = part.rows // 2
    side = lax.shift_right_logical(lax.axis_index("rows"), bit) & 1
    first = part.row + (1 - side) * half
    pairs = []
    for piece in range(half // 128):
        rows = pl.ds(pl.multiple_of(first + piece * 128, 128), 128)
        place = pl.ds(spot * 128, 128)
        cols = pl.ds(piece * part.cols, part.cols)
        pairs.append((source.at[rows, pl.ds(part.col, part.cols)], dest.at[place, cols]))
    return pairs


def first_steps(parts):
    filled = [0, 0, 0]
    found = []
    for part in parts:
        if part.out < 2:
            bit = part.order[0]
            found.append((part, bit, filled[bit]))
            filled[bit] += 1
    return found, [128 * max(1, n) for n in filled]


def run_middle(parts, gain, bias, args, units):
    share, width = args[0].shape
    local = args[2].shape[1]
    found, heights = first_steps(parts)
    chunk = 1024 if units % 1024 == 0 else 512
    vm = lambda kind, *dims: pltpu.VMEM(dims, kind)
    token, token_low = vm(F32, share, width), vm(BF16, share, width)
    scratch = [
        token, token_low, vm(BF16, share, local), vm(BF16, share, local),
        vm(BF16, local, width), vm(BF16, local, width), vm(BF16, width, units), vm(BF16, width, units),
        vm(BF16, units, width), vm(BF16, units, width),
        token, token_low, token, vm(F32, share, 1), token,
        vm(BF16, 2 * units // chunk, share, chunk), vm(F32, 2 * units // chunk, share, chunk),
        token_low, token, token, token,
        *[vm(BF16, units, width)] * 3, *[vm(BF16, width, units)] * 3, *[vm(BF16, local, width)] * 3,
        vm(BF16, share, local), vm(BF16, share, local),
    ]
    sems = [10, 6, 2 * len(found), 4 + share // 256, 4 + share // 256]
    anyspace = pl.BlockSpec(memory_space=pl.ANY)
    return pl.pallas_call(
        functools.partial(middle_remote_kernel, found),
        out_shape=[
            shape_of((share, width), F32), shape_of((share, width), F32), shape_of((8, width), F32),
            shape_of((units, width), BF16), shape_of((width, units), BF16), shape_of((local, width), BF16),
            shape_of((2 * share, local), BF16), *[shape_of((h, width), BF16) for h in heights],
        ],
        in_specs=[VMEM] * 2 + [anyspace] * len(args),
        out_specs=[anyspace] * 2 + [VMEM] + [anyspace] * 7,
        scratch_shapes=scratch + [pltpu.SemaphoreType.DMA((n,)) for n in sems],
        compiler_params=pltpu.CompilerParams(
            vmem_limit_bytes=VMEM_BYTES, collective_id=1, has_side_effects=True
        ),
    )(gain, bias, *args)


def cross_back_kernel(parts, dec_ref, enc_ref, qx, kx, vx, ctx, enc, w_kv, *refs):
    pieces = refs[:parts]
    (gq_keep, gq_send, g_kv, enc_keep, enc_send, grad, gx, dq, kt, sums, sq, sk, sv, wide) = refs[parts:]
    length = ctx.shape[0]
    dec_starts, dec_ends = segment_bounds(dec_ref)
    enc_starts, enc_ends = segment_bounds(enc_ref)
    gather_rows(grad, pieces[0], pieces[1:])
    attend_back(
        enc_starts, enc_ends, dec_starts, dec_ends, qx, kx, vx, ctx, grad, gx, dq, kt, sums, sq, sk, sv
    )
    split_out(sq, gq_keep, gq_send, gq_keep.shape[0])
    g_kv[0] = dot_tn(enc[...], sk[...]).astype(BF16)
    g_kv[1] = dot_tn(enc[...], sv[...]).astype(BF16)

    def step(block, carry):
        rows = pl.ds(pl.multiple_of(block * SPAN, SPAN), SPAN)
        wide[rows, :] = dot_nt(sk[rows, :], w_kv[0]) + dot_nt(sv[rows, :], w_kv[1])
        return carry

    lax.fori_loop(0, length // SPAN, step, 0)
    split_out(wide, enc_keep, enc_send, enc_keep.shape[0])


def cross_back_fast(dec_ref, enc_ref, *refs):
    rest = list(refs)
    take = lambda number: [rest.pop(0) for _ in range(number)]
    sources = take(8)
    gq_out, g_kv, enc_keep, enc_send, layer_out = take(5)
    loaded = take(8)
    grad, ctx, kx, vx, qx, enc, w_kv, layer = loaded
    gx, dq, kt, sums, sq, sk, sv, wide, load_sem, store_sem = rest
    length = ctx.shape[0]
    heads = qx.shape[0]
    loads = [pltpu.make_async_copy(a, b, load_sem.at[k]) for k, (a, b) in enumerate(zip(sources, loaded))]
    for load in loads:
        load.start()
    dec_starts, dec_ends = segment_bounds(dec_ref)
    enc_starts, enc_ends = segment_bounds(enc_ref)
    sums[...] = head_sums(ctx.shape[1], heads)
    for load in loads[:3]:
        load.wait()
    prepare_back(grad, ctx, kx, gx, dq, kt, sums)
    for load in loads[3:5]:
        load.wait()
    each_span(
        length, enc_starts, dec_starts, dec_ends,
        functools.partial(attend_back_body, qx, kx, vx, gx, dq, kt, sk, sv),
    )
    for load in loads[5:]:
        load.wait()
    turn_queries(dq, sq, range(max(1, heads // 2)))
    stores = [
        pltpu.make_async_copy(layer, layer_out, store_sem.at[0]),
        pltpu.make_async_copy(sq, gq_out, store_sem.at[1]),
    ]
    for store in stores:
        store.start()
    g_kv[0] = dot_tn(enc[...], sk[...]).astype(BF16)
    g_kv[1] = dot_tn(enc[...], sv[...]).astype(BF16)

    def step(block, carry):
        rows = pl.ds(pl.multiple_of(block * SPAN, SPAN), SPAN)
        wide[rows, :] = dot_nt(sk[rows, :], w_kv[0]) + dot_nt(sv[rows, :], w_kv[1])
        return carry

    unrolled(length // SPAN, step)
    split_out(wide, enc_keep, enc_send, enc_keep.shape[0])
    for store in stores:
        store.wait()


def first_back_kernel(parts, gain, grad_mid, first_low, normed, dev, *refs):
    groups = [refs[g * parts : (g + 1) * parts] for g in range(4)]
    gq, w_query, ctx, w_out = groups
    (grad_base, gains, biases, g_query_keep, g_query_send, g_out_keep, g_out_send,
     back_keep, back_send, low_ref) = refs[4 * parts :]
    share = grad_mid.shape[0]
    block = share_block(share)
    gains[...] = jnp.zeros_like(gains)
    biases[...] = jnp.zeros_like(biases)

    def step(index, carry):
        rows = pl.ds(pl.multiple_of(index * block, block), block)
        grad = grad_mid[rows, :]
        for k in range(parts):
            grad = grad + dot_nt(gq[k][rows, :], w_query[k][...])
        back, gain_grad, bias_grad = norm_back(grad, normed[rows, :], dev[rows, :], gain[0:1, :])
        gains[...] += gain_grad
        biases[...] += bias_grad
        grad_base[rows, :] = back
        low = back.astype(BF16)
        low_ref[rows, :] = low
        for k in range(parts):
            value = dot_nt(low, w_out[k][...]).astype(BF16)
            if k == 0:
                back_keep[rows, :] = value
            else:
                back_send[k - 1, rows, :] = value
        return carry

    lax.fori_loop(0, share // block, step, 0)
    for k in range(parts):
        query_grad = dot_tn(first_low[...], gq[k][...]).astype(BF16)
        out_grad = dot_tn(ctx[k][...], low_ref[...]).astype(BF16)
        if k == 0:
            g_query_keep[...] = query_grad
            g_out_keep[...] = out_grad
        else:
            g_query_send[k - 1] = query_grad
            g_out_send[k - 1] = out_grad


def self_back_kernel(parts, dec_ref, qx, kx, vx, ctx, x_ref, w_qkv, *refs):
    pieces = refs[:parts]
    g_qkv, in_keep, in_send, grad, gx, dq, kt, sums, sq, sk, sv, wide = refs[parts:]
    length = ctx.shape[0]
    starts, ends = segment_bounds(dec_ref)
    gather_rows(grad, pieces[0], pieces[1:])
    attend_back(starts, ends, starts, ends, qx, kx, vx, ctx, grad, gx, dq, kt, sums, sq, sk, sv)
    for c, source in enumerate((sq, sk, sv)):
        g_qkv[c] = dot_tn(x_ref[...], source[...]).astype(BF16)

    def step(block, carry):
        rows = pl.ds(pl.multiple_of(block * SPAN, SPAN), SPAN)
        wide[rows, :] = (
            dot_nt(sq[rows, :], w_qkv[0])
            + dot_nt(sk[rows, :], w_qkv[1])
            + dot_nt(sv[rows, :], w_qkv[2])
        )
        return carry

    lax.fori_loop(0, length // SPAN, step, 0)
    split_out(wide, in_keep, in_send, in_keep.shape[0])


LINK_RATE = 0.06
HOP_TIME = 3.0
TAKE_TIME = 0.05
ADD_RATE = 1.3
SEND_TIME = 0.03
SLACK = 0.5
AHEAD = 2.0
LAST_AHEAD = 3.0


class Part:
    def __init__(self, out, row, col, rows, cols, ready):
        self.out, self.row, self.col, self.rows, self.cols = out, row, col, rows, cols
        self.ready = ready
        self.order = None
        self.first = 0

    def window(self):
        return (pl.ds(self.row, self.rows), pl.ds(self.col, self.cols))


def step_shape(part, step, bits):
    depth = step if step < bits else 2 * bits - 2 - step
    return part.order[depth], part.rows >> min(depth + 1, bits - 1)


def link_cost(part, step, bits):
    bit, rows = step_shape(part, step, bits)
    amount = rows * part.cols * 2e-6 * 2 / LINK_RATE
    return {bit: 2 * amount, bit - 1: amount} if bit == bits - 1 else {bit: amount}


def choose_orders(parts, bits):
    last = bits - 1
    options = [(0, 1, 2, last), (1, 0, 2, last), (2, 0, 1, last), (2, 1, 0, last)]
    load = dict.fromkeys(range(bits), 0.0)
    for part in parts:
        best = None
        for order in options:
            part.order = order
            trial = dict(load)
            for step in range(2 * bits - 1):
                for bit, amount in link_cost(part, step, bits).items():
                    trial[bit] += amount
            score = sum(value * value for value in trial.values())
            if best is None or score < best[0]:
                best = (score, order, trial)
        _, part.order, load = best


def plan_transfers(parts, bits, spans):
    steps = 2 * bits - 1
    busy = dict.fromkeys(range(bits), 0.0)
    left = [part.first for part in parts]
    since = [None] * len(parts)
    flying = []

    def rest(p):
        return sum(max(link_cost(parts[p], s, bits).values()) + HOP_TIME for s in range(left[p], steps))

    def serve(clock, ahead, slack, found):
        for entry in sorted(flying):
            if entry[0] + slack <= clock:
                flying.remove(entry)
                p = entry[1]
                found.append(("take", p, left[p]))
                clock += TAKE_TIME
                if left[p] < bits:
                    clock += step_shape(parts[p], left[p], bits)[1] * parts[p].cols * 2e-6 / ADD_RATE
                left[p] += 1
                since[p] = clock if left[p] < steps else None
        waiting = [p for p in range(len(parts)) if since[p] is not None]
        for p in sorted(waiting, key=lambda p: (-parts[p].ready[0], -rest(p), p)):
            cost = link_cost(parts[p], left[p], bits)
            if since[p] <= clock and all(busy[b] <= clock + ahead for b in cost):
                done = clock
                for b, amount in cost.items():
                    busy[b] = max(busy[b], clock) + amount
                    done = max(done, busy[b])
                clock += SEND_TIME
                found.append(("send", p, left[p]))
                flying.append((done + HOP_TIME, p))
                since[p] = None
        return clock

    slots, clock = [], 0.0
    for unit, span in enumerate(spans):
        for p, part in enumerate(parts):
            if part.ready[0] == unit:
                since[p] = clock + part.ready[1]
        found = []
        clock = serve(clock, span + AHEAD, SLACK, found)
        slots.append(found)
        clock += span
    for p, part in enumerate(parts):
        if part.ready[0] >= len(spans):
            since[p] = clock + part.ready[1]
    found = []
    while flying or any(value is not None for value in since):
        before = len(found)
        clock = serve(clock, LAST_AHEAD, 0.0, found)
        if len(found) == before:
            clock += 0.05
    slots.append(found)
    return slots


class RowsSum:
    def __init__(self, parts, bits, held, landing, final, outs, send_sem, land_sem, store_sem):
        self.parts, self.bits = parts, bits
        self.held, self.landing, self.final, self.outs = held, landing, final, outs
        self.send_sem, self.land_sem, self.store_sem = send_sem, land_sem, store_sem
        self.begin = [lambda: None] * len(parts)

    def side(self, bit):
        return lax.shift_right_logical(lax.axis_index("rows"), bit) & 1

    def peer(self, bit):
        me = lax.axis_index("rows")
        return {"rows": me + (1 << bit) - 2 * (me & (1 << bit)), "heads": lax.axis_index("heads")}

    def offset(self, p, depth):
        part, total = self.parts[p], jnp.int32(0)
        for d in range(depth):
            total = total + self.side(part.order[d]) * (part.rows >> (d + 1))
        return total

    def copy(self, p, step):
        part = self.parts[p]
        bit, size = step_shape(part, step, self.bits)
        if step < self.bits - 1:
            first = self.offset(p, step) + (1 - self.side(bit)) * size
        else:
            first = self.offset(p, min(step, 2 * self.bits - 2 - step) + (step >= self.bits))
        rows = pl.ds(pl.multiple_of(first, 16), size)
        if step < self.bits:
            source = self.held[p].at[rows, :]
            dest = self.landing[p].at[pl.ds(self.spot(p, step), size), :]
        else:
            source = self.final[p].at[rows, :]
            dest = source
        return pltpu.make_async_remote_copy(
            src_ref=source, dst_ref=dest, send_sem=self.send_sem.at[p, step],
            recv_sem=self.land_sem.at[p, step], device_id=self.peer(bit),
            device_id_type=pl.DeviceIdType.MESH,
        )

    def spot(self, p, step):
        part = self.parts[p]
        return part.rows - (part.rows >> step)

    def absorb(self, p, step):
        part = self.parts[p]
        size = step_shape(part, step, self.bits)[1]
        depth = min(step + 1, self.bits - 1)
        mine = pl.ds(pl.multiple_of(self.offset(p, depth), 16), size)
        spot = pl.ds(self.spot(p, step), size)
        total = self.held[p][mine, :].astype(F32) + self.landing[p][spot, :].astype(F32)
        dest = self.final[p] if step == self.bits - 1 else self.held[p]
        dest[mine, :] = total.astype(BF16)

    def store(self, p):
        part = self.parts[p]
        return pltpu.make_async_copy(
            self.final[p], self.outs[part.out].at[part.window()], self.store_sem.at[p]
        )

    def run(self, ops):
        for kind, p, step in ops:
            if kind == "send":
                if step == self.parts[p].first:
                    self.begin[p]()
                self.copy(p, step).start()
                continue
            self.copy(p, step).wait()
            if step < self.bits:
                self.absorb(p, step)
            elif step == 2 * self.bits - 2:
                self.store(p).start()


def add_into(dest, other):
    dest[...] = (dest[...].astype(F32) + other[...].astype(F32)).astype(dest.dtype)


def back_unit(qx, kx, vx, gx, dq, kt, sk, sv, head, rows, queries):
    scale = LOG2_E * HEAD_DIM**-0.5
    keys = kx[head, rows, :]
    query = qx[head, queries, :]
    grads = gx[head, queries, :]
    weights = jnp.exp2(dot_nt(keys, query) * scale)
    raised = dot_nt(vx[head, rows, :], grads)
    value_slab = dot(weights.astype(BF16), grads)
    inner = (weights * raised).astype(BF16)
    key_slab = dot(inner, query) * (HEAD_DIM**-0.5)
    dq[head, :, queries] += dot(kt[head, :, rows], inner)
    merge_head(sk, rows, head, key_slab)
    merge_head(sv, rows, head, value_slab)


def tail_kernel(parts, bits, plan, gain, small_in, *refs):
    rest = list(refs)
    take = lambda number: [rest.pop(0) for _ in range(number)]
    (gq_in, grad_mid_in, first_low_in, normed_in, dev_in, wq0_in, wq1_in, ctx1_in,
     wo0_in, wo1_in, qx_in, kx_in, vx_in, ctx_in, x_in, w_in, enc_in) = take(17)
    ffn_out_own, ffn_in_own, cross_own, kv_own, *arrived = take(7)
    outs = take(7)
    small_out, in_keep, in_land_out, enc_out = take(4)
    count = len(parts)
    held, landing, final = take(count), take(count), take(count)
    mates = dict(zip([p for p in range(count) if parts[p].out in (3, 5)], rest))
    take(len(mates))
    (gq, gq_land, grad_mid, first_low, normed, dev, wq0, wq1, ctx0, ctx1, wo0, wo1, qx, kx, vx, ctx, x_ref, w_ref,
     grad, gx, dq, kt, sums, sq, sk, sv, wide, low, back_out, query_out, self_out, in_out, in_land, small_land, base) = take(35)
    (send_sem, land_sem, store_sem, load_sem, part_sem, mate_send, mate_land, core_send, core_land,
     small_send, small_sem, out_sem) = rest
    share, width = grad_mid.shape
    length = x_ref.shape[0]
    heads = qx.shape[0]
    block = 256
    me, core = lax.axis_index("rows"), lax.axis_index("heads")
    other_core = {"rows": me, "heads": 1 - core}
    mine_rows = core_half(core, share)
    summing = RowsSum(parts, bits, held, landing, final, outs, send_sem, land_sem, store_sem)

    def across(source, dest, send, land, peer=other_core):
        return pltpu.make_async_remote_copy(
            src_ref=source, dst_ref=dest, send_sem=send, recv_sem=land,
            device_id=peer, device_id_type=pl.DeviceIdType.MESH,
        )

    pairs = [
        (gq_in.at[mine_rows, :], gq), (grad_mid_in, grad_mid), (wq0_in, wq0), (wq1_in, wq1), (normed_in, normed), (dev_in, dev),
        (wo0_in, wo0), (wo1_in, wo1), (first_low_in, first_low), (ctx_in.at[mine_rows, :], ctx0), (ctx1_in, ctx1), (ctx_in, ctx),
        (qx_in, qx), (kx_in, kx), (vx_in, vx), (x_in, x_ref), (w_in, w_ref),
    ]
    loads = [pltpu.make_async_copy(a, b, load_sem.at[k]) for k, (a, b) in enumerate(pairs)]
    own_arrays = {0: ffn_out_own, 1: ffn_in_own, 2: cross_own, 4: kv_own}
    early = {id(part): (bit, spot) for part, bit, spot in first_steps(parts)[0]}
    part_loads, mate_copies = {}, {}
    for p, part in enumerate(parts):
        part_loads[p] = []
        if part.first:
            half = part.rows // 2
            bit, spot = early[id(part)]
            keep = part.row + summing.side(bit) * half
            rows = pl.ds(pl.multiple_of(keep, 128), half)
            here = pl.ds(pl.multiple_of(keep - part.row, 128), half)
            moves = [(own_arrays[part.out].at[rows, pl.ds(part.col, part.cols)], held[p].at[here, :])]
            for piece in range(half // 128):
                window = (pl.ds(spot * 128, 128), pl.ds(piece * part.cols, part.cols))
                moves.append((arrived[bit].at[window], landing[p].at[pl.ds(piece * 128, 128), :]))
        elif part.out in own_arrays:
            moves = [(own_arrays[part.out].at[part.window()], held[p])]
        else:
            moves = []
        for k, (source, dest) in enumerate(moves):
            part_loads[p].append(pltpu.make_async_copy(source, dest, part_sem.at[p, k]))
            part_loads[p][-1].start()
    for load in loads[:6]:
        load.start()
    peers = [summing.peer(bit) for bit in range(bits)] + [other_core]
    barrier = pltpu.get_barrier_semaphore()
    for peer in peers:
        pl.semaphore_signal(barrier, inc=1, device_id=peer, device_id_type=pl.DeviceIdType.MESH)
    pl.semaphore_wait(barrier, len(peers))
    gq_copy = across(gq_in.at[core_half(1 - core, share), :], gq_land, core_send.at[0], core_land.at[0])
    gq_copy.start()
    enc_copy = across(
        enc_in.at[0], enc_out, core_send.at[2 + share // block], core_land.at[2 + share // block]
    )
    for load in loads[6:]:
        load.start()
    for p, part in enumerate(parts):
        if part.out == 3:
            mate_copies[p] = across(query_out, mates[p], mate_send.at[p], mate_land.at[p])
        if part.out == 5:
            mate_copies[p] = across(self_out, mates[p], mate_send.at[p], mate_land.at[p])

        def begin(p=p):
            for load in part_loads[p]:
                load.wait()
            if parts[p].first:
                summing.absorb(p, 0)
            if p in mate_copies:
                mate_copies[p].wait()
                add_into(held[p], mates[p])

        summing.begin[p] = begin

    slots = list(plan)
    summing.run(slots.pop(0))
    for load in loads[:6]:
        load.wait()
    gq_copy.wait()
    for load in loads[6:8]:
        load.wait()
    small_out[...] = small_in[...]
    back_copies = []
    for index in range(share // block):
        summing.run(slots.pop(0))
        rows = pl.ds(index * block, block)
        mine = own_rows(share, index * block, block)
        value = grad_mid[rows, :] + dot_nt(gq[rows, :], wq0[...]) + dot_nt(gq_land[rows, :], wq1[...])
        back, gain_grad, bias_grad = norm_back(value, normed[rows, :], dev[rows, :], gain[0:1, :])
        small_out[0:1, :] += gain_grad
        small_out[3:4, :] += bias_grad
        base[rows, :] = back
        low_part = back.astype(BF16)
        low[rows, :] = low_part
        grad[mine, :] = dot_nt(low_part, wo0[...]).astype(BF16)
        back_out[rows, :] = dot_nt(low_part, wo1[...]).astype(BF16)
        copy = across(back_out.at[rows, :], grad.at[mine, :], core_send.at[1 + index], core_land.at[1 + index])
        copy.start()
        back_copies.append(copy)
    summing.run(slots.pop(0))
    for load in loads[8:12]:
        load.wait()
    query_out[...] = dot_tn(first_low[...], gq_land[...]).astype(BF16)
    self_out[...] = dot_tn(ctx1[...], low[...]).astype(BF16)
    for p, part in enumerate(parts):
        if part.out in (3, 5):
            mate_copies[p].start()
        if part.out == 3:
            held[p][...] = dot_tn(first_low[...], gq[...]).astype(BF16)
        if part.out == 5:
            held[p][...] = dot_tn(ctx0[...], low[...]).astype(BF16)
    summing.run(slots.pop(0))
    enc_copy.start()
    for copy in back_copies:
        copy.wait()
    for load in loads[12:]:
        load.wait()
    sums[...] = head_sums(ctx.shape[1], heads)
    prepare_back(grad, ctx, kx, gx, dq, kt, sums)
    blocks = length // KEY_SPAN
    in_copy = across(in_out, in_land, core_send.at[1 + share // block], core_land.at[1 + share // block])
    for pair in range(heads // 2):
        mine = [slots.pop(0) for _ in range(2 * blocks)]

        def unit(index, carry):
            lax.switch(index, [functools.partial(summing.run, ops) for ops in mine])
            rows = pl.ds(pl.multiple_of(lax.rem(index, blocks) * KEY_SPAN, KEY_SPAN), KEY_SPAN)
            head = 2 * pair + lax.div(index, blocks)
            back_unit(qx, kx, vx, gx, dq, kt, sk, sv, head, rows, pl.ds(0, length))
            return carry

        lax.fori_loop(0, 2 * blocks, unit, 0)
        cols = pl.ds(pair * LANES, LANES)
        summing.run(slots.pop(0))
        turn_queries(dq, sq, [pair])
        for p, part in enumerate(parts):
            if part.out == 6 and part.col == pair * LANES:
                source = (sq, sk, sv)[part.row // width]
                held[p][...] = dot_tn(x_ref[...], source[:, cols]).astype(BF16)
    last = slots.pop(0)
    early_ops = 24
    summing.run(last[:early_ops])
    last = last[early_ops:]

    def spread(index, carry):
        rows = pl.ds(pl.multiple_of(index * SPAN, SPAN), SPAN)
        value = dot_nt(sq[rows, :], w_ref[0]) + dot_nt(sk[rows, :], w_ref[1])
        wide[rows, :] = value + dot_nt(sv[rows, :], w_ref[2])
        return carry

    unrolled(length // SPAN, spread)
    away = pl.ds(pl.multiple_of((1 - core) * share, share), share)
    in_out[...] = wide[away, :].astype(BF16)
    in_copy.start()
    here = pl.ds(pl.multiple_of(core * share, share), share)
    in_keep[...] = (base[...] + wide[here, :]).astype(BF16)
    enc_copy.wait()
    small_copy = None
    for k in range(len(peers) + 1):
        cut = len(last) * k // (len(peers) + 1), len(last) * (k + 1) // (len(peers) + 1)
        if small_copy is not None:
            small_copy.wait()
            small_out[...] += small_land[k - 1]
        if k < len(peers):
            small_copy = across(
                small_out, small_land.at[k], small_send.at[k], small_sem.at[k], peers[k]
            )
            small_copy.start()
        if k == len(peers):
            in_copy.wait()
            in_store = pltpu.make_async_copy(in_land, in_land_out, out_sem)
            in_store.start()
        summing.run(last[cut[0] : cut[1]])
    in_store.wait()
    for p in range(count):
        summing.store(p).wait()


def widen_kernel(table, small, *refs):
    sources = 1 + max(max(e[0], -1 if e[1] is None else e[1]) for e in table)
    outs = 1 + max(e[2] for e in table)
    arrays, dests = refs[:sources], refs[sources : sources + outs]
    gain_out, bias_out = refs[sources + outs : sources + outs + 2]
    rest = list(refs[sources + outs + 2 :])
    low = [rest.pop(0) for _ in table]
    more = {k: rest.pop(0) for k, e in enumerate(table) if e[1] is not None}
    wide = [rest.pop(0) for _ in table]
    load_sem, more_sem, store_sem = rest
    loads, stores = [], []
    for k, (source, second, out, window) in enumerate(table):
        window = tuple(pl.ds(*w) for w in window)
        loads.append([pltpu.make_async_copy(arrays[source].at[window], low[k], load_sem.at[k])])
        if second is not None:
            loads[k].append(pltpu.make_async_copy(arrays[second].at[window], more[k], more_sem.at[k]))
        stores.append(pltpu.make_async_copy(wide[k], dests[out].at[window], store_sem.at[k]))
        for load in loads[k]:
            load.start()
    gain_out[...] = small[0:3, :]
    bias_out[...] = small[3:6, :]
    for k in range(len(table)):
        for load in loads[k]:
            load.wait()
        value = low[k][...].astype(F32)
        if k in more:
            value = value + more[k][...].astype(F32)
        wide[k][...] = value
        stores[k].start()
    for store in stores:
        store.wait()


def widen_all(small, entries):
    arrays, table, shapes = [], [], []
    for out, (first, second) in enumerate(entries):
        source = len(arrays)
        arrays.append(first)
        if second is not None:
            arrays.append(second)
        rows, cols = first.shape
        shapes.append(shape_of((rows, cols), F32))
        high = 256 if cols >= 512 else 512
        for row in range(0, rows, high):
            table.append((source, None if second is None else source + 1, out, ((row, high), (0, cols))))
    spaces = [pl.BlockSpec(memory_space=pl.ANY)]
    sized = lambda e: (e[3][0][1], e[3][1][1])
    return pl.pallas_call(
        functools.partial(widen_kernel, table),
        out_shape=shapes + [shape_of((3, small.shape[1]), F32)] * 2,
        in_specs=[VMEM] + spaces * len(arrays),
        out_specs=spaces * len(shapes) + [VMEM] * 2,
        scratch_shapes=[pltpu.VMEM(sized(e), arrays[e[0]].dtype) for e in table]
        + [pltpu.VMEM(sized(e), arrays[e[1]].dtype) for e in table if e[1] is not None]
        + [pltpu.VMEM(sized(e), F32) for e in table]
        + [pltpu.SemaphoreType.DMA((len(table),))] * 3,
        compiler_params=pltpu.CompilerParams(vmem_limit_bytes=VMEM_BYTES),
    )(small, *arrays)


def unit_spans(share, heads):
    spans = [3.0] + [1.3] * (share // 256) + [1.8, 2.0]
    made = len(spans) - 1
    pair_end = []
    for _ in range(heads // 2):
        spans += [2.2] * (4 * share // KEY_SPAN) + [1.8]
        pair_end.append(len(spans))
    return spans, made, pair_end


def gradient_parts(shapes, share, heads, bits):
    spans, made, pair_end = unit_spans(share, heads)
    parts = []
    for out, (rows, cols) in enumerate(shapes):
        high, broad = (256, 512) if cols == 512 else (512, 256)
        if out == 6:
            broad = LANES
        for col in range(0, cols, broad):
            for row in range(0, rows, high):
                ready = (0, 0.0)
                if out in (3, 5):
                    ready = (made, 1.0)
                if out == 6:
                    ready = (pair_end[col // LANES], 0.0)
                parts.append(Part(out, row, col, high, broad, ready))
                parts[-1].first = 1 if out < 2 else 0
    choose_orders(parts, bits)
    return parts


def run_tail(parts, gain, small, first_args, halves, shapes):
    bits = lax.axis_size("rows").bit_length() - 1
    length, local = first_args[0].shape
    width = first_args[1].shape[1]
    share = length // 2
    heads = local // HEAD_DIM
    norm_units = share // 256
    plan = plan_transfers(parts, bits, unit_spans(share, heads)[0])
    count = len(parts)
    buffers = [pltpu.VMEM((p.rows, p.cols), BF16) for p in parts]
    mated = [b for b, p in zip(buffers, parts) if p.out in (3, 5)]
    vm = lambda kind, *dims: pltpu.VMEM(dims, kind)
    wide_heads = vm(BF16, heads, length, LANES)
    own = [
        vm(BF16, share, local), vm(BF16, share, local), vm(F32, share, width), vm(BF16, share, width),
        vm(F32, share, width), vm(F32, share, 1), vm(BF16, width, local), vm(BF16, width, local),
        vm(BF16, share, local), vm(BF16, share, local), vm(BF16, local, width), vm(BF16, local, width),
        wide_heads, wide_heads, wide_heads, vm(BF16, length, local), vm(BF16, length, width),
        vm(BF16, 3, width, local),
        vm(BF16, length, local), wide_heads, vm(F32, heads, HEAD_DIM, length),
        vm(BF16, heads, HEAD_DIM, length), vm(BF16, local, heads * LANES),
        vm(BF16, length, local), vm(BF16, length, local), vm(BF16, length, local), vm(F32, length, width),
        vm(BF16, share, width), vm(BF16, share, local), vm(BF16, width, local), vm(BF16, local, width),
        vm(BF16, share, width), vm(BF16, share, width), vm(F32, bits + 1, 8, width),
        vm(F32, share, width),
    ]
    sems = [
        (count, 2 * bits - 1), (count, 2 * bits - 1), (count,), (17,), (count, 3), (count,), (count,),
        (3 + norm_units,), (3 + norm_units,), (bits + 1,), (bits + 1,),
    ]
    anyspace = pl.BlockSpec(memory_space=pl.ANY)
    return pl.pallas_call(
        functools.partial(tail_kernel, parts, bits, plan),
        out_shape=[shape_of(dims, BF16) for dims in shapes]
        + [shape_of((8, width), F32)] + [shape_of((share, width), BF16)] * 3,
        in_specs=[VMEM] * 2 + [anyspace] * (len(first_args) + len(halves)),
        out_specs=[anyspace] * len(shapes) + [VMEM, VMEM, anyspace, anyspace],
        scratch_shapes=buffers * 3 + mated + own
        + [pltpu.SemaphoreType.DMA(dims) for dims in sems] + [pltpu.SemaphoreType.DMA],
        compiler_params=pltpu.CompilerParams(
            vmem_limit_bytes=VMEM_BYTES, collective_id=0, has_side_effects=True
        ),
    )(gain, small, *first_args, *halves)


def fits_tail(length, width, local, units):
    return (
        lax.axis_size("rows") == 16
        and lax.axis_size("heads") == 2
        and (width, local) == (512, 256)
        and length % 512 == 0
        and units % 512 == 0
    )


def fast_body(
    dec_input, enc_output, dec_lengths, enc_lengths, w_self_qkv, w_self_out, w_cross_q, w_cross_kv,
    w_cross_out, w_ffn_in, w_ffn_out, norm_gain, norm_bias, out_grad,
):
    length, width = dec_input.shape
    local = w_self_out.shape[0]
    heads = local // HEAD_DIM
    share = length // 2
    units = w_ffn_in.shape[1]
    size = lax.axis_size("rows")
    bits = size.bit_length() - 1
    blocks = length // SPAN
    vm = lambda kind, *dims: pltpu.VMEM(dims, kind)
    low, full = (lambda *dims: shape_of(dims, BF16)), (lambda *dims: shape_of(dims, F32))
    wide_heads, wide_scratch = low(heads, length, LANES), vm(BF16, heads, length, LANES)
    sems = [pltpu.SemaphoreType.DMA((2, blocks)), pltpu.SemaphoreType.DMA((2,))]
    self_ctx, self_qx, self_kx, self_vx = call(
        self_forward_fast, [low(length, local), wide_heads, wide_heads, wide_heads],
        [vm(BF16, length, local), wide_scratch, wide_scratch, wide_scratch] + sems, 0,
        dec_lengths, dec_input, w_self_qkv, smem=1, out_far=4,
    )
    (first_out, first_low, first_normed, first_dev, query, cross_kx, cross_vx, far_ctx, far_self_out,
     far_cross_q, far_cross_out, far_ffn_in, far_ffn_out) = run_entry(
        enc_lengths, norm_gain, norm_bias,
        [dec_input, enc_output, w_cross_kv, self_ctx, w_self_out, w_cross_q, w_cross_out, w_ffn_in, w_ffn_out],
    )
    cross_ctx, cross_qx = call(
        cross_forward_fast, [low(length, local), wide_heads],
        [vm(BF16, length, local), wide_scratch, wide_scratch, wide_scratch] + sems, 0,
        dec_lengths, enc_lengths, query, cross_kx, cross_vx, smem=2, far=2, out_far=2,
    )
    shapes = [
        (units, width), (width, units), (local, width), (width, local),
        (2 * width, local), (local, width), (3 * width, local),
    ]
    pieces = gradient_parts(shapes, share, heads, bits)
    (layer_out, grad_mid, small, g_ffn_out, g_ffn_in, g_cross_out, cross_grad, *away) = run_middle(
        pieces, norm_gain, norm_bias,
        [first_out, out_grad, cross_ctx, w_cross_out, far_cross_out, w_ffn_in, far_ffn_in,
         w_ffn_out, far_ffn_out], units,
    )
    arrived = [
        lax.ppermute(value, "rows", [(r, r ^ (1 << bit)) for r in range(size)])
        for bit, value in enumerate(away)
    ]
    flat = vm(BF16, length, local)
    gq, g_cross_kv, enc_keep, enc_send, layer_out = call(
        cross_back_fast,
        [low(length, local), low(2, width, local), low(share, width), low(1, share, width), full(share, width)],
        [flat, flat, wide_scratch, wide_scratch, wide_scratch, vm(BF16, length, width),
         vm(BF16, 2, width, local), vm(F32, share, width), wide_scratch, vm(F32, heads, HEAD_DIM, length),
         vm(BF16, heads, HEAD_DIM, length), vm(BF16, local, heads * LANES), flat, flat, flat,
         vm(F32, length, width), pltpu.SemaphoreType.DMA((8,)), pltpu.SemaphoreType.DMA((2,))],
        0, dec_lengths, enc_lengths, cross_grad, cross_ctx, cross_kx, cross_vx, cross_qx, enc_output,
        w_cross_kv, layer_out, smem=2, far=8, out_places=(0, 4),
    )
    *sums, small, in_keep, in_land, enc_land = run_tail(
        pieces, norm_gain, small,
        [gq, grad_mid, first_low, first_normed, first_dev, w_cross_q, far_cross_q, far_ctx,
         w_self_out, far_self_out, self_qx, self_kx, self_vx, self_ctx, dec_input, w_self_qkv, enc_send],
        [g_ffn_out, g_ffn_in, g_cross_out, g_cross_kv.reshape(2 * width, local), *arrived],
        shapes,
    )
    (s_ffn_out, s_ffn_in, s_cross_out, s_cross_q, s_cross_kv, s_self_out, s_self_qkv,
     input_grad, enc_grad, gain_grad, bias_grad) = widen_all(
        small, [(value, None) for value in sums] + [(in_keep, in_land), (enc_keep, enc_land)]
    )
    return (
        layer_out, input_grad, enc_grad, s_self_qkv.reshape(3, width, local), s_self_out, s_cross_q,
        s_cross_kv.reshape(2, width, local), s_cross_out, s_ffn_in, s_ffn_out, gain_grad, bias_grad,
    )


def body(*args):
    dec_input, w_self_out, w_ffn_in = args[0], args[5], args[9]
    if fits_tail(*dec_input.shape, w_self_out.shape[0], w_ffn_in.shape[1]):
        return fast_body(*args)
    return plain_body(*args)


def plain_body(
    dec_input,
    enc_output,
    dec_lengths,
    enc_lengths,
    w_self_qkv,
    w_self_out,
    w_cross_q,
    w_cross_kv,
    w_cross_out,
    w_ffn_in,
    w_ffn_out,
    norm_gain,
    norm_bias,
    out_grad,
):
    parts = lax.axis_size("heads")
    length, width = dec_input.shape
    local = w_self_out.shape[0]
    heads = local // HEAD_DIM
    share = length // parts
    units = w_ffn_in.shape[1]
    chunk = min(256, units)
    chunks = parts * units // chunk

    def shift(value, k):
        return lax.ppermute(value, "heads", [(d, (d + k) % parts) for d in range(parts)])

    def slots(shard):
        return [shard] + [shift(shard, parts - k) for k in range(1, parts)]

    def swap(keep, send):
        return [keep] + [shift(send[parts - k - 1], parts - k) for k in range(1, parts)]

    def collect(keep, send):
        total = keep.astype(F32)
        for k in range(1, parts):
            total = total + shift(send[k - 1], k).astype(F32)
        return total

    self_out, cross_q, cross_out = slots(w_self_out), slots(w_cross_q), slots(w_cross_out)
    ffn_in, ffn_out = slots(w_ffn_in), slots(w_ffn_out)

    def sent(*dims, kind=BF16):
        return shape_of((parts - 1, *dims), kind)

    def own(*dims, kind=BF16):
        return shape_of(dims, kind)

    wide_heads = own(heads, length, LANES)
    self_keep, self_send, self_ctx, self_qx, self_kx, self_vx = call(
        self_forward_kernel,
        [own(share, local), sent(share, local), own(length, local), wide_heads, wide_heads, wide_heads],
        [], 40, dec_lengths, dec_input, w_self_qkv, smem=1,
    )
    self_slots = swap(self_keep, self_send)
    cross_kx, cross_vx = call(
        cross_keys_kernel, [wide_heads, wide_heads], [], 32,
        enc_lengths, enc_output, w_cross_kv, smem=1,
    )
    first_out, first_low, first_normed, first_dev, query_keep, query_send = call(
        functools.partial(first_norm_kernel, parts),
        [own(share, width, kind=F32), own(share, width), own(share, width, kind=F32),
         own(share, 1, kind=F32), own(share, local), sent(share, local)],
        [], 32, dec_input, norm_gain, norm_bias, *self_slots, *self_out, *cross_q,
    )
    cross_keep, cross_send, cross_ctx, cross_qx = call(
        functools.partial(cross_forward_kernel, parts),
        [own(share, local), sent(share, local), own(length, local), wide_heads],
        [pltpu.VMEM((length, local), BF16)], 40,
        dec_lengths, enc_lengths, cross_kx, cross_vx, *swap(query_keep, query_send), smem=2,
    )
    cross_slots = swap(cross_keep, cross_send)
    (layer_out, grad_mid, gains_high, biases_high, g_ffn_out, g_ffn_out_send, g_ffn_in,
     g_ffn_in_send, g_cross_out, g_cross_out_send, back_keep, back_send) = call(
        functools.partial(middle_kernel, parts),
        [own(share, width, kind=F32), own(share, width, kind=F32),
         own(2, width, kind=F32), own(2, width, kind=F32),
         own(units, width), sent(units, width), own(width, units), sent(width, units),
         own(local, width), sent(local, width), own(share, local), sent(share, local)],
        [pltpu.VMEM((share, width), F32), pltpu.VMEM((share, width), BF16),
         pltpu.VMEM((share, width), F32), pltpu.VMEM((share, 1), F32),
         pltpu.VMEM((share, width), F32), pltpu.VMEM((chunks, share, chunk), BF16),
         pltpu.VMEM((chunks, share, chunk), F32), pltpu.VMEM((share, width), BF16),
         pltpu.VMEM((share, width), F32)],
        56, norm_gain, norm_bias, first_out, out_grad,
        *cross_slots, *cross_out, *ffn_in, *ffn_out,
    )
    grad_slots = swap(back_keep, back_send)
    back_scratch = [
        pltpu.VMEM((length, local), BF16),
        pltpu.VMEM((heads, length, LANES), BF16),
        pltpu.VMEM((heads, HEAD_DIM, length), F32),
        pltpu.VMEM((heads, HEAD_DIM, length), BF16),
        pltpu.VMEM((local, heads * LANES), BF16),
        pltpu.VMEM((length, local), BF16),
        pltpu.VMEM((length, local), BF16),
        pltpu.VMEM((length, local), BF16),
        pltpu.VMEM((length, width), F32),
    ]
    gq_keep, gq_send, g_cross_kv, enc_keep, enc_send = call(
        functools.partial(cross_back_kernel, len(grad_slots)),
        [own(share, local), sent(share, local), own(2, width, local),
         own(share, width, kind=F32), sent(share, width)],
        back_scratch, 56, dec_lengths, enc_lengths, cross_qx, cross_kx, cross_vx, cross_ctx,
        enc_output, w_cross_kv, *grad_slots, smem=2,
    )
    enc_grad = collect(enc_keep, enc_send)
    (grad_base, gains_low, biases_low, g_cross_q, g_cross_q_send, g_self_out, g_self_out_send,
     self_back_keep, self_back_send) = call(
        functools.partial(first_back_kernel, parts),
        [own(share, width, kind=F32), own(1, width, kind=F32), own(1, width, kind=F32),
         own(width, local), sent(width, local), own(local, width), sent(local, width),
         own(share, local), sent(share, local)],
        [pltpu.VMEM((share, width), BF16)], 40,
        norm_gain, grad_mid, first_low, first_normed, first_dev,
        *swap(gq_keep, gq_send), *cross_q, *self_slots, *self_out,
    )
    g_self_qkv, in_keep, in_send = call(
        functools.partial(self_back_kernel, parts),
        [own(3, width, local), own(share, width, kind=F32), sent(share, width)],
        back_scratch, 56, dec_lengths, self_qx, self_kx, self_vx, self_ctx, dec_input,
        w_self_qkv, *swap(self_back_keep, self_back_send), smem=1,
    )
    input_grad = grad_base + collect(in_keep, in_send)

    def over_rows(value):
        return lax.psum(value.astype(BF16), "rows").astype(F32)

    return (
        layer_out,
        input_grad,
        enc_grad,
        over_rows(g_self_qkv),
        over_rows(collect(g_self_out, g_self_out_send)),
        over_rows(collect(g_cross_q, g_cross_q_send)),
        over_rows(g_cross_kv),
        over_rows(collect(g_cross_out, g_cross_out_send)),
        over_rows(collect(g_ffn_in, g_ffn_in_send)),
        over_rows(collect(g_ffn_out, g_ffn_out_send)),
        lax.psum(jnp.concatenate([gains_low, gains_high]), ("rows", "heads")),
        lax.psum(jnp.concatenate([biases_low, biases_high]), ("rows", "heads")),
    )


def solution(mesh):
    in_specs = (
        P("rows", None),
        P("rows", None),
        P("rows", None),
        P("rows", None),
        P(None, None, "heads"),
        P("heads", None),
        P(None, "heads"),
        P(None, None, "heads"),
        P("heads", None),
        P(None, "heads"),
        P("heads", None),
        P(),
        P(),
        P("rows", None),
    )
    out_specs = (
        P(("rows", "heads"), None),
        P(("rows", "heads"), None),
        P(("rows", "heads"), None),
        P(None, None, "heads"),
        P("heads", None),
        P(None, "heads"),
        P(None, None, "heads"),
        P("heads", None),
        P(None, "heads"),
        P("heads", None),
        P(),
        P(),
    )
    return jax.shard_map(body, mesh=mesh, in_specs=in_specs, out_specs=out_specs, check_vma=False)
```

```python
import functools

import jax
import jax.numpy as jnp
from jax import lax
from jax.experimental import pallas as pl
from jax.experimental.pallas import tpu as pltpu
from jax.sharding import PartitionSpec as P

HEAD_DIM = 64
LANES = 128
SPAN = 256
KEY_SPAN = 512
CROSS_SPAN = 256
BACK_SPAN = 256
VMEM_BYTES = 2**26 - 2**17
NORM_EPS = 1e-05
MASKED_SCORE = -1e30
LOG2_E = 1.4426950408889634
GELU_RATE = 0.7978845608028654
GELU_CUBE = 0.044715
F32 = jnp.float32
BF16 = jnp.bfloat16
NT = (((1,), (1,)), ((), ()))
TN = (((0,), (0,)), ((), ()))
VMEM = pl.BlockSpec(memory_space=pltpu.VMEM)
SMEM = pl.BlockSpec(memory_space=pltpu.SMEM)


def dot(left, right):
    return jnp.dot(left, right, preferred_element_type=F32)


def dot_nt(left, right):
    return lax.dot_general(left, right, NT, preferred_element_type=F32)


def dot_tn(left, right):
    return lax.dot_general(left, right, TN, preferred_element_type=F32)


def shape_of(dims, kind):
    return jax.ShapeDtypeStruct(dims, kind)


def call(kernel, outs, scratch, mib, *args, smem=0, far=0, out_far=0, out_places=()):
    anyspace = pl.BlockSpec(memory_space=pl.ANY)
    return pl.pallas_call(
        kernel,
        out_shape=outs,
        in_specs=[SMEM] * smem + [VMEM] * (len(args) - smem - far) + [anyspace] * far,
        out_specs=[
            anyspace if k in out_places or k >= len(outs) - out_far else VMEM for k in range(len(outs))
        ],
        scratch_shapes=scratch,
        compiler_params=pltpu.CompilerParams(vmem_limit_bytes=VMEM_BYTES),
        cost_estimate=pl.CostEstimate(flops=2 * 10**10, bytes_accessed=2 * 10**7, transcendentals=0),
    )(*args)


def unrolled(count, body):
    for index in range(count):
        body(index, 0)


def segment_bounds(len_ref):
    starts, ends, total = [], [], jnp.int32(0)
    for k in range(len_ref.shape[1]):
        starts.append(total)
        total = total + len_ref[0, k]
        ends.append(total)
    return starts, ends


def bound_lanes(starts, ends):
    lane = lax.broadcasted_iota(jnp.int32, (1, LANES), 1)
    first = jnp.full((1, LANES), 1 << 30, jnp.int32)
    last = jnp.zeros((1, LANES), jnp.int32)
    for k, (start, end) in enumerate(zip(starts, ends)):
        first = jnp.where(lane == HEAD_DIM + k, start, first)
        last = jnp.where(lane == HEAD_DIM + k, end, last)
    return first, last


def lanes_of(rows):
    return lax.broadcasted_iota(jnp.int32, (rows, LANES), 1)


def membership(first_row, rows, bounds):
    place = lax.broadcasted_iota(jnp.int32, (rows, LANES), 0) + first_row
    return (place >= bounds[0]) & (place < bounds[1])


def query_extra(first_row, rows, bounds):
    return jnp.where(membership(first_row, rows, bounds), F32(MASKED_SCORE), F32(0.0))


def key_extra(first_row, rows, bounds, segs):
    lane = lanes_of(rows)
    used = (lane >= HEAD_DIM) & (lane < HEAD_DIM + segs + 3)
    return jnp.where(used & ~membership(first_row, rows, bounds), F32(1.0), F32(0.0))


def value_extra(rows):
    return jnp.full((rows, LANES), 1.0, F32)


def head_slab(wide, head):
    if wide.shape[1] < LANES:
        return jnp.concatenate([wide, jnp.zeros_like(wide)], axis=1)
    first = head // 2 * LANES
    slab = wide[:, first : first + LANES]
    if head % 2:
        slab = pltpu.roll(slab, HEAD_DIM, 1)
    return slab


def put_heads(dest, where, wide, extra):
    low_lanes = lanes_of(wide.shape[0]) < HEAD_DIM
    for head in range(dest.shape[0]):
        dest[head, where, :] = jnp.where(low_lanes, head_slab(wide, head), extra).astype(dest.dtype)


def join_heads(dest, where, slabs):
    if len(slabs) == 1:
        dest[where, :] = slabs[0][:, :HEAD_DIM].astype(dest.dtype)
        return
    low_lanes = lanes_of(slabs[0].shape[0]) < HEAD_DIM
    for pair in range(len(slabs) // 2):
        both = jnp.where(low_lanes, slabs[2 * pair], pltpu.roll(slabs[2 * pair + 1], HEAD_DIM, 1))
        dest[where, pair * LANES : (pair + 1) * LANES] = both.astype(dest.dtype)


def span_for(block, size, length, from_starts, to_starts, to_ends):
    first_row = block * size
    last_row = first_row + size - 1
    low, high = jnp.int32(0), jnp.int32(0)
    for start, to_start, to_end in zip(from_starts, to_starts, to_ends):
        low = jnp.where(start <= first_row, to_start, low)
        high = jnp.where(start <= last_row, to_end, high)
    low = (low >> 7) << 7
    pieces = (high - low + SPAN - 1) >> 8
    return jnp.minimum(low, length - pieces * SPAN), pieces


def each_span(length, starts_from, starts_to, ends_to, body, after=None, size=SPAN):
    def step(block, carry):
        start, pieces = span_for(block, size, length, starts_from, starts_to, ends_to)
        start = pl.multiple_of(start, LANES)
        rows = pl.ds(pl.multiple_of(block * size, size), size)
        for count in range(1, length // SPAN + 1):

            @pl.when(pieces == count)
            def _():
                body(rows, pl.ds(start, count * SPAN))

        if after is not None:
            after(block, rows)
        return carry

    lax.fori_loop(0, length // size, step, 0)


def merge_head(dest, rows, head, slab):
    if dest.shape[1] < LANES:
        dest[rows, :] = slab[:, :HEAD_DIM].astype(dest.dtype)
        return
    odd = (head & 1) == 1
    low_lanes = lanes_of(slab.shape[0]) < HEAD_DIM
    cols = pl.ds(pl.multiple_of((head >> 1) * LANES, LANES), LANES)
    old = dest[rows, cols].astype(F32)
    first = jnp.where(odd, old, slab)
    second = jnp.where(odd, pltpu.roll(slab, HEAD_DIM, 1), slab)
    dest[rows, cols] = jnp.where(low_lanes, first, second).astype(dest.dtype)


def attend_body(qx, kx, vx, ctx, segs, rows, keys):
    scale = LOG2_E * HEAD_DIM**-0.5
    base = HEAD_DIM + segs
    lane = lanes_of(rows.size)
    slabs = []
    for head in range(qx.shape[0]):
        query = qx[head, rows, :]
        scores = dot_nt(query, kx[head, keys, :])
        peak = jnp.max(scores, axis=1, keepdims=True)
        raised = jnp.exp2((scores - peak) * scale).astype(BF16)
        mixed = dot(raised, vx[head, keys, :])
        total = jnp.where(lane < HEAD_DIM, 1.0, mixed)
        slabs.append(mixed * pltpu.roll(1.0 / total, HEAD_DIM, 1))
        level = -(peak + jnp.log(total) * (HEAD_DIM**0.5))
        high = level.astype(BF16).astype(F32)
        middle = (level - high).astype(BF16).astype(F32)
        low = level - high - middle
        wide = query.astype(F32)
        wide = jnp.where(lane == base, high, wide)
        wide = jnp.where(lane == base + 1, middle, wide)
        wide = jnp.where(lane == base + 2, low, wide)
        qx[head, rows, :] = wide.astype(BF16)
    join_heads(ctx, rows, slabs)


def split_out(source, keep, send, share):
    me = lax.axis_index("heads")
    parts = send.shape[0] + 1
    for k in range(parts):
        owner = lax.rem(me + k, parts)
        rows = pl.ds(pl.multiple_of(owner * share, share), share)
        if k == 0:
            keep[...] = source[rows, :].astype(keep.dtype)
        else:
            send[k - 1] = source[rows, :].astype(send.dtype)


def self_forward_kernel(len_ref, x_ref, w_ref, keep, send, ctx, qx, kx, vx):
    length = x_ref.shape[0]
    segs = len_ref.shape[1]
    starts, ends = segment_bounds(len_ref)
    bounds = bound_lanes(starts, ends)

    def project(block, carry):
        first = pl.multiple_of(block * SPAN, SPAN)
        rows = pl.ds(first, SPAN)
        tokens = x_ref[rows, :]
        put_heads(qx, rows, dot(tokens, w_ref[0]), query_extra(first, SPAN, bounds))
        put_heads(kx, rows, dot(tokens, w_ref[1]), key_extra(first, SPAN, bounds, segs))
        put_heads(vx, rows, dot(tokens, w_ref[2]), value_extra(SPAN))
        return carry

    lax.fori_loop(0, length // SPAN, project, 0)
    each_span(
        length, starts, starts, ends, functools.partial(attend_body, qx, kx, vx, ctx, segs)
    )
    split_out(ctx, keep, send, keep.shape[0])


def cross_keys_kernel(len_ref, x_ref, w_ref, kx, vx):
    length = x_ref.shape[0]
    bounds = bound_lanes(*segment_bounds(len_ref))
    segs = len_ref.shape[1]

    def project(block, carry):
        first = pl.multiple_of(block * SPAN, SPAN)
        rows = pl.ds(first, SPAN)
        tokens = x_ref[rows, :]
        put_heads(kx, rows, dot(tokens, w_ref[0]), key_extra(first, SPAN, bounds, segs))
        put_heads(vx, rows, dot(tokens, w_ref[1]), value_extra(SPAN))
        return carry

    lax.fori_loop(0, length // SPAN, project, 0)


def gather_rows(dest, own, others):
    me = lax.axis_index("heads")
    parts = len(others) + 1
    share = own.shape[0]
    for k, source in enumerate([own, *others]):
        owner = lax.rem(me + k, parts)
        dest[pl.ds(pl.multiple_of(owner * share, share), share), :] = source[...]


def cross_forward_kernel(parts, dec_ref, enc_ref, kx, vx, *refs):
    pieces, (keep, send, ctx, qx, flat) = refs[:parts], refs[parts:]
    length = ctx.shape[0]
    segs = dec_ref.shape[1]
    dec_starts, dec_ends = segment_bounds(dec_ref)
    enc_starts, enc_ends = segment_bounds(enc_ref)
    bounds = bound_lanes(dec_starts, dec_ends)
    gather_rows(flat, pieces[0], pieces[1:])

    def widen(block, carry):
        first = pl.multiple_of(block * SPAN, SPAN)
        rows = pl.ds(first, SPAN)
        put_heads(qx, rows, flat[rows, :].astype(F32), query_extra(first, SPAN, bounds))
        return carry

    lax.fori_loop(0, length // SPAN, widen, 0)
    each_span(
        length, dec_starts, enc_starts, enc_ends,
        functools.partial(attend_body, qx, kx, vx, ctx, segs),
    )
    split_out(ctx, keep, send, keep.shape[0])


def row_store(source, dest, rows, sem, block, heads):
    where = (slice(None), rows, slice(None)) if heads else (rows, slice(None))
    return pltpu.make_async_copy(source.at[where], dest.at[where], sem.at[block])


def self_forward_fast(len_ref, x_ref, w_ref, ctx_out, qx_out, kx_out, vx_out, ctx, qx, kx, vx, sems, far):
    length = x_ref.shape[0]
    segs = len_ref.shape[1]
    starts, ends = segment_bounds(len_ref)
    bounds = bound_lanes(starts, ends)

    def project(block, carry):
        first = pl.multiple_of(block * SPAN, SPAN)
        rows = pl.ds(first, SPAN)
        tokens = x_ref[rows, :]
        put_heads(qx, rows, dot(tokens, w_ref[0]), query_extra(first, SPAN, bounds))
        put_heads(kx, rows, dot(tokens, w_ref[1]), key_extra(first, SPAN, bounds, segs))
        put_heads(vx, rows, dot(tokens, w_ref[2]), value_extra(SPAN))
        return carry

    unrolled(length // SPAN, project)
    whole = [pltpu.make_async_copy(kx, kx_out, far.at[0]), pltpu.make_async_copy(vx, vx_out, far.at[1])]
    for copy in whole:
        copy.start()

    def after(block, rows):
        row_store(ctx, ctx_out, rows, sems.at[0], block, False).start()
        row_store(qx, qx_out, rows, sems.at[1], block, True).start()

    each_span(
        length, starts, starts, ends, functools.partial(attend_body, qx, kx, vx, ctx, segs), after
    )
    for block in range(length // SPAN):
        rows = pl.ds(block * SPAN, SPAN)
        row_store(ctx, ctx_out, rows, sems.at[0], block, False).wait()
        row_store(qx, qx_out, rows, sems.at[1], block, True).wait()
    for copy in whole:
        copy.wait()


def cross_forward_fast(dec_ref, enc_ref, flat, kx_in, vx_in, ctx_out, qx_out, ctx, qx, kx, vx, sems, far):
    length = ctx.shape[0]
    segs = dec_ref.shape[1]
    loads = [pltpu.make_async_copy(kx_in, kx, far.at[0]), pltpu.make_async_copy(vx_in, vx, far.at[1])]
    for load in loads:
        load.start()
    dec_starts, dec_ends = segment_bounds(dec_ref)
    enc_starts, enc_ends = segment_bounds(enc_ref)
    bounds = bound_lanes(dec_starts, dec_ends)

    def widen(block, carry):
        first = pl.multiple_of(block * SPAN, SPAN)
        rows = pl.ds(first, SPAN)
        put_heads(qx, rows, flat[rows, :].astype(F32), query_extra(first, SPAN, bounds))
        return carry

    unrolled(length // SPAN, widen)
    for load in loads:
        load.wait()

    def after(block, rows):
        row_store(ctx, ctx_out, rows, sems.at[0], block, False).start()
        row_store(qx, qx_out, rows, sems.at[1], block, True).start()

    each_span(
        length, dec_starts, enc_starts, enc_ends,
        functools.partial(attend_body, qx, kx, vx, ctx, segs), after, CROSS_SPAN,
    )
    for block in range(length // CROSS_SPAN):
        rows = pl.ds(block * CROSS_SPAN, CROSS_SPAN)
        row_store(ctx, ctx_out, rows, sems.at[0], block, False).wait()
        row_store(qx, qx_out, rows, sems.at[1], block, True).wait()


def core_half(core, share):
    return pl.ds(pl.multiple_of(core * share, share), share)


def entry_remote_kernel(enc_ref, gain, bias, *refs):
    rest = list(refs)
    take = lambda number: [rest.pop(0) for _ in range(number)]
    x_in, enc_in, w_kv_in, ctx_in, wo_in, wq_in, far_cross, far_in, far_out = take(9)
    first_out, first_low, normed_out, dev_out, q_out, kx_out, vx_out, ctx_far, wo_far, wq_far = take(10)
    away_cross, away_in, away_out = take(3)
    x, enc, w_kv, ctx0, ctx1, wo0, wo1, wq0, wq1 = take(9)
    first, low, normed, q_own, q_gone, kx, vx = take(7)
    load_sem, store_sem, core_send, core_land = rest
    share, width = first.shape
    length = enc.shape[0]
    block = 256
    segs = enc_ref.shape[1]
    core = lax.axis_index("heads")
    other = {"rows": lax.axis_index("rows"), "heads": 1 - core}
    mine, theirs = core_half(core, share), core_half(1 - core, share)

    def across(number, source, dest):
        return pltpu.make_async_remote_copy(
            src_ref=source, dst_ref=dest, send_sem=core_send.at[number], recv_sem=core_land.at[number],
            device_id=other, device_id_type=pl.DeviceIdType.MESH,
        )

    moves = [(enc_in, enc), (w_kv_in, w_kv), (x_in.at[mine, :], x), (ctx_in.at[mine, :], ctx0), (wo_in, wo0), (wq_in, wq0)]
    loads = [pltpu.make_async_copy(a, b, load_sem.at[k]) for k, (a, b) in enumerate(moves)]
    barrier = pltpu.get_barrier_semaphore()
    pl.semaphore_signal(barrier, inc=1, device_id=other, device_id_type=pl.DeviceIdType.MESH)
    for load in loads:
        load.start()
    pl.semaphore_wait(barrier, 1)
    exchange = [
        across(0, ctx_in.at[theirs, :], ctx1), across(1, wo_in, wo1), across(2, wq_in, wq1),
        across(3, far_cross, away_cross), across(4, far_in, away_in), across(5, far_out, away_out),
    ]
    for copy in exchange:
        copy.start()
    bounds = bound_lanes(*segment_bounds(enc_ref))
    for load in loads[:2]:
        load.wait()

    def project(index, carry):
        top = pl.multiple_of(index * SPAN, SPAN)
        rows = pl.ds(top, SPAN)
        tokens = enc[rows, :]
        put_heads(kx, rows, dot(tokens, w_kv[0]), key_extra(top, SPAN, bounds, segs))
        put_heads(vx, rows, dot(tokens, w_kv[1]), value_extra(SPAN))
        return carry

    unrolled(length // SPAN, project)
    stores = []

    def store(source, dest):
        stores.append(pltpu.make_async_copy(source, dest, store_sem.at[len(stores)]))
        stores[-1].start()

    store(kx, kx_out)
    store(vx, vx_out)
    for load in loads[2:]:
        load.wait()
    for copy in exchange[:3]:
        copy.wait()
    store(ctx1, ctx_far)
    store(wo1, wo_far)
    store(wq1, wq_far)
    copies = []
    for index in range(share // block):
        rows = pl.ds(index * block, block)
        total = x[rows, :].astype(F32) + dot(ctx0[rows, :], wo0[...]) + dot(ctx1[rows, :], wo1[...])
        result, spread, inverse_dev = norm_forward(total, gain[0:1, :], bias[0:1, :])
        low_part = result.astype(BF16)
        first[rows, :] = result
        low[rows, :] = low_part
        normed[rows, :] = spread
        dev_out[rows, :] = inverse_dev
        q_gone[rows, :] = dot(low_part, wq1[...]).astype(BF16)
        here = own_rows(share, index * block, block)
        copies.append(across(6 + index, q_gone.at[rows, :], q_out.at[here, :]))
        copies[-1].start()
        q_own[rows, :] = dot(low_part, wq0[...]).astype(BF16)
        store(q_own.at[rows, :], q_out.at[here, :])
        store(first.at[rows, :], first_out.at[rows, :])
        store(low.at[rows, :], first_low.at[rows, :])
        store(normed.at[rows, :], normed_out.at[rows, :])
    for copy in exchange[3:] + copies:
        copy.wait()
    for copy in stores:
        copy.wait()


def run_entry(enc_lengths, gain, bias, args):
    length, width = args[0].shape
    local = args[4].shape[0]
    share, heads, units = length // 2, local // HEAD_DIM, args[7].shape[1]
    vm = lambda kind, *dims: pltpu.VMEM(dims, kind)
    wide_heads = (heads, length, LANES)
    blocks = share // 256
    anyspace = pl.BlockSpec(memory_space=pl.ANY)
    return pl.pallas_call(
        entry_remote_kernel,
        out_shape=[
            shape_of((share, width), F32), shape_of((share, width), BF16), shape_of((share, width), F32),
            shape_of((share, 1), F32), shape_of((length, local), BF16),
            shape_of(wide_heads, BF16), shape_of(wide_heads, BF16),
            shape_of((share, local), BF16), shape_of((local, width), BF16), shape_of((width, local), BF16),
            shape_of((local, width), BF16), shape_of((width, units), BF16), shape_of((units, width), BF16),
        ],
        in_specs=[SMEM, VMEM, VMEM] + [anyspace] * len(args),
        out_specs=[anyspace] * 3 + [VMEM] + [anyspace] * 9,
        scratch_shapes=[
            vm(BF16, share, width), vm(BF16, length, width), vm(BF16, 2, width, local),
            vm(BF16, share, local), vm(BF16, share, local), vm(BF16, local, width), vm(BF16, local, width),
            vm(BF16, width, local), vm(BF16, width, local),
            vm(F32, share, width), vm(BF16, share, width), vm(F32, share, width),
            vm(BF16, share, local), vm(BF16, share, local), vm(BF16, *wide_heads), vm(BF16, *wide_heads),
        ] + [pltpu.SemaphoreType.DMA((n,)) for n in (6, 5 + 4 * blocks, 6 + blocks, 6 + blocks)],
        compiler_params=pltpu.CompilerParams(
            vmem_limit_bytes=VMEM_BYTES, collective_id=2, has_side_effects=True
        ),
    )(enc_lengths, gain, bias, *args)


def attend_back_body(qx, kx, vx, gx, dq, kt, dk, dv, rows, queries):
    heads = qx.shape[0]
    group = 2 if heads % 2 == 0 else 1

    def unit(index, carry):
        for k in range(group):
            back_unit(qx, kx, vx, gx, dq, kt, dk, dv, group * index + k, rows, queries)
        return carry

    lax.fori_loop(0, heads // group, unit, 0)


def head_sums(width, heads):
    row = lax.broadcasted_iota(jnp.int32, (width, heads * LANES), 0)
    col = lax.broadcasted_iota(jnp.int32, (width, heads * LANES), 1)
    lane = col & (LANES - 1)
    hit = ((row >> 6) == (col >> 7)) & (lane >= HEAD_DIM) & (lane < HEAD_DIM + 2)
    return jnp.where(hit, F32(1.0), F32(0.0)).astype(BF16)


def prepare_back(grad, ctx, kx, gx, dq, kt, sums):
    heads = gx.shape[0]
    lane = lanes_of(SPAN)

    def widen(block, carry):
        rows = pl.ds(pl.multiple_of(block * SPAN, SPAN), SPAN)
        wide = grad[rows, :].astype(F32)
        product = wide * ctx[rows, :].astype(F32)
        high = product.astype(BF16)
        low = (product - high.astype(F32)).astype(BF16)
        totals = dot(high, sums[...]) + dot(low, sums[...])
        for head in range(heads):
            level = -totals[:, head * LANES : (head + 1) * LANES]
            rounded = level.astype(BF16).astype(F32)
            extra = jnp.where(lane == HEAD_DIM + 1, level - rounded, rounded)
            full = jnp.where(lane < HEAD_DIM, head_slab(wide, head), extra)
            gx[head, rows, :] = full.astype(BF16)
            dq[head, :, rows] = jnp.zeros((HEAD_DIM, SPAN), F32)
            kt[head, :, rows] = kx[head, rows, :].astype(F32).T[:HEAD_DIM].astype(BF16)
        return carry

    unrolled(grad.shape[0] // SPAN, widen)


def turn_queries(dq, sq, pairs):
    length = sq.shape[0]

    def finish(block, carry):
        rows = pl.ds(pl.multiple_of(block * SPAN, SPAN), SPAN)
        for pair in pairs:
            if dq.shape[0] == 1:
                sq[rows, :] = (dq[0, :, rows].T * (HEAD_DIM**-0.5)).astype(BF16)
            else:
                both = jnp.concatenate([dq[2 * pair, :, rows], dq[2 * pair + 1, :, rows]], axis=0)
                sq[rows, pair * LANES : (pair + 1) * LANES] = (both.T * (HEAD_DIM**-0.5)).astype(BF16)
        return carry

    unrolled(length // SPAN, finish)


def attend_back(key_starts, key_ends, query_starts, query_ends, qx, kx, vx, ctx, grad, gx, dq, kt, sums, sq, sk, sv):
    length = ctx.shape[0]
    heads = qx.shape[0]
    sums[...] = head_sums(ctx.shape[1], heads)
    prepare_back(grad, ctx, kx, gx, dq, kt, sums)
    each_span(
        length, key_starts, query_starts, query_ends,
        functools.partial(attend_back_body, qx, kx, vx, gx, dq, kt, sk, sv),
    )
    turn_queries(dq, sq, range(max(1, heads // 2)))


def norm_forward(summed, gain, bias):
    center = summed - jnp.mean(summed, axis=1, keepdims=True)
    inverse_dev = lax.rsqrt(jnp.mean(center * center, axis=1, keepdims=True) + NORM_EPS)
    normed = center * inverse_dev
    return normed * gain + bias, normed, inverse_dev


def norm_back(grad, normed, inverse_dev, gain):
    scaled = grad * gain
    back = inverse_dev * (
        scaled
        - jnp.mean(scaled, axis=1, keepdims=True)
        - normed * jnp.mean(scaled * normed, axis=1, keepdims=True)
    )
    gain_grad = jnp.sum(grad * normed, axis=0, keepdims=True)
    return back, gain_grad, jnp.sum(grad, axis=0, keepdims=True)


def share_block(share):
    return 256 if share % 256 == 0 else share


def own_rows(share, first, rows):
    start = lax.axis_index("heads") * share + first
    return pl.ds(pl.multiple_of(start, 64), rows)


def first_norm_kernel(parts, x_ref, gain, bias, *refs):
    ctx, w_out, w_query = refs[:parts], refs[parts : 2 * parts], refs[2 * parts : 3 * parts]
    first_out, first_low, normed_out, dev_out, keep, send = refs[3 * parts :]
    share = first_out.shape[0]
    block = share_block(share)

    def step(index, carry):
        first = pl.multiple_of(index * block, block)
        rows = pl.ds(first, block)
        total = x_ref[own_rows(share, first, block), :].astype(F32)
        for k in range(parts):
            total = total + dot(ctx[k][rows, :], w_out[k][...])
        result, normed, inverse_dev = norm_forward(total, gain[0:1, :], bias[0:1, :])
        low = result.astype(BF16)
        first_out[rows, :] = result
        first_low[rows, :] = low
        normed_out[rows, :] = normed
        dev_out[rows, :] = inverse_dev
        for k in range(parts):
            value = dot(low, w_query[k][...]).astype(BF16)
            if k == 0:
                keep[rows, :] = value
            else:
                send[k - 1, rows, :] = value
        return carry

    lax.fori_loop(0, share // block, step, 0)


def middle_kernel(parts, gain, bias, first_out, out_grad, *refs):
    groups = [refs[g * parts : (g + 1) * parts] for g in range(4)]
    ctx, w_cross, w_in, w_out = groups
    (layer_out, grad_mid, gains, biases, g_out_keep, g_out_send, g_in_keep, g_in_send,
     g_cross_keep, g_cross_send, back_keep, back_send,
     second, second_low, normed2, dev2, total, hidden, slope, top_low, back_sum) = refs[4 * parts :]
    share = first_out.shape[0]
    block = share_block(share)
    units = w_in[0].shape[1]
    chunk = min(256, units)

    def enter(index, carry):
        rows = pl.ds(pl.multiple_of(index * block, block), block)
        summed = first_out[rows, :]
        for k in range(parts):
            summed = summed + dot(ctx[k][rows, :], w_cross[k][...])
        result, normed, inverse_dev = norm_forward(summed, gain[1:2, :], bias[1:2, :])
        second[rows, :] = result
        second_low[rows, :] = result.astype(BF16)
        normed2[rows, :] = normed
        dev2[rows, :] = inverse_dev
        return carry

    lax.fori_loop(0, share // block, enter, 0)
    total[...] = second[...]
    for k in range(parts):

        def expand(index, carry):
            cols = pl.ds(pl.multiple_of(index * chunk, chunk), chunk)
            spot = k * (units // chunk) + index
            pre = dot(second_low[...], w_in[k][:, cols])
            square = pre * pre
            bent = jnp.tanh(pre * (GELU_RATE + (GELU_RATE * GELU_CUBE) * square))
            half = 0.5 + 0.5 * bent
            act = (pre * half).astype(BF16)
            hidden[spot] = act
            bend = (0.5 - 0.5 * bent * bent) * (
                GELU_RATE + (3.0 * GELU_RATE * GELU_CUBE) * square
            )
            slope[spot] = half + pre * bend
            total[...] += dot(act, w_out[k][cols, :])
            return carry

        lax.fori_loop(0, units // chunk, expand, 0)

    gains[...] = jnp.zeros_like(gains)
    biases[...] = jnp.zeros_like(biases)

    def turn(index, carry):
        first = pl.multiple_of(index * block, block)
        rows = pl.ds(first, block)
        result, normed, inverse_dev = norm_forward(total[rows, :], gain[2:3, :], bias[2:3, :])
        layer_out[rows, :] = result
        grad = out_grad[own_rows(share, first, block), :].astype(F32)
        back, gain_grad, bias_grad = norm_back(grad, normed, inverse_dev, gain[2:3, :])
        gains[1:2, :] += gain_grad
        biases[1:2, :] += bias_grad
        back_sum[rows, :] = back
        top_low[rows, :] = back.astype(BF16)
        return carry

    lax.fori_loop(0, share // block, turn, 0)
    for k in range(parts):

        def contract(index, carry):
            cols = pl.ds(pl.multiple_of(index * chunk, chunk), chunk)
            spot = k * (units // chunk) + index
            weight_out = dot_tn(hidden[spot], top_low[...]).astype(BF16)
            pre = (dot_nt(top_low[...], w_out[k][cols, :]) * slope[spot]).astype(BF16)
            weight_in = dot_tn(second_low[...], pre).astype(BF16)
            if k == 0:
                g_out_keep[cols, :] = weight_out
                g_in_keep[:, cols] = weight_in
            else:
                g_out_send[k - 1, cols, :] = weight_out
                g_in_send[k - 1, :, cols] = weight_in
            back_sum[...] += dot_nt(pre, w_in[k][:, cols])
            return carry

        lax.fori_loop(0, units // chunk, contract, 0)

    def leave(index, carry):
        rows = pl.ds(pl.multiple_of(index * block, block), block)
        back, gain_grad, bias_grad = norm_back(
            back_sum[rows, :], normed2[rows, :], dev2[rows, :], gain[1:2, :]
        )
        gains[0:1, :] += gain_grad
        biases[0:1, :] += bias_grad
        grad_mid[rows, :] = back
        low = back.astype(BF16)
        top_low[rows, :] = low
        for k in range(parts):
            value = dot_nt(low, w_cross[k][...]).astype(BF16)
            if k == 0:
                back_keep[rows, :] = value
            else:
                back_send[k - 1, rows, :] = value
        return carry

    lax.fori_loop(0, share // block, leave, 0)
    for k in range(parts):
        value = dot_tn(ctx[k][...], top_low[...]).astype(BF16)
        if k == 0:
            g_cross_keep[...] = value
        else:
            g_cross_send[k - 1] = value


def middle_remote_kernel(parts, gain, bias, *refs):
    rest = list(refs)
    take = lambda number: [rest.pop(0) for _ in range(number)]
    first_in, top_in, ctx_in, wc0_in, wc1_in, wi0_in, wi1_in, wo0_in, wo1_in = take(9)
    layer_out, mid_out, small_out, sum_out, sum_in, sum_cross, cgrad_out = take(7)
    away_out = take(3)
    (first, top, ctx0, ctx1, wc0, wc1, wi0, wi1, wo0, wo1) = loaded = take(10)
    (second, second_low, normed2, dev2, total, hidden, slope, top_low, back_sum, layer, mid,
     own_out, land_out, gone_out, own_in, land_in, gone_in, own_cross, land_cross, gone_cross, own_back, gone_back) = take(22)
    load_sem, store_sem, part_sem, core_send, core_land = rest
    share, width = first.shape
    units = wi0.shape[1]
    block = 256
    chunk = hidden.shape[2]
    chunks = units // chunk
    core = lax.axis_index("heads")
    other = {"rows": lax.axis_index("rows"), "heads": 1 - core}
    mine = pl.ds(pl.multiple_of(core * share, share), share)
    w_in, w_out, w_cross, ctx = (wi0, wi1), (wo0, wo1), (wc0, wc1), (ctx0, ctx1)
    own_sends = {}

    def across(number, source, dest):
        copy = pltpu.make_async_remote_copy(
            src_ref=source, dst_ref=dest, send_sem=core_send.at[number], recv_sem=core_land.at[number],
            device_id=other, device_id_type=pl.DeviceIdType.MESH,
        )
        own_sends[number] = copy
        return copy

    sources = [first_in, top_in.at[mine, :], ctx_in.at[mine, :], None, wc0_in, wc1_in, wi0_in, wi1_in, wo0_in, wo1_in]
    loads = [
        None if source is None else pltpu.make_async_copy(source, dest, load_sem.at[k])
        for k, (source, dest) in enumerate(zip(sources, loaded))
    ]
    barrier = pltpu.get_barrier_semaphore()
    pl.semaphore_signal(barrier, inc=1, device_id=other, device_id_type=pl.DeviceIdType.MESH)
    for k in (0, 2, 4, 5, 6, 7, 8, 9, 1):
        loads[k].start()
    pl.semaphore_wait(barrier, 1)
    across(0, ctx_in.at[core_half(1 - core, share), :], ctx1).start()
    for k in (0, 2, 4, 5):
        loads[k].wait()
    own_sends[0].wait()

    def enter(index, carry):
        rows = pl.ds(pl.multiple_of(index * block, block), block)
        summed = first[rows, :] + dot(ctx0[rows, :], wc0[...]) + dot(ctx1[rows, :], wc1[...])
        result, normed, inverse_dev = norm_forward(summed, gain[1:2, :], bias[1:2, :])
        second[rows, :] = result
        second_low[rows, :] = result.astype(BF16)
        normed2[rows, :] = normed
        dev2[rows, :] = inverse_dev
        return carry

    unrolled(share // block, enter)
    total[...] = second[...]
    for k in range(2):
        loads[6 + k].wait()
        loads[8 + k].wait()

        def expand(index, carry):
            cols = pl.ds(pl.multiple_of(index * chunk, chunk), chunk)
            spot = k * chunks + index
            pre = dot(second_low[...], w_in[k][:, cols])
            square = pre * pre
            bent = jnp.tanh(pre * (GELU_RATE + (GELU_RATE * GELU_CUBE) * square))
            half = 0.5 + 0.5 * bent
            act = (pre * half).astype(BF16)
            hidden[spot] = act
            bend = (0.5 - 0.5 * bent * bent) * (
                GELU_RATE + (3.0 * GELU_RATE * GELU_CUBE) * square
            )
            slope[spot] = half + pre * bend
            total[...] += dot(act, w_out[k][cols, :])
            return carry

        unrolled(chunks, expand)
    loads[1].wait()
    small_out[...] = jnp.zeros_like(small_out)

    def turn(index, carry):
        rows = pl.ds(pl.multiple_of(index * block, block), block)
        result, normed, inverse_dev = norm_forward(total[rows, :], gain[2:3, :], bias[2:3, :])
        layer[rows, :] = result
        grad = top[rows, :].astype(F32)
        back, gain_grad, bias_grad = norm_back(grad, normed, inverse_dev, gain[2:3, :])
        small_out[2:3, :] += gain_grad
        small_out[5:6, :] += bias_grad
        back_sum[rows, :] = back
        top_low[rows, :] = back.astype(BF16)
        return carry

    unrolled(share // block, turn)
    stores = [pltpu.make_async_copy(layer, layer_out, store_sem.at[0])]
    stores[0].start()
    for k in (1, 0):
        weight_out, weight_in = (own_out, own_in) if k == 0 else (gone_out, gone_in)

        def contract(index, carry):
            cols = pl.ds(pl.multiple_of(index * chunk, chunk), chunk)
            spot = k * chunks + index
            weight_out[cols, :] = dot_tn(hidden[spot], top_low[...]).astype(BF16)
            pre = (dot_nt(top_low[...], w_out[k][cols, :]) * slope[spot]).astype(BF16)
            weight_in[:, cols] = dot_tn(second_low[...], pre).astype(BF16)
            back_sum[...] += dot_nt(pre, w_in[k][:, cols])
            return carry

        unrolled(chunks, contract)
        if k == 1:
            across(1, gone_out, land_out).start()
            across(2, gone_in, land_in).start()
    count = share // block
    for index in range(count):
        rows = pl.ds(index * block, block)
        back, gain_grad, bias_grad = norm_back(
            back_sum[rows, :], normed2[rows, :], dev2[rows, :], gain[1:2, :]
        )
        small_out[1:2, :] += gain_grad
        small_out[4:5, :] += bias_grad
        mid[rows, :] = back
        low = back.astype(BF16)
        top_low[rows, :] = low
        gone_back[rows, :] = dot_nt(low, wc1[...]).astype(BF16)
        across(
            4 + index, gone_back.at[rows, :], cgrad_out.at[own_rows(share, index * block, block), :]
        ).start()
        own_back[rows, :] = dot_nt(low, wc0[...]).astype(BF16)
    stores.append(pltpu.make_async_copy(mid, mid_out, store_sem.at[1]))
    stores.append(pltpu.make_async_copy(own_back, cgrad_out.at[mine, :], store_sem.at[2]))
    for store in stores[1:]:
        store.start()
    gone_cross[...] = dot_tn(ctx1[...], top_low[...]).astype(BF16)
    across(3, gone_cross, land_cross).start()
    own_sends[1].wait()
    add_into(own_out, land_out)
    stores.append(pltpu.make_async_copy(own_out, sum_out, store_sem.at[3]))
    stores[-1].start()
    own_sends[2].wait()
    add_into(own_in, land_in)
    stores.append(pltpu.make_async_copy(own_in, sum_in, store_sem.at[4]))
    stores[-1].start()
    for number, (part, bit, spot) in enumerate(parts):
        for source, dest in away_windows(part, bit, spot, (own_out, own_in)[part.out], away_out[bit]):
            stores.append(pltpu.make_async_copy(source, dest, part_sem.at[len(stores) - 5]))
            stores[-1].start()
    own_cross[...] = dot_tn(ctx0[...], top_low[...]).astype(BF16)
    own_sends[3].wait()
    add_into(own_cross, land_cross)
    stores.append(pltpu.make_async_copy(own_cross, sum_cross, store_sem.at[5]))
    stores[-1].start()
    for index in range(count):
        own_sends[4 + index].wait()
    for store in stores:
        store.wait()


def away_windows(part, bit, spot, source, dest):
    half = part.rows // 2
    side = lax.shift_right_logical(lax.axis_index("rows"), bit) & 1
    first = part.row + (1 - side) * half
    pairs = []
    for piece in range(half // 128):
        rows = pl.ds(pl.multiple_of(first + piece * 128, 128), 128)
        pairs.append((source.at[rows, pl.ds(part.col, part.cols)], dest.at[away_place(part, spot, piece)]))
    return pairs


def away_place(part, spot, piece):
    across = 512 // part.cols
    return (
        pl.ds((spot + piece // across) * 128, 128),
        pl.ds(piece % across * part.cols, part.cols),
    )


def first_steps(parts):
    filled = [0, 0, 0]
    found = []
    for part in parts:
        if part.out < 2:
            bit = part.order[0]
            found.append((part, bit, filled[bit]))
            filled[bit] += part.rows * part.cols // (2 * 128 * 512)
    return found, [128 * max(1, n) for n in filled]


def run_middle(parts, gain, bias, args, units):
    share, width = args[0].shape
    local = args[2].shape[1]
    found, heights = first_steps(parts)
    chunk = 1024 if units % 1024 == 0 else 512
    vm = lambda kind, *dims: pltpu.VMEM(dims, kind)
    token, token_low = vm(F32, share, width), vm(BF16, share, width)
    scratch = [
        token, token_low, vm(BF16, share, local), vm(BF16, share, local),
        vm(BF16, local, width), vm(BF16, local, width), vm(BF16, width, units), vm(BF16, width, units),
        vm(BF16, units, width), vm(BF16, units, width),
        token, token_low, token, vm(F32, share, 1), token,
        vm(BF16, 2 * units // chunk, share, chunk), vm(F32, 2 * units // chunk, share, chunk),
        token_low, token, token, token,
        *[vm(BF16, units, width)] * 3, *[vm(BF16, width, units)] * 3, *[vm(BF16, local, width)] * 3,
        vm(BF16, share, local), vm(BF16, share, local),
    ]
    sems = [10, 6, 4 * len(found), 4 + share // 256, 4 + share // 256]
    anyspace = pl.BlockSpec(memory_space=pl.ANY)
    return pl.pallas_call(
        functools.partial(middle_remote_kernel, found),
        out_shape=[
            shape_of((share, width), F32), shape_of((share, width), F32), shape_of((8, width), F32),
            shape_of((units, width), BF16), shape_of((width, units), BF16), shape_of((local, width), BF16),
            shape_of((2 * share, local), BF16), *[shape_of((h, width), BF16) for h in heights],
        ],
        in_specs=[VMEM] * 2 + [anyspace] * len(args),
        out_specs=[anyspace] * 2 + [VMEM] + [anyspace] * 7,
        scratch_shapes=scratch + [pltpu.SemaphoreType.DMA((n,)) for n in sems],
        compiler_params=pltpu.CompilerParams(
            vmem_limit_bytes=VMEM_BYTES, collective_id=1, has_side_effects=True
        ),
    )(gain, bias, *args)


def cross_back_kernel(parts, dec_ref, enc_ref, qx, kx, vx, ctx, enc, w_kv, *refs):
    pieces = refs[:parts]
    (gq_keep, gq_send, g_kv, enc_keep, enc_send, grad, gx, dq, kt, sums, sq, sk, sv, wide) = refs[parts:]
    length = ctx.shape[0]
    dec_starts, dec_ends = segment_bounds(dec_ref)
    enc_starts, enc_ends = segment_bounds(enc_ref)
    gather_rows(grad, pieces[0], pieces[1:])
    attend_back(
        enc_starts, enc_ends, dec_starts, dec_ends, qx, kx, vx, ctx, grad, gx, dq, kt, sums, sq, sk, sv
    )
    split_out(sq, gq_keep, gq_send, gq_keep.shape[0])
    g_kv[0] = dot_tn(enc[...], sk[...]).astype(BF16)
    g_kv[1] = dot_tn(enc[...], sv[...]).astype(BF16)

    def step(block, carry):
        rows = pl.ds(pl.multiple_of(block * SPAN, SPAN), SPAN)
        wide[rows, :] = dot_nt(sk[rows, :], w_kv[0]) + dot_nt(sv[rows, :], w_kv[1])
        return carry

    lax.fori_loop(0, length // SPAN, step, 0)
    split_out(wide, enc_keep, enc_send, enc_keep.shape[0])


def cross_back_fast(dec_ref, enc_ref, *refs):
    rest = list(refs)
    take = lambda number: [rest.pop(0) for _ in range(number)]
    sources = take(7)
    gq_out, sk_out, sv_out, g_kv, layer_out = take(5)
    loaded = take(7)
    grad, ctx, kx, vx, qx, enc, layer = loaded
    gx, dq, kt, sums, sq, sk, sv, load_sem, store_sem = rest
    length = ctx.shape[0]
    heads = qx.shape[0]
    loads = [pltpu.make_async_copy(a, b, load_sem.at[k]) for k, (a, b) in enumerate(zip(sources, loaded))]
    for load in loads:
        load.start()
    dec_starts, dec_ends = segment_bounds(dec_ref)
    enc_starts, enc_ends = segment_bounds(enc_ref)
    sums[...] = head_sums(ctx.shape[1], heads)
    for load in loads[:3]:
        load.wait()
    prepare_back(grad, ctx, kx, gx, dq, kt, sums)
    for load in loads[3:5]:
        load.wait()
    each_span(
        length, enc_starts, dec_starts, dec_ends,
        functools.partial(attend_back_body, qx, kx, vx, gx, dq, kt, sk, sv), None, BACK_SPAN,
    )
    for load in loads[5:]:
        load.wait()
    stores = [
        pltpu.make_async_copy(layer, layer_out, store_sem.at[0]),
        pltpu.make_async_copy(sk, sk_out, store_sem.at[1]),
        pltpu.make_async_copy(sv, sv_out, store_sem.at[2]),
        pltpu.make_async_copy(sq, gq_out, store_sem.at[3]),
    ]
    for store in stores[:3]:
        store.start()
    turn_queries(dq, sq, range(max(1, heads // 2)))
    stores[3].start()
    g_kv[0] = dot_tn(enc[...], sk[...]).astype(BF16)
    g_kv[1] = dot_tn(enc[...], sv[...]).astype(BF16)
    for store in stores:
        store.wait()


def first_back_kernel(parts, gain, grad_mid, first_low, normed, dev, *refs):
    groups = [refs[g * parts : (g + 1) * parts] for g in range(4)]
    gq, w_query, ctx, w_out = groups
    (grad_base, gains, biases, g_query_keep, g_query_send, g_out_keep, g_out_send,
     back_keep, back_send, low_ref) = refs[4 * parts :]
    share = grad_mid.shape[0]
    block = share_block(share)
    gains[...] = jnp.zeros_like(gains)
    biases[...] = jnp.zeros_like(biases)

    def step(index, carry):
        rows = pl.ds(pl.multiple_of(index * block, block), block)
        grad = grad_mid[rows, :]
        for k in range(parts):
            grad = grad + dot_nt(gq[k][rows, :], w_query[k][...])
        back, gain_grad, bias_grad = norm_back(grad, normed[rows, :], dev[rows, :], gain[0:1, :])
        gains[...] += gain_grad
        biases[...] += bias_grad
        grad_base[rows, :] = back
        low = back.astype(BF16)
        low_ref[rows, :] = low
        for k in range(parts):
            value = dot_nt(low, w_out[k][...]).astype(BF16)
            if k == 0:
                back_keep[rows, :] = value
            else:
                back_send[k - 1, rows, :] = value
        return carry

    lax.fori_loop(0, share // block, step, 0)
    for k in range(parts):
        query_grad = dot_tn(first_low[...], gq[k][...]).astype(BF16)
        out_grad = dot_tn(ctx[k][...], low_ref[...]).astype(BF16)
        if k == 0:
            g_query_keep[...] = query_grad
            g_out_keep[...] = out_grad
        else:
            g_query_send[k - 1] = query_grad
            g_out_send[k - 1] = out_grad


def self_back_kernel(parts, dec_ref, qx, kx, vx, ctx, x_ref, w_qkv, *refs):
    pieces = refs[:parts]
    g_qkv, in_keep, in_send, grad, gx, dq, kt, sums, sq, sk, sv, wide = refs[parts:]
    length = ctx.shape[0]
    starts, ends = segment_bounds(dec_ref)
    gather_rows(grad, pieces[0], pieces[1:])
    attend_back(starts, ends, starts, ends, qx, kx, vx, ctx, grad, gx, dq, kt, sums, sq, sk, sv)
    for c, source in enumerate((sq, sk, sv)):
        g_qkv[c] = dot_tn(x_ref[...], source[...]).astype(BF16)

    def step(block, carry):
        rows = pl.ds(pl.multiple_of(block * SPAN, SPAN), SPAN)
        wide[rows, :] = (
            dot_nt(sq[rows, :], w_qkv[0])
            + dot_nt(sk[rows, :], w_qkv[1])
            + dot_nt(sv[rows, :], w_qkv[2])
        )
        return carry

    lax.fori_loop(0, length // SPAN, step, 0)
    split_out(wide, in_keep, in_send, in_keep.shape[0])


LINK_RATE = 0.06
HOP_TIME = 3.0
TAKE_TIME = 0.05
ADD_RATE = 1.3
SEND_TIME = 0.03
SLACK = 0.5
FFN_PART = (256, 512)
AHEAD = 2.0
LAST_AHEAD = 3.0


class Part:
    def __init__(self, out, row, col, rows, cols, ready):
        self.out, self.row, self.col, self.rows, self.cols = out, row, col, rows, cols
        self.ready = ready
        self.order = None
        self.first = 0

    def window(self):
        return (pl.ds(self.row, self.rows), pl.ds(self.col, self.cols))


def step_shape(part, step, bits):
    depth = step if step < bits else 2 * bits - 2 - step
    return part.order[depth], part.rows >> min(depth + 1, bits - 1)


def link_cost(part, step, bits):
    bit, rows = step_shape(part, step, bits)
    amount = rows * part.cols * 2e-6 * 2 / LINK_RATE
    return {bit: 2 * amount, bit - 1: amount} if bit == bits - 1 else {bit: amount}


def choose_orders(parts, bits):
    last = bits - 1
    options = [(0, 1, 2, last), (1, 0, 2, last), (2, 0, 1, last), (2, 1, 0, last)]
    load = dict.fromkeys(range(bits), 0.0)
    for part in parts:
        best = None
        for order in options:
            part.order = order
            trial = dict(load)
            for step in range(2 * bits - 1):
                for bit, amount in link_cost(part, step, bits).items():
                    trial[bit] += amount
            score = sum(value * value for value in trial.values())
            if best is None or score < best[0]:
                best = (score, order, trial)
        _, part.order, load = best


def plan_transfers(parts, bits, spans):
    steps = 2 * bits - 1
    busy = dict.fromkeys(range(bits), 0.0)
    left = [part.first for part in parts]
    since = [None] * len(parts)
    flying = []

    def rest(p):
        return sum(max(link_cost(parts[p], s, bits).values()) + HOP_TIME for s in range(left[p], steps))

    def serve(clock, ahead, slack, found):
        for entry in sorted(flying):
            if entry[0] + slack <= clock:
                flying.remove(entry)
                p = entry[1]
                found.append(("take", p, left[p]))
                clock += TAKE_TIME
                if left[p] < bits:
                    clock += step_shape(parts[p], left[p], bits)[1] * parts[p].cols * 2e-6 / ADD_RATE
                left[p] += 1
                since[p] = clock if left[p] < steps else None
        waiting = [p for p in range(len(parts)) if since[p] is not None]
        for p in sorted(waiting, key=lambda p: (-parts[p].ready[0], -rest(p), p)):
            cost = link_cost(parts[p], left[p], bits)
            if since[p] <= clock and all(busy[b] <= clock + ahead for b in cost):
                done = clock
                for b, amount in cost.items():
                    busy[b] = max(busy[b], clock) + amount
                    done = max(done, busy[b])
                clock += SEND_TIME
                found.append(("send", p, left[p]))
                flying.append((done + HOP_TIME, p))
                since[p] = None
        return clock

    slots, clock = [], 0.0
    for unit, span in enumerate(spans):
        for p, part in enumerate(parts):
            if part.ready[0] == unit:
                since[p] = clock + part.ready[1]
        found = []
        clock = serve(clock, span + AHEAD, SLACK, found)
        slots.append(found)
        clock += span
    for p, part in enumerate(parts):
        if part.ready[0] >= len(spans):
            since[p] = clock + part.ready[1]
    found = []
    while flying or any(value is not None for value in since):
        before = len(found)
        clock = serve(clock, LAST_AHEAD, 0.0, found)
        if len(found) == before:
            clock += 0.05
    slots.append(found)
    return slots


class RowsSum:
    def __init__(self, parts, bits, held, landing, final, outs, send_sem, land_sem, store_sem):
        self.parts, self.bits = parts, bits
        self.held, self.landing, self.final, self.outs = held, landing, final, outs
        self.send_sem, self.land_sem, self.store_sem = send_sem, land_sem, store_sem
        self.begin = [lambda: None] * len(parts)

    def side(self, bit):
        return lax.shift_right_logical(lax.axis_index("rows"), bit) & 1

    def peer(self, bit):
        me = lax.axis_index("rows")
        return {"rows": me + (1 << bit) - 2 * (me & (1 << bit)), "heads": lax.axis_index("heads")}

    def offset(self, p, depth):
        part, total = self.parts[p], jnp.int32(0)
        for d in range(depth):
            total = total + self.side(part.order[d]) * (part.rows >> (d + 1))
        return total

    def copy(self, p, step):
        part = self.parts[p]
        bit, size = step_shape(part, step, self.bits)
        if step < self.bits - 1:
            first = self.offset(p, step) + (1 - self.side(bit)) * size
        else:
            first = self.offset(p, min(step, 2 * self.bits - 2 - step) + (step >= self.bits))
        rows = pl.ds(pl.multiple_of(first, 16), size)
        if step < self.bits:
            source = self.held[p].at[rows, :]
            dest = self.landing[p].at[pl.ds(self.spot(p, step), size), :]
        else:
            source = self.final[p].at[rows, :]
            dest = source
        return pltpu.make_async_remote_copy(
            src_ref=source, dst_ref=dest, send_sem=self.send_sem.at[p, step],
            recv_sem=self.land_sem.at[p, step], device_id=self.peer(bit),
            device_id_type=pl.DeviceIdType.MESH,
        )

    def spot(self, p, step):
        part = self.parts[p]
        return part.rows - (part.rows >> step)

    def absorb(self, p, step):
        part = self.parts[p]
        size = step_shape(part, step, self.bits)[1]
        depth = min(step + 1, self.bits - 1)
        mine = pl.ds(pl.multiple_of(self.offset(p, depth), 16), size)
        spot = pl.ds(self.spot(p, step), size)
        total = self.held[p][mine, :].astype(F32) + self.landing[p][spot, :].astype(F32)
        dest = self.final[p] if step == self.bits - 1 else self.held[p]
        dest[mine, :] = total.astype(BF16)

    def store(self, p):
        part = self.parts[p]
        return pltpu.make_async_copy(
            self.final[p], self.outs[part.out].at[part.window()], self.store_sem.at[p]
        )

    def run(self, ops):
        for kind, p, step in ops:
            if kind == "send":
                if step == self.parts[p].first:
                    self.begin[p]()
                self.copy(p, step).start()
                continue
            self.copy(p, step).wait()
            if step < self.bits:
                self.absorb(p, step)
            elif step == 2 * self.bits - 2:
                self.store(p).start()


def add_into(dest, other):
    dest[...] = (dest[...].astype(F32) + other[...].astype(F32)).astype(dest.dtype)


def back_unit(qx, kx, vx, gx, dq, kt, sk, sv, head, rows, queries):
    scale = LOG2_E * HEAD_DIM**-0.5
    keys = kx[head, rows, :]
    query = qx[head, queries, :]
    grads = gx[head, queries, :]
    weights = jnp.exp2(dot_nt(keys, query) * scale)
    raised = dot_nt(vx[head, rows, :], grads)
    value_slab = dot(weights.astype(BF16), grads)
    inner = (weights * raised).astype(BF16)
    key_slab = dot(inner, query) * (HEAD_DIM**-0.5)
    dq[head, :, queries] += dot(kt[head, :, rows], inner)
    merge_head(sk, rows, head, key_slab)
    merge_head(sv, rows, head, value_slab)


def tail_kernel(parts, bits, plan, gain, small_in, *refs):
    rest = list(refs)
    take = lambda number: [rest.pop(0) for _ in range(number)]
    (gq_in, grad_mid_in, first_low_in, normed_in, dev_in, wq0_in, wq1_in, ctx1_in,
     wo0_in, wo1_in, qx_in, kx_in, vx_in, ctx_in, x_in, w_in, esk_in, esv_in, ekv_in) = take(19)
    ffn_out_own, ffn_in_own, cross_own, kv_own, *arrived = take(7)
    outs = take(7)
    small_out, in_keep, in_land_out, enc_keep, enc_out = take(5)
    count = len(parts)
    held, landing, final = take(count), take(count), take(count)
    mates = dict(zip([p for p in range(count) if parts[p].out in (3, 5)], rest))
    take(len(mates))
    (gq, gq_land, grad_mid, first_low, normed, dev, wq0, wq1, ctx0, ctx1, wo0, wo1, qx, kx, vx, ctx, x_ref, w_ref,
     grad, gx, dq, kt, sums, sq, sk, sv, wide, low, back_out, query_out, self_out, in_out, in_land, small_land, base, in_held, esk, esv, ekv, enc_gone, enc_held) = take(41)
    (send_sem, land_sem, store_sem, load_sem, part_sem, mate_send, mate_land, core_send, core_land,
     small_send, small_sem, out_sem) = rest
    share, width = grad_mid.shape
    length = x_ref.shape[0]
    heads = qx.shape[0]
    block = 256
    me, core = lax.axis_index("rows"), lax.axis_index("heads")
    other_core = {"rows": me, "heads": 1 - core}
    mine_rows = core_half(core, share)
    summing = RowsSum(parts, bits, held, landing, final, outs, send_sem, land_sem, store_sem)

    def across(source, dest, send, land, peer=other_core):
        return pltpu.make_async_remote_copy(
            src_ref=source, dst_ref=dest, send_sem=send, recv_sem=land,
            device_id=peer, device_id_type=pl.DeviceIdType.MESH,
        )

    pairs = [
        (gq_in.at[mine_rows, :], gq), (grad_mid_in, grad_mid), (wq0_in, wq0), (wq1_in, wq1), (normed_in, normed), (dev_in, dev),
        (wo0_in, wo0), (wo1_in, wo1), (first_low_in, first_low), (ctx_in.at[mine_rows, :], ctx0), (ctx1_in, ctx1), (ctx_in, ctx),
        (qx_in, qx), (kx_in, kx), (vx_in, vx), (x_in, x_ref), (w_in, w_ref),
        (esk_in, esk), (esv_in, esv), (ekv_in, ekv),
    ]
    loads = [pltpu.make_async_copy(a, b, load_sem.at[k]) for k, (a, b) in enumerate(pairs)]
    own_arrays = {0: ffn_out_own, 1: ffn_in_own, 2: cross_own, 4: kv_own}
    early = {id(part): (bit, spot) for part, bit, spot in first_steps(parts)[0]}
    peers = [summing.peer(bit) for bit in range(bits)] + [other_core]
    barrier = pltpu.get_barrier_semaphore()
    for peer in peers:
        pl.semaphore_signal(barrier, inc=1, device_id=peer, device_id_type=pl.DeviceIdType.MESH)
    part_loads, mate_copies = {}, {}
    for p, part in enumerate(parts):
        part_loads[p] = []
        if part.first:
            half = part.rows // 2
            bit, spot = early[id(part)]
            keep = part.row + summing.side(bit) * half
            rows = pl.ds(pl.multiple_of(keep, 128), half)
            here = pl.ds(pl.multiple_of(keep - part.row, 128), half)
            moves = [(own_arrays[part.out].at[rows, pl.ds(part.col, part.cols)], held[p].at[here, :])]
            for piece in range(half // 128):
                window = away_place(part, spot, piece)
                moves.append((arrived[bit].at[window], landing[p].at[pl.ds(piece * 128, 128), :]))
        elif part.out in own_arrays:
            moves = [(own_arrays[part.out].at[part.window()], held[p])]
        else:
            moves = []
        for k, (source, dest) in enumerate(moves):
            part_loads[p].append(pltpu.make_async_copy(source, dest, part_sem.at[p, k]))
            part_loads[p][-1].start()
    for load in loads[:6]:
        load.start()
    pl.semaphore_wait(barrier, len(peers))
    gq_copy = across(gq_in.at[core_half(1 - core, share), :], gq_land, core_send.at[0], core_land.at[0])
    gq_copy.start()
    enc_copy = across(
        enc_gone, enc_out, core_send.at[2 + share // block], core_land.at[2 + share // block]
    )
    for load in loads[6:]:
        load.start()
    for p, part in enumerate(parts):
        if part.out == 3:
            mate_copies[p] = across(query_out, mates[p], mate_send.at[p], mate_land.at[p])
        if part.out == 5:
            mate_copies[p] = across(self_out, mates[p], mate_send.at[p], mate_land.at[p])

        def begin(p=p):
            for load in part_loads[p]:
                load.wait()
            if parts[p].first:
                summing.absorb(p, 0)
            if p in mate_copies:
                mate_copies[p].wait()
                add_into(held[p], mates[p])

        summing.begin[p] = begin

    slots = list(plan)
    summing.run(slots.pop(0))
    for load in loads[:6]:
        load.wait()
    gq_copy.wait()
    for load in loads[6:8]:
        load.wait()
    small_out[...] = small_in[...]
    back_copies = []
    for index in range(share // block):
        summing.run(slots.pop(0))
        rows = pl.ds(index * block, block)
        mine = own_rows(share, index * block, block)
        value = grad_mid[rows, :] + dot_nt(gq[rows, :], wq0[...]) + dot_nt(gq_land[rows, :], wq1[...])
        back, gain_grad, bias_grad = norm_back(value, normed[rows, :], dev[rows, :], gain[0:1, :])
        small_out[0:1, :] += gain_grad
        small_out[3:4, :] += bias_grad
        base[rows, :] = back
        low_part = back.astype(BF16)
        low[rows, :] = low_part
        grad[mine, :] = dot_nt(low_part, wo0[...]).astype(BF16)
        back_out[rows, :] = dot_nt(low_part, wo1[...]).astype(BF16)
        copy = across(back_out.at[rows, :], grad.at[mine, :], core_send.at[1 + index], core_land.at[1 + index])
        copy.start()
        back_copies.append(copy)
    summing.run(slots.pop(0))
    for load in loads[8:12]:
        load.wait()
    query_out[...] = dot_tn(first_low[...], gq_land[...]).astype(BF16)
    self_out[...] = dot_tn(ctx1[...], low[...]).astype(BF16)
    for p, part in enumerate(parts):
        if part.out in (3, 5):
            mate_copies[p].start()
        if part.out == 3:
            held[p][...] = dot_tn(first_low[...], gq[...]).astype(BF16)
        if part.out == 5:
            held[p][...] = dot_tn(ctx0[...], low[...]).astype(BF16)
    summing.run(slots.pop(0))
    for copy in back_copies:
        copy.wait()
    for load in loads[12:17]:
        load.wait()
    sums[...] = head_sums(ctx.shape[1], heads)
    prepare_back(grad, ctx, kx, gx, dq, kt, sums)
    blocks = length // KEY_SPAN
    in_copy = across(in_out, in_land, core_send.at[1 + share // block], core_land.at[1 + share // block])
    for pair in range(heads // 2):
        mine = [slots.pop(0) for _ in range(2 * blocks)]

        def unit(index, carry):
            lax.switch(index, [functools.partial(summing.run, ops) for ops in mine])
            rows = pl.ds(pl.multiple_of(lax.rem(index, blocks) * KEY_SPAN, KEY_SPAN), KEY_SPAN)
            head = 2 * pair + lax.div(index, blocks)
            back_unit(qx, kx, vx, gx, dq, kt, sk, sv, head, rows, pl.ds(0, length))
            return carry

        lax.fori_loop(0, 2 * blocks, unit, 0)
        cols = pl.ds(pair * LANES, LANES)
        summing.run(slots.pop(0))
        turn_queries(dq, sq, [pair])
        for p, part in enumerate(parts):
            if part.out == 6 and part.col == pair * LANES:
                source = (sq, sk, sv)[part.row // width]
                held[p][...] = dot_tn(x_ref[...], source[:, cols]).astype(BF16)
    last = slots.pop(0)
    portion = (len(last) - 20) // (2 * (length // SPAN) + 2)

    def serve(number):
        summing.run(last[:number])
        del last[:number]

    def small_copy(k):
        return across(small_out, small_land.at[k], small_send.at[k], small_sem.at[k], peers[k])

    def small_step(k):
        if k:
            small_copy(k - 1).wait()
            small_out[...] += small_land[k - 1]
        if k < len(peers):
            small_copy(k).start()

    serve(20)
    small_step(0)

    def spread(index, carry):
        rows = pl.ds(pl.multiple_of(index * SPAN, SPAN), SPAN)
        value = dot_nt(sq[rows, :], w_ref[0]) + dot_nt(sk[rows, :], w_ref[1])
        wide[rows, :] = value + dot_nt(sv[rows, :], w_ref[2])
        serve(portion)
        if index % 3 == 2:
            small_step(1 + index // 3)

    unrolled(length // SPAN, spread)
    away = pl.ds(pl.multiple_of((1 - core) * share, share), share)
    in_out[...] = wide[away, :].astype(BF16)
    in_copy.start()
    here = pl.ds(pl.multiple_of(core * share, share), share)
    in_held[...] = (base[...] + wide[here, :]).astype(BF16)
    keep_store = pltpu.make_async_copy(in_held, in_keep, out_sem.at[1])
    keep_store.start()
    serve(portion)
    for load in loads[17:]:
        load.wait()

    def spread_encoder(index, carry):
        rows = pl.ds(pl.multiple_of(index * SPAN, SPAN), SPAN)
        wide[rows, :] = dot_nt(esk[rows, :], ekv[0]) + dot_nt(esv[rows, :], ekv[1])
        serve(portion)
        if index % 2 == 1:
            small_step(3 + index // 2)

    unrolled(length // SPAN, spread_encoder)
    enc_gone[...] = wide[away, :].astype(BF16)
    enc_copy.start()
    enc_held[...] = wide[here, :].astype(BF16)
    enc_store = pltpu.make_async_copy(enc_held, enc_keep, out_sem.at[2])
    enc_store.start()
    in_copy.wait()
    in_store = pltpu.make_async_copy(in_land, in_land_out, out_sem.at[0])
    in_store.start()
    serve(len(last))
    in_store.wait()
    keep_store.wait()
    enc_copy.wait()
    enc_store.wait()
    for p in range(count):
        summing.store(p).wait()


def widen_kernel(table, small, *refs):
    sources = 1 + max(max(e[0], -1 if e[1] is None else e[1]) for e in table)
    outs = 1 + max(e[2] for e in table)
    arrays, dests = refs[:sources], refs[sources : sources + outs]
    gain_out, bias_out = refs[sources + outs : sources + outs + 2]
    rest = list(refs[sources + outs + 2 :])
    low = [rest.pop(0) for _ in table]
    more = {k: rest.pop(0) for k, e in enumerate(table) if e[1] is not None}
    wide = [rest.pop(0) for _ in table]
    load_sem, more_sem, store_sem = rest
    loads, stores = [], []
    for k, (source, second, out, window) in enumerate(table):
        window = tuple(pl.ds(*w) for w in window)
        loads.append([pltpu.make_async_copy(arrays[source].at[window], low[k], load_sem.at[k])])
        if second is not None:
            loads[k].append(pltpu.make_async_copy(arrays[second].at[window], more[k], more_sem.at[k]))
        stores.append(pltpu.make_async_copy(wide[k], dests[out].at[window], store_sem.at[k]))
        for load in loads[k]:
            load.start()
    gain_out[...] = small[0:3, :]
    bias_out[...] = small[3:6, :]
    for k in range(len(table)):
        for load in loads[k]:
            load.wait()
        value = low[k][...].astype(F32)
        if k in more:
            value = value + more[k][...].astype(F32)
        wide[k][...] = value
        stores[k].start()
    for store in stores:
        store.wait()


def widen_all(small, entries):
    arrays, table, shapes = [], [], []
    for out, (first, second) in enumerate(entries):
        source = len(arrays)
        arrays.append(first)
        if second is not None:
            arrays.append(second)
        rows, cols = first.shape
        shapes.append(shape_of((rows, cols), F32))
        high = min(rows, 512 if cols >= 512 else 1024)
        high = high if rows % high == 0 else rows // 2
        for row in range(0, rows, high):
            table.append((source, None if second is None else source + 1, out, ((row, high), (0, cols))))
    spaces = [pl.BlockSpec(memory_space=pl.ANY)]
    sized = lambda e: (e[3][0][1], e[3][1][1])
    return pl.pallas_call(
        functools.partial(widen_kernel, table),
        out_shape=shapes + [shape_of((3, small.shape[1]), F32)] * 2,
        in_specs=[VMEM] + spaces * len(arrays),
        out_specs=spaces * len(shapes) + [VMEM] * 2,
        scratch_shapes=[pltpu.VMEM(sized(e), arrays[e[0]].dtype) for e in table]
        + [pltpu.VMEM(sized(e), arrays[e[1]].dtype) for e in table if e[1] is not None]
        + [pltpu.VMEM(sized(e), F32) for e in table]
        + [pltpu.SemaphoreType.DMA((len(table),))] * 3,
        compiler_params=pltpu.CompilerParams(vmem_limit_bytes=VMEM_BYTES),
    )(small, *arrays)


def unit_spans(share, heads):
    spans = [3.0] + [1.3] * (share // 256) + [1.8, 2.0]
    made = len(spans) - 1
    pair_end = []
    for _ in range(heads // 2):
        spans += [2.2] * (4 * share // KEY_SPAN) + [1.8]
        pair_end.append(len(spans))
    return spans, made, pair_end


def gradient_parts(shapes, share, heads, bits):
    spans, made, pair_end = unit_spans(share, heads)
    parts = []
    for out, (rows, cols) in enumerate(shapes):
        high, broad = (256, 512) if cols == 512 else (512, 256)
        if out < 2:
            high, broad = FFN_PART
        if out == 6:
            broad = LANES
        for col in range(0, cols, broad):
            for row in range(0, rows, high):
                ready = (0, 0.0)
                if out in (3, 5):
                    ready = (made, 1.0)
                if out == 6:
                    ready = (pair_end[col // LANES], 0.0)
                parts.append(Part(out, row, col, high, broad, ready))
                parts[-1].first = 1 if out < 2 else 0
    choose_orders(parts, bits)
    return parts


def run_tail(parts, gain, small, first_args, halves, shapes):
    bits = lax.axis_size("rows").bit_length() - 1
    length, local = first_args[0].shape
    width = first_args[1].shape[1]
    share = length // 2
    heads = local // HEAD_DIM
    norm_units = share // 256
    plan = plan_transfers(parts, bits, unit_spans(share, heads)[0])
    count = len(parts)
    buffers = [pltpu.VMEM((p.rows, p.cols), BF16) for p in parts]
    mated = [b for b, p in zip(buffers, parts) if p.out in (3, 5)]
    vm = lambda kind, *dims: pltpu.VMEM(dims, kind)
    wide_heads = vm(BF16, heads, length, LANES)
    own = [
        vm(BF16, share, local), vm(BF16, share, local), vm(F32, share, width), vm(BF16, share, width),
        vm(F32, share, width), vm(F32, share, 1), vm(BF16, width, local), vm(BF16, width, local),
        vm(BF16, share, local), vm(BF16, share, local), vm(BF16, local, width), vm(BF16, local, width),
        wide_heads, wide_heads, wide_heads, vm(BF16, length, local), vm(BF16, length, width),
        vm(BF16, 3, width, local),
        vm(BF16, length, local), wide_heads, vm(F32, heads, HEAD_DIM, length),
        vm(BF16, heads, HEAD_DIM, length), vm(BF16, local, heads * LANES),
        vm(BF16, length, local), vm(BF16, length, local), vm(BF16, length, local), vm(F32, length, width),
        vm(BF16, share, width), vm(BF16, share, local), vm(BF16, width, local), vm(BF16, local, width),
        vm(BF16, share, width), vm(BF16, share, width), vm(F32, bits + 1, 8, width),
        vm(F32, share, width), vm(BF16, share, width),
        vm(BF16, length, local), vm(BF16, length, local), vm(BF16, 2, width, local),
        vm(BF16, share, width), vm(BF16, share, width),
    ]
    sems = [
        (count, 2 * bits - 1), (count, 2 * bits - 1), (count,), (20,), (count, 5), (count,), (count,),
        (3 + norm_units,), (3 + norm_units,), (bits + 1,), (bits + 1,),
    ]
    anyspace = pl.BlockSpec(memory_space=pl.ANY)
    return pl.pallas_call(
        functools.partial(tail_kernel, parts, bits, plan),
        out_shape=[shape_of(dims, BF16) for dims in shapes]
        + [shape_of((8, width), F32)] + [shape_of((share, width), BF16)] * 4,
        in_specs=[VMEM] * 2 + [anyspace] * (len(first_args) + len(halves)),
        out_specs=[anyspace] * len(shapes) + [VMEM] + [anyspace] * 4,
        scratch_shapes=buffers * 3 + mated + own
        + [pltpu.SemaphoreType.DMA(dims) for dims in sems] + [pltpu.SemaphoreType.DMA((3,))],
        compiler_params=pltpu.CompilerParams(
            vmem_limit_bytes=VMEM_BYTES, collective_id=0, has_side_effects=True
        ),
    )(gain, small, *first_args, *halves)


def fits_tail(length, width, local, units):
    return (
        lax.axis_size("rows") == 16
        and lax.axis_size("heads") == 2
        and (width, local) == (512, 256)
        and length // SPAN == 6
        and units % 512 == 0
    )


def fast_body(
    dec_input, enc_output, dec_lengths, enc_lengths, w_self_qkv, w_self_out, w_cross_q, w_cross_kv,
    w_cross_out, w_ffn_in, w_ffn_out, norm_gain, norm_bias, out_grad,
):
    length, width = dec_input.shape
    local = w_self_out.shape[0]
    heads = local // HEAD_DIM
    share = length // 2
    units = w_ffn_in.shape[1]
    size = lax.axis_size("rows")
    bits = size.bit_length() - 1
    blocks = length // SPAN
    vm = lambda kind, *dims: pltpu.VMEM(dims, kind)
    low, full = (lambda *dims: shape_of(dims, BF16)), (lambda *dims: shape_of(dims, F32))
    wide_heads, wide_scratch = low(heads, length, LANES), vm(BF16, heads, length, LANES)
    sems = [pltpu.SemaphoreType.DMA((2, blocks)), pltpu.SemaphoreType.DMA((2,))]
    self_ctx, self_qx, self_kx, self_vx = call(
        self_forward_fast, [low(length, local), wide_heads, wide_heads, wide_heads],
        [vm(BF16, length, local), wide_scratch, wide_scratch, wide_scratch] + sems, 0,
        dec_lengths, dec_input, w_self_qkv, smem=1, out_far=4,
    )
    (first_out, first_low, first_normed, first_dev, query, cross_kx, cross_vx, far_ctx, far_self_out,
     far_cross_q, far_cross_out, far_ffn_in, far_ffn_out) = run_entry(
        enc_lengths, norm_gain, norm_bias,
        [dec_input, enc_output, w_cross_kv, self_ctx, w_self_out, w_cross_q, w_cross_out, w_ffn_in, w_ffn_out],
    )
    cross_ctx, cross_qx = call(
        cross_forward_fast, [low(length, local), wide_heads],
        [vm(BF16, length, local), wide_scratch, wide_scratch, wide_scratch] + sems, 0,
        dec_lengths, enc_lengths, query, cross_kx, cross_vx, smem=2, far=2, out_far=2,
    )
    shapes = [
        (units, width), (width, units), (local, width), (width, local),
        (2 * width, local), (local, width), (3 * width, local),
    ]
    pieces = gradient_parts(shapes, share, heads, bits)
    (layer_out, grad_mid, small, g_ffn_out, g_ffn_in, g_cross_out, cross_grad, *away) = run_middle(
        pieces, norm_gain, norm_bias,
        [first_out, out_grad, cross_ctx, w_cross_out, far_cross_out, w_ffn_in, far_ffn_in,
         w_ffn_out, far_ffn_out], units,
    )
    arrived = [
        lax.ppermute(value, "rows", [(r, r ^ (1 << bit)) for r in range(size)])
        for bit, value in enumerate(away)
    ]
    flat = vm(BF16, length, local)
    gq, cross_sk, cross_sv, g_cross_kv, layer_out = call(
        cross_back_fast,
        [low(length, local), low(length, local), low(length, local), low(2, width, local), full(share, width)],
        [flat, flat, wide_scratch, wide_scratch, wide_scratch, vm(BF16, length, width),
         vm(F32, share, width), wide_scratch, vm(F32, heads, HEAD_DIM, length),
         vm(BF16, heads, HEAD_DIM, length), vm(BF16, local, heads * LANES), flat, flat, flat,
         pltpu.SemaphoreType.DMA((7,)), pltpu.SemaphoreType.DMA((4,))],
        0, dec_lengths, enc_lengths, cross_grad, cross_ctx, cross_kx, cross_vx, cross_qx, enc_output,
        layer_out, smem=2, far=7, out_places=(0, 1, 2, 4),
    )
    *sums, small, in_keep, in_land, enc_keep, enc_land = run_tail(
        pieces, norm_gain, small,
        [gq, grad_mid, first_low, first_normed, first_dev, w_cross_q, far_cross_q, far_ctx,
         w_self_out, far_self_out, self_qx, self_kx, self_vx, self_ctx, dec_input, w_self_qkv,
         cross_sk, cross_sv, w_cross_kv],
        [g_ffn_out, g_ffn_in, g_cross_out, g_cross_kv.reshape(2 * width, local), *arrived],
        shapes,
    )
    (s_ffn_out, s_ffn_in, s_cross_out, s_cross_q, s_cross_kv, s_self_out, s_self_qkv,
     input_grad, enc_grad, gain_grad, bias_grad) = widen_all(
        small, [(value, None) for value in sums] + [(in_keep, in_land), (enc_keep, enc_land)]
    )
    return (
        layer_out, input_grad, enc_grad, s_self_qkv.reshape(3, width, local), s_self_out, s_cross_q,
        s_cross_kv.reshape(2, width, local), s_cross_out, s_ffn_in, s_ffn_out, gain_grad, bias_grad,
    )


def body(*args):
    dec_input, w_self_out, w_ffn_in = args[0], args[5], args[9]
    if fits_tail(*dec_input.shape, w_self_out.shape[0], w_ffn_in.shape[1]):
        return fast_body(*args)
    return plain_body(*args)


def plain_body(
    dec_input,
    enc_output,
    dec_lengths,
    enc_lengths,
    w_self_qkv,
    w_self_out,
    w_cross_q,
    w_cross_kv,
    w_cross_out,
    w_ffn_in,
    w_ffn_out,
    norm_gain,
    norm_bias,
    out_grad,
):
    parts = lax.axis_size("heads")
    length, width = dec_input.shape
    local = w_self_out.shape[0]
    heads = local // HEAD_DIM
    share = length // parts
    units = w_ffn_in.shape[1]
    chunk = min(256, units)
    chunks = parts * units // chunk

    def shift(value, k):
        return lax.ppermute(value, "heads", [(d, (d + k) % parts) for d in range(parts)])

    def slots(shard):
        return [shard] + [shift(shard, parts - k) for k in range(1, parts)]

    def swap(keep, send):
        return [keep] + [shift(send[parts - k - 1], parts - k) for k in range(1, parts)]

    def collect(keep, send):
        total = keep.astype(F32)
        for k in range(1, parts):
            total = total + shift(send[k - 1], k).astype(F32)
        return total

    self_out, cross_q, cross_out = slots(w_self_out), slots(w_cross_q), slots(w_cross_out)
    ffn_in, ffn_out = slots(w_ffn_in), slots(w_ffn_out)

    def sent(*dims, kind=BF16):
        return shape_of((parts - 1, *dims), kind)

    def own(*dims, kind=BF16):
        return shape_of(dims, kind)

    wide_heads = own(heads, length, LANES)
    self_keep, self_send, self_ctx, self_qx, self_kx, self_vx = call(
        self_forward_kernel,
        [own(share, local), sent(share, local), own(length, local), wide_heads, wide_heads, wide_heads],
        [], 40, dec_lengths, dec_input, w_self_qkv, smem=1,
    )
    self_slots = swap(self_keep, self_send)
    cross_kx, cross_vx = call(
        cross_keys_kernel, [wide_heads, wide_heads], [], 32,
        enc_lengths, enc_output, w_cross_kv, smem=1,
    )
    first_out, first_low, first_normed, first_dev, query_keep, query_send = call(
        functools.partial(first_norm_kernel, parts),
        [own(share, width, kind=F32), own(share, width), own(share, width, kind=F32),
         own(share, 1, kind=F32), own(share, local), sent(share, local)],
        [], 32, dec_input, norm_gain, norm_bias, *self_slots, *self_out, *cross_q,
    )
    cross_keep, cross_send, cross_ctx, cross_qx = call(
        functools.partial(cross_forward_kernel, parts),
        [own(share, local), sent(share, local), own(length, local), wide_heads],
        [pltpu.VMEM((length, local), BF16)], 40,
        dec_lengths, enc_lengths, cross_kx, cross_vx, *swap(query_keep, query_send), smem=2,
    )
    cross_slots = swap(cross_keep, cross_send)
    (layer_out, grad_mid, gains_high, biases_high, g_ffn_out, g_ffn_out_send, g_ffn_in,
     g_ffn_in_send, g_cross_out, g_cross_out_send, back_keep, back_send) = call(
        functools.partial(middle_kernel, parts),
        [own(share, width, kind=F32), own(share, width, kind=F32),
         own(2, width, kind=F32), own(2, width, kind=F32),
         own(units, width), sent(units, width), own(width, units), sent(width, units),
         own(local, width), sent(local, width), own(share, local), sent(share, local)],
        [pltpu.VMEM((share, width), F32), pltpu.VMEM((share, width), BF16),
         pltpu.VMEM((share, width), F32), pltpu.VMEM((share, 1), F32),
         pltpu.VMEM((share, width), F32), pltpu.VMEM((chunks, share, chunk), BF16),
         pltpu.VMEM((chunks, share, chunk), F32), pltpu.VMEM((share, width), BF16),
         pltpu.VMEM((share, width), F32)],
        56, norm_gain, norm_bias, first_out, out_grad,
        *cross_slots, *cross_out, *ffn_in, *ffn_out,
    )
    grad_slots = swap(back_keep, back_send)
    back_scratch = [
        pltpu.VMEM((length, local), BF16),
        pltpu.VMEM((heads, length, LANES), BF16),
        pltpu.VMEM((heads, HEAD_DIM, length), F32),
        pltpu.VMEM((heads, HEAD_DIM, length), BF16),
        pltpu.VMEM((local, heads * LANES), BF16),
        pltpu.VMEM((length, local), BF16),
        pltpu.VMEM((length, local), BF16),
        pltpu.VMEM((length, local), BF16),
        pltpu.VMEM((length, width), F32),
    ]
    gq_keep, gq_send, g_cross_kv, enc_keep, enc_send = call(
        functools.partial(cross_back_kernel, len(grad_slots)),
        [own(share, local), sent(share, local), own(2, width, local),
         own(share, width, kind=F32), sent(share, width)],
        back_scratch, 56, dec_lengths, enc_lengths, cross_qx, cross_kx, cross_vx, cross_ctx,
        enc_output, w_cross_kv, *grad_slots, smem=2,
    )
    enc_grad = collect(enc_keep, enc_send)
    (grad_base, gains_low, biases_low, g_cross_q, g_cross_q_send, g_self_out, g_self_out_send,
     self_back_keep, self_back_send) = call(
        functools.partial(first_back_kernel, parts),
        [own(share, width, kind=F32), own(1, width, kind=F32), own(1, width, kind=F32),
         own(width, local), sent(width, local), own(local, width), sent(local, width),
         own(share, local), sent(share, local)],
        [pltpu.VMEM((share, width), BF16)], 40,
        norm_gain, grad_mid, first_low, first_normed, first_dev,
        *swap(gq_keep, gq_send), *cross_q, *self_slots, *self_out,
    )
    g_self_qkv, in_keep, in_send = call(
        functools.partial(self_back_kernel, parts),
        [own(3, width, local), own(share, width, kind=F32), sent(share, width)],
        back_scratch, 56, dec_lengths, self_qx, self_kx, self_vx, self_ctx, dec_input,
        w_self_qkv, *swap(self_back_keep, self_back_send), smem=1,
    )
    input_grad = grad_base + collect(in_keep, in_send)

    def over_rows(value):
        return lax.psum(value.astype(BF16), "rows").astype(F32)

    return (
        layer_out,
        input_grad,
        enc_grad,
        over_rows(g_self_qkv),
        over_rows(collect(g_self_out, g_self_out_send)),
        over_rows(collect(g_cross_q, g_cross_q_send)),
        over_rows(g_cross_kv),
        over_rows(collect(g_cross_out, g_cross_out_send)),
        over_rows(collect(g_ffn_in, g_ffn_in_send)),
        over_rows(collect(g_ffn_out, g_ffn_out_send)),
        lax.psum(jnp.concatenate([gains_low, gains_high]), ("rows", "heads")),
        lax.psum(jnp.concatenate([biases_low, biases_high]), ("rows", "heads")),
    )


def solution(mesh):
    in_specs = (
        P("rows", None),
        P("rows", None),
        P("rows", None),
        P("rows", None),
        P(None, None, "heads"),
        P("heads", None),
        P(None, "heads"),
        P(None, None, "heads"),
        P("heads", None),
        P(None, "heads"),
        P("heads", None),
        P(),
        P(),
        P("rows", None),
    )
    out_specs = (
        P(("rows", "heads"), None),
        P(("rows", "heads"), None),
        P(("rows", "heads"), None),
        P(None, None, "heads"),
        P("heads", None),
        P(None, "heads"),
        P(None, None, "heads"),
        P("heads", None),
        P(None, "heads"),
        P("heads", None),
        P(),
        P(),
    )
    return jax.shard_map(body, mesh=mesh, in_specs=in_specs, out_specs=out_specs, check_vma=False)
```

```python
import functools

import jax
import jax.numpy as jnp
from jax import lax
from jax.experimental import pallas as pl
from jax.experimental.pallas import tpu as pltpu
from jax.sharding import PartitionSpec as P

HEAD_DIM = 64
LANES = 128
SPAN = 256
KEY_SPAN = 512
CROSS_SPAN = 256
BACK_SPAN = 256
VMEM_BYTES = 2**26 - 2**17
NORM_EPS = 1e-05
MASKED_SCORE = -1e30
LOG2_E = 1.4426950408889634
GELU_RATE = 0.7978845608028654
GELU_CUBE = 0.044715
F32 = jnp.float32
BF16 = jnp.bfloat16
NT = (((1,), (1,)), ((), ()))
TN = (((0,), (0,)), ((), ()))
VMEM = pl.BlockSpec(memory_space=pltpu.VMEM)
SMEM = pl.BlockSpec(memory_space=pltpu.SMEM)


def dot(left, right):
    return jnp.dot(left, right, preferred_element_type=F32)


def dot_nt(left, right):
    return lax.dot_general(left, right, NT, preferred_element_type=F32)


def dot_tn(left, right):
    return lax.dot_general(left, right, TN, preferred_element_type=F32)


def shape_of(dims, kind):
    return jax.ShapeDtypeStruct(dims, kind)


def call(kernel, outs, scratch, mib, *args, smem=0, far=0, out_far=0, out_places=()):
    anyspace = pl.BlockSpec(memory_space=pl.ANY)
    return pl.pallas_call(
        kernel,
        out_shape=outs,
        in_specs=[SMEM] * smem + [VMEM] * (len(args) - smem - far) + [anyspace] * far,
        out_specs=[
            anyspace if k in out_places or k >= len(outs) - out_far else VMEM for k in range(len(outs))
        ],
        scratch_shapes=scratch,
        compiler_params=pltpu.CompilerParams(vmem_limit_bytes=VMEM_BYTES),
        cost_estimate=pl.CostEstimate(flops=2 * 10**10, bytes_accessed=2 * 10**7, transcendentals=0),
    )(*args)


def unrolled(count, body):
    for index in range(count):
        body(index, 0)


def segment_bounds(len_ref):
    starts, ends, total = [], [], jnp.int32(0)
    for k in range(len_ref.shape[1]):
        starts.append(total)
        total = total + len_ref[0, k]
        ends.append(total)
    return starts, ends


def bound_lanes(starts, ends):
    lane = lax.broadcasted_iota(jnp.int32, (1, LANES), 1)
    first = jnp.full((1, LANES), 1 << 30, jnp.int32)
    last = jnp.zeros((1, LANES), jnp.int32)
    for k, (start, end) in enumerate(zip(starts, ends)):
        first = jnp.where(lane == HEAD_DIM + k, start, first)
        last = jnp.where(lane == HEAD_DIM + k, end, last)
    return first, last


def lanes_of(rows):
    return lax.broadcasted_iota(jnp.int32, (rows, LANES), 1)


def membership(first_row, rows, bounds):
    place = lax.broadcasted_iota(jnp.int32, (rows, LANES), 0) + first_row
    return (place >= bounds[0]) & (place < bounds[1])


def query_extra(first_row, rows, bounds):
    return jnp.where(membership(first_row, rows, bounds), F32(MASKED_SCORE), F32(0.0))


def key_extra(first_row, rows, bounds, segs):
    lane = lanes_of(rows)
    used = (lane >= HEAD_DIM) & (lane < HEAD_DIM + segs + 3)
    return jnp.where(used & ~membership(first_row, rows, bounds), F32(1.0), F32(0.0))


def value_extra(rows):
    return jnp.full((rows, LANES), 1.0, F32)


def head_slab(wide, head):
    if wide.shape[1] < LANES:
        return jnp.concatenate([wide, jnp.zeros_like(wide)], axis=1)
    first = head // 2 * LANES
    slab = wide[:, first : first + LANES]
    if head % 2:
        slab = pltpu.roll(slab, HEAD_DIM, 1)
    return slab


def put_heads(dest, where, wide, extra):
    low_lanes = lanes_of(wide.shape[0]) < HEAD_DIM
    for head in range(dest.shape[0]):
        dest[head, where, :] = jnp.where(low_lanes, head_slab(wide, head), extra).astype(dest.dtype)


def join_heads(dest, where, slabs):
    if len(slabs) == 1:
        dest[where, :] = slabs[0][:, :HEAD_DIM].astype(dest.dtype)
        return
    low_lanes = lanes_of(slabs[0].shape[0]) < HEAD_DIM
    for pair in range(len(slabs) // 2):
        both = jnp.where(low_lanes, slabs[2 * pair], pltpu.roll(slabs[2 * pair + 1], HEAD_DIM, 1))
        dest[where, pair * LANES : (pair + 1) * LANES] = both.astype(dest.dtype)


def span_for(block, size, length, from_starts, to_starts, to_ends):
    first_row = block * size
    last_row = first_row + size - 1
    low, high = jnp.int32(0), jnp.int32(0)
    for start, to_start, to_end in zip(from_starts, to_starts, to_ends):
        low = jnp.where(start <= first_row, to_start, low)
        high = jnp.where(start <= last_row, to_end, high)
    low = (low >> 7) << 7
    pieces = (high - low + SPAN - 1) >> 8
    return jnp.minimum(low, length - pieces * SPAN), pieces


def each_span(length, starts_from, starts_to, ends_to, body, after=None, size=SPAN):
    def step(block, carry):
        start, pieces = span_for(block, size, length, starts_from, starts_to, ends_to)
        start = pl.multiple_of(start, LANES)
        rows = pl.ds(pl.multiple_of(block * size, size), size)
        for count in range(1, length // SPAN + 1):

            @pl.when(pieces == count)
            def _():
                body(rows, pl.ds(start, count * SPAN))

        if after is not None:
            after(block, rows)
        return carry

    lax.fori_loop(0, length // size, step, 0)


def merge_head(dest, rows, head, slab):
    if dest.shape[1] < LANES:
        dest[rows, :] = slab[:, :HEAD_DIM].astype(dest.dtype)
        return
    odd = (head & 1) == 1
    low_lanes = lanes_of(slab.shape[0]) < HEAD_DIM
    cols = pl.ds(pl.multiple_of((head >> 1) * LANES, LANES), LANES)
    old = dest[rows, cols].astype(F32)
    first = jnp.where(odd, old, slab)
    second = jnp.where(odd, pltpu.roll(slab, HEAD_DIM, 1), slab)
    dest[rows, cols] = jnp.where(low_lanes, first, second).astype(dest.dtype)


def attend_body(qx, kx, vx, ctx, segs, rows, keys):
    scale = LOG2_E * HEAD_DIM**-0.5
    base = HEAD_DIM + segs
    lane = lanes_of(rows.size)
    slabs = []
    for head in range(qx.shape[0]):
        query = qx[head, rows, :]
        scores = dot_nt(query, kx[head, keys, :])
        peak = jnp.max(scores, axis=1, keepdims=True)
        raised = jnp.exp2((scores - peak) * scale).astype(BF16)
        mixed = dot(raised, vx[head, keys, :])
        total = jnp.where(lane < HEAD_DIM, 1.0, mixed)
        slabs.append(mixed * pltpu.roll(1.0 / total, HEAD_DIM, 1))
        level = -(peak + jnp.log(total) * (HEAD_DIM**0.5))
        high = level.astype(BF16).astype(F32)
        middle = (level - high).astype(BF16).astype(F32)
        low = level - high - middle
        wide = query.astype(F32)
        wide = jnp.where(lane == base, high, wide)
        wide = jnp.where(lane == base + 1, middle, wide)
        wide = jnp.where(lane == base + 2, low, wide)
        qx[head, rows, :] = wide.astype(BF16)
    join_heads(ctx, rows, slabs)


def split_out(source, keep, send, share):
    me = lax.axis_index("heads")
    parts = send.shape[0] + 1
    for k in range(parts):
        owner = lax.rem(me + k, parts)
        rows = pl.ds(pl.multiple_of(owner * share, share), share)
        if k == 0:
            keep[...] = source[rows, :].astype(keep.dtype)
        else:
            send[k - 1] = source[rows, :].astype(send.dtype)


def self_forward_kernel(len_ref, x_ref, w_ref, keep, send, ctx, qx, kx, vx):
    length = x_ref.shape[0]
    segs = len_ref.shape[1]
    starts, ends = segment_bounds(len_ref)
    bounds = bound_lanes(starts, ends)

    def project(block, carry):
        first = pl.multiple_of(block * SPAN, SPAN)
        rows = pl.ds(first, SPAN)
        tokens = x_ref[rows, :]
        put_heads(qx, rows, dot(tokens, w_ref[0]), query_extra(first, SPAN, bounds))
        put_heads(kx, rows, dot(tokens, w_ref[1]), key_extra(first, SPAN, bounds, segs))
        put_heads(vx, rows, dot(tokens, w_ref[2]), value_extra(SPAN))
        return carry

    lax.fori_loop(0, length // SPAN, project, 0)
    each_span(
        length, starts, starts, ends, functools.partial(attend_body, qx, kx, vx, ctx, segs)
    )
    split_out(ctx, keep, send, keep.shape[0])


def cross_keys_kernel(len_ref, x_ref, w_ref, kx, vx):
    length = x_ref.shape[0]
    bounds = bound_lanes(*segment_bounds(len_ref))
    segs = len_ref.shape[1]

    def project(block, carry):
        first = pl.multiple_of(block * SPAN, SPAN)
        rows = pl.ds(first, SPAN)
        tokens = x_ref[rows, :]
        put_heads(kx, rows, dot(tokens, w_ref[0]), key_extra(first, SPAN, bounds, segs))
        put_heads(vx, rows, dot(tokens, w_ref[1]), value_extra(SPAN))
        return carry

    lax.fori_loop(0, length // SPAN, project, 0)


def gather_rows(dest, own, others):
    me = lax.axis_index("heads")
    parts = len(others) + 1
    share = own.shape[0]
    for k, source in enumerate([own, *others]):
        owner = lax.rem(me + k, parts)
        dest[pl.ds(pl.multiple_of(owner * share, share), share), :] = source[...]


def cross_forward_kernel(parts, dec_ref, enc_ref, kx, vx, *refs):
    pieces, (keep, send, ctx, qx, flat) = refs[:parts], refs[parts:]
    length = ctx.shape[0]
    segs = dec_ref.shape[1]
    dec_starts, dec_ends = segment_bounds(dec_ref)
    enc_starts, enc_ends = segment_bounds(enc_ref)
    bounds = bound_lanes(dec_starts, dec_ends)
    gather_rows(flat, pieces[0], pieces[1:])

    def widen(block, carry):
        first = pl.multiple_of(block * SPAN, SPAN)
        rows = pl.ds(first, SPAN)
        put_heads(qx, rows, flat[rows, :].astype(F32), query_extra(first, SPAN, bounds))
        return carry

    lax.fori_loop(0, length // SPAN, widen, 0)
    each_span(
        length, dec_starts, enc_starts, enc_ends,
        functools.partial(attend_body, qx, kx, vx, ctx, segs),
    )
    split_out(ctx, keep, send, keep.shape[0])


def row_store(source, dest, rows, sem, block, heads):
    where = (slice(None), rows, slice(None)) if heads else (rows, slice(None))
    return pltpu.make_async_copy(source.at[where], dest.at[where], sem.at[block])


def self_forward_fast(len_ref, x_ref, w_ref, ctx_out, qx_out, kx_out, vx_out, ctx, qx, kx, vx, sems, far):
    length = x_ref.shape[0]
    segs = len_ref.shape[1]
    starts, ends = segment_bounds(len_ref)
    bounds = bound_lanes(starts, ends)

    def project(block, carry):
        first = pl.multiple_of(block * SPAN, SPAN)
        rows = pl.ds(first, SPAN)
        tokens = x_ref[rows, :]
        put_heads(qx, rows, dot(tokens, w_ref[0]), query_extra(first, SPAN, bounds))
        put_heads(kx, rows, dot(tokens, w_ref[1]), key_extra(first, SPAN, bounds, segs))
        put_heads(vx, rows, dot(tokens, w_ref[2]), value_extra(SPAN))
        return carry

    unrolled(length // SPAN, project)
    whole = [pltpu.make_async_copy(kx, kx_out, far.at[0]), pltpu.make_async_copy(vx, vx_out, far.at[1])]
    for copy in whole:
        copy.start()

    def after(block, rows):
        row_store(ctx, ctx_out, rows, sems.at[0], block, False).start()
        row_store(qx, qx_out, rows, sems.at[1], block, True).start()

    each_span(
        length, starts, starts, ends, functools.partial(attend_body, qx, kx, vx, ctx, segs), after
    )
    for block in range(length // SPAN):
        rows = pl.ds(block * SPAN, SPAN)
        row_store(ctx, ctx_out, rows, sems.at[0], block, False).wait()
        row_store(qx, qx_out, rows, sems.at[1], block, True).wait()
    for copy in whole:
        copy.wait()


def cross_forward_fast(dec_ref, enc_ref, flat, kx_in, vx_in, ctx_out, qx_out, ctx, qx, kx, vx, sems, far):
    length = ctx.shape[0]
    segs = dec_ref.shape[1]
    loads = [pltpu.make_async_copy(kx_in, kx, far.at[0]), pltpu.make_async_copy(vx_in, vx, far.at[1])]
    for load in loads:
        load.start()
    dec_starts, dec_ends = segment_bounds(dec_ref)
    enc_starts, enc_ends = segment_bounds(enc_ref)
    bounds = bound_lanes(dec_starts, dec_ends)

    def widen(block, carry):
        first = pl.multiple_of(block * SPAN, SPAN)
        rows = pl.ds(first, SPAN)
        put_heads(qx, rows, flat[rows, :].astype(F32), query_extra(first, SPAN, bounds))
        return carry

    unrolled(length // SPAN, widen)
    for load in loads:
        load.wait()

    def after(block, rows):
        row_store(ctx, ctx_out, rows, sems.at[0], block, False).start()
        row_store(qx, qx_out, rows, sems.at[1], block, True).start()

    each_span(
        length, dec_starts, enc_starts, enc_ends,
        functools.partial(attend_body, qx, kx, vx, ctx, segs), after, CROSS_SPAN,
    )
    for block in range(length // CROSS_SPAN):
        rows = pl.ds(block * CROSS_SPAN, CROSS_SPAN)
        row_store(ctx, ctx_out, rows, sems.at[0], block, False).wait()
        row_store(qx, qx_out, rows, sems.at[1], block, True).wait()


def core_half(core, share):
    return pl.ds(pl.multiple_of(core * share, share), share)


def entry_remote_kernel(enc_ref, gain, bias, *refs):
    rest = list(refs)
    take = lambda number: [rest.pop(0) for _ in range(number)]
    x_in, enc_in, w_kv_in, ctx_in, wo_in, wq_in, far_cross, far_in, far_out = take(9)
    first_out, first_low, normed_out, dev_out, q_out, kx_out, vx_out, ctx_far, wo_far, wq_far = take(10)
    away_cross, away_in, away_out = take(3)
    x, enc, w_kv, ctx0, ctx1, wo0, wo1, wq0, wq1 = take(9)
    first, low, normed, q_own, q_gone, kx, vx = take(7)
    load_sem, store_sem, core_send, core_land = rest
    share, width = first.shape
    length = enc.shape[0]
    block = 256
    segs = enc_ref.shape[1]
    core = lax.axis_index("heads")
    other = {"rows": lax.axis_index("rows"), "heads": 1 - core}
    mine, theirs = core_half(core, share), core_half(1 - core, share)

    def across(number, source, dest):
        return pltpu.make_async_remote_copy(
            src_ref=source, dst_ref=dest, send_sem=core_send.at[number], recv_sem=core_land.at[number],
            device_id=other, device_id_type=pl.DeviceIdType.MESH,
        )

    moves = [(enc_in, enc), (w_kv_in, w_kv), (x_in.at[mine, :], x), (ctx_in.at[mine, :], ctx0), (wo_in, wo0), (wq_in, wq0)]
    loads = [pltpu.make_async_copy(a, b, load_sem.at[k]) for k, (a, b) in enumerate(moves)]
    barrier = pltpu.get_barrier_semaphore()
    pl.semaphore_signal(barrier, inc=1, device_id=other, device_id_type=pl.DeviceIdType.MESH)
    for load in loads:
        load.start()
    pl.semaphore_wait(barrier, 1)
    exchange = [
        across(0, ctx_in.at[theirs, :], ctx1), across(1, wo_in, wo1), across(2, wq_in, wq1),
        across(3, far_cross, away_cross), across(4, far_in, away_in), across(5, far_out, away_out),
    ]
    for copy in exchange:
        copy.start()
    bounds = bound_lanes(*segment_bounds(enc_ref))
    for load in loads[:2]:
        load.wait()

    def project(index, carry):
        top = pl.multiple_of(index * SPAN, SPAN)
        rows = pl.ds(top, SPAN)
        tokens = enc[rows, :]
        put_heads(kx, rows, dot(tokens, w_kv[0]), key_extra(top, SPAN, bounds, segs))
        put_heads(vx, rows, dot(tokens, w_kv[1]), value_extra(SPAN))
        return carry

    unrolled(length // SPAN, project)
    stores = []

    def store(source, dest):
        stores.append(pltpu.make_async_copy(source, dest, store_sem.at[len(stores)]))
        stores[-1].start()

    store(kx, kx_out)
    store(vx, vx_out)
    for load in loads[2:]:
        load.wait()
    for copy in exchange[:3]:
        copy.wait()
    store(ctx1, ctx_far)
    store(wo1, wo_far)
    store(wq1, wq_far)
    copies = []
    for index in range(share // block):
        rows = pl.ds(index * block, block)
        total = x[rows, :].astype(F32) + dot(ctx0[rows, :], wo0[...]) + dot(ctx1[rows, :], wo1[...])
        result, spread, inverse_dev = norm_forward(total, gain[0:1, :], bias[0:1, :])
        low_part = result.astype(BF16)
        first[rows, :] = result
        low[rows, :] = low_part
        normed[rows, :] = spread
        dev_out[rows, :] = inverse_dev
        q_gone[rows, :] = dot(low_part, wq1[...]).astype(BF16)
        here = own_rows(share, index * block, block)
        copies.append(across(6 + index, q_gone.at[rows, :], q_out.at[here, :]))
        copies[-1].start()
        q_own[rows, :] = dot(low_part, wq0[...]).astype(BF16)
        store(q_own.at[rows, :], q_out.at[here, :])
        store(first.at[rows, :], first_out.at[rows, :])
        store(low.at[rows, :], first_low.at[rows, :])
        store(normed.at[rows, :], normed_out.at[rows, :])
    for copy in exchange[3:] + copies:
        copy.wait()
    for copy in stores:
        copy.wait()


def run_entry(enc_lengths, gain, bias, args):
    length, width = args[0].shape
    local = args[4].shape[0]
    share, heads, units = length // 2, local // HEAD_DIM, args[7].shape[1]
    vm = lambda kind, *dims: pltpu.VMEM(dims, kind)
    wide_heads = (heads, length, LANES)
    blocks = share // 256
    anyspace = pl.BlockSpec(memory_space=pl.ANY)
    return pl.pallas_call(
        entry_remote_kernel,
        out_shape=[
            shape_of((share, width), F32), shape_of((share, width), BF16), shape_of((share, width), F32),
            shape_of((share, 1), F32), shape_of((length, local), BF16),
            shape_of(wide_heads, BF16), shape_of(wide_heads, BF16),
            shape_of((share, local), BF16), shape_of((local, width), BF16), shape_of((width, local), BF16),
            shape_of((local, width), BF16), shape_of((width, units), BF16), shape_of((units, width), BF16),
        ],
        in_specs=[SMEM, VMEM, VMEM] + [anyspace] * len(args),
        out_specs=[anyspace] * 3 + [VMEM] + [anyspace] * 9,
        scratch_shapes=[
            vm(BF16, share, width), vm(BF16, length, width), vm(BF16, 2, width, local),
            vm(BF16, share, local), vm(BF16, share, local), vm(BF16, local, width), vm(BF16, local, width),
            vm(BF16, width, local), vm(BF16, width, local),
            vm(F32, share, width), vm(BF16, share, width), vm(F32, share, width),
            vm(BF16, share, local), vm(BF16, share, local), vm(BF16, *wide_heads), vm(BF16, *wide_heads),
        ] + [pltpu.SemaphoreType.DMA((n,)) for n in (6, 5 + 4 * blocks, 6 + blocks, 6 + blocks)],
        compiler_params=pltpu.CompilerParams(
            vmem_limit_bytes=VMEM_BYTES, collective_id=2, has_side_effects=True
        ),
    )(enc_lengths, gain, bias, *args)


def attend_back_body(qx, kx, vx, gx, dq, kt, dk, dv, rows, queries):
    heads = qx.shape[0]
    group = 2 if heads % 2 == 0 else 1

    def unit(index, carry):
        for k in range(group):
            back_unit(qx, kx, vx, gx, dq, kt, dk, dv, group * index + k, rows, queries)
        return carry

    lax.fori_loop(0, heads // group, unit, 0)


def head_sums(width, heads):
    row = lax.broadcasted_iota(jnp.int32, (width, heads * LANES), 0)
    col = lax.broadcasted_iota(jnp.int32, (width, heads * LANES), 1)
    lane = col & (LANES - 1)
    hit = ((row >> 6) == (col >> 7)) & (lane >= HEAD_DIM) & (lane < HEAD_DIM + 2)
    return jnp.where(hit, F32(1.0), F32(0.0)).astype(BF16)


def prepare_back(grad, ctx, kx, gx, dq, kt, sums):
    heads = gx.shape[0]
    lane = lanes_of(SPAN)

    def widen(block, carry):
        rows = pl.ds(pl.multiple_of(block * SPAN, SPAN), SPAN)
        wide = grad[rows, :].astype(F32)
        product = wide * ctx[rows, :].astype(F32)
        high = product.astype(BF16)
        low = (product - high.astype(F32)).astype(BF16)
        totals = dot(high, sums[...]) + dot(low, sums[...])
        for head in range(heads):
            level = -totals[:, head * LANES : (head + 1) * LANES]
            rounded = level.astype(BF16).astype(F32)
            extra = jnp.where(lane == HEAD_DIM + 1, level - rounded, rounded)
            full = jnp.where(lane < HEAD_DIM, head_slab(wide, head), extra)
            gx[head, rows, :] = full.astype(BF16)
            dq[head, :, rows] = jnp.zeros((HEAD_DIM, SPAN), F32)
            kt[head, :, rows] = kx[head, rows, :].astype(F32).T[:HEAD_DIM].astype(BF16)
        return carry

    unrolled(grad.shape[0] // SPAN, widen)


def turn_queries(dq, sq, pairs):
    length = sq.shape[0]

    def finish(block, carry):
        rows = pl.ds(pl.multiple_of(block * SPAN, SPAN), SPAN)
        for pair in pairs:
            if dq.shape[0] == 1:
                sq[rows, :] = (dq[0, :, rows].T * (HEAD_DIM**-0.5)).astype(BF16)
            else:
                both = jnp.concatenate([dq[2 * pair, :, rows], dq[2 * pair + 1, :, rows]], axis=0)
                sq[rows, pair * LANES : (pair + 1) * LANES] = (both.T * (HEAD_DIM**-0.5)).astype(BF16)
        return carry

    unrolled(length // SPAN, finish)


def attend_back(key_starts, key_ends, query_starts, query_ends, qx, kx, vx, ctx, grad, gx, dq, kt, sums, sq, sk, sv):
    length = ctx.shape[0]
    heads = qx.shape[0]
    sums[...] = head_sums(ctx.shape[1], heads)
    prepare_back(grad, ctx, kx, gx, dq, kt, sums)
    each_span(
        length, key_starts, query_starts, query_ends,
        functools.partial(attend_back_body, qx, kx, vx, gx, dq, kt, sk, sv),
    )
    turn_queries(dq, sq, range(max(1, heads // 2)))


def norm_forward(summed, gain, bias):
    center = summed - jnp.mean(summed, axis=1, keepdims=True)
    inverse_dev = lax.rsqrt(jnp.mean(center * center, axis=1, keepdims=True) + NORM_EPS)
    normed = center * inverse_dev
    return normed * gain + bias, normed, inverse_dev


def norm_back(grad, normed, inverse_dev, gain):
    scaled = grad * gain
    back = inverse_dev * (
        scaled
        - jnp.mean(scaled, axis=1, keepdims=True)
        - normed * jnp.mean(scaled * normed, axis=1, keepdims=True)
    )
    gain_grad = jnp.sum(grad * normed, axis=0, keepdims=True)
    return back, gain_grad, jnp.sum(grad, axis=0, keepdims=True)


def share_block(share):
    return 256 if share % 256 == 0 else share


def own_rows(share, first, rows):
    start = lax.axis_index("heads") * share + first
    return pl.ds(pl.multiple_of(start, 64), rows)


def first_norm_kernel(parts, x_ref, gain, bias, *refs):
    ctx, w_out, w_query = refs[:parts], refs[parts : 2 * parts], refs[2 * parts : 3 * parts]
    first_out, first_low, normed_out, dev_out, keep, send = refs[3 * parts :]
    share = first_out.shape[0]
    block = share_block(share)

    def step(index, carry):
        first = pl.multiple_of(index * block, block)
        rows = pl.ds(first, block)
        total = x_ref[own_rows(share, first, block), :].astype(F32)
        for k in range(parts):
            total = total + dot(ctx[k][rows, :], w_out[k][...])
        result, normed, inverse_dev = norm_forward(total, gain[0:1, :], bias[0:1, :])
        low = result.astype(BF16)
        first_out[rows, :] = result
        first_low[rows, :] = low
        normed_out[rows, :] = normed
        dev_out[rows, :] = inverse_dev
        for k in range(parts):
            value = dot(low, w_query[k][...]).astype(BF16)
            if k == 0:
                keep[rows, :] = value
            else:
                send[k - 1, rows, :] = value
        return carry

    lax.fori_loop(0, share // block, step, 0)


def middle_kernel(parts, gain, bias, first_out, out_grad, *refs):
    groups = [refs[g * parts : (g + 1) * parts] for g in range(4)]
    ctx, w_cross, w_in, w_out = groups
    (layer_out, grad_mid, gains, biases, g_out_keep, g_out_send, g_in_keep, g_in_send,
     g_cross_keep, g_cross_send, back_keep, back_send,
     second, second_low, normed2, dev2, total, hidden, slope, top_low, back_sum) = refs[4 * parts :]
    share = first_out.shape[0]
    block = share_block(share)
    units = w_in[0].shape[1]
    chunk = min(256, units)

    def enter(index, carry):
        rows = pl.ds(pl.multiple_of(index * block, block), block)
        summed = first_out[rows, :]
        for k in range(parts):
            summed = summed + dot(ctx[k][rows, :], w_cross[k][...])
        result, normed, inverse_dev = norm_forward(summed, gain[1:2, :], bias[1:2, :])
        second[rows, :] = result
        second_low[rows, :] = result.astype(BF16)
        normed2[rows, :] = normed
        dev2[rows, :] = inverse_dev
        return carry

    lax.fori_loop(0, share // block, enter, 0)
    total[...] = second[...]
    for k in range(parts):

        def expand(index, carry):
            cols = pl.ds(pl.multiple_of(index * chunk, chunk), chunk)
            spot = k * (units // chunk) + index
            pre = dot(second_low[...], w_in[k][:, cols])
            square = pre * pre
            bent = jnp.tanh(pre * (GELU_RATE + (GELU_RATE * GELU_CUBE) * square))
            half = 0.5 + 0.5 * bent
            act = (pre * half).astype(BF16)
            hidden[spot] = act
            bend = (0.5 - 0.5 * bent * bent) * (
                GELU_RATE + (3.0 * GELU_RATE * GELU_CUBE) * square
            )
            slope[spot] = half + pre * bend
            total[...] += dot(act, w_out[k][cols, :])
            return carry

        lax.fori_loop(0, units // chunk, expand, 0)

    gains[...] = jnp.zeros_like(gains)
    biases[...] = jnp.zeros_like(biases)

    def turn(index, carry):
        first = pl.multiple_of(index * block, block)
        rows = pl.ds(first, block)
        result, normed, inverse_dev = norm_forward(total[rows, :], gain[2:3, :], bias[2:3, :])
        layer_out[rows, :] = result
        grad = out_grad[own_rows(share, first, block), :].astype(F32)
        back, gain_grad, bias_grad = norm_back(grad, normed, inverse_dev, gain[2:3, :])
        gains[1:2, :] += gain_grad
        biases[1:2, :] += bias_grad
        back_sum[rows, :] = back
        top_low[rows, :] = back.astype(BF16)
        return carry

    lax.fori_loop(0, share // block, turn, 0)
    for k in range(parts):

        def contract(index, carry):
            cols = pl.ds(pl.multiple_of(index * chunk, chunk), chunk)
            spot = k * (units // chunk) + index
            weight_out = dot_tn(hidden[spot], top_low[...]).astype(BF16)
            pre = (dot_nt(top_low[...], w_out[k][cols, :]) * slope[spot]).astype(BF16)
            weight_in = dot_tn(second_low[...], pre).astype(BF16)
            if k == 0:
                g_out_keep[cols, :] = weight_out
                g_in_keep[:, cols] = weight_in
            else:
                g_out_send[k - 1, cols, :] = weight_out
                g_in_send[k - 1, :, cols] = weight_in
            back_sum[...] += dot_nt(pre, w_in[k][:, cols])
            return carry

        lax.fori_loop(0, units // chunk, contract, 0)

    def leave(index, carry):
        rows = pl.ds(pl.multiple_of(index * block, block), block)
        back, gain_grad, bias_grad = norm_back(
            back_sum[rows, :], normed2[rows, :], dev2[rows, :], gain[1:2, :]
        )
        gains[0:1, :] += gain_grad
        biases[0:1, :] += bias_grad
        grad_mid[rows, :] = back
        low = back.astype(BF16)
        top_low[rows, :] = low
        for k in range(parts):
            value = dot_nt(low, w_cross[k][...]).astype(BF16)
            if k == 0:
                back_keep[rows, :] = value
            else:
                back_send[k - 1, rows, :] = value
        return carry

    lax.fori_loop(0, share // block, leave, 0)
    for k in range(parts):
        value = dot_tn(ctx[k][...], top_low[...]).astype(BF16)
        if k == 0:
            g_cross_keep[...] = value
        else:
            g_cross_send[k - 1] = value


def middle_remote_kernel(parts, gain, bias, *refs):
    rest = list(refs)
    take = lambda number: [rest.pop(0) for _ in range(number)]
    first_in, top_in, ctx_in, wc0_in, wc1_in, wi0_in, wi1_in, wo0_in, wo1_in = take(9)
    layer_out, mid_out, small_out, sum_out, sum_in, sum_cross, cgrad_out = take(7)
    away_out = take(3)
    (first, top, ctx0, ctx1, wc0, wc1, wi0, wi1, wo0, wo1) = loaded = take(10)
    (second, second_low, normed2, dev2, total, hidden, slope, top_low, back_sum, layer, mid,
     own_out, land_out, gone_out, own_in, land_in, gone_in, own_cross, land_cross, gone_cross, own_back, gone_back) = take(22)
    load_sem, store_sem, part_sem, core_send, core_land = rest
    share, width = first.shape
    units = wi0.shape[1]
    block = 256
    chunk = hidden.shape[2]
    chunks = units // chunk
    core = lax.axis_index("heads")
    other = {"rows": lax.axis_index("rows"), "heads": 1 - core}
    mine = pl.ds(pl.multiple_of(core * share, share), share)
    w_in, w_out, w_cross, ctx = (wi0, wi1), (wo0, wo1), (wc0, wc1), (ctx0, ctx1)
    own_sends = {}

    def across(number, source, dest):
        copy = pltpu.make_async_remote_copy(
            src_ref=source, dst_ref=dest, send_sem=core_send.at[number], recv_sem=core_land.at[number],
            device_id=other, device_id_type=pl.DeviceIdType.MESH,
        )
        own_sends[number] = copy
        return copy

    sources = [first_in, top_in.at[mine, :], ctx_in.at[mine, :], None, wc0_in, wc1_in, wi0_in, wi1_in, wo0_in, wo1_in]
    loads = [
        None if source is None else pltpu.make_async_copy(source, dest, load_sem.at[k])
        for k, (source, dest) in enumerate(zip(sources, loaded))
    ]
    barrier = pltpu.get_barrier_semaphore()
    pl.semaphore_signal(barrier, inc=1, device_id=other, device_id_type=pl.DeviceIdType.MESH)
    for k in (0, 2, 4, 5, 6, 7, 8, 9, 1):
        loads[k].start()
    pl.semaphore_wait(barrier, 1)
    across(0, ctx_in.at[core_half(1 - core, share), :], ctx1).start()
    for k in (0, 2, 4, 5):
        loads[k].wait()
    own_sends[0].wait()

    def enter(index, carry):
        rows = pl.ds(pl.multiple_of(index * block, block), block)
        summed = first[rows, :] + dot(ctx0[rows, :], wc0[...]) + dot(ctx1[rows, :], wc1[...])
        result, normed, inverse_dev = norm_forward(summed, gain[1:2, :], bias[1:2, :])
        second[rows, :] = result
        second_low[rows, :] = result.astype(BF16)
        normed2[rows, :] = normed
        dev2[rows, :] = inverse_dev
        return carry

    unrolled(share // block, enter)
    total[...] = second[...]
    for k in range(2):
        loads[6 + k].wait()
        loads[8 + k].wait()

        def expand(index, carry):
            cols = pl.ds(pl.multiple_of(index * chunk, chunk), chunk)
            spot = k * chunks + index
            pre = dot(second_low[...], w_in[k][:, cols])
            square = pre * pre
            bent = jnp.tanh(pre * (GELU_RATE + (GELU_RATE * GELU_CUBE) * square))
            half = 0.5 + 0.5 * bent
            act = (pre * half).astype(BF16)
            hidden[spot] = act
            bend = (0.5 - 0.5 * bent * bent) * (
                GELU_RATE + (3.0 * GELU_RATE * GELU_CUBE) * square
            )
            slope[spot] = half + pre * bend
            total[...] += dot(act, w_out[k][cols, :])
            return carry

        unrolled(chunks, expand)
    loads[1].wait()
    small_out[...] = jnp.zeros_like(small_out)

    def turn(index, carry):
        rows = pl.ds(pl.multiple_of(index * block, block), block)
        result, normed, inverse_dev = norm_forward(total[rows, :], gain[2:3, :], bias[2:3, :])
        layer[rows, :] = result
        grad = top[rows, :].astype(F32)
        back, gain_grad, bias_grad = norm_back(grad, normed, inverse_dev, gain[2:3, :])
        small_out[2:3, :] += gain_grad
        small_out[5:6, :] += bias_grad
        back_sum[rows, :] = back
        top_low[rows, :] = back.astype(BF16)
        return carry

    unrolled(share // block, turn)
    stores = [pltpu.make_async_copy(layer, layer_out, store_sem.at[0])]
    stores[0].start()
    for k in (1, 0):
        weight_out, weight_in = (own_out, own_in) if k == 0 else (gone_out, gone_in)

        def contract(index, carry):
            cols = pl.ds(pl.multiple_of(index * chunk, chunk), chunk)
            spot = k * chunks + index
            weight_out[cols, :] = dot_tn(hidden[spot], top_low[...]).astype(BF16)
            pre = (dot_nt(top_low[...], w_out[k][cols, :]) * slope[spot]).astype(BF16)
            weight_in[:, cols] = dot_tn(second_low[...], pre).astype(BF16)
            back_sum[...] += dot_nt(pre, w_in[k][:, cols])
            return carry

        unrolled(chunks, contract)
        if k == 1:
            across(1, gone_out, land_out).start()
            across(2, gone_in, land_in).start()
    count = share // block
    for index in range(count):
        rows = pl.ds(index * block, block)
        back, gain_grad, bias_grad = norm_back(
            back_sum[rows, :], normed2[rows, :], dev2[rows, :], gain[1:2, :]
        )
        small_out[1:2, :] += gain_grad
        small_out[4:5, :] += bias_grad
        mid[rows, :] = back
        low = back.astype(BF16)
        top_low[rows, :] = low
        gone_back[rows, :] = dot_nt(low, wc1[...]).astype(BF16)
        across(
            4 + index, gone_back.at[rows, :], cgrad_out.at[own_rows(share, index * block, block), :]
        ).start()
        own_back[rows, :] = dot_nt(low, wc0[...]).astype(BF16)
    stores.append(pltpu.make_async_copy(mid, mid_out, store_sem.at[1]))
    stores.append(pltpu.make_async_copy(own_back, cgrad_out.at[mine, :], store_sem.at[2]))
    for store in stores[1:]:
        store.start()
    gone_cross[...] = dot_tn(ctx1[...], top_low[...]).astype(BF16)
    across(3, gone_cross, land_cross).start()
    own_sends[1].wait()
    add_into(own_out, land_out)
    stores.append(pltpu.make_async_copy(own_out, sum_out, store_sem.at[3]))
    stores[-1].start()
    own_sends[2].wait()
    add_into(own_in, land_in)
    stores.append(pltpu.make_async_copy(own_in, sum_in, store_sem.at[4]))
    stores[-1].start()
    for number, (part, bit, spot) in enumerate(parts):
        for source, dest in away_windows(part, bit, spot, (own_out, own_in)[part.out], away_out[bit]):
            stores.append(pltpu.make_async_copy(source, dest, part_sem.at[len(stores) - 5]))
            stores[-1].start()
    own_cross[...] = dot_tn(ctx0[...], top_low[...]).astype(BF16)
    own_sends[3].wait()
    add_into(own_cross, land_cross)
    stores.append(pltpu.make_async_copy(own_cross, sum_cross, store_sem.at[5]))
    stores[-1].start()
    for index in range(count):
        own_sends[4 + index].wait()
    for store in stores:
        store.wait()


def away_windows(part, bit, spot, source, dest):
    half = part.rows // 2
    side = lax.shift_right_logical(lax.axis_index("rows"), bit) & 1
    first = part.row + (1 - side) * half
    pairs = []
    for piece in range(half // 128):
        rows = pl.ds(pl.multiple_of(first + piece * 128, 128), 128)
        pairs.append((source.at[rows, pl.ds(part.col, part.cols)], dest.at[away_place(part, spot, piece)]))
    return pairs


def away_place(part, spot, piece):
    across = 512 // part.cols
    return (
        pl.ds((spot + piece // across) * 128, 128),
        pl.ds(piece % across * part.cols, part.cols),
    )


def first_steps(parts):
    filled = [0, 0, 0]
    found = []
    for part in parts:
        if part.out < 2:
            bit = part.order[0]
            found.append((part, bit, filled[bit]))
            filled[bit] += part.rows * part.cols // (2 * 128 * 512)
    return found, [128 * max(1, n) for n in filled]


def run_middle(parts, gain, bias, args, units):
    share, width = args[0].shape
    local = args[2].shape[1]
    found, heights = first_steps(parts)
    chunk = 1024 if units % 1024 == 0 else 512
    vm = lambda kind, *dims: pltpu.VMEM(dims, kind)
    token, token_low = vm(F32, share, width), vm(BF16, share, width)
    scratch = [
        token, token_low, vm(BF16, share, local), vm(BF16, share, local),
        vm(BF16, local, width), vm(BF16, local, width), vm(BF16, width, units), vm(BF16, width, units),
        vm(BF16, units, width), vm(BF16, units, width),
        token, token_low, token, vm(F32, share, 1), token,
        vm(BF16, 2 * units // chunk, share, chunk), vm(F32, 2 * units // chunk, share, chunk),
        token_low, token, token, token,
        *[vm(BF16, units, width)] * 3, *[vm(BF16, width, units)] * 3, *[vm(BF16, local, width)] * 3,
        vm(BF16, share, local), vm(BF16, share, local),
    ]
    sems = [10, 6, 4 * len(found), 4 + share // 256, 4 + share // 256]
    anyspace = pl.BlockSpec(memory_space=pl.ANY)
    return pl.pallas_call(
        functools.partial(middle_remote_kernel, found),
        out_shape=[
            shape_of((share, width), F32), shape_of((share, width), F32), shape_of((8, width), F32),
            shape_of((units, width), BF16), shape_of((width, units), BF16), shape_of((local, width), BF16),
            shape_of((2 * share, local), BF16), *[shape_of((h, width), BF16) for h in heights],
        ],
        in_specs=[VMEM] * 2 + [anyspace] * len(args),
        out_specs=[anyspace] * 2 + [VMEM] + [anyspace] * 7,
        scratch_shapes=scratch + [pltpu.SemaphoreType.DMA((n,)) for n in sems],
        compiler_params=pltpu.CompilerParams(
            vmem_limit_bytes=VMEM_BYTES, collective_id=1, has_side_effects=True
        ),
    )(gain, bias, *args)


def cross_back_kernel(parts, dec_ref, enc_ref, qx, kx, vx, ctx, enc, w_kv, *refs):
    pieces = refs[:parts]
    (gq_keep, gq_send, g_kv, enc_keep, enc_send, grad, gx, dq, kt, sums, sq, sk, sv, wide) = refs[parts:]
    length = ctx.shape[0]
    dec_starts, dec_ends = segment_bounds(dec_ref)
    enc_starts, enc_ends = segment_bounds(enc_ref)
    gather_rows(grad, pieces[0], pieces[1:])
    attend_back(
        enc_starts, enc_ends, dec_starts, dec_ends, qx, kx, vx, ctx, grad, gx, dq, kt, sums, sq, sk, sv
    )
    split_out(sq, gq_keep, gq_send, gq_keep.shape[0])
    g_kv[0] = dot_tn(enc[...], sk[...]).astype(BF16)
    g_kv[1] = dot_tn(enc[...], sv[...]).astype(BF16)

    def step(block, carry):
        rows = pl.ds(pl.multiple_of(block * SPAN, SPAN), SPAN)
        wide[rows, :] = dot_nt(sk[rows, :], w_kv[0]) + dot_nt(sv[rows, :], w_kv[1])
        return carry

    lax.fori_loop(0, length // SPAN, step, 0)
    split_out(wide, enc_keep, enc_send, enc_keep.shape[0])


def cross_back_fast(dec_ref, enc_ref, *refs):
    rest = list(refs)
    take = lambda number: [rest.pop(0) for _ in range(number)]
    sources = take(7)
    gq_out, sk_out, sv_out, g_kv, layer_out = take(5)
    loaded = take(7)
    grad, ctx, kx, vx, qx, enc, layer = loaded
    gx, dq, kt, sums, sq, sk, sv, load_sem, store_sem = rest
    length = ctx.shape[0]
    heads = qx.shape[0]
    loads = [pltpu.make_async_copy(a, b, load_sem.at[k]) for k, (a, b) in enumerate(zip(sources, loaded))]
    for load in loads:
        load.start()
    dec_starts, dec_ends = segment_bounds(dec_ref)
    enc_starts, enc_ends = segment_bounds(enc_ref)
    sums[...] = head_sums(ctx.shape[1], heads)
    for load in loads[:3]:
        load.wait()
    prepare_back(grad, ctx, kx, gx, dq, kt, sums)
    for load in loads[3:5]:
        load.wait()
    each_span(
        length, enc_starts, dec_starts, dec_ends,
        functools.partial(attend_back_body, qx, kx, vx, gx, dq, kt, sk, sv), None, BACK_SPAN,
    )
    for load in loads[5:]:
        load.wait()
    stores = [
        pltpu.make_async_copy(layer, layer_out, store_sem.at[0]),
        pltpu.make_async_copy(sk, sk_out, store_sem.at[1]),
        pltpu.make_async_copy(sv, sv_out, store_sem.at[2]),
        pltpu.make_async_copy(sq, gq_out, store_sem.at[3]),
    ]
    for store in stores[:3]:
        store.start()
    turn_queries(dq, sq, range(max(1, heads // 2)))
    stores[3].start()
    g_kv[0] = dot_tn(enc[...], sk[...]).astype(BF16)
    g_kv[1] = dot_tn(enc[...], sv[...]).astype(BF16)
    for store in stores:
        store.wait()


def first_back_kernel(parts, gain, grad_mid, first_low, normed, dev, *refs):
    groups = [refs[g * parts : (g + 1) * parts] for g in range(4)]
    gq, w_query, ctx, w_out = groups
    (grad_base, gains, biases, g_query_keep, g_query_send, g_out_keep, g_out_send,
     back_keep, back_send, low_ref) = refs[4 * parts :]
    share = grad_mid.shape[0]
    block = share_block(share)
    gains[...] = jnp.zeros_like(gains)
    biases[...] = jnp.zeros_like(biases)

    def step(index, carry):
        rows = pl.ds(pl.multiple_of(index * block, block), block)
        grad = grad_mid[rows, :]
        for k in range(parts):
            grad = grad + dot_nt(gq[k][rows, :], w_query[k][...])
        back, gain_grad, bias_grad = norm_back(grad, normed[rows, :], dev[rows, :], gain[0:1, :])
        gains[...] += gain_grad
        biases[...] += bias_grad
        grad_base[rows, :] = back
        low = back.astype(BF16)
        low_ref[rows, :] = low
        for k in range(parts):
            value = dot_nt(low, w_out[k][...]).astype(BF16)
            if k == 0:
                back_keep[rows, :] = value
            else:
                back_send[k - 1, rows, :] = value
        return carry

    lax.fori_loop(0, share // block, step, 0)
    for k in range(parts):
        query_grad = dot_tn(first_low[...], gq[k][...]).astype(BF16)
        out_grad = dot_tn(ctx[k][...], low_ref[...]).astype(BF16)
        if k == 0:
            g_query_keep[...] = query_grad
            g_out_keep[...] = out_grad
        else:
            g_query_send[k - 1] = query_grad
            g_out_send[k - 1] = out_grad


def self_back_kernel(parts, dec_ref, qx, kx, vx, ctx, x_ref, w_qkv, *refs):
    pieces = refs[:parts]
    g_qkv, in_keep, in_send, grad, gx, dq, kt, sums, sq, sk, sv, wide = refs[parts:]
    length = ctx.shape[0]
    starts, ends = segment_bounds(dec_ref)
    gather_rows(grad, pieces[0], pieces[1:])
    attend_back(starts, ends, starts, ends, qx, kx, vx, ctx, grad, gx, dq, kt, sums, sq, sk, sv)
    for c, source in enumerate((sq, sk, sv)):
        g_qkv[c] = dot_tn(x_ref[...], source[...]).astype(BF16)

    def step(block, carry):
        rows = pl.ds(pl.multiple_of(block * SPAN, SPAN), SPAN)
        wide[rows, :] = (
            dot_nt(sq[rows, :], w_qkv[0])
            + dot_nt(sk[rows, :], w_qkv[1])
            + dot_nt(sv[rows, :], w_qkv[2])
        )
        return carry

    lax.fori_loop(0, length // SPAN, step, 0)
    split_out(wide, in_keep, in_send, in_keep.shape[0])


LINK_RATE = 0.06
HOP_TIME = 3.0
TAKE_TIME = 0.05
ADD_RATE = 1.3
SEND_TIME = 0.03
SLACK = 0.5
FFN_PART = (256, 512)
AHEAD = 2.0
LAST_AHEAD = 3.0


class Part:
    def __init__(self, out, row, col, rows, cols, ready):
        self.out, self.row, self.col, self.rows, self.cols = out, row, col, rows, cols
        self.ready = ready
        self.order = None
        self.first = 0

    def window(self):
        return (pl.ds(self.row, self.rows), pl.ds(self.col, self.cols))


def step_shape(part, step, bits):
    depth = step if step < bits else 2 * bits - 2 - step
    return part.order[depth], part.rows >> min(depth + 1, bits - 1)


def link_cost(part, step, bits):
    bit, rows = step_shape(part, step, bits)
    amount = rows * part.cols * 2e-6 * 2 / LINK_RATE
    return {bit: 2 * amount, bit - 1: amount} if bit == bits - 1 else {bit: amount}


def choose_orders(parts, bits):
    last = bits - 1
    options = [(0, 1, 2, last), (1, 0, 2, last), (2, 0, 1, last), (2, 1, 0, last)]
    load = dict.fromkeys(range(bits), 0.0)
    for part in parts:
        best = None
        for order in options:
            part.order = order
            trial = dict(load)
            for step in range(2 * bits - 1):
                for bit, amount in link_cost(part, step, bits).items():
                    trial[bit] += amount
            score = sum(value * value for value in trial.values())
            if best is None or score < best[0]:
                best = (score, order, trial)
        _, part.order, load = best


def plan_transfers(parts, bits, spans):
    steps = 2 * bits - 1
    busy = dict.fromkeys(range(bits), 0.0)
    left = [part.first for part in parts]
    since = [None] * len(parts)
    flying = []

    def rest(p):
        return sum(max(link_cost(parts[p], s, bits).values()) + HOP_TIME for s in range(left[p], steps))

    def serve(clock, ahead, slack, found):
        for entry in sorted(flying):
            if entry[0] + slack <= clock:
                flying.remove(entry)
                p = entry[1]
                found.append(("take", p, left[p]))
                clock += TAKE_TIME
                if left[p] < bits:
                    clock += step_shape(parts[p], left[p], bits)[1] * parts[p].cols * 2e-6 / ADD_RATE
                left[p] += 1
                since[p] = clock if left[p] < steps else None
        waiting = [p for p in range(len(parts)) if since[p] is not None]
        for p in sorted(waiting, key=lambda p: (-parts[p].ready[0], -rest(p), p)):
            cost = link_cost(parts[p], left[p], bits)
            if since[p] <= clock and all(busy[b] <= clock + ahead for b in cost):
                done = clock
                for b, amount in cost.items():
                    busy[b] = max(busy[b], clock) + amount
                    done = max(done, busy[b])
                clock += SEND_TIME
                found.append(("send", p, left[p]))
                flying.append((done + HOP_TIME, p))
                since[p] = None
        return clock

    slots, clock = [], 0.0
    for unit, span in enumerate(spans):
        for p, part in enumerate(parts):
            if part.ready[0] == unit:
                since[p] = clock + part.ready[1]
        found = []
        clock = serve(clock, span + AHEAD, SLACK, found)
        slots.append(found)
        clock += span
    for p, part in enumerate(parts):
        if part.ready[0] >= len(spans):
            since[p] = clock + part.ready[1]
    found = []
    while flying or any(value is not None for value in since):
        before = len(found)
        clock = serve(clock, LAST_AHEAD, 0.0, found)
        if len(found) == before:
            clock += 0.05
    slots.append(found)
    return slots


class RowsSum:
    def __init__(self, parts, bits, held, landing, final, outs, send_sem, land_sem, store_sem):
        self.parts, self.bits = parts, bits
        self.held, self.landing, self.final, self.outs = held, landing, final, outs
        self.send_sem, self.land_sem, self.store_sem = send_sem, land_sem, store_sem
        self.begin = [lambda: None] * len(parts)

    def side(self, bit):
        return lax.shift_right_logical(lax.axis_index("rows"), bit) & 1

    def peer(self, bit):
        me = lax.axis_index("rows")
        return {"rows": me + (1 << bit) - 2 * (me & (1 << bit)), "heads": lax.axis_index("heads")}

    def offset(self, p, depth):
        part, total = self.parts[p], jnp.int32(0)
        for d in range(depth):
            total = total + self.side(part.order[d]) * (part.rows >> (d + 1))
        return total

    def copy(self, p, step):
        part = self.parts[p]
        bit, size = step_shape(part, step, self.bits)
        if step < self.bits - 1:
            first = self.offset(p, step) + (1 - self.side(bit)) * size
        else:
            first = self.offset(p, min(step, 2 * self.bits - 2 - step) + (step >= self.bits))
        rows = pl.ds(pl.multiple_of(first, 16), size)
        if step < self.bits:
            source = self.held[p].at[rows, :]
            dest = self.landing[p].at[pl.ds(self.spot(p, step), size), :]
        else:
            source = self.final[p].at[rows, :]
            dest = source
        return pltpu.make_async_remote_copy(
            src_ref=source, dst_ref=dest, send_sem=self.send_sem.at[p, step],
            recv_sem=self.land_sem.at[p, step], device_id=self.peer(bit),
            device_id_type=pl.DeviceIdType.MESH,
        )

    def spot(self, p, step):
        part = self.parts[p]
        return part.rows - (part.rows >> step)

    def absorb(self, p, step):
        part = self.parts[p]
        size = step_shape(part, step, self.bits)[1]
        depth = min(step + 1, self.bits - 1)
        mine = pl.ds(pl.multiple_of(self.offset(p, depth), 16), size)
        spot = pl.ds(self.spot(p, step), size)
        total = self.held[p][mine, :].astype(F32) + self.landing[p][spot, :].astype(F32)
        dest = self.final[p] if step == self.bits - 1 else self.held[p]
        dest[mine, :] = total.astype(BF16)

    def store(self, p):
        part = self.parts[p]
        return pltpu.make_async_copy(
            self.final[p], self.outs[part.out].at[part.window()], self.store_sem.at[p]
        )

    def run(self, ops):
        for kind, p, step in ops:
            if kind == "send":
                if step == self.parts[p].first:
                    self.begin[p]()
                self.copy(p, step).start()
                continue
            self.copy(p, step).wait()
            if step < self.bits:
                self.absorb(p, step)
            elif step == 2 * self.bits - 2:
                self.store(p).start()


def add_into(dest, other):
    dest[...] = (dest[...].astype(F32) + other[...].astype(F32)).astype(dest.dtype)


def back_unit(qx, kx, vx, gx, dq, kt, sk, sv, head, rows, queries):
    scale = LOG2_E * HEAD_DIM**-0.5
    keys = kx[head, rows, :]
    query = qx[head, queries, :]
    grads = gx[head, queries, :]
    weights = jnp.exp2(dot_nt(keys, query) * scale)
    raised = dot_nt(vx[head, rows, :], grads)
    value_slab = dot(weights.astype(BF16), grads)
    inner = (weights * raised).astype(BF16)
    key_slab = dot(inner, query) * (HEAD_DIM**-0.5)
    dq[head, :, queries] += dot(kt[head, :, rows], inner)
    merge_head(sk, rows, head, key_slab)
    merge_head(sv, rows, head, value_slab)


def tail_kernel(parts, bits, plan, gain, small_in, *refs):
    rest = list(refs)
    take = lambda number: [rest.pop(0) for _ in range(number)]
    (gq_in, grad_mid_in, first_low_in, normed_in, dev_in, wq0_in, wq1_in, ctx1_in,
     wo0_in, wo1_in, qx_in, kx_in, vx_in, ctx_in, x_in, w_in, esk_in, esv_in, ekv_in) = take(19)
    ffn_out_own, ffn_in_own, cross_own, kv_own, *arrived = take(7)
    outs = take(7)
    small_out, in_keep, in_land_out, enc_keep, enc_out = take(5)
    count = len(parts)
    held, landing, final = take(count), take(count), take(count)
    mates = dict(zip([p for p in range(count) if parts[p].out in (3, 5)], rest))
    take(len(mates))
    (gq, gq_land, grad_mid, first_low, normed, dev, wq0, wq1, ctx0, ctx1, wo0, wo1, qx, kx, vx, ctx, x_ref, w_ref,
     grad, gx, dq, kt, sums, sq, sk, sv, wide, low, back_out, query_out, self_out, in_out, in_land, small_land, base, in_held, esk, esv, ekv, enc_gone, enc_held) = take(41)
    (send_sem, land_sem, store_sem, load_sem, part_sem, mate_send, mate_land, core_send, core_land,
     small_send, small_sem, out_sem) = rest
    share, width = grad_mid.shape
    length = x_ref.shape[0]
    heads = qx.shape[0]
    block = 256
    me, core = lax.axis_index("rows"), lax.axis_index("heads")
    other_core = {"rows": me, "heads": 1 - core}
    mine_rows = core_half(core, share)
    summing = RowsSum(parts, bits, held, landing, final, outs, send_sem, land_sem, store_sem)

    def across(source, dest, send, land, peer=other_core):
        return pltpu.make_async_remote_copy(
            src_ref=source, dst_ref=dest, send_sem=send, recv_sem=land,
            device_id=peer, device_id_type=pl.DeviceIdType.MESH,
        )

    pairs = [
        (gq_in.at[mine_rows, :], gq), (grad_mid_in, grad_mid), (wq0_in, wq0), (wq1_in, wq1), (normed_in, normed), (dev_in, dev),
        (wo0_in, wo0), (wo1_in, wo1), (first_low_in, first_low), (ctx_in.at[mine_rows, :], ctx0), (ctx1_in, ctx1), (ctx_in, ctx),
        (qx_in, qx), (kx_in, kx), (vx_in, vx), (x_in, x_ref), (w_in, w_ref),
        (esk_in, esk), (esv_in, esv), (ekv_in, ekv),
    ]
    loads = [pltpu.make_async_copy(a, b, load_sem.at[k]) for k, (a, b) in enumerate(pairs)]
    own_arrays = {0: ffn_out_own, 1: ffn_in_own, 2: cross_own, 4: kv_own}
    early = {id(part): (bit, spot) for part, bit, spot in first_steps(parts)[0]}
    peers = [summing.peer(bit) for bit in range(bits)] + [other_core]
    barrier = pltpu.get_barrier_semaphore()
    for peer in peers:
        pl.semaphore_signal(barrier, inc=1, device_id=peer, device_id_type=pl.DeviceIdType.MESH)
    part_loads, mate_copies = {}, {}
    for p, part in enumerate(parts):
        part_loads[p] = []
        if part.first:
            half = part.rows // 2
            bit, spot = early[id(part)]
            keep = part.row + summing.side(bit) * half
            rows = pl.ds(pl.multiple_of(keep, 128), half)
            here = pl.ds(pl.multiple_of(keep - part.row, 128), half)
            moves = [(own_arrays[part.out].at[rows, pl.ds(part.col, part.cols)], held[p].at[here, :])]
            for piece in range(half // 128):
                window = away_place(part, spot, piece)
                moves.append((arrived[bit].at[window], landing[p].at[pl.ds(piece * 128, 128), :]))
        elif part.out in own_arrays:
            moves = [(own_arrays[part.out].at[part.window()], held[p])]
        else:
            moves = []
        for k, (source, dest) in enumerate(moves):
            part_loads[p].append(pltpu.make_async_copy(source, dest, part_sem.at[p, k]))
            part_loads[p][-1].start()
    for load in loads[:6]:
        load.start()
    pl.semaphore_wait(barrier, len(peers))
    gq_copy = across(gq_in.at[core_half(1 - core, share), :], gq_land, core_send.at[0], core_land.at[0])
    gq_copy.start()
    enc_copy = across(
        enc_gone, enc_out, core_send.at[2 + share // block], core_land.at[2 + share // block]
    )
    for load in loads[6:]:
        load.start()
    for p, part in enumerate(parts):
        if part.out == 3:
            mate_copies[p] = across(query_out, mates[p], mate_send.at[p], mate_land.at[p])
        if part.out == 5:
            mate_copies[p] = across(self_out, mates[p], mate_send.at[p], mate_land.at[p])

        def begin(p=p):
            for load in part_loads[p]:
                load.wait()
            if parts[p].first:
                summing.absorb(p, 0)
            if p in mate_copies:
                mate_copies[p].wait()
                add_into(held[p], mates[p])

        summing.begin[p] = begin

    slots = list(plan)
    summing.run(slots.pop(0))
    for load in loads[:6]:
        load.wait()
    gq_copy.wait()
    for load in loads[6:8]:
        load.wait()
    small_out[...] = small_in[...]
    back_copies = []
    for index in range(share // block):
        summing.run(slots.pop(0))
        rows = pl.ds(index * block, block)
        mine = own_rows(share, index * block, block)
        value = grad_mid[rows, :] + dot_nt(gq[rows, :], wq0[...]) + dot_nt(gq_land[rows, :], wq1[...])
        back, gain_grad, bias_grad = norm_back(value, normed[rows, :], dev[rows, :], gain[0:1, :])
        small_out[0:1, :] += gain_grad
        small_out[3:4, :] += bias_grad
        base[rows, :] = back
        low_part = back.astype(BF16)
        low[rows, :] = low_part
        grad[mine, :] = dot_nt(low_part, wo0[...]).astype(BF16)
        back_out[rows, :] = dot_nt(low_part, wo1[...]).astype(BF16)
        copy = across(back_out.at[rows, :], grad.at[mine, :], core_send.at[1 + index], core_land.at[1 + index])
        copy.start()
        back_copies.append(copy)
    summing.run(slots.pop(0))
    for load in loads[8:12]:
        load.wait()
    query_out[...] = dot_tn(first_low[...], gq_land[...]).astype(BF16)
    self_out[...] = dot_tn(ctx1[...], low[...]).astype(BF16)
    for p, part in enumerate(parts):
        if part.out in (3, 5):
            mate_copies[p].start()
        if part.out == 3:
            held[p][...] = dot_tn(first_low[...], gq[...]).astype(BF16)
        if part.out == 5:
            held[p][...] = dot_tn(ctx0[...], low[...]).astype(BF16)
    summing.run(slots.pop(0))
    for copy in back_copies:
        copy.wait()
    for load in loads[12:17]:
        load.wait()
    sums[...] = head_sums(ctx.shape[1], heads)
    prepare_back(grad, ctx, kx, gx, dq, kt, sums)
    blocks = length // KEY_SPAN
    in_copy = across(in_out, in_land, core_send.at[1 + share // block], core_land.at[1 + share // block])
    for pair in range(heads // 2):
        mine = [slots.pop(0) for _ in range(2 * blocks)]

        def unit(index, carry):
            lax.switch(index, [functools.partial(summing.run, ops) for ops in mine])
            rows = pl.ds(pl.multiple_of(lax.rem(index, blocks) * KEY_SPAN, KEY_SPAN), KEY_SPAN)
            head = 2 * pair + lax.div(index, blocks)
            back_unit(qx, kx, vx, gx, dq, kt, sk, sv, head, rows, pl.ds(0, length))
            return carry

        lax.fori_loop(0, 2 * blocks, unit, 0)
        cols = pl.ds(pair * LANES, LANES)
        summing.run(slots.pop(0))
        turn_queries(dq, sq, [pair])
        for p, part in enumerate(parts):
            if part.out == 6 and part.col == pair * LANES:
                source = (sq, sk, sv)[part.row // width]
                held[p][...] = dot_tn(x_ref[...], source[:, cols]).astype(BF16)
    last = slots.pop(0)
    portion = (len(last) - 8) // (2 * (length // SPAN) + 2)

    def serve(number):
        summing.run(last[:number])
        del last[:number]

    def small_copy(k):
        return across(small_out, small_land.at[k], small_send.at[k], small_sem.at[k], peers[k])

    def small_step(k):
        if k:
            small_copy(k - 1).wait()
            small_out[...] += small_land[k - 1]
        if k < len(peers):
            small_copy(k).start()

    serve(8)
    small_step(0)

    def spread(index, carry):
        rows = pl.ds(pl.multiple_of(index * SPAN, SPAN), SPAN)
        value = dot_nt(sq[rows, :], w_ref[0]) + dot_nt(sk[rows, :], w_ref[1])
        wide[rows, :] = value + dot_nt(sv[rows, :], w_ref[2])
        serve(portion)
        if index % 3 == 2:
            small_step(1 + index // 3)

    unrolled(length // SPAN, spread)
    away = pl.ds(pl.multiple_of((1 - core) * share, share), share)
    in_out[...] = wide[away, :].astype(BF16)
    in_copy.start()
    here = pl.ds(pl.multiple_of(core * share, share), share)
    in_held[...] = (base[...] + wide[here, :]).astype(BF16)
    keep_store = pltpu.make_async_copy(in_held, in_keep, out_sem.at[1])
    keep_store.start()
    serve(portion)
    for load in loads[17:]:
        load.wait()

    def spread_encoder(index, carry):
        rows = pl.ds(pl.multiple_of(index * SPAN, SPAN), SPAN)
        wide[rows, :] = dot_nt(esk[rows, :], ekv[0]) + dot_nt(esv[rows, :], ekv[1])
        serve(portion)
        if index % 2 == 1:
            small_step(3 + index // 2)

    unrolled(length // SPAN, spread_encoder)
    enc_gone[...] = wide[away, :].astype(BF16)
    enc_copy.start()
    enc_held[...] = wide[here, :].astype(BF16)
    enc_store = pltpu.make_async_copy(enc_held, enc_keep, out_sem.at[2])
    enc_store.start()
    in_copy.wait()
    in_store = pltpu.make_async_copy(in_land, in_land_out, out_sem.at[0])
    in_store.start()
    serve(len(last))
    in_store.wait()
    keep_store.wait()
    enc_copy.wait()
    enc_store.wait()
    for p in range(count):
        summing.store(p).wait()


def widen_kernel(table, small, *refs):
    sources = 1 + max(max(e[0], -1 if e[1] is None else e[1]) for e in table)
    outs = 1 + max(e[2] for e in table)
    arrays, dests = refs[:sources], refs[sources : sources + outs]
    gain_out, bias_out = refs[sources + outs : sources + outs + 2]
    rest = list(refs[sources + outs + 2 :])
    low = [rest.pop(0) for _ in table]
    more = {k: rest.pop(0) for k, e in enumerate(table) if e[1] is not None}
    wide = [rest.pop(0) for _ in table]
    load_sem, more_sem, store_sem = rest
    loads, stores = [], []
    for k, (source, second, out, window) in enumerate(table):
        window = tuple(pl.ds(*w) for w in window)
        loads.append([pltpu.make_async_copy(arrays[source].at[window], low[k], load_sem.at[k])])
        if second is not None:
            loads[k].append(pltpu.make_async_copy(arrays[second].at[window], more[k], more_sem.at[k]))
        stores.append(pltpu.make_async_copy(wide[k], dests[out].at[window], store_sem.at[k]))
        for load in loads[k]:
            load.start()
    gain_out[...] = small[0:3, :]
    bias_out[...] = small[3:6, :]
    for k in range(len(table)):
        for load in loads[k]:
            load.wait()
        value = low[k][...].astype(F32)
        if k in more:
            value = value + more[k][...].astype(F32)
        wide[k][...] = value
        stores[k].start()
    for store in stores:
        store.wait()


def widen_all(small, entries):
    arrays, table, shapes = [], [], []
    for out, (first, second) in enumerate(entries):
        source = len(arrays)
        arrays.append(first)
        if second is not None:
            arrays.append(second)
        rows, cols = first.shape
        shapes.append(shape_of((rows, cols), F32))
        high = min(rows, 512 if cols >= 512 else 1024)
        high = high if rows % high == 0 else rows // 2
        for row in range(0, rows, high):
            table.append((source, None if second is None else source + 1, out, ((row, high), (0, cols))))
    spaces = [pl.BlockSpec(memory_space=pl.ANY)]
    sized = lambda e: (e[3][0][1], e[3][1][1])
    return pl.pallas_call(
        functools.partial(widen_kernel, table),
        out_shape=shapes + [shape_of((3, small.shape[1]), F32)] * 2,
        in_specs=[VMEM] + spaces * len(arrays),
        out_specs=spaces * len(shapes) + [VMEM] * 2,
        scratch_shapes=[pltpu.VMEM(sized(e), arrays[e[0]].dtype) for e in table]
        + [pltpu.VMEM(sized(e), arrays[e[1]].dtype) for e in table if e[1] is not None]
        + [pltpu.VMEM(sized(e), F32) for e in table]
        + [pltpu.SemaphoreType.DMA((len(table),))] * 3,
        compiler_params=pltpu.CompilerParams(vmem_limit_bytes=VMEM_BYTES),
    )(small, *arrays)


def unit_spans(share, heads):
    spans = [3.0] + [1.3] * (share // 256) + [1.8, 2.0]
    made = len(spans) - 1
    pair_end = []
    for _ in range(heads // 2):
        spans += [2.2] * (4 * share // KEY_SPAN) + [1.8]
        pair_end.append(len(spans))
    return spans, made, pair_end


def gradient_parts(shapes, share, heads, bits):
    spans, made, pair_end = unit_spans(share, heads)
    parts = []
    for out, (rows, cols) in enumerate(shapes):
        high, broad = (256, 512) if cols == 512 else (512, 256)
        if out < 2:
            high, broad = FFN_PART
        if out == 6:
            broad = LANES
        for col in range(0, cols, broad):
            for row in range(0, rows, high):
                ready = (0, 0.0)
                if out in (3, 5):
                    ready = (made, 1.0)
                if out == 6:
                    ready = (pair_end[col // LANES], 0.0)
                parts.append(Part(out, row, col, high, broad, ready))
                parts[-1].first = 1 if out < 2 else 0
    choose_orders(parts, bits)
    return parts


def run_tail(parts, gain, small, first_args, halves, shapes):
    bits = lax.axis_size("rows").bit_length() - 1
    length, local = first_args[0].shape
    width = first_args[1].shape[1]
    share = length // 2
    heads = local // HEAD_DIM
    norm_units = share // 256
    plan = plan_transfers(parts, bits, unit_spans(share, heads)[0])
    count = len(parts)
    buffers = [pltpu.VMEM((p.rows, p.cols), BF16) for p in parts]
    mated = [b for b, p in zip(buffers, parts) if p.out in (3, 5)]
    vm = lambda kind, *dims: pltpu.VMEM(dims, kind)
    wide_heads = vm(BF16, heads, length, LANES)
    own = [
        vm(BF16, share, local), vm(BF16, share, local), vm(F32, share, width), vm(BF16, share, width),
        vm(F32, share, width), vm(F32, share, 1), vm(BF16, width, local), vm(BF16, width, local),
        vm(BF16, share, local), vm(BF16, share, local), vm(BF16, local, width), vm(BF16, local, width),
        wide_heads, wide_heads, wide_heads, vm(BF16, length, local), vm(BF16, length, width),
        vm(BF16, 3, width, local),
        vm(BF16, length, local), wide_heads, vm(F32, heads, HEAD_DIM, length),
        vm(BF16, heads, HEAD_DIM, length), vm(BF16, local, heads * LANES),
        vm(BF16, length, local), vm(BF16, length, local), vm(BF16, length, local), vm(F32, length, width),
        vm(BF16, share, width), vm(BF16, share, local), vm(BF16, width, local), vm(BF16, local, width),
        vm(BF16, share, width), vm(BF16, share, width), vm(F32, bits + 1, 8, width),
        vm(F32, share, width), vm(BF16, share, width),
        vm(BF16, length, local), vm(BF16, length, local), vm(BF16, 2, width, local),
        vm(BF16, share, width), vm(BF16, share, width),
    ]
    sems = [
        (count, 2 * bits - 1), (count, 2 * bits - 1), (count,), (20,), (count, 5), (count,), (count,),
        (3 + norm_units,), (3 + norm_units,), (bits + 1,), (bits + 1,),
    ]
    anyspace = pl.BlockSpec(memory_space=pl.ANY)
    return pl.pallas_call(
        functools.partial(tail_kernel, parts, bits, plan),
        out_shape=[shape_of(dims, BF16) for dims in shapes]
        + [shape_of((8, width), F32)] + [shape_of((share, width), BF16)] * 4,
        in_specs=[VMEM] * 2 + [anyspace] * (len(first_args) + len(halves)),
        out_specs=[anyspace] * len(shapes) + [VMEM] + [anyspace] * 4,
        scratch_shapes=buffers * 3 + mated + own
        + [pltpu.SemaphoreType.DMA(dims) for dims in sems] + [pltpu.SemaphoreType.DMA((3,))],
        compiler_params=pltpu.CompilerParams(
            vmem_limit_bytes=VMEM_BYTES, collective_id=0, has_side_effects=True
        ),
    )(gain, small, *first_args, *halves)


def fits_tail(length, width, local, units):
    return (
        lax.axis_size("rows") == 16
        and lax.axis_size("heads") == 2
        and (width, local) == (512, 256)
        and length // SPAN == 6
        and units % 512 == 0
    )


def fast_body(
    dec_input, enc_output, dec_lengths, enc_lengths, w_self_qkv, w_self_out, w_cross_q, w_cross_kv,
    w_cross_out, w_ffn_in, w_ffn_out, norm_gain, norm_bias, out_grad,
):
    length, width = dec_input.shape
    local = w_self_out.shape[0]
    heads = local // HEAD_DIM
    share = length // 2
    units = w_ffn_in.shape[1]
    size = lax.axis_size("rows")
    bits = size.bit_length() - 1
    blocks = length // SPAN
    vm = lambda kind, *dims: pltpu.VMEM(dims, kind)
    low, full = (lambda *dims: shape_of(dims, BF16)), (lambda *dims: shape_of(dims, F32))
    wide_heads, wide_scratch = low(heads, length, LANES), vm(BF16, heads, length, LANES)
    sems = [pltpu.SemaphoreType.DMA((2, blocks)), pltpu.SemaphoreType.DMA((2,))]
    self_ctx, self_qx, self_kx, self_vx = call(
        self_forward_fast, [low(length, local), wide_heads, wide_heads, wide_heads],
        [vm(BF16, length, local), wide_scratch, wide_scratch, wide_scratch] + sems, 0,
        dec_lengths, dec_input, w_self_qkv, smem=1, out_far=4,
    )
    (first_out, first_low, first_normed, first_dev, query, cross_kx, cross_vx, far_ctx, far_self_out,
     far_cross_q, far_cross_out, far_ffn_in, far_ffn_out) = run_entry(
        enc_lengths, norm_gain, norm_bias,
        [dec_input, enc_output, w_cross_kv, self_ctx, w_self_out, w_cross_q, w_cross_out, w_ffn_in, w_ffn_out],
    )
    cross_ctx, cross_qx = call(
        cross_forward_fast, [low(length, local), wide_heads],
        [vm(BF16, length, local), wide_scratch, wide_scratch, wide_scratch] + sems, 0,
        dec_lengths, enc_lengths, query, cross_kx, cross_vx, smem=2, far=2, out_far=2,
    )
    shapes = [
        (units, width), (width, units), (local, width), (width, local),
        (2 * width, local), (local, width), (3 * width, local),
    ]
    pieces = gradient_parts(shapes, share, heads, bits)
    (layer_out, grad_mid, small, g_ffn_out, g_ffn_in, g_cross_out, cross_grad, *away) = run_middle(
        pieces, norm_gain, norm_bias,
        [first_out, out_grad, cross_ctx, w_cross_out, far_cross_out, w_ffn_in, far_ffn_in,
         w_ffn_out, far_ffn_out], units,
    )
    arrived = [
        lax.ppermute(value, "rows", [(r, r ^ (1 << bit)) for r in range(size)])
        for bit, value in enumerate(away)
    ]
    flat = vm(BF16, length, local)
    gq, cross_sk, cross_sv, g_cross_kv, layer_out = call(
        cross_back_fast,
        [low(length, local), low(length, local), low(length, local), low(2, width, local), full(share, width)],
        [flat, flat, wide_scratch, wide_scratch, wide_scratch, vm(BF16, length, width),
         vm(F32, share, width), wide_scratch, vm(F32, heads, HEAD_DIM, length),
         vm(BF16, heads, HEAD_DIM, length), vm(BF16, local, heads * LANES), flat, flat, flat,
         pltpu.SemaphoreType.DMA((7,)), pltpu.SemaphoreType.DMA((4,))],
        0, dec_lengths, enc_lengths, cross_grad, cross_ctx, cross_kx, cross_vx, cross_qx, enc_output,
        layer_out, smem=2, far=7, out_places=(0, 1, 2, 4),
    )
    *sums, small, in_keep, in_land, enc_keep, enc_land = run_tail(
        pieces, norm_gain, small,
        [gq, grad_mid, first_low, first_normed, first_dev, w_cross_q, far_cross_q, far_ctx,
         w_self_out, far_self_out, self_qx, self_kx, self_vx, self_ctx, dec_input, w_self_qkv,
         cross_sk, cross_sv, w_cross_kv],
        [g_ffn_out, g_ffn_in, g_cross_out, g_cross_kv.reshape(2 * width, local), *arrived],
        shapes,
    )
    (s_ffn_out, s_ffn_in, s_cross_out, s_cross_q, s_cross_kv, s_self_out, s_self_qkv,
     input_grad, enc_grad, gain_grad, bias_grad) = widen_all(
        small, [(value, None) for value in sums] + [(in_keep, in_land), (enc_keep, enc_land)]
    )
    return (
        layer_out, input_grad, enc_grad, s_self_qkv.reshape(3, width, local), s_self_out, s_cross_q,
        s_cross_kv.reshape(2, width, local), s_cross_out, s_ffn_in, s_ffn_out, gain_grad, bias_grad,
    )


def body(*args):
    dec_input, w_self_out, w_ffn_in = args[0], args[5], args[9]
    if fits_tail(*dec_input.shape, w_self_out.shape[0], w_ffn_in.shape[1]):
        return fast_body(*args)
    return plain_body(*args)


def plain_body(
    dec_input,
    enc_output,
    dec_lengths,
    enc_lengths,
    w_self_qkv,
    w_self_out,
    w_cross_q,
    w_cross_kv,
    w_cross_out,
    w_ffn_in,
    w_ffn_out,
    norm_gain,
    norm_bias,
    out_grad,
):
    parts = lax.axis_size("heads")
    length, width = dec_input.shape
    local = w_self_out.shape[0]
    heads = local // HEAD_DIM
    share = length // parts
    units = w_ffn_in.shape[1]
    chunk = min(256, units)
    chunks = parts * units // chunk

    def shift(value, k):
        return lax.ppermute(value, "heads", [(d, (d + k) % parts) for d in range(parts)])

    def slots(shard):
        return [shard] + [shift(shard, parts - k) for k in range(1, parts)]

    def swap(keep, send):
        return [keep] + [shift(send[parts - k - 1], parts - k) for k in range(1, parts)]

    def collect(keep, send):
        total = keep.astype(F32)
        for k in range(1, parts):
            total = total + shift(send[k - 1], k).astype(F32)
        return total

    self_out, cross_q, cross_out = slots(w_self_out), slots(w_cross_q), slots(w_cross_out)
    ffn_in, ffn_out = slots(w_ffn_in), slots(w_ffn_out)

    def sent(*dims, kind=BF16):
        return shape_of((parts - 1, *dims), kind)

    def own(*dims, kind=BF16):
        return shape_of(dims, kind)

    wide_heads = own(heads, length, LANES)
    self_keep, self_send, self_ctx, self_qx, self_kx, self_vx = call(
        self_forward_kernel,
        [own(share, local), sent(share, local), own(length, local), wide_heads, wide_heads, wide_heads],
        [], 40, dec_lengths, dec_input, w_self_qkv, smem=1,
    )
    self_slots = swap(self_keep, self_send)
    cross_kx, cross_vx = call(
        cross_keys_kernel, [wide_heads, wide_heads], [], 32,
        enc_lengths, enc_output, w_cross_kv, smem=1,
    )
    first_out, first_low, first_normed, first_dev, query_keep, query_send = call(
        functools.partial(first_norm_kernel, parts),
        [own(share, width, kind=F32), own(share, width), own(share, width, kind=F32),
         own(share, 1, kind=F32), own(share, local), sent(share, local)],
        [], 32, dec_input, norm_gain, norm_bias, *self_slots, *self_out, *cross_q,
    )
    cross_keep, cross_send, cross_ctx, cross_qx = call(
        functools.partial(cross_forward_kernel, parts),
        [own(share, local), sent(share, local), own(length, local), wide_heads],
        [pltpu.VMEM((length, local), BF16)], 40,
        dec_lengths, enc_lengths, cross_kx, cross_vx, *swap(query_keep, query_send), smem=2,
    )
    cross_slots = swap(cross_keep, cross_send)
    (layer_out, grad_mid, gains_high, biases_high, g_ffn_out, g_ffn_out_send, g_ffn_in,
     g_ffn_in_send, g_cross_out, g_cross_out_send, back_keep, back_send) = call(
        functools.partial(middle_kernel, parts),
        [own(share, width, kind=F32), own(share, width, kind=F32),
         own(2, width, kind=F32), own(2, width, kind=F32),
         own(units, width), sent(units, width), own(width, units), sent(width, units),
         own(local, width), sent(local, width), own(share, local), sent(share, local)],
        [pltpu.VMEM((share, width), F32), pltpu.VMEM((share, width), BF16),
         pltpu.VMEM((share, width), F32), pltpu.VMEM((share, 1), F32),
         pltpu.VMEM((share, width), F32), pltpu.VMEM((chunks, share, chunk), BF16),
         pltpu.VMEM((chunks, share, chunk), F32), pltpu.VMEM((share, width), BF16),
         pltpu.VMEM((share, width), F32)],
        56, norm_gain, norm_bias, first_out, out_grad,
        *cross_slots, *cross_out, *ffn_in, *ffn_out,
    )
    grad_slots = swap(back_keep, back_send)
    back_scratch = [
        pltpu.VMEM((length, local), BF16),
        pltpu.VMEM((heads, length, LANES), BF16),
        pltpu.VMEM((heads, HEAD_DIM, length), F32),
        pltpu.VMEM((heads, HEAD_DIM, length), BF16),
        pltpu.VMEM((local, heads * LANES), BF16),
        pltpu.VMEM((length, local), BF16),
        pltpu.VMEM((length, local), BF16),
        pltpu.VMEM((length, local), BF16),
        pltpu.VMEM((length, width), F32),
    ]
    gq_keep, gq_send, g_cross_kv, enc_keep, enc_send = call(
        functools.partial(cross_back_kernel, len(grad_slots)),
        [own(share, local), sent(share, local), own(2, width, local),
         own(share, width, kind=F32), sent(share, width)],
        back_scratch, 56, dec_lengths, enc_lengths, cross_qx, cross_kx, cross_vx, cross_ctx,
        enc_output, w_cross_kv, *grad_slots, smem=2,
    )
    enc_grad = collect(enc_keep, enc_send)
    (grad_base, gains_low, biases_low, g_cross_q, g_cross_q_send, g_self_out, g_self_out_send,
     self_back_keep, self_back_send) = call(
        functools.partial(first_back_kernel, parts),
        [own(share, width, kind=F32), own(1, width, kind=F32), own(1, width, kind=F32),
         own(width, local), sent(width, local), own(local, width), sent(local, width),
         own(share, local), sent(share, local)],
        [pltpu.VMEM((share, width), BF16)], 40,
        norm_gain, grad_mid, first_low, first_normed, first_dev,
        *swap(gq_keep, gq_send), *cross_q, *self_slots, *self_out,
    )
    g_self_qkv, in_keep, in_send = call(
        functools.partial(self_back_kernel, parts),
        [own(3, width, local), own(share, width, kind=F32), sent(share, width)],
        back_scratch, 56, dec_lengths, self_qx, self_kx, self_vx, self_ctx, dec_input,
        w_self_qkv, *swap(self_back_keep, self_back_send), smem=1,
    )
    input_grad = grad_base + collect(in_keep, in_send)

    def over_rows(value):
        return lax.psum(value.astype(BF16), "rows").astype(F32)

    return (
        layer_out,
        input_grad,
        enc_grad,
        over_rows(g_self_qkv),
        over_rows(collect(g_self_out, g_self_out_send)),
        over_rows(collect(g_cross_q, g_cross_q_send)),
        over_rows(g_cross_kv),
        over_rows(collect(g_cross_out, g_cross_out_send)),
        over_rows(collect(g_ffn_in, g_ffn_in_send)),
        over_rows(collect(g_ffn_out, g_ffn_out_send)),
        lax.psum(jnp.concatenate([gains_low, gains_high]), ("rows", "heads")),
        lax.psum(jnp.concatenate([biases_low, biases_high]), ("rows", "heads")),
    )


def solution(mesh):
    in_specs = (
        P("rows", None),
        P("rows", None),
        P("rows", None),
        P("rows", None),
        P(None, None, "heads"),
        P("heads", None),
        P(None, "heads"),
        P(None, None, "heads"),
        P("heads", None),
        P(None, "heads"),
        P("heads", None),
        P(),
        P(),
        P("rows", None),
    )
    out_specs = (
        P(("rows", "heads"), None),
        P(("rows", "heads"), None),
        P(("rows", "heads"), None),
        P(None, None, "heads"),
        P("heads", None),
        P(None, "heads"),
        P(None, None, "heads"),
        P("heads", None),
        P(None, "heads"),
        P("heads", None),
        P(),
        P(),
    )
    return jax.shard_map(body, mesh=mesh, in_specs=in_specs, out_specs=out_specs, check_vma=False)
```
